32 devices in a mesh: wide: 16 (over z, y, core), narrow: 2 (over x).
Axes of the slice: x: 2, y: 2, z: 4, core: 2. Of those that a mesh axis runs over, the one named last changes fastest.
Arguments:
- tokens: bfloat16 [4096, 1024], P(('wide', 'narrow')), may hold values from -6 to 6
- cotangent: bfloat16 [4096, 1024], P(('wide', 'narrow')), may hold values from -6 to 6
- seq_lengths: int32 [16, 2], P('wide'), may hold values from 1 to 254, as said below
- bucket_map: int32 [128], replicated, may hold values from 0 to 31
- norm1_gain: float32 [1024], replicated, may hold values from 0.1 to 1.9
- norm1_bias: float32 [1024], replicated, may hold values from -3 to 3
- ema_rate: float32 [16, 1024], replicated, may hold values from 0.00390625 to 0.06
- ema_damp: float32 [16, 1024], replicated, may hold values from 0.5 to 1
- ema_in: float32 [16, 1024], replicated, may hold values from -6 to 6
- ema_out: float32 [16, 1024], replicated, may hold values from -1.5 to 1.5
- ema_skip: float32 [1024], replicated, may hold values from -6 to 6
- w_shared: bfloat16 [1024, 128], replicated, may hold values from -0.1875 to 0.1875
- qk_gain: float32 [2, 128], replicated, may hold values from -8 to 8
- qk_bias: float32 [2, 128], replicated, may hold values from -3 to 3
- rel_bias: float32 [32], replicated, may hold values from -4 to 4
- w_value: bfloat16 [1024, 2048], P(None, 'narrow'), may hold values from -0.1875 to 0.1875
- w_reset: bfloat16 [1024, 2048], P(None, 'narrow'), may hold values from -0.1875 to 0.1875
- w_mix: bfloat16 [2048, 1024], P('narrow'), may hold values from -0.5 to 0.5
- w_hidden: bfloat16 [1024, 1024], replicated, may hold values from -0.1875 to 0.1875
- w_update: bfloat16 [1024, 1024], replicated, may hold values from -0.1875 to 0.1875
- b_update: float32 [1024], replicated, may hold values from -4 to 4
- norm2_gain: float32 [1024], replicated, may hold values from 0.1 to 1.9
- norm2_bias: float32 [1024], replicated, may hold values from -3 to 3
- w_up: bfloat16 [1024, 4096], P(None, 'narrow'), may hold values from -0.1875 to 0.1875
- b_up: bfloat16 [4096], P('narrow'), may hold values from -3 to 3
- w_down: bfloat16 [4096, 1024], P('narrow'), may hold values from -0.09375 to 0.09375
Outputs:
- block_out: bfloat16 [4096, 1024], P(('wide', 'narrow'))
- grad_tokens: float32 [4096, 1024], P(('wide', 'narrow'))
- grad_norm1_gain: float32 [1024], replicated
- grad_norm1_bias: float32 [1024], replicated
- grad_ema_rate: float32 [16, 1024], replicated
- grad_ema_damp: float32 [16, 1024], replicated
- grad_ema_in: float32 [16, 1024], replicated
- grad_ema_out: float32 [16, 1024], replicated
- grad_ema_skip: float32 [1024], replicated
- grad_w_shared: float32 [1024, 128], replicated
- grad_qk_gain: float32 [2, 128], replicated
- grad_qk_bias: float32 [2, 128], replicated
- grad_rel_bias: float32 [32], replicated
- grad_w_value: float32 [1024, 2048], P(None, 'narrow')
- grad_w_reset: float32 [1024, 2048], P(None, 'narrow')
- grad_w_mix: float32 [2048, 1024], P('narrow')
- grad_w_hidden: float32 [1024, 1024], replicated
- grad_w_update: float32 [1024, 1024], replicated
- grad_b_update: float32 [1024], replicated
- grad_norm2_gain: float32 [1024], replicated
- grad_norm2_bias: float32 [1024], replicated
- grad_w_up: float32 [1024, 4096], P(None, 'narrow')
- grad_b_up: float32 [4096], P('narrow')
- grad_w_down: float32 [4096, 1024], P('narrow')
The draws below stay inside these ranges and needn't reach their ends.
Inputs may be any that keep to these rules, and one draw needn't show every extreme that they name: `seq_lengths`: in each group the two lengths leave at least one position of padding at the group's end; one of the two sequences starts on the group's first device and ends on its last.
All inputs are finite; a program needn't handle non-finite values.
Results may differ from the reference program's by a relative error of at most 0.02.
The reference program's roundings to bfloat16 on the way count: a program that leaves them out, or rounds other values in their place, can miss the bound.
Values may be sent and summed in bfloat16 or wider, within the bound.
A program may use at most 384 MiB of HBM per device.

```python
import math
import jax
import jax.numpy as jnp
from jax import lax

D = 1024
Z = 128
V = 2048
F = 4096
NDIM = 16
BLOCK = 128
NBUCK = 32
TOK_DEV = 128
GROUP_TOK = 256
GROUPS = 16
TOKENS = 4096


def draw_seq_lengths(key, part):
    key = jax.random.fold_in(key, 7)
    key_list = jax.random.split(key, 4)
    padding = jax.random.randint(key_list[0], (GROUPS,), 1, TOK_DEV // 2)
    shorter = jax.random.randint(key_list[1], (GROUPS,), 1, TOK_DEV // 2)
    chosen = jax.random.randint(key_list[2], (), 0, GROUPS)
    flipped = jax.random.randint(key_list[3], (GROUPS,), 0, 2)
    group_index = jnp.arange(GROUPS)
    padding = jnp.where(group_index == chosen, 1, padding)
    shorter = jnp.where(group_index == chosen, 1, shorter)
    longer = GROUP_TOK - padding - shorter
    first_len = jnp.where(flipped == 1, longer, shorter)
    second_len = jnp.where(flipped == 1, shorter, longer)
    return jnp.stack([first_len, second_len], axis=1).astype(jnp.int32)


def draw_bucket_map(key, part):
    key = jax.random.fold_in(key, 11)
    first_key, second_key = jax.random.split(key)
    buckets = jax.random.randint(first_key, (BLOCK,), 0, NBUCK)
    shuffled = jax.random.permutation(second_key, BLOCK)
    buckets = buckets.at[shuffled[0]].set(0)
    buckets = buckets.at[shuffled[1]].set(NBUCK - 1)
    return buckets.astype(jnp.int32)


def level_of(own_key, extent, pieces, least, high):
    loudness = 1.0
    for axis_at, blocks in pieces:
        draws = jax.random.uniform(jax.random.fold_in(jax.random.fold_in(own_key, 6), axis_at), (blocks,), jnp.float32, least / len(pieces), high / len(pieces))
        loudness = loudness * jnp.repeat(jnp.exp(draws), extent[axis_at] // blocks).reshape((-1,) + (1,) * (len(extent) - 1 - axis_at))
    return loudness


def noise(own_key, shape, scale, limit, cuts=(), kind=jnp.bfloat16):
    drawn = scale * jax.random.normal(own_key, shape, jnp.float32)
    if cuts:
        drawn = drawn * level_of(own_key, shape, cuts, -0.22, 0.18)
    return jnp.clip(drawn, -limit, limit).astype(kind)


def setup_inputs(seed: int = 0) -> dict:
    splits = jax.random.split(jax.random.key(seed), 27)
    return {
        "tokens": noise(splits[0], (TOKENS, D), 1.0, 6.0, ((0, 32),)),
        "cotangent": noise(splits[1], (TOKENS, D), 1.0, 6.0, ((0, 32),)),
        "seq_lengths": draw_seq_lengths(jax.random.fold_in(splits[26], 71), 0),
        "bucket_map": draw_bucket_map(jax.random.fold_in(splits[26], 71), 0),
        "norm1_gain": jnp.clip(1.0 + 0.18 * jax.random.normal(splits[4], (D,), jnp.float32), 0.1, 1.9),
        "norm1_bias": noise(splits[5], (D,), 0.5, 3.0, (), jnp.float32),
        "ema_rate": jnp.clip(jnp.exp(jax.random.uniform(splits[6], (NDIM, D), jnp.float32, math.log(0.00390625), math.log(0.06))), 0.00390625, 0.06),
        "ema_damp": jnp.clip(jax.random.uniform(splits[7], (NDIM, D), jnp.float32, 0.5, 1.0), 0.5, 1.0),
        "ema_in": noise(splits[8], (NDIM, D), 1.0, 6.0, (), jnp.float32),
        "ema_out": noise(splits[9], (NDIM, D), NDIM ** -0.5, 1.5, (), jnp.float32),
        "ema_skip": noise(splits[10], (D,), 1.0, 6.0, (), jnp.float32),
        "w_shared": noise(splits[11], (D, Z), D ** -0.5, 0.1875),
        "qk_gain": noise(splits[12], (2, Z), 2.0, 8.0, (), jnp.float32),
        "qk_bias": noise(splits[13], (2, Z), 0.5, 3.0, (), jnp.float32),
        "rel_bias": noise(splits[14], (NBUCK,), 1.0, 4.0, (), jnp.float32),
        "w_value": noise(splits[15], (D, V), D ** -0.5, 0.1875, ((1, 2),)),
        "w_reset": noise(splits[16], (D, V), D ** -0.5, 0.1875, ((1, 2),)),
        "w_mix": noise(splits[17], (V, D), (V // 16) ** -0.5, 0.5, ((0, 2),)),
        "w_hidden": noise(splits[18], (D, D), D ** -0.5, 0.1875),
        "w_update": noise(splits[19], (D, D), D ** -0.5, 0.1875),
        "b_update": noise(splits[20], (D,), 1.0, 4.0, (), jnp.float32),
        "norm2_gain": jnp.clip(1.0 + 0.18 * jax.random.normal(splits[21], (D,), jnp.float32), 0.1, 1.9),
        "norm2_bias": noise(splits[22], (D,), 0.5, 3.0, (), jnp.float32),
        "w_up": noise(splits[23], (D, F), D ** -0.5, 0.1875, ((1, 2),)),
        "b_up": noise(splits[24], (F,), 0.5, 3.0, ((0, 2),)),
        "w_down": noise(splits[25], (F, D), F ** -0.5, 0.09375, ((0, 2),)),
    }


EPSILON = 1e-05
NEGATIVE = -1000000000.0
HIGHEST = lax.Precision.HIGHEST

@jax.custom_vjp
def low(v):
    return lax.optimization_barrier(v.astype(jnp.bfloat16)).astype(jnp.float32)

@jax.custom_vjp
def low_back(v):
    return v

def low_keep(v):
    return (low(v), None)

def low_pass(kept, grad):
    return (grad,)

def back_keep(v):
    return (v, None)

def back_low(kept, grad):
    return (low(grad),)
low.defvjp(low_keep, low_pass)
low_back.defvjp(back_keep, back_low)

def matmul_high(left, right):
    return jnp.dot(left, right, precision=HIGHEST, preferred_element_type=jnp.float32)

def layer_norm(rows_in, gain, shift):
    row_mean = lax.optimization_barrier(jnp.mean(rows_in, axis=-1, keepdims=True))
    centred = rows_in - row_mean
    row_var = lax.optimization_barrier(jnp.mean(centred * centred, axis=-1, keepdims=True))
    return centred * lax.rsqrt(row_var + EPSILON) * gain + shift

def segment_info(lengths, positions):
    first_end = lengths[0]
    second_end = lengths[0] + lengths[1]
    segment = (positions >= first_end).astype(jnp.int32) + (positions >= second_end).astype(jnp.int32)
    starts = ((positions == 0) | (positions == first_end) | (positions == second_end)).astype(jnp.float32)
    live_rows = (segment < 2).astype(jnp.float32)
    return (segment, starts, live_rows)

def combine_pair(earlier, following):
    return (earlier[0] * following[0], earlier[1] * following[0] + following[1])

def ema_mix(normed, live_rows, starts, ema_rate, ema_damp, ema_in, ema_out, ema_skip):
    inputs = normed * live_rows[:, None]
    decay = (1.0 - ema_rate * ema_damp)[None] * (1.0 - starts)[:, None, None]
    drive = (ema_rate * ema_in)[None] * inputs[:, None, :]
    states = lax.associative_scan(combine_pair, (decay, drive), axis=0)[1]
    smooth = lax.optimization_barrier(jnp.sum(states * ema_out[None], axis=1))
    return jax.nn.silu(smooth + ema_skip * normed)

def block_bias(rel_bias, bucket_map):
    by_offset = jnp.take(rel_bias, bucket_map)
    row_index = jnp.arange(BLOCK, dtype=jnp.int32)
    offsets = row_index[:, None] - row_index[None, :]
    return (jnp.take(by_offset, jnp.clip(offsets, 0, BLOCK - 1)), offsets)

def attention(queries, keys_low, values, segment, rel_bias, bucket_map):
    row_count = queries.shape[0]
    blocks = row_count // BLOCK
    bias_table, offsets = block_bias(rel_bias, bucket_map)
    query_blocks = queries.reshape(blocks, BLOCK, -1)
    key_blocks = keys_low.reshape(blocks, BLOCK, -1)
    value_blocks = values.reshape(blocks, BLOCK, -1)
    seg_blocks = segment.reshape(blocks, BLOCK)
    allowed = (seg_blocks[:, :, None] == seg_blocks[:, None, :]) & (offsets >= 0)[None]
    score_scale = queries.shape[-1] ** (-0.5)
    scores = jnp.einsum('bik,bjk->bij', query_blocks, key_blocks, precision=HIGHEST) * score_scale
    scores = low_back(scores + bias_table[None])
    scores = jnp.where(allowed, scores, NEGATIVE)
    row_max = lax.optimization_barrier(jnp.max(scores, axis=-1, keepdims=True))
    weighted = jnp.exp(scores - row_max)
    prob_low = low(weighted / lax.optimization_barrier(jnp.sum(weighted, axis=-1, keepdims=True)))
    attended = jnp.einsum('bij,bjv->biv', prob_low, value_blocks, precision=HIGHEST)
    return attended.reshape(row_count, -1)

def forward(tokens_in, weights, lengths, bucket_map):
    norm1_gain, norm1_bias, ema_rate, ema_damp, ema_in, ema_out, ema_skip, w_shared, qk_gain, qk_bias, rel_bias, w_value, w_reset, w_mix, w_hidden, w_update, b_update, norm2_gain, norm2_bias, w_up, b_up, w_down = weights
    positions = jnp.arange(tokens_in.shape[0], dtype=jnp.int32)
    segment, starts, live_rows = segment_info(lengths, positions)
    normed = layer_norm(tokens_in, norm1_gain, norm1_bias)
    ema_mixed = ema_mix(normed, live_rows, starts, ema_rate, ema_damp, ema_in, ema_out, ema_skip)
    normed_low = low(normed)
    mixed_low = low(ema_mixed)
    pre_shared = low_back(matmul_high(mixed_low, w_shared))
    shared = jax.nn.silu(pre_shared)
    queries = low(shared * qk_gain[0] + qk_bias[0])
    keys_low = low(shared * qk_gain[1] + qk_bias[1])
    pre_value = low_back(matmul_high(normed_low, w_value))
    values = low(jax.nn.silu(pre_value))
    pre_reset = low_back(matmul_high(mixed_low, w_reset))
    reset_gate = jax.nn.silu(pre_reset)
    attended = low_back(attention(queries, keys_low, values, segment, rel_bias, bucket_map))
    gated_low = low(reset_gate * attended)
    pre_hidden = low_back(matmul_high(mixed_low, w_hidden) + matmul_high(gated_low, w_mix))
    hidden_act = jax.nn.silu(pre_hidden)
    pre_update = low_back(matmul_high(mixed_low, w_update) + b_update)
    update_gate = jax.nn.sigmoid(pre_update)
    blended = update_gate * hidden_act + (1.0 - update_gate) * tokens_in
    normed2 = low(layer_norm(blended, norm2_gain, norm2_bias))
    pre_up = low_back(matmul_high(normed2, w_up) + b_up)
    up_low = low(jax.nn.silu(pre_up))
    return blended + matmul_high(up_low, w_down)

def reference(tokens, cotangent, seq_lengths, bucket_map, norm1_gain, norm1_bias, ema_rate, ema_damp, ema_in, ema_out, ema_skip, w_shared, qk_gain, qk_bias, rel_bias, w_value, w_reset, w_mix, w_hidden, w_update, b_update, norm2_gain, norm2_bias, w_up, b_up, w_down):
    weights = tuple((item.astype(jnp.float32) for item in (norm1_gain, norm1_bias, ema_rate, ema_damp, ema_in, ema_out, ema_skip, w_shared, qk_gain, qk_bias, rel_bias, w_value, w_reset, w_mix, w_hidden, w_update, b_update, norm2_gain, norm2_bias, w_up, b_up, w_down)))
    token_groups = tokens.astype(jnp.float32).reshape(GROUPS, GROUP_TOK, D)
    cot_groups = cotangent.astype(jnp.float32).reshape(GROUPS, GROUP_TOK, D)

    def one_group(totals, items):
        group_tokens, group_cot, lengths = items
        live_rows = segment_info(lengths, jnp.arange(GROUP_TOK, dtype=jnp.int32))[2]

        def wrapped(tokens_in, weight_tuple):
            return forward(tokens_in, weight_tuple, lengths, bucket_map)
        out_values, backward = jax.vjp(wrapped, group_tokens, weights)
        grad_rows, grad_weights = backward(group_cot * live_rows[:, None])
        totals = jax.tree.map(lambda summed, addend: summed + addend, totals, grad_weights)
        return (totals, (out_values.astype(jnp.bfloat16), grad_rows))
    zero_grads = jax.tree.map(jnp.zeros_like, weights)
    totals, (out_rows, grad_rows) = lax.scan(one_group, zero_grads, (token_groups, cot_groups, seq_lengths))
    return (out_rows.reshape(TOKENS, D), grad_rows.reshape(TOKENS, D), totals[0], totals[1], totals[2], totals[3], totals[4], totals[5], totals[6], totals[7], totals[8], totals[9], totals[10], totals[11], totals[12], totals[13], totals[14], totals[15], totals[16], totals[17], totals[18], totals[19], totals[20], totals[21])
```

```python
import jax
import jax.numpy as jnp
from jax import lax
from jax.experimental import pallas as pl
from jax.experimental.pallas import tpu as pltpu
from jax.sharding import PartitionSpec as P

BLOCK = 128


EPSILON = 1e-05
NEGATIVE = -1000000000.0


def carried_in(part, axis, combine, identity, reverse):
    count = lax.axis_size(axis)
    place = lax.axis_index(axis)
    ahead = count - 1 - place if reverse else place
    gathered = jax.tree.map(lambda a: lax.all_gather(a, axis), part)
    state = jax.tree.map(lambda a, e: jnp.zeros_like(a) + jnp.asarray(e, a.dtype), part, identity)

    def one(lap, state):
        source = count - 1 - lap if reverse else lap
        return combine(
            state, jax.tree.map(lambda a: lax.dynamic_index_in_dim(a, source, 0, False), gathered)
        )

    return lax.fori_loop(0, ahead, one, state)


def layer_norm(rows_in, gain, shift):
    row_mean = jnp.mean(rows_in, axis=-1, keepdims=True)
    centred = rows_in - row_mean
    row_var = jnp.mean(centred * centred, axis=-1, keepdims=True)
    return centred * lax.rsqrt(row_var + EPSILON) * gain + shift


def silu_slope(pre_act):
    sigmoid_val = jax.nn.sigmoid(pre_act)
    return sigmoid_val * (1.0 + pre_act * (1.0 - sigmoid_val))


def segment_info(lengths, positions):
    first_end = lengths[0]
    second_end = lengths[0] + lengths[1]
    segment = (positions >= first_end).astype(jnp.int32) + (positions >= second_end).astype(
        jnp.int32
    )
    starts = ((positions == 0) | (positions == first_end) | (positions == second_end)).astype(
        jnp.float32
    )
    live_rows = (segment < 2).astype(jnp.float32)
    return (segment, starts, live_rows)


def combine_pair(earlier, following):
    return (earlier[0] * following[0], earlier[1] * following[0] + following[1])


def ema_local(normed, live_rows, starts, ema_rate, ema_damp, ema_in, ema_out, ema_skip, state_in):
    inputs = normed * live_rows[:, None]
    keep_rate = 1.0 - ema_rate * ema_damp
    drive_rate = ema_rate * ema_in
    decay = keep_rate[None] * (1.0 - starts)[:, None, None]
    drive = drive_rate[None] * inputs[:, None, :]
    decay_cum, partial_state = lax.associative_scan(combine_pair, (decay, drive), axis=0)
    states = partial_state + decay_cum * state_in[None]
    smooth = jnp.sum(states * ema_out[None], axis=1)
    ema_mixed = jax.nn.silu(smooth + ema_skip * normed)
    return (ema_mixed, states[-1])


def block_bias(rel_bias, bucket_map):
    by_offset = jnp.take(rel_bias, bucket_map)
    row_index = jnp.arange(BLOCK, dtype=jnp.int32)
    offsets = row_index[:, None] - row_index[None, :]
    return (jnp.take(by_offset, jnp.clip(offsets, 0, BLOCK - 1)), offsets)


def attention_probs(query_all, key_all, segment_all, bias_table, offsets):
    blocks = query_all.shape[0] // BLOCK
    query_blocks = query_all.reshape(blocks, BLOCK, -1)
    key_blocks = key_all.reshape(blocks, BLOCK, -1)
    seg_blocks = segment_all.reshape(blocks, BLOCK)
    allowed = (seg_blocks[:, :, None] == seg_blocks[:, None, :]) & (offsets >= 0)[None]
    score_scale = query_all.shape[-1] ** (-0.5)
    scores = (
        jnp.einsum("bik,bjk->bij", query_blocks, key_blocks, preferred_element_type=jnp.float32)
        * score_scale
    )
    scores = jnp.where(allowed, scores + bias_table[None], NEGATIVE)
    row_max = jnp.max(scores, axis=-1, keepdims=True)
    weighted = jnp.exp(scores - row_max)
    return weighted / jnp.sum(weighted, axis=-1, keepdims=True)


def shards(
    tokens,
    cotangent,
    seq_lengths,
    bucket_map,
    norm1_gain,
    norm1_bias,
    ema_rate,
    ema_damp,
    ema_in,
    ema_out,
    ema_skip,
    w_shared,
    qk_gain,
    qk_bias,
    rel_bias,
    w_value,
    w_reset,
    w_mix,
    w_hidden,
    w_update,
    b_update,
    norm2_gain,
    norm2_bias,
    w_up,
    b_up,
    w_down,
):
    row_count = tokens.shape[0]
    narrow_count = lax.axis_size("narrow")
    narrow_rank = lax.axis_index("narrow")
    group_rows = row_count * narrow_count
    blocks = group_rows // BLOCK
    local_blocks = row_count // BLOCK
    lengths = seq_lengths[0]
    local_positions = narrow_rank * row_count + jnp.arange(row_count, dtype=jnp.int32)
    segment_local, starts, live_rows = segment_info(lengths, local_positions)
    segment_all = segment_info(lengths, jnp.arange(group_rows, dtype=jnp.int32))[0]
    tokens_f = tokens.astype(jnp.float32)
    normed, norm1_back = jax.vjp(layer_norm, tokens_f, norm1_gain, norm1_bias)

    def ema_apply(normed_in, rate_in, damp_in, in_weight, out_weight, skip_in, state_in):
        return ema_local(
            normed_in, live_rows, starts, rate_in, damp_in, in_weight, out_weight, skip_in, state_in
        )

    zero_state = jnp.zeros_like(ema_rate)
    ones_state = jnp.ones_like(ema_rate)
    local_final = ema_apply(normed, ema_rate, ema_damp, ema_in, ema_out, ema_skip, zero_state)[1]
    through = jnp.power(1.0 - ema_rate * ema_damp, row_count) * (1.0 - jnp.max(starts))
    state_in = carried_in(
        (through, local_final), "narrow", combine_pair, (ones_state, zero_state), False
    )[1]
    (ema_mixed, final_state), ema_back = jax.vjp(
        ema_apply, normed, ema_rate, ema_damp, ema_in, ema_out, ema_skip, state_in
    )
    normed_low = normed.astype(jnp.bfloat16)
    mixed_low = ema_mixed.astype(jnp.bfloat16)
    pre_shared = jnp.dot(mixed_low, w_shared, preferred_element_type=jnp.float32)
    shared_act = jax.nn.silu(pre_shared)
    query_low = (shared_act * qk_gain[0] + qk_bias[0]).astype(jnp.bfloat16)
    key_low = (shared_act * qk_gain[1] + qk_bias[1]).astype(jnp.bfloat16)
    normed_all, mixed_all, query_all, key_all = (
        lax.all_gather(normed_low, "narrow", axis=0, tiled=True),
        lax.all_gather(mixed_low, "narrow", axis=0, tiled=True),
        lax.all_gather(query_low, "narrow", axis=0, tiled=True),
        lax.all_gather(key_low, "narrow", axis=0, tiled=True),
    )
    bias_table, offsets = block_bias(rel_bias, bucket_map)
    probs_low = attention_probs(query_all, key_all, segment_all, bias_table, offsets).astype(
        jnp.bfloat16
    )
    pre_value = jnp.dot(normed_all, w_value, preferred_element_type=jnp.float32)
    value_low = jax.nn.silu(pre_value).astype(jnp.bfloat16)
    value_blocks = value_low.reshape(blocks, BLOCK, -1)
    pre_reset = jnp.dot(mixed_all, w_reset, preferred_element_type=jnp.float32)
    reset_gate = jax.nn.silu(pre_reset)
    attended = jnp.einsum(
        "bij,bjv->biv", probs_low, value_blocks, preferred_element_type=jnp.float32
    ).reshape(group_rows, -1)
    gated_low = (reset_gate * attended).astype(jnp.bfloat16)
    piece = gated_low
    mix_part = lax.psum_scatter(
        jnp.dot(piece, w_mix, preferred_element_type=jnp.float32),
        "narrow",
        scatter_dimension=0,
        tiled=True,
    )
    pre_hidden = jnp.dot(mixed_low, w_hidden, preferred_element_type=jnp.float32) + mix_part
    hidden_act = jax.nn.silu(pre_hidden)
    pre_update = jnp.dot(mixed_low, w_update, preferred_element_type=jnp.float32) + b_update
    update_gate = jax.nn.sigmoid(pre_update)
    blended = update_gate * hidden_act + (1.0 - update_gate) * tokens_f
    normed2, norm2_back = jax.vjp(layer_norm, blended, norm2_gain, norm2_bias)
    normed2_low = normed2.astype(jnp.bfloat16)
    grad_out = cotangent.astype(jnp.float32) * live_rows[:, None]
    grad_out_low = grad_out.astype(jnp.bfloat16)
    normed2_all = lax.all_gather(normed2_low, "narrow", axis=0, tiled=True)
    pre_up = jnp.dot(normed2_all, w_up, preferred_element_type=jnp.float32) + b_up.astype(
        jnp.float32
    )
    up_low = jax.nn.silu(pre_up).astype(jnp.bfloat16)
    piece = up_low
    ffn_out = lax.psum_scatter(
        jnp.dot(piece, w_down, preferred_element_type=jnp.float32),
        "narrow",
        scatter_dimension=0,
        tiled=True,
    )
    grad_out_all = lax.all_gather(grad_out_low, "narrow", axis=0, tiled=True)
    grad_up = jnp.einsum("sd,fd->sf", grad_out_all, w_down, preferred_element_type=jnp.float32)
    grad_pre_up = (grad_up * silu_slope(pre_up)).astype(jnp.bfloat16)
    grad_w_down = jnp.einsum("sf,sd->fd", up_low, grad_out_all, preferred_element_type=jnp.float32)
    grad_w_up = jnp.einsum(
        "sd,sf->df", normed2_all, grad_pre_up, preferred_element_type=jnp.float32
    )
    grad_b_up = jnp.sum(grad_pre_up.astype(jnp.float32), axis=0)
    piece = grad_pre_up
    grad_normed2 = lax.psum_scatter(
        jnp.einsum("sf,df->sd", piece, w_up, preferred_element_type=jnp.float32),
        "narrow",
        scatter_dimension=0,
        tiled=True,
    )
    block_out = (blended + ffn_out).astype(jnp.bfloat16)
    grad_blended_norm, grad_norm2_gain, grad_norm2_bias = norm2_back(grad_normed2)
    grad_blended = grad_out + grad_blended_norm
    grad_hidden = grad_blended * update_gate
    grad_gate = grad_blended * (hidden_act - tokens_f)
    grad_tokens = grad_blended * (1.0 - update_gate)
    grad_pre_update = (grad_gate * update_gate * (1.0 - update_gate)).astype(jnp.bfloat16)
    grad_pre_hidden = (grad_hidden * silu_slope(pre_hidden)).astype(jnp.bfloat16)
    grad_b_update = jnp.sum(grad_pre_update.astype(jnp.float32), axis=0)
    grad_w_update = jnp.einsum(
        "sd,se->de", mixed_low, grad_pre_update, preferred_element_type=jnp.float32
    )
    grad_w_hidden = jnp.einsum(
        "sd,se->de", mixed_low, grad_pre_hidden, preferred_element_type=jnp.float32
    )
    hidden_all = lax.all_gather(grad_pre_hidden, "narrow", axis=0, tiled=True)
    grad_w_mix = jnp.einsum("sv,sd->vd", gated_low, hidden_all, preferred_element_type=jnp.float32)
    grad_gated = jnp.einsum("sd,vd->sv", hidden_all, w_mix, preferred_element_type=jnp.float32)
    grad_reset = grad_gated * attended
    grad_attended = (grad_gated * reset_gate).astype(jnp.bfloat16)
    grad_pre_reset = (grad_reset * silu_slope(pre_reset)).astype(jnp.bfloat16)
    grad_w_reset = jnp.einsum(
        "sd,sv->dv", mixed_all, grad_pre_reset, preferred_element_type=jnp.float32
    )
    attended_blocks = grad_attended.reshape(blocks, BLOCK, -1)
    probs_again = attention_probs(query_all, key_all, segment_all, bias_table, offsets)
    grad_probs = jnp.einsum(
        "biv,bjv->bij", attended_blocks, value_blocks, preferred_element_type=jnp.float32
    )
    grad_value = jnp.einsum(
        "bij,biv->bjv",
        probs_again.astype(jnp.bfloat16),
        attended_blocks,
        preferred_element_type=jnp.float32,
    ).reshape(group_rows, -1)
    grad_pre_value = (grad_value * silu_slope(pre_value)).astype(jnp.bfloat16)
    grad_w_value = jnp.einsum(
        "sd,sv->dv", normed_all, grad_pre_value, preferred_element_type=jnp.float32
    )
    mixed_cols = jnp.einsum(
        "sv,dv->sd", grad_pre_reset, w_reset, preferred_element_type=jnp.float32
    )
    normed_cols = jnp.einsum(
        "sv,dv->sd", grad_pre_value, w_value, preferred_element_type=jnp.float32
    )
    probs_rows, mixed_back, normed_back = (
        lax.psum_scatter(
            grad_probs.reshape(group_rows, BLOCK), "narrow", scatter_dimension=0, tiled=True
        ),
        lax.psum_scatter(mixed_cols, "narrow", scatter_dimension=0, tiled=True),
        lax.psum_scatter(normed_cols, "narrow", scatter_dimension=0, tiled=True),
    )
    probs_local = lax.dynamic_slice_in_dim(probs_again, narrow_rank * local_blocks, local_blocks, 0)
    grad_probs_local = probs_rows.reshape(local_blocks, BLOCK, BLOCK)
    grad_scores = probs_local * (
        grad_probs_local - jnp.sum(grad_probs_local * probs_local, axis=-1, keepdims=True)
    )
    grad_scores_low = grad_scores.astype(jnp.bfloat16)
    score_scale = query_low.shape[-1] ** (-0.5)
    query_blocks = query_low.reshape(local_blocks, BLOCK, -1)
    key_blocks = key_low.reshape(local_blocks, BLOCK, -1)
    grad_query = (
        jnp.einsum(
            "bij,bjk->bik", grad_scores_low, key_blocks, preferred_element_type=jnp.float32
        ).reshape(row_count, -1)
        * score_scale
    )
    grad_key = (
        jnp.einsum(
            "bij,bik->bjk", grad_scores_low, query_blocks, preferred_element_type=jnp.float32
        ).reshape(row_count, -1)
        * score_scale
    )
    score_total = jnp.sum(grad_scores_low.astype(jnp.float32), axis=0)
    offset_hits = (offsets[:, :, None] == jnp.arange(BLOCK, dtype=jnp.int32)[None, None, :]).astype(
        jnp.float32
    )
    grad_offset = jnp.sum(score_total[:, :, None] * offset_hits, axis=(0, 1))
    bucket_hits = (
        bucket_map[:, None] == jnp.arange(rel_bias.shape[0], dtype=jnp.int32)[None, :]
    ).astype(jnp.float32)
    grad_rel_bias = jnp.sum(grad_offset[:, None] * bucket_hits, axis=0)
    grad_shared_act = grad_query * qk_gain[0] + grad_key * qk_gain[1]
    grad_qk_gain = jnp.stack(
        [jnp.sum(grad_query * shared_act, axis=0), jnp.sum(grad_key * shared_act, axis=0)]
    )
    grad_qk_bias = jnp.stack([jnp.sum(grad_query, axis=0), jnp.sum(grad_key, axis=0)])
    grad_pre_shared = (grad_shared_act * silu_slope(pre_shared)).astype(jnp.bfloat16)
    grad_w_shared = jnp.einsum(
        "sd,sz->dz", mixed_low, grad_pre_shared, preferred_element_type=jnp.float32
    )
    grad_mixed = (
        mixed_back
        + jnp.einsum("sz,dz->sd", grad_pre_shared, w_shared, preferred_element_type=jnp.float32)
        + jnp.einsum("se,de->sd", grad_pre_hidden, w_hidden, preferred_element_type=jnp.float32)
        + jnp.einsum("se,de->sd", grad_pre_update, w_update, preferred_element_type=jnp.float32)
    )
    direct = ema_back((grad_mixed, zero_state))
    later_state = carried_in(
        (through, direct[6]), "narrow", combine_pair, (ones_state, zero_state), True
    )[1]
    chained = ema_back((jnp.zeros_like(ema_mixed), later_state))
    grad_normed = normed_back + direct[0] + chained[0]
    grad_tokens_norm, grad_norm1_gain, grad_norm1_bias = norm1_back(grad_normed)
    grad_tokens = grad_tokens + grad_tokens_norm
    grad_ema_rate = direct[1] + chained[1]
    grad_ema_damp = direct[2] + chained[2]
    grad_ema_in = direct[3] + chained[3]
    grad_ema_out = direct[4] + chained[4]
    grad_ema_skip = direct[5] + chained[5]
    grad_w_value, grad_w_reset, grad_w_mix, grad_w_up, grad_b_up, grad_w_down = lax.psum(
        (grad_w_value, grad_w_reset, grad_w_mix, grad_w_up, grad_b_up, grad_w_down), "wide"
    )
    (
        grad_norm1_gain,
        grad_norm1_bias,
        grad_ema_rate,
        grad_ema_damp,
        grad_ema_in,
        grad_ema_out,
        grad_ema_skip,
        grad_w_shared,
        grad_qk_gain,
        grad_qk_bias,
        grad_rel_bias,
        grad_w_hidden,
        grad_w_update,
        grad_b_update,
        grad_norm2_gain,
        grad_norm2_bias,
    ) = lax.psum(
        (
            grad_norm1_gain,
            grad_norm1_bias,
            grad_ema_rate,
            grad_ema_damp,
            grad_ema_in,
            grad_ema_out,
            grad_ema_skip,
            grad_w_shared,
            grad_qk_gain,
            grad_qk_bias,
            grad_rel_bias,
            grad_w_hidden,
            grad_w_update,
            grad_b_update,
            grad_norm2_gain,
            grad_norm2_bias,
        ),
        ("wide", "narrow"),
    )
    return (
        block_out,
        grad_tokens,
        grad_norm1_gain,
        grad_norm1_bias,
        grad_ema_rate,
        grad_ema_damp,
        grad_ema_in,
        grad_ema_out,
        grad_ema_skip,
        grad_w_shared,
        grad_qk_gain,
        grad_qk_bias,
        grad_rel_bias,
        grad_w_value,
        grad_w_reset,
        grad_w_mix,
        grad_w_hidden,
        grad_w_update,
        grad_b_update,
        grad_norm2_gain,
        grad_norm2_bias,
        grad_w_up,
        grad_b_up,
        grad_w_down,
    )


NZ = 4
ROOT = 1
NEAR = (0, 2, 3)
EVEN, ENDS = (0, 1, 2, 3), (0, 3, 0, 3)
MIXED = (0, 3, 1, 2)
UNITS = (
    (0, 1, 0, 512, ENDS), (0, 0, 512, 512, MIXED), (1, 2, 0, 512, EVEN), (1, 0, 512, 512, ENDS), (2, 0, 0, 256, ENDS), (2, 1, 256, 768, ENDS),
    (3, 1, 0, 768, EVEN), (3, 1, 768, 256, MIXED), (4, 1, 0, 768, ENDS), (4, 1, 768, 256, ENDS), (5, 2, 0, 512, EVEN), (5, 0, 512, 512, EVEN),
    (6, 2, 0, 256, ENDS), (6, 2, 256, 768, ENDS), (7, 1, 0, 512, ENDS), (7, 1, 512, 512, ENDS),
)
PHASES = (1.5, 1.0, 2.0, 1.5, 3.5, 1.2, 5.5, 1.5, 1.5, 1.5, 1.0, 1.0, 0.8, 1.5, 0.8, 2.0, 0.8, 1.0, 2.0, 1.3, 1.3, 1.3, 1.3, 4.0, 1.0)
RELEASE = {0: 0, 1: 0, 2: 3, 3: 3, 4: 12, 5: 14, 6: 16, 7: 17}
EARLY = tuple(u for u, t in enumerate(UNITS) if t[0] < 2)
UNIT, LAG = 3.0, 2.0
MARGIN, WINDOW = 0.0, 1000.0
RANKS = {"G": 1, "P": 1, "C": 1, "D": 1, "F": 1, "W": 1, "Y": 4, "X": 4, "S": 0}
BY_UNIT = False


def far_first(z, roots):
    return sorted(range(NZ), key=lambda k: (-abs(roots[k] - z), k))


def line_events(z):
    found = []
    for u, (i, first, _, rows, roots) in enumerate(UNITS):
        size = rows / (1024.0 if first else 512.0)
        late = RELEASE[i]
        for k in range(NZ):
            g = roots[k]
            left = ("l", z - 1, ("zr", u, k), size)
            right = ("r", z + 1, ("zl", u, k), size)
            cross = [("y", z, ("yf", u, k), size)]
            far = [("x", z, ("xf", u, k, 0), size)] if i == 5 else []
            far += [("c", z, ("cf", u, k, 0), size)]
            on = (cross if first == 1 else []) + far
            both = ([left] if z > 0 else []) + ([right] if z < NZ - 1 else []) + (cross if first else []) + far
            need = [("yr", u, k)] if first else []
            if first:
                found.append((("G", u, k), late, None, [], [("y", z, ("yr", u, k), size)], 0.1))
            if z > 0 and g >= z:
                need.append(("zl", u, k))
            if z < NZ - 1 and g <= z:
                need.append(("zr", u, k))
            if g != z:
                found.append((("P", u, k), late, None, need, [right if g > z else left], 0.4))
                further = [left] if g > z > 0 else [right] if g < z < NZ - 1 else []
                found.append((("F", u, k), late, ("P", u, k), [("zr" if g > z else "zl", u, k)], further + on, 0.2))
            else:
                swap = both if first else [("y", z, ("yr", u, k), size)]
                found.append((("C", u, k), late, None, need, swap, 0.4))
                if not first:
                    found.append((("D", u, k), late, ("C", u, k), [("yr", u, k)], both, 0.4))
            other = [("x", z, ("xf", u, k, 1), size)] if i == 5 else []
            other += [("c", z, ("cf", u, k, 1), size)]
            if first == 1:
                found.append((("Y", u, k), late, ("G", u, k), [("yf", u, k)], other, 0.2))
            if first == 2:
                left = ("l", z - 1, ("wr", u, k), size)
                right = ("r", z + 1, ("wl", u, k), size)
                if g == z:
                    both = ([left] if z > 0 else []) + ([right] if z < NZ - 1 else []) + other
                    found.append((("Y", u, k), late, ("G", u, k), [("yf", u, k)], both, 0.2))
                else:
                    further = [left] if g > z > 0 else [right] if g < z < NZ - 1 else []
                    found.append((("W", u, k), late, ("G", u, k), [("wr" if g > z else "wl", u, k)], further + other, 0.2))
            if i == 5:
                for h in range(2 if first else 1):
                    found.append((("X", u, k, h), late, None, [("xf", u, k, h)], [("c", z, ("cf", u, k, 2 + h), size)], 0.2))
    last = len(PHASES) - 1

    def small(n, after, need, out):
        found.append((("S", n, 0), last, after, need, out, 0.4))

    small(1, None, [], [("x", z, ("s1",), 0.7), ("c", z, ("s1c",), 0.7)])
    small(3, ("S", 1, 0), [("s1",)], [("y", z, ("s3",), 1.35)])
    inward = [] if z == ROOT else [("r" if z < ROOT else "l", ROOT, ("s4", z), 1.35)]
    small(4, ("S", 3, 0), [("s3",)], inward)
    tail = [("c", z, ("s6",), 1.35), ("x", z, ("s7",), 1.35)]
    if z == ROOT:
        out = [("l" if q < ROOT else "r", q, ("s5",), 1.35) for q in NEAR]
        small(6, ("S", 4, 0), [("s4", q) for q in NEAR], out + tail)
    else:
        small(7, ("S", 4, 0), [("s5",)], tail)
    return found


def make_plan():
    todo = [line_events(z) for z in range(NZ)]
    clock = [0.0] * NZ
    phase = [0] * NZ
    done = [set() for _ in range(NZ)]
    arrive = [{} for _ in range(NZ)]
    link = {}
    plan = [[[] for _ in range(len(PHASES) + 1)] for _ in range(NZ)]
    while any(todo) or min(phase) < len(PHASES):
        z = min(range(NZ), key=lambda q: (clock[q], q) if (todo[q] or phase[q] < len(PHASES)) else (1e9, q))
        now = clock[z]
        best = None
        for item in todo[z]:
            key, late, after, need, out, cost = item
            if phase[z] <= late or (after is not None and after not in done[z]):
                continue
            latest = 0.0
            for m in need:
                latest = max(latest, arrive[z].get(m, 1e9))
            if need and latest + (MARGIN if phase[z] < len(PHASES) else 0.0) > now:
                continue
            full = phase[z] >= len(PHASES) and key[0] != "S" and any(
                link.get((z, lane), 0.0) > now + WINDOW for lane, _, _, _ in out if lane in "ylr")
            if full:
                continue
            away = -abs(UNITS[key[1]][4][key[2]] - z) if key[0] != "S" else 0
            rank = RANKS[key[0]]
            if key[0] == "Y" and UNITS[key[1]][1] == 2:
                rank = RANKS["F"]
            order = (rank, key[1] if BY_UNIT else latest, away, key[1], key[2])
            if best is None or order < best[0]:
                best = (order, item)
        if best is not None:
            item = best[1]
            todo[z].remove(item)
            key, _, _, _, out, cost = item
            done[z].add(key)
            plan[z][phase[z]].append(key)
            clock[z] += cost
            for lane, dest, message, size in out:
                begin = max(link.get((z, lane), 0.0), clock[z])
                took = size * UNIT * (0.2 if lane == "c" else 1.0)
                link[(z, lane)] = begin + took
                arrive[dest][message] = begin + took + LAG
        elif phase[z] < len(PHASES):
            clock[z] += PHASES[phase[z]]
            phase[z] += 1
        else:
            clock[z] += 0.1
    ends = [max([clock[z]] + list(arrive[z].values())) for z in range(NZ)]
    return plan, ends

F32 = jnp.float32
BF = jnp.bfloat16
MESH = pl.DeviceIdType.MESH


def mm(a, b):
    return lax.dot_general(a, b, (((1,), (0,)), ((), ())), preferred_element_type=F32)


def mm_nt(a, b):
    return lax.dot_general(a, b, (((1,), (1,)), ((), ())), preferred_element_type=F32)


def mm_tn(a, b):
    return lax.dot_general(a, b, (((0,), (0,)), ((), ())), preferred_element_type=F32)


def sigm(v):
    return 1.0 / (1.0 + jnp.exp(-v))


def slope_of(pre, sig):
    return sig * (1.0 + pre * (1.0 - sig))


def cols(i, n):
    return pl.ds(pl.multiple_of(i * n, n), n)


def main_kernel(
    tok_h, cot_h, wsh_h, wv_h, wr_h, wm_h, wh_h, wu_h, wup_h, wdn_h,
    lens, relb, bmap, in_n1g, in_n1b, in_skip, in_bupd, in_n2g, in_n2b, rate, damp, ein, eout, qkg, qkb, in_bup,
    bo, gt, o_down, o_up, o_mix, o_hu, o_reset, o_value, o_shared, o_small,
    wsh, wv, wr, wm, wh, wu, wup, wdn,
    tok, gout, normed, nlow, mlow, pre_ema, xs, smo, pre_sh, qlow, klow, probs, plow,
    pre_v, att, pre_r, vlow, gated, part_s, mix_r, own_f, pre_hid, gate, blend, n2,
    gup, up, gpu, gn2_r, ffn_s, ffn_r, hid, upd, gpr, gpv, gp_acc, gp_r, gps,
    nb_s, mb_r, nb_r,
    p_normed, p_mixed, p_gout, p_up, p_n2, p_gpu, p_gated, p_hid, p_upd, p_gpr, p_gpv, p_gps,
    a_s, w_s, snap_s, snap_r, carry, carry_r, acc, keep, live, segc, vec, bup,
    g_v, ext, small, s_q, s_own, s_y, s_in,
    wsem, xsend, xrecv, csend, crecv, lsem, asend, arecv, ready,
):
    x = lax.axis_index("narrow")
    w = lax.axis_index("wide")
    other = 1 - x
    c = w % 2
    wpart = w + 1 - 2 * c
    y = (w // 2) % 2
    wy = w + 2 - 4 * y
    zi = w // 4
    wl = w - 4
    wr_ = w + 4
    H = tok.shape[0] // 2
    R = 2 * H
    own = pl.ds(pl.multiple_of(x * H, H), H)
    oth = pl.ds(pl.multiple_of(other * H, H), H)
    D = 1024
    VL = wv.shape[1]
    FL = wup.shape[1]
    EPS = EPSILON

    weights = [
        (tok_h, tok.at[own]), (cot_h, gout.at[own]), (wsh_h, wsh), (wv_h, wv), (wr_h, wr), (wm_h, wm), (wh_h, wh), (wu_h, wu), (wdn_h, wdn),
        (wup_h, wup),
    ]
    wcopies = [pltpu.make_async_copy(s, d, wsem.at[i]) for i, (s, d) in enumerate(weights)]
    wcopies[0].start()
    wcopies[1].start()

    barrier = pltpu.get_barrier_semaphore()
    w_root = w + 4 * (ROOT - zi)
    w_last = w + 4 * (NZ - 1 - zi)

    def greet(to):
        pl.semaphore_signal(barrier, inc=1, device_id=to, device_id_type=MESH)

    for to in ((w, other), (wpart, x), (wpart, other), (wy, x)):
        greet(to)
    for z in range(NZ):
        met = [wl] * (z > 0) + [wr_] * (z < NZ - 1) + [w_last] * (z == ROOT) + [w_root] * (z == NZ - 1)

        @pl.when(zi == z)
        def _(met=met):
            for to in met:
                greet((to, x))
            pl.semaphore_wait(barrier, 4 + len(met))

    def xcopy(i, src, dst):
        return pltpu.make_async_remote_copy(
            src_ref=src, dst_ref=dst, send_sem=xsend.at[i], recv_sem=xrecv.at[i],
            device_id=(w, other), device_id_type=MESH,
        )

    def ccopy(i, src, dst):
        return pltpu.make_async_remote_copy(
            src_ref=src, dst_ref=dst, send_sem=csend.at[i], recv_sem=crecv.at[i],
            device_id=(wpart, x), device_id_type=MESH,
        )

    HC = H // 4
    x_tok = [
        xcopy(0 if j == 0 else 16 + j, tok_h.at[j * HC : (j + 1) * HC], tok.at[pl.ds(pl.multiple_of(x * H + j * HC, HC), HC)])
        for j in range(4)
    ]
    x_cot = xcopy(1, cot_h, gout.at[own])
    for copy in x_tok:
        copy.start()
    for copy in wcopies[2:]:
        copy.start()

    gs = smo.at[0 : H * 8]
    gxs = smo.at[H * 8 : R * 8]
    nb_o = gup.at[0:H, 0:D]
    gres = gup.at[0:H, D : 2 * D]
    ffn_o = gup.at[H:R, 0:D]

    first_end = lens[0, 0]
    second_end = first_end + lens[0, 1]
    place = lax.broadcasted_iota(jnp.int32, (R, 128), 0)
    begins = (place == 0) | (place == first_end) | (place == second_end)
    keep[...] = jnp.where(begins, 0.0, 1.0)
    live[...] = jnp.where(place >= second_end, 0.0, 1.0)

    def segment_of(at):
        return jnp.where(at >= first_end, 1.0, 0.0) + jnp.where(at >= second_end, 1.0, 0.0)

    segc[...] = segment_of(place)

    for t in range(2):
        for j in range(8):
            rows_ = slice(t * 8, t * 8 + 8)
            lanes = slice(j * 128, j * 128 + 128)
            r_ = rate[rows_, lanes]
            a_s[pl.ds(t * 64 + j, 8, stride=8), :] = 1.0 - r_ * damp[rows_, lanes]
            w_s[pl.ds(t * 64 + j, 8, stride=8), :] = r_ * ein[rows_, lanes] * eout[rows_, lanes]

    for k, ref in enumerate((in_n1g, in_n1b, in_skip, in_bupd, in_n2g, in_n2b)):
        for j in range(8):
            vec[k : k + 1, j * 128 : (j + 1) * 128] = ref[j : j + 1, :]
    wide_bias = in_bup[...].astype(F32)
    for j in range(16):
        bup[0:1, j * 128 : (j + 1) * 128] = wide_bias[j : j + 1, :]

    def norm_rows(v):
        m = jnp.mean(v, axis=-1, keepdims=True)
        cen = v - m
        var = jnp.mean(cen * cen, axis=-1, keepdims=True)
        return cen, lax.rsqrt(var + EPS)

    def norm1(t):
        rr = cols(t, 16)
        cen, rstd = norm_rows(tok[rr, :].astype(F32))
        v = cen * rstd * vec[0:1, :] + vec[1:2, :]
        normed[rr, :] = v
        nlow[rr, :] = v.astype(BF)
        for j in range(8):
            xs[pl.ds(t * 128 + j, 16, stride=8), :] = v[:, j * 128 : (j + 1) * 128]

    HT = H // 16
    wcopies[0].wait()
    pl.loop(0, HT)(lambda t: norm1(x * HT + t))
    N = 16

    def coef(ref):
        return ref[...].reshape(N, 8, 128)

    zeros = jnp.zeros((N, 8, 128), F32)

    def forward(p, s):
        k = keep[pl.ds(p, 1), :]
        at = cols(p, 8)
        xr = xs[at, :] * live[pl.ds(p, 1), :]
        s = coef(a_s) * (s * k) + xr
        smo[at, :] = jnp.sum(coef(w_s) * s, axis=0)
        return s

    def mixed_rows(t):
        rr = cols(t, 16)
        for j in range(8):
            ll = slice(j * 128, (j + 1) * 128)
            pre = smo[pl.ds(t * 128 + j, 16, stride=8), :] + vec[2:3, ll] * normed[rr, ll]
            pre_ema[rr, ll] = pre
            mlow[rr, ll] = (pre * sigm(pre)).astype(BF)

    T = 256

    def value_tile(i, rows_):
        cc = cols(i, T)
        pv = mm(nlow[rows_, :], wv[:, cc])
        pre_v[rows_, cc] = pv
        vlow[rows_, cc] = (pv * sigm(pv)).astype(BF)

    wcopies[3].wait()
    pl.loop(0, VL // T, unroll=2)(lambda i: value_tile(i, own))
    state = zeros
    for j in range(8):

        @pl.when(x == (1 if j < 4 else 0))
        def _(j=j):
            x_tok[j % 4].wait_recv()
            pl.loop(j * (HC // 16), (j + 1) * (HC // 16))(norm1)

        state = lax.fori_loop(j * HC, (j + 1) * HC, forward, state, unroll=4)
        pl.loop(j * (HC // 16), (j + 1) * (HC // 16))(mixed_rows)

    for copy in x_tok:
        copy.wait_send()
    x_cot.start()
    c_normed = ccopy(0, nlow, p_normed)
    c_normed.start()
    c_mixed = ccopy(1, mlow, p_mixed)
    c_mixed.start()

    wcopies[2].wait()
    psh = mm(mlow[...], wsh[...])
    pre_sh[...] = psh
    sh = psh * sigm(psh)
    qlow[...] = (sh * qkg[0:1, :] + qkb[0:1, :]).astype(BF)
    klow[...] = (sh * qkg[1:2, :] + qkb[1:2, :]).astype(BF)

    BL = BLOCK
    ii = lax.broadcasted_iota(jnp.int32, (BL, BL), 0)
    jj = lax.broadcasted_iota(jnp.int32, (BL, BL), 1)

    def skew(tbl, left):
        for b in range(7):
            moved = pltpu.roll(tbl, (BL - (1 << b)) if left else (1 << b), 1)
            tbl = jnp.where(lax.rem(ii // (1 << b), 2) == 1, moved, tbl)
        return tbl

    buckets = bmap[0:1, :]
    by_offset = jnp.zeros((1, BL), F32)
    for b in range(relb.shape[1]):
        by_offset = by_offset + jnp.where(buckets == b, relb[0, b], 0.0)
    table = skew(jnp.broadcast_to(by_offset, (BL, BL)), False).T
    scale = float(qkg.shape[1]) ** (-0.5)
    for b in range(2):
        rb = slice(b * BL, (b + 1) * BL)
        sc = mm_nt(qlow[rb, :], klow[rb, :]) * scale
        ok = (segc[rb, :] == segment_of(lax.broadcasted_iota(jnp.int32, (1, BL), 1) + b * BL)) & (jj <= ii)
        sc = jnp.where(ok, sc + table, NEGATIVE)
        ex = jnp.exp(sc - jnp.max(sc, axis=-1, keepdims=True))
        pr = ex / jnp.sum(ex, axis=-1, keepdims=True)
        probs[rb, :] = pr
        plow[rb, :] = pr.astype(BF)

    wcopies[4].wait()

    def reset_tile(i):
        cc = cols(i, T)
        for b in range(2):
            rb = slice(b * BL, (b + 1) * BL)
            att[rb, cc] = mm(plow[rb, :], vlow[rb, cc])
        pr = mm(mlow[...], wr[:, cc])
        pre_r[:, cc] = pr
        gated[:, cc] = (pr * sigm(pr) * att[:, cc]).astype(BF)

    pl.loop(0, VL // T, unroll=2)(lambda i: value_tile(i, oth))
    pl.loop(0, VL // T, unroll=2)(reset_tile)

    wcopies[5].wait()

    HH = H // 2
    x_mix = []
    for h in range(2):
        src = pl.ds(pl.multiple_of(other * H + h * HH, HH), HH)
        hr = slice(h * HH, (h + 1) * HH)

        @pl.loop(0, D // T, unroll=2)
        def _(i, src=src, hr=hr):
            cc = cols(i, T)
            part_s[hr, cc] = mm(gated[src, :], wm[:, cc]).astype(BF)

        x_mix.append(xcopy((2, 13)[h], part_s.at[hr], mix_r.at[hr]))
        x_mix[h].start()

    c_gated = ccopy(2, gated, p_gated)
    c_gated.start()
    wcopies[6].wait()
    wcopies[7].wait()

    @pl.loop(0, D // T, unroll=2)
    def _(i):
        cc = cols(i, T)
        own_f[:, cc] = mm(gated[own, :], wm[:, cc])
        pre_hid[:, cc] = mm(mlow[own, :], wh[:, cc])
        gate[:, cc] = sigm(mm(mlow[own, :], wu[:, cc]) + vec[3:4, cc])

    wcopies[1].wait()
    x_cot.wait()

    @pl.loop(0, R // 16)
    def _(t):
        rr = cols(t, 16)
        gout[rr, :] = (gout[rr, :].astype(F32) * live[rr, 0:1]).astype(BF)

    c_gout = ccopy(3, gout, p_gout)
    c_gout.start()
    wcopies[8].wait()

    @pl.loop(0, FL // T, unroll=2)
    def _(i):
        cc = cols(i, T)
        gup[:, cc] = mm_nt(gout[...], wdn[cc, :])


    def blend_rows(t):
        rr = cols(t, 16)
        ro = pl.ds(pl.multiple_of(x * H + t * 16, 16), 16)
        ph = pre_hid[rr, :] + (own_f[rr, :] + mix_r[rr, :].astype(F32))
        pre_hid[rr, :] = ph
        u = gate[rr, :]
        bl = u * (ph * sigm(ph)) + (1.0 - u) * tok[ro, :].astype(F32)
        blend[rr, :] = bl
        cen, rstd = norm_rows(bl)
        n2[ro, :] = (cen * rstd * vec[4:5, :] + vec[5:6, :]).astype(BF)

    x_n2 = []
    for h in range(4):
        if h % 2 == 0:
            x_mix[h // 2].wait()
        pl.loop(h * (HT // 4), (h + 1) * (HT // 4))(blend_rows)
        part = pl.ds(pl.multiple_of(x * H + h * (H // 4), H // 4), H // 4)
        x_n2.append(xcopy(3 if h == 0 else 13 + h, n2.at[part], n2.at[part]))
        x_n2[h].start()

    wcopies[9].wait()
    FT = FL // T

    def up_tile(i, rows_, first):
        cc = cols(i, T)
        pu = mm(n2[rows_, :], wup[:, cc]) + bup[0:1, cc]
        sg = sigm(pu)
        up[rows_, cc] = (pu * sg).astype(BF)
        gp = (gup[rows_, cc] * slope_of(pu, sg)).astype(BF)
        gpu[rows_, cc] = gp
        sums = jnp.sum(gp.astype(F32), axis=0, keepdims=True)
        for h in range(2):
            at = pl.ds(304 + x * 16 + i * 2 + h, 1)
            part = sums[:, h * 128 : (h + 1) * 128]
            if first:
                small[at, :] = part
                small[pl.ds(304 + other * 16 + i * 2 + h, 1), :] = jnp.zeros((1, 128), F32)
            else:
                small[at, :] += part

    pl.loop(0, FT, unroll=2)(lambda i: up_tile(i, own, True))
    for copy in x_n2:
        copy.wait()
    c_n2 = ccopy(4, n2, p_n2)
    c_n2.start()
    halfF = FL // 2
    theirs_f = pl.ds(pl.multiple_of((1 - c) * halfF, halfF), halfF)
    pl.loop(0, FT // 2, unroll=2)(lambda i: up_tile((1 - c) * (FT // 2) + i, oth, False))
    c_up = ccopy(5, up.at[:, theirs_f], p_up)
    c_gpu = ccopy(6, gpu.at[:, theirs_f], p_gpu)
    c_up.start()
    c_gpu.start()
    pl.loop(0, FT // 2, unroll=2)(lambda i: up_tile(c * (FT // 2) + i, oth, False))
    P2 = g_v.shape[2]
    plan = make_plan()[0]
    numbers = {}
    locals_ = {}

    def number(*key):
        return numbers.setdefault(key, len(numbers))

    shelves = [[wup, 0, j, 0] for j in range(wup.shape[1] // P2)]
    shelves += [[wdn, 0, j, 0] for j in range(wdn.shape[1] // P2)] + [[ext, 0, 0, 0]]
    places = {}

    def place_of(key, n):
        if key not in places:
            for shelf in shelves:
                if (shelf[0] is ext) == (key[0] in EARLY) and shelf[1] + n <= shelf[0].shape[0]:
                    places[key] = (shelf[0], shelf[1], shelf[2] * P2)
                    shelf[1] += n
                    break
        ref, r0, c0 = places[key]
        return ref.at[r0 : r0 + n, c0 : c0 + P2]

    def chunk_rows(u):
        _, first, _, rows, _ = UNITS[u]
        return rows // 8 if first else rows // 4

    def earlier(u, k):
        roots = UNITS[u][4]
        return sum(roots[q] == roots[k] for q in range(k))

    def line_place(u, k):
        return place_of((u, "z", k), chunk_rows(u))

    def second_place(u, k):
        return place_of((u, "s", earlier(u, k)), chunk_rows(u))

    def cross_place(u, k):
        return place_of((u, "y", k if UNITS[u][1] else earlier(u, k)), chunk_rows(u))

    def from_right(u, k, z):
        return second_place(u, k) if UNITS[u][4][k] == z and z > 0 else line_place(u, k)

    def first_row(u, k, half):
        _, first, row0, rows, _ = UNITS[u]
        n = chunk_rows(u)
        if first:
            return row0 + half * (rows // 2) + k * n
        return row0 + k * n

    def rows_at(u, k, half):
        n = chunk_rows(u)
        if UNITS[u][1]:
            return pl.ds(pl.multiple_of(first_row(u, k, half), 16), n)
        return pl.ds(first_row(u, k, half), n)

    def chunk(u, k, half):
        return g_v.at[UNITS[u][0], rows_at(u, k, half)]

    def result(u, k, half, core, side):
        i = UNITS[u][0]
        n = chunk_rows(u)
        r0 = first_row(u, k, half)
        j = i % 2
        if i < 2:
            return o_down.at[pl.ds(pl.multiple_of(core * D + r0, 16), n), j * P2 : (j + 1) * P2]
        rr = pl.ds(pl.multiple_of(r0, 16), n)
        if i < 4:
            return o_up.at[rr, pl.ds(pl.multiple_of(core * D + j * P2, P2), P2)]
        if i == 5:
            return o_hu.at[2 * side + core, rr]
        ref = {4: o_mix, 6: o_reset, 7: o_value}[i]
        return ref.at[rr, pl.ds(pl.multiple_of(core * P2, P2), P2)]

    sent = [[] for _ in range(NZ)]

    def send(z, way, key, src, dst):
        dev = {
            "y": (wy, x), "l": (wl, x), "r": (wr_, x), "c": (wpart, x), "x": (w, other), "d": (wpart, other),
            "root": (w_root, x), "last": (w_last, x),
        }[way]
        n = number(*key)
        copy = pltpu.make_async_remote_copy(
            src_ref=src, dst_ref=dst, send_sem=asend.at[n], recv_sem=arecv.at[n],
            device_id=dev, device_id_type=MESH,
        )
        copy.start()
        sent[z].append((n, src.shape, src.dtype))

    def arrived(key, ref):
        n = number(*key)
        pltpu.make_async_remote_copy(
            src_ref=ref, dst_ref=ref, send_sem=asend.at[n], recv_sem=arecv.at[n],
            device_id=(w, other), device_id_type=MESH,
        ).wait_recv()

    def add_up(dst, terms):
        if terms:

            @pl.loop(0, dst.shape[0] // 32)
            def _(t):
                rr = cols(t, 32)
                v = dst[rr, :].astype(F32)
                for term in terms:
                    v = v + term[rr, :].astype(F32)
                dst[rr, :] = v.astype(BF)

    def own_copy(u, k, src, half):
        at = locals_.setdefault((u, k), len(locals_))
        return pltpu.make_async_copy(src, result(u, k, half, c, x), lsem.at[at])

    def share(z, u, k, src, half):
        dst = result(u, k, half, c, x)
        if z > 0:
            send(z, "l", ("zr", u, k), src, dst)
        if z < NZ - 1:
            send(z, "r", ("zl", u, k), src, dst)
        if UNITS[u][1]:
            send(z, "y", ("yf", u, k), src, dst)
        if UNITS[u][0] == 5:
            send(z, "x", ("xf", u, k, 0), src, dst)
        send(z, "c", ("cf", u, k, 0), src, dst)
        own_copy(u, k, src, half).start()

    def happen(z, key):
        kind, u, k = key[:3]
        if kind == "S":
            small_step(z, u)
            return
        i, first, _, _, roots = UNITS[u]
        own_half = y if first else 0
        g = roots[k]
        if kind == "G":
            send(z, "y", ("yr", u, k), chunk(u, k, 1 - y), cross_place(u, k))
            return
        if kind in "PC":
            terms = []
            if first:
                arrived(("yr", u, k), cross_place(u, k))
                terms.append(cross_place(u, k))
            if g >= z and z > 0:
                arrived(("zl", u, k), line_place(u, k))
                terms.append(line_place(u, k))
            if g <= z and z < NZ - 1:
                arrived(("zr", u, k), from_right(u, k, z))
                terms.append(from_right(u, k, z))
            mine = chunk(u, k, own_half)
            add_up(mine, terms)
            if kind == "P" and g > z:
                send(z, "r", ("zl", u, k), mine, line_place(u, k))
            elif kind == "P":
                send(z, "l", ("zr", u, k), mine, from_right(u, k, z - 1))
            elif first:
                share(z, u, k, mine, own_half)
            else:
                send(z, "y", ("yr", u, k), mine, cross_place(u, k))
        elif kind == "D":
            mine = cross_place(u, k)
            arrived(("yr", u, k), mine)
            add_up(mine, [chunk(u, k, 0)])
            share(z, u, k, mine, 0)
        elif kind == "F":
            ref = result(u, k, own_half, c, x)
            arrived(("zr" if g > z else "zl", u, k), ref)
            if g > z > 0:
                send(z, "l", ("zr", u, k), ref, ref)
            if g < z < NZ - 1:
                send(z, "r", ("zl", u, k), ref, ref)
            if first == 1:
                send(z, "y", ("yf", u, k), ref, ref)
            if i == 5:
                send(z, "x", ("xf", u, k, 0), ref, ref)
            send(z, "c", ("cf", u, k, 0), ref, ref)
        elif kind in "YW":
            ref = result(u, k, 1 - y, c, x)
            arrived(("yf" if kind == "Y" else "wr" if g > z else "wl", u, k), ref)
            if first == 2 and g >= z > 0:
                send(z, "l", ("wr", u, k), ref, ref)
            if first == 2 and g <= z < NZ - 1:
                send(z, "r", ("wl", u, k), ref, ref)
            if i == 5:
                send(z, "x", ("xf", u, k, 1), ref, ref)
            send(z, "c", ("cf", u, k, 1), ref, ref)
        elif kind == "X":
            h = key[3]
            half = (y if h == 0 else 1 - y) if first else 0
            ref = result(u, k, half, c, other)
            arrived(("xf", u, k, h), ref)
            send(z, "c", ("cf", u, k, 2 + h), ref, ref)

    def slot(n):
        for z in range(NZ):
            if plan[z][n]:

                @pl.when(zi == z)
                def _(z=z):
                    for key in plan[z][n]:
                        happen(z, key)

    def eight(start, n):
        return pl.ds(pl.multiple_of(start, 8), n)

    def quarter(side, core):
        return eight(side * 176 + core * 88, 88)

    def quarter_sh(side, core):
        return eight((2 * side + core) * 256, 256)

    around = (("x", other, c), ("c", x, 1 - c), ("d", other, 1 - c))

    def small_step(z, n):
        mine, mine_sh = quarter(x, c), quarter_sh(x, c)

        def give(total):
            o_small[mine, :] = total[0:88, :]
            o_shared[mine_sh, :] = total[88:344, :]
            for way, _, _ in around:
                send(z, way, ("s6", way), o_small.at[mine], o_small.at[mine])
                send(z, way, ("s7", way), o_shared.at[mine_sh], o_shared.at[mine_sh])

        if n == 1:
            for at, (way, side, core) in enumerate(around):
                send(z, way, ("s1", way), small.at[quarter(side, core)], s_q.at[at])
        elif n == 3:
            for at, (way, _, _) in enumerate(around):
                arrived(("s1", way), s_q.at[at])
            s_own[0:88, :] = (small[mine, :] + s_q[0]) + (s_q[1] + s_q[2])
            send(z, "y", ("s3",), s_own, s_y)
        elif n == 4:
            arrived(("s3",), s_y)
            s_y[...] = s_y[...] + s_own[...]
            if z != ROOT:
                send(z, "root", ("s4", z), s_y, s_in.at[NEAR.index(z)])
        elif n == 6:
            for at, q in enumerate(NEAR):
                arrived(("s4", q), s_in.at[at])
            s_y[...] = (s_y[...] + s_in[0]) + (s_in[1] + s_in[2])
            for q, way in zip(NEAR, ("l", "r", "last")):
                send(z, way, ("s5", q), s_y, s_in.at[0])
            give(s_y)
        elif n == 7:
            arrived(("s5", z), s_in.at[0])
            give(s_in.at[0])

    def finish():
        for z in range(NZ):

            @pl.when(zi == z)
            def _(z=z):
                for way, side, core in around:
                    arrived(("s6", way), o_small.at[quarter(side, core)])
                    arrived(("s7", way), o_shared.at[quarter_sh(side, core)])
                for u, (i, first, _, _, roots) in enumerate(UNITS):
                    for k in range(NZ):
                        half = y if first else 0
                        arrived(("cf", u, k, 0), result(u, k, half, 1 - c, x))
                        if first:
                            arrived(("cf", u, k, 1), result(u, k, 1 - y, 1 - c, x))
                        if i == 5:
                            for h in range(2 if first else 1):
                                at = (y if h == 0 else 1 - y) if first else 0
                                arrived(("cf", u, k, 2 + h), result(u, k, at, 1 - c, other))
                        if roots[k] == z:
                            own_copy(u, k, chunk(u, k, half), half).wait()
                for n, shape, dtype in sent[z]:
                    like = g_v.at[0, 0 : shape[0]] if dtype == BF else o_shared.at[0 : shape[0]]
                    pltpu.make_async_remote_copy(
                        src_ref=like, dst_ref=like, send_sem=asend.at[n], recv_sem=arecv.at[n],
                        device_id=(w, other), device_id_type=MESH,
                    ).wait_send()


    c_gout.wait()
    c_up.wait()
    P2 = g_v.shape[2]

    @pl.loop(0, 4)
    def _(i):
        mt = cols(i, 256)
        mf = pl.ds(pl.multiple_of(c * halfF + i * 256, 256), 256)
        la = up[:, mf]
        lb = p_up[:, mt]
        for j in range(2):
            nn = slice(j * P2, (j + 1) * P2)
            g_v[j, mt, :] = (mm_tn(la, gout[:, nn]) + mm_tn(lb, p_gout[:, nn])).astype(BF)

    slot(1)

    @pl.loop(0, D // T)
    def _(i):
        cc = cols(i, T)
        part_s[:, cc] = mm_nt(gpu[oth, :], wup[cc, :]).astype(BF)

    x_gn2 = xcopy(4, part_s, gn2_r)
    x_gn2.start()
    slot(2)

    @pl.loop(0, D // T)
    def _(i):
        cc = cols(i, T)
        own_f[:, cc] = mm_nt(gpu[own, :], wup[cc, :])
        ffn_s[:, cc] = mm(up[oth, :], wdn[:, cc]).astype(BF)
        ffn_o[:, cc] = mm(up[own, :], wdn[:, cc])


    pl.semaphore_signal(ready.at[0], inc=1, device_id=(wy, x), device_id_type=MESH)

    @pl.when(zi > 0)
    def _():
        pl.semaphore_signal(ready.at[2], inc=1, device_id=(wl, x), device_id_type=MESH)

    @pl.when(zi < NZ - 1)
    def _():
        pl.semaphore_signal(ready.at[1], inc=1, device_id=(wr_, x), device_id_type=MESH)

    pl.semaphore_wait(ready.at[0], 1)

    @pl.when(zi > 0)
    def _():
        pl.semaphore_wait(ready.at[1], 1)

    @pl.when(zi < NZ - 1)
    def _():
        pl.semaphore_wait(ready.at[2], 1)

    slot(3)
    c_n2.wait()
    c_gpu.wait()

    @pl.loop(0, 4)
    def _(i):
        mt = cols(i, 256)
        la = n2[:, mt]
        lb = p_n2[:, mt]
        for j in range(2):
            nf = pl.ds(pl.multiple_of(c * halfF + j * P2, P2), P2)
            nn = slice(j * P2, (j + 1) * P2)
            g_v[2 + j, mt, :] = (mm_tn(la, gpu[:, nf]) + mm_tn(lb, p_gpu[:, nn])).astype(BF)

    slot(4)
    x_gn2.wait()

    acc[...] = jnp.zeros_like(acc)

    def add_rows(k, v):
        acc[k * 8 : k * 8 + 8, :] += v[0:8, :] + v[8:16, :]

    def norm2_back(t):
        rr = cols(t, 16)
        ro = pl.ds(pl.multiple_of(x * H + t * 16, 16), 16)
        g = own_f[rr, :] + gn2_r[rr, :].astype(F32)
        cen, rstd = norm_rows(blend[rr, :])
        xh = cen * rstd
        add_rows(0, g * xh)
        add_rows(1, g)
        gy = g * vec[4:5, :]
        gb = rstd * (gy - jnp.mean(gy, axis=-1, keepdims=True) - xh * jnp.mean(gy * xh, axis=-1, keepdims=True))
        gb = gb + gout[ro, :].astype(F32)
        u = gate[rr, :]
        ph = pre_hid[rr, :]
        sg = sigm(ph)
        tk = tok[ro, :].astype(F32)
        gud = (gb * (ph * sg - tk) * u * (1.0 - u)).astype(BF)
        ghd = (gb * u * slope_of(ph, sg)).astype(BF)
        hid[ro, :] = ghd
        upd[ro, :] = gud
        add_rows(2, gud.astype(F32))
        gres[rr, :] = gb * (1.0 - u)

    halves = [pl.ds(pl.multiple_of(x * H + h * (H // 2), H // 2), H // 2) for h in range(2)]
    x_hid = [xcopy((5, 22)[h], hid.at[halves[h]], hid.at[halves[h]]) for h in range(2)]
    pl.loop(0, HT // 2)(norm2_back)
    x_hid[0].start()
    slot(5)
    pl.loop(HT // 2, HT)(norm2_back)
    x_hid[1].start()
    x_upd = xcopy(6, upd.at[own], upd.at[own])
    x_ffn = xcopy(7, ffn_s, ffn_r)

    def put_small(row, k):
        v = jnp.sum(acc[k * 8 : k * 8 + 8, :], axis=0, keepdims=True)
        for j in range(8):
            small[row + j : row + j + 1, :] = v[:, j * 128 : (j + 1) * 128]

    put_small(256 + 32, 0)
    put_small(256 + 40, 1)
    put_small(256 + 24, 2)
    slot(6)

    snap_s[...] = jnp.zeros_like(snap_s)
    snap_r[...] = jnp.zeros_like(snap_r)

    def sense(p, state):
        s, r = state
        k = keep[pl.ds(p, 1), :]
        a = coef(a_s)
        sk = s * k
        return a * sk + xs[cols(p, 8), :] * live[pl.ds(p, 1), :], a * (r * k) + sk

    @pl.when(x == 1)
    def _():
        s_mid, r_mid = lax.fori_loop(0, H, sense, (zeros, zeros), unroll=2)
        snap_s[...] = s_mid.reshape(N * 8, 128)
        snap_r[...] = r_mid.reshape(N * 8, 128)

    for copy in x_hid:
        copy.wait()
    x_upd.start()
    c_hid = ccopy(7, hid, p_hid)
    c_hid.start()
    gp_acc[...] = jnp.zeros_like(gp_acc)

    def gated_back(i):
        cc = cols(i, T)
        gg = mm_nt(hid[...], wm[cc, :])
        pr = pre_r[:, cc]
        sg = sigm(pr)
        ga = (gg * (pr * sg)).astype(BF)
        gpr[:, cc] = (gg * att[:, cc] * slope_of(pr, sg)).astype(BF)
        pv = pre_v[:, cc]
        sv = slope_of(pv, sigm(pv))
        for b in range(2):
            rb = slice(b * BL, (b + 1) * BL)
            gp_acc[rb, :] += mm_nt(ga[rb, :], vlow[rb, cc])
            gv = mm_tn(plow[rb, :], ga[rb, :])
            gpv[rb, cc] = (gv * sv[rb, :]).astype(BF)

    for i in range(VL // T):
        pl.loop(i, i + 1)(gated_back)
        slot(7 + i)
    x_gp = xcopy(8, gp_acc.at[oth], gp_r)
    x_gp.start()
    x_upd.wait()

    @pl.loop(0, D // T)
    def _(i):
        cc = cols(i, T)
        part_s[:, cc] = mm_nt(gpr[oth, :], wr[cc, :]).astype(BF)

    x_mb = xcopy(9, part_s, mb_r)
    x_mb.start()
    slot(11)

    @pl.loop(0, D // T)
    def _(i):
        cc = cols(i, T)
        nb_s[:, cc] = mm_nt(gpv[oth, :], wv[cc, :]).astype(BF)

    x_nb = xcopy(10, nb_s, nb_r)
    halfV = VL // 2
    c_gpr = ccopy(8, gpr.at[:, pl.ds(pl.multiple_of((1 - c) * halfV, halfV), halfV)], p_gpr)
    c_gpv = ccopy(9, gpv.at[:, pl.ds(pl.multiple_of((1 - c) * halfV, halfV), halfV)], p_gpv)
    c_upd = ccopy(10, upd, p_upd)
    c_gpr.start()
    c_gpv.start()
    c_upd.start()

    slot(12)
    c_hid.wait()
    c_gated.wait()
    hv = pl.ds(pl.multiple_of(c * P2, P2), P2)
    q4 = pl.ds(pl.multiple_of((2 * x + c) * 256, 256), 256)

    @pl.loop(0, 4)
    def _(i):
        mt = cols(i, 256)
        g_v[4, mt, :] = (mm_tn(gated[:, mt], hid[:, hv]) + mm_tn(p_gated[:, mt], p_hid[:, hv])).astype(BF)

    slot(13)

    x_gp.wait()
    gpb = gp_acc[own, :] + gp_r[...]
    po = probs[own, :]
    gsc = (po * (gpb - jnp.sum(gpb * po, axis=-1, keepdims=True))).astype(BF)
    gq = mm(gsc, klow[own, :]) * scale
    gk = mm_tn(gsc, qlow[own, :]) * scale
    psh = pre_sh[own, :]
    sgs = sigm(psh)
    sh = psh * sgs
    small[336:337, :] = jnp.sum(gq * sh, axis=0, keepdims=True)
    small[337:338, :] = jnp.sum(gk * sh, axis=0, keepdims=True)
    small[338:339, :] = jnp.sum(gq, axis=0, keepdims=True)
    small[339:340, :] = jnp.sum(gk, axis=0, keepdims=True)
    small[340:341, :] = jnp.sum(skew(gsc.astype(F32).T, True), axis=0, keepdims=True)
    small[341:352, :] = jnp.zeros((11, 128), F32)
    gps[own, :] = ((gq * qkg[0:1, :] + gk * qkg[1:2, :]) * slope_of(psh, sgs)).astype(BF)
    x_gps = xcopy(11, gps.at[own], gps.at[own])
    x_gps.start()
    x_nb.start()
    slot(14)
    c_mixed.wait()
    c_upd.wait()

    la = mlow[:, q4]
    lb = p_mixed[:, q4]
    for j in range(2):
        nn = slice(j * P2, (j + 1) * P2)
        g_v[5, j * 256 : j * 256 + 256, :] = (mm_tn(la, hid[:, nn]) + mm_tn(lb, p_hid[:, nn])).astype(BF)
        g_v[5, 512 + j * 256 : 768 + j * 256, :] = (mm_tn(la, upd[:, nn]) + mm_tn(lb, p_upd[:, nn])).astype(BF)

    slot(15)

    @pl.loop(0, D // T)
    def _(i):
        cc = cols(i, T)
        own_f[:, cc] = (
            mm_nt(gpr[own, :], wr[cc, :])
            + mm_nt(gps[own, :], wsh[cc, :])
            + mm_nt(hid[own, :], wh[cc, :])
            + mm_nt(upd[own, :], wu[cc, :])
        )
        nb_o[:, cc] = mm_nt(gpv[own, :], wv[cc, :])

    slot(16)
    x_gps.wait()
    c_gps = ccopy(11, gps, p_gps)
    c_gps.start()
    c_gpr.wait()

    @pl.loop(0, 4)
    def _(i):
        mt = cols(i, 256)
        g_v[6, mt, :] = (mm_tn(mlow[:, mt], gpr[:, hv]) + mm_tn(p_mixed[:, mt], p_gpr[...])).astype(BF)

    slot(17)
    c_normed.wait()
    c_gpv.wait()

    @pl.loop(0, 4)
    def _(i):
        mt = cols(i, 256)
        g_v[7, mt, :] = (mm_tn(nlow[:, mt], gpv[:, hv]) + mm_tn(p_normed[:, mt], p_gpv[...])).astype(BF)

    c_gps.wait()
    s_own[88:344, :] = mm_tn(mlow[:, q4], gps[...]) + mm_tn(p_mixed[:, q4], p_gps[...])
    slot(18)
    x_mb.wait()
    x_ffn.start()

    acc[...] = jnp.zeros_like(acc)

    @pl.loop(0, H // 16)
    def _(t):
        rr = cols(t, 16)
        ro = pl.ds(pl.multiple_of(x * H + t * 16, 16), 16)
        pre = pre_ema[ro, :]
        g = (own_f[rr, :] + mb_r[rr, :].astype(F32)) * slope_of(pre, sigm(pre))
        own_f[rr, :] = g
        add_rows(0, g * normed[ro, :])
        for j in range(8):
            gs[pl.ds(t * 128 + j, 16, stride=8), :] = g[:, j * 128 : (j + 1) * 128]

    put_small(256, 0)
    slot(19)

    def back(p_, cy):
        p = H - 1 - p_
        at = cols(p, 8)
        po_ = x * H + p
        mu = gs[at, :] + cy
        gxs[at, :] = jnp.sum(coef(w_s) * mu, axis=0) * live[pl.ds(po_, 1), :]
        return coef(a_s) * (mu * keep[pl.ds(po_, 1), :])

    x_carry = xcopy(12, carry, carry_r)

    @pl.when(x == 1)
    def _():
        cy = lax.fori_loop(0, H, back, zeros)
        carry[...] = cy.reshape(N * 8, 128)
        x_carry.start()

    slot(20)
    for q in range(2):
        nq = slice(q * 64, q * 64 + 64)

        def fwd(p, state, nq=nq):
            s, r, gw, gr = state
            at = cols(p, 8)
            po_ = x * H + p
            k = keep[pl.ds(po_, 1), :]
            xr = xs[cols(po_, 8), :] * live[pl.ds(po_, 1), :]
            a = a_s[nq, :].reshape(8, 8, 128)
            sk = s * k
            r = a * (r * k) + sk
            s = a * sk + xr
            g = gs[at, :]
            return s, r, gw + g * s, gr + g * r

        z8 = jnp.zeros((8, 8, 128), F32)
        s0 = snap_s[nq, :].reshape(8, 8, 128)
        r0 = snap_r[nq, :].reshape(8, 8, 128)
        _, _, gw, gr = lax.fori_loop(0, H, fwd, (s0, r0, z8, z8))
        small[nq, :] = gw.reshape(64, 128)
        small[128 + q * 64 : 192 + q * 64, :] = gr.reshape(64, 128) * w_s[nq, :]
        slot(21 + q)

    @pl.when(x == 0)
    def _():
        x_carry.wait_recv()
        lax.fori_loop(0, H, back, coef(carry_r))

    @pl.when(x == 1)
    def _():
        x_carry.wait_send()

    slot(23)
    x_nb.wait()

    @pl.loop(0, H // 16)
    def _(t):
        rr = cols(t, 16)
        ro = pl.ds(pl.multiple_of(x * H + t * 16, 16), 16)
        gx = jnp.concatenate([gxs[pl.ds(t * 128 + j, 16, stride=8), :] for j in range(8)], axis=1)
        g = nb_o[rr, :] + nb_r[rr, :].astype(F32) + vec[2:3, :] * own_f[rr, :] + gx
        cen, rstd = norm_rows(tok[ro, :].astype(F32))
        xh = cen * rstd
        add_rows(1, g * xh)
        add_rows(2, g)
        gy = g * vec[0:1, :]
        gb = rstd * (gy - jnp.mean(gy, axis=-1, keepdims=True) - xh * jnp.mean(gy * xh, axis=-1, keepdims=True))
        gt[rr, :] = gres[rr, :] + gb

    put_small(256 + 8, 1)
    put_small(256 + 16, 2)

    slot(24)

    x_ffn.wait()

    @pl.loop(0, H // 16)
    def _(t):
        rr = cols(t, 16)
        bo[rr, :] = (blend[rr, :] + (ffn_o[rr, :] + ffn_r[rr, :].astype(F32))).astype(BF)

    slot(25)
    finish()

def vm(shape, dtype=F32):
    return pltpu.VMEM(shape, dtype)


SEMS = 440


def run_main(tokens, cotangent, seq_lengths, bucket_map, norm1_gain, norm1_bias, ema_rate, ema_damp, ema_in, ema_out,
             ema_skip, w_shared, qk_gain, qk_bias, rel_bias, w_value, w_reset, w_mix, w_hidden, w_update, b_update,
             norm2_gain, norm2_bias, w_up, b_up, w_down):
    H = tokens.shape[0]
    R = 2 * H
    D = tokens.shape[1]
    VL = w_value.shape[1]
    FL = w_up.shape[1]
    Z = w_shared.shape[1]
    rows8 = [v.reshape(8, D // 8) for v in (norm1_gain, norm1_bias, ema_skip, b_update, norm2_gain, norm2_bias)]
    anyspec = pl.BlockSpec(memory_space=pl.ANY)
    vspec = pl.BlockSpec(memory_space=pltpu.VMEM)
    sspec = pl.BlockSpec(memory_space=pltpu.SMEM)
    P2 = D // 2
    outs = (
        jax.ShapeDtypeStruct((H, D), BF),
        jax.ShapeDtypeStruct((H, D), F32),
        jax.ShapeDtypeStruct((FL, D), BF),
        jax.ShapeDtypeStruct((D, FL), BF),
        jax.ShapeDtypeStruct((VL, D), BF),
        jax.ShapeDtypeStruct((4, D, P2), BF),
        jax.ShapeDtypeStruct((D, VL), BF),
        jax.ShapeDtypeStruct((D, VL), BF),
        jax.ShapeDtypeStruct((D, Z), F32),
        jax.ShapeDtypeStruct((352, 128), F32),
    )
    dma = pltpu.SemaphoreType.DMA
    scratch = [
        vm((D, Z), BF), vm((D, VL), BF), vm((D, VL), BF), vm((VL, D), BF), vm((D, D), BF), vm((D, D), BF), vm((D, FL), BF), vm((FL, D), BF),
        vm((R, D), BF), vm((R, D), BF), vm((R, D)), vm((R, D), BF), vm((R, D), BF), vm((R, D)), vm((R * 8, 128)), vm((R * 8, 128)),
        vm((R, Z)), vm((R, Z), BF), vm((R, Z), BF), vm((R, BLOCK)), vm((R, BLOCK), BF),
        vm((R, VL)), vm((R, VL)), vm((R, VL)), vm((R, VL), BF), vm((R, VL), BF), vm((H, D), BF), vm((H, D), BF), vm((H, D)), vm((H, D)), vm((H, D)), vm((H, D)), vm((R, D), BF),
        vm((R, FL)), vm((R, FL), BF), vm((R, FL), BF), vm((H, D), BF), vm((H, D), BF), vm((H, D), BF), vm((R, D), BF), vm((R, D), BF), vm((R, VL), BF), vm((R, VL), BF), vm((R, BLOCK)), vm((H, BLOCK)), vm((R, Z), BF),
        vm((H, D), BF), vm((H, D), BF), vm((H, D), BF),
        vm((R, D), BF), vm((R, D), BF), vm((R, D), BF), vm((R, FL // 2), BF), vm((R, D), BF), vm((R, FL // 2), BF), vm((R, VL), BF), vm((R, D), BF), vm((R, D), BF), vm((R, VL // 2), BF), vm((R, VL // 2), BF), vm((R, Z), BF),
        vm((128, 128)), vm((128, 128)), vm((128, 128)), vm((128, 128)), vm((128, 128)), vm((128, 128)), vm((24, D)), vm((R, 128)), vm((R, 128)), vm((R, 128)), vm((8, D)), vm((8, FL)),
        vm((8, D, P2), BF), vm((11 * 256, P2), BF), vm((352, 128)), vm((3, 88, 128)), vm((344, 128)), vm((344, 128)), vm((NZ - 1, 344, 128)),
        dma((10,)), dma((23,)), dma((23,)), dma((12,)), dma((12,)), dma((96,)), dma((SEMS,)), dma((SEMS,)), pltpu.SemaphoreType.REGULAR((3,)),
    ]
    return pl.pallas_call(
        main_kernel,
        out_shape=outs,
        in_specs=[anyspec] * 10 + [sspec, sspec] + [vspec] * 14,
        out_specs=(vspec, vspec) + (anyspec,) * 6 + (vspec, vspec),
        scratch_shapes=scratch,
        compiler_params=pltpu.CompilerParams(collective_id=0, has_side_effects=True, vmem_limit_bytes=63 * 1024 * 1024),
        cost_estimate=pl.CostEstimate(flops=15_000_000_000, bytes_accessed=40_000_000, transcendentals=0),
    )(
        tokens, cotangent, w_shared, w_value, w_reset, w_mix, w_hidden, w_update, w_up, w_down,
        seq_lengths, rel_bias.reshape(1, -1), bucket_map.reshape(1, -1), *rows8, ema_rate, ema_damp, ema_in, ema_out,
        qk_gain, qk_bias, b_up.reshape(-1, 128),
    )


def finish_kernel(down, up, mix, reset, value, h0, h1, u0, u1, small, rate, damp, ein, eout, bmap, bo, gt, shared,
                  f_down, f_up, f_mix, f_reset, f_value, f_hid, f_upd, g_rate, g_damp, g_in, g_out, v0, v1, v2, v3, v4, v5, g_bup, g_gain, g_bias, g_rel, f_bo, f_gt, f_shared):
    for src, dst in ((down, f_down), (up, f_up), (mix, f_mix), (reset, f_reset), (value, f_value)):
        dst[...] = src[...].astype(F32)
    half = h0.shape[2]
    for left, right, dst in ((h0, h1, f_hid), (u0, u1, f_upd)):
        dst[:, 0:half] = left[0].astype(F32)
        dst[:, half : 2 * half] = right[0].astype(F32)

    @pl.when(pl.program_id(0) == 0)
    def _():
        for t in range(2):
            for j in range(8):
                rows_ = slice(t * 8, t * 8 + 8)
                lanes = slice(j * 128, j * 128 + 128)
                gw = small[pl.ds(t * 64 + j, 8, stride=8), :]
                ga = small[pl.ds(128 + t * 64 + j, 8, stride=8), :]
                r_, d_ = rate[rows_, lanes], damp[rows_, lanes]
                i_, o_ = ein[rows_, lanes], eout[rows_, lanes]
                g_rate[rows_, lanes] = gw * (i_ * o_) - ga * d_
                g_damp[rows_, lanes] = -ga * r_
                g_in[rows_, lanes] = gw * (r_ * o_)
                g_out[rows_, lanes] = gw * (r_ * i_)
        for k, ref in enumerate((v0, v1, v2, v3, v4, v5)):
            ref[...] = small[256 + 8 * k : 264 + 8 * k, :]
        f_bo[...] = bo[...]
        f_gt[...] = gt[...]
        f_shared[...] = shared[...]
        me = lax.axis_index("narrow")
        g_bup[...] = small[pl.ds(pl.multiple_of(304 + me * 16, 8), 16), :]
        g_gain[...] = small[336:338, :]
        g_bias[...] = small[338:340, :]
        n = bmap.shape[1]
        offs = jnp.broadcast_to(small[340:341, :], (n, n)).T
        which = jnp.broadcast_to(bmap[...].astype(F32), (n, n)).T
        lane = lax.broadcasted_iota(jnp.int32, (n, n), 1).astype(F32)
        hits = jnp.sum(jnp.where(which == lane, offs, 0.0), axis=0, keepdims=True)
        g_rel[...] = hits[:, 0 : g_rel.shape[1]]


def run_finish(grads, hu, whole, small, rate, damp, ein, eout, bucket_map, nbuck):
    steps = 8

    def part(a):
        return pl.BlockSpec((a.shape[0] // steps, a.shape[1]), lambda i: (i, 0))

    def full(shape):
        return pl.BlockSpec(shape, lambda i: (0,) * len(shape))

    bmap = bucket_map.reshape(1, -1)
    D = rate.shape[1]
    square = jax.ShapeDtypeStruct((D, D), F32)
    outs = [jax.ShapeDtypeStruct(a.shape, F32) for a in grads] + [square, square]
    per = steps // 4
    hu_specs = [pl.BlockSpec((1, D // steps, D // 2), lambda i, b=b: (i // per, b * per + i % per, 0)) for b in range(4)]
    outs += [jax.ShapeDtypeStruct(rate.shape, F32) for _ in range(4)]
    outs += [jax.ShapeDtypeStruct((8, 128), F32) for _ in range(6)]
    outs += [jax.ShapeDtypeStruct((16, 128), F32), jax.ShapeDtypeStruct((2, 128), F32), jax.ShapeDtypeStruct((2, 128), F32),
             jax.ShapeDtypeStruct((1, nbuck), F32)]
    outs += [jax.ShapeDtypeStruct(a.shape, a.dtype) for a in whole]
    smalls = (small, rate, damp, ein, eout, bmap) + tuple(whole)
    return pl.pallas_call(
        finish_kernel,
        grid=(steps,),
        out_shape=tuple(outs),
        in_specs=[part(a) for a in grads] + hu_specs + [full(a.shape) for a in smalls],
        out_specs=tuple([part(a) for a in outs[:7]] + [full(o.shape) for o in outs[7:]]),
        compiler_params=pltpu.CompilerParams(vmem_limit_bytes=60 * 1024 * 1024),
    )(*grads, hu, hu, hu, hu, *smalls)


def shards_fast(*args):
    bo, gt, down, up, mix, hu, reset, value, shared, small = run_main(*args)
    (tokens, cotangent, seq_lengths, bucket_map, norm1_gain, norm1_bias, ema_rate, ema_damp, ema_in, ema_out,
     ema_skip, w_shared, qk_gain, qk_bias, rel_bias) = args[:15]
    (down, up, mix, reset, value, hidden, update, g_rate, g_damp, g_in, g_out, skip, n1g, n1b, bupd, n2g, n2b,
     g_bup, g_gain, g_bias, g_rel, bo, gt, shared) = run_finish(
        (down, up, mix, reset, value), hu, (bo, gt, shared), small, ema_rate, ema_damp, ema_in, ema_out, bucket_map,
        rel_bias.shape[0])
    skip, n1g, n1b, bupd, n2g, n2b = [v.reshape(-1) for v in (skip, n1g, n1b, bupd, n2g, n2b)]
    return (bo, gt, n1g, n1b, g_rate, g_damp, g_in, g_out, skip, shared, g_gain, g_bias, g_rel.reshape(-1),
            value, reset, mix, hidden, update, bupd, n2g, n2b, up, g_bup.reshape(-1), down)


def solution(mesh):
    in_specs = (
        P(("wide", "narrow"), None),
        P(("wide", "narrow"), None),
        P("wide", None),
        P(),
        P(),
        P(),
        P(),
        P(),
        P(),
        P(),
        P(),
        P(),
        P(),
        P(),
        P(),
        P(None, "narrow"),
        P(None, "narrow"),
        P("narrow", None),
        P(),
        P(),
        P(),
        P(),
        P(),
        P(None, "narrow"),
        P("narrow"),
        P("narrow", None),
    )
    out_specs = (
        P(("wide", "narrow"), None),
        P(("wide", "narrow"), None),
        P(),
        P(),
        P(),
        P(),
        P(),
        P(),
        P(),
        P(),
        P(),
        P(),
        P(),
        P(None, "narrow"),
        P(None, "narrow"),
        P("narrow", None),
        P(),
        P(),
        P(),
        P(),
        P(),
        P(None, "narrow"),
        P("narrow"),
        P("narrow", None),
    )
    body = shards_fast if (mesh.shape["wide"], mesh.shape["narrow"]) == (16, 2) else shards
    return jax.shard_map(body, mesh=mesh, in_specs=in_specs, out_specs=out_specs, check_vma=False)
```

```python
import jax
import jax.numpy as jnp
from jax import lax
from jax.experimental import pallas as pl
from jax.experimental.pallas import tpu as pltpu
from jax.sharding import PartitionSpec as P

BLOCK = 128


EPSILON = 1e-05
NEGATIVE = -1000000000.0


def carried_in(part, axis, combine, identity, reverse):
    count = lax.axis_size(axis)
    place = lax.axis_index(axis)
    ahead = count - 1 - place if reverse else place
    gathered = jax.tree.map(lambda a: lax.all_gather(a, axis), part)
    state = jax.tree.map(lambda a, e: jnp.zeros_like(a) + jnp.asarray(e, a.dtype), part, identity)

    def one(lap, state):
        source = count - 1 - lap if reverse else lap
        return combine(
            state, jax.tree.map(lambda a: lax.dynamic_index_in_dim(a, source, 0, False), gathered)
        )

    return lax.fori_loop(0, ahead, one, state)


def layer_norm(rows_in, gain, shift):
    row_mean = jnp.mean(rows_in, axis=-1, keepdims=True)
    centred = rows_in - row_mean
    row_var = jnp.mean(centred * centred, axis=-1, keepdims=True)
    return centred * lax.rsqrt(row_var + EPSILON) * gain + shift


def silu_slope(pre_act):
    sigmoid_val = jax.nn.sigmoid(pre_act)
    return sigmoid_val * (1.0 + pre_act * (1.0 - sigmoid_val))


def segment_info(lengths, positions):
    first_end = lengths[0]
    second_end = lengths[0] + lengths[1]
    segment = (positions >= first_end).astype(jnp.int32) + (positions >= second_end).astype(
        jnp.int32
    )
    starts = ((positions == 0) | (positions == first_end) | (positions == second_end)).astype(
        jnp.float32
    )
    live_rows = (segment < 2).astype(jnp.float32)
    return (segment, starts, live_rows)


def combine_pair(earlier, following):
    return (earlier[0] * following[0], earlier[1] * following[0] + following[1])


def ema_local(normed, live_rows, starts, ema_rate, ema_damp, ema_in, ema_out, ema_skip, state_in):
    inputs = normed * live_rows[:, None]
    keep_rate = 1.0 - ema_rate * ema_damp
    drive_rate = ema_rate * ema_in
    decay = keep_rate[None] * (1.0 - starts)[:, None, None]
    drive = drive_rate[None] * inputs[:, None, :]
    decay_cum, partial_state = lax.associative_scan(combine_pair, (decay, drive), axis=0)
    states = partial_state + decay_cum * state_in[None]
    smooth = jnp.sum(states * ema_out[None], axis=1)
    ema_mixed = jax.nn.silu(smooth + ema_skip * normed)
    return (ema_mixed, states[-1])


def block_bias(rel_bias, bucket_map):
    by_offset = jnp.take(rel_bias, bucket_map)
    row_index = jnp.arange(BLOCK, dtype=jnp.int32)
    offsets = row_index[:, None] - row_index[None, :]
    return (jnp.take(by_offset, jnp.clip(offsets, 0, BLOCK - 1)), offsets)


def attention_probs(query_all, key_all, segment_all, bias_table, offsets):
    blocks = query_all.shape[0] // BLOCK
    query_blocks = query_all.reshape(blocks, BLOCK, -1)
    key_blocks = key_all.reshape(blocks, BLOCK, -1)
    seg_blocks = segment_all.reshape(blocks, BLOCK)
    allowed = (seg_blocks[:, :, None] == seg_blocks[:, None, :]) & (offsets >= 0)[None]
    score_scale = query_all.shape[-1] ** (-0.5)
    scores = (
        jnp.einsum("bik,bjk->bij", query_blocks, key_blocks, preferred_element_type=jnp.float32)
        * score_scale
    )
    scores = jnp.where(allowed, scores + bias_table[None], NEGATIVE)
    row_max = jnp.max(scores, axis=-1, keepdims=True)
    weighted = jnp.exp(scores - row_max)
    return weighted / jnp.sum(weighted, axis=-1, keepdims=True)


def shards(
    tokens,
    cotangent,
    seq_lengths,
    bucket_map,
    norm1_gain,
    norm1_bias,
    ema_rate,
    ema_damp,
    ema_in,
    ema_out,
    ema_skip,
    w_shared,
    qk_gain,
    qk_bias,
    rel_bias,
    w_value,
    w_reset,
    w_mix,
    w_hidden,
    w_update,
    b_update,
    norm2_gain,
    norm2_bias,
    w_up,
    b_up,
    w_down,
):
    row_count = tokens.shape[0]
    narrow_count = lax.axis_size("narrow")
    narrow_rank = lax.axis_index("narrow")
    group_rows = row_count * narrow_count
    blocks = group_rows // BLOCK
    local_blocks = row_count // BLOCK
    lengths = seq_lengths[0]
    local_positions = narrow_rank * row_count + jnp.arange(row_count, dtype=jnp.int32)
    segment_local, starts, live_rows = segment_info(lengths, local_positions)
    segment_all = segment_info(lengths, jnp.arange(group_rows, dtype=jnp.int32))[0]
    tokens_f = tokens.astype(jnp.float32)
    normed, norm1_back = jax.vjp(layer_norm, tokens_f, norm1_gain, norm1_bias)

    def ema_apply(normed_in, rate_in, damp_in, in_weight, out_weight, skip_in, state_in):
        return ema_local(
            normed_in, live_rows, starts, rate_in, damp_in, in_weight, out_weight, skip_in, state_in
        )

    zero_state = jnp.zeros_like(ema_rate)
    ones_state = jnp.ones_like(ema_rate)
    local_final = ema_apply(normed, ema_rate, ema_damp, ema_in, ema_out, ema_skip, zero_state)[1]
    through = jnp.power(1.0 - ema_rate * ema_damp, row_count) * (1.0 - jnp.max(starts))
    state_in = carried_in(
        (through, local_final), "narrow", combine_pair, (ones_state, zero_state), False
    )[1]
    (ema_mixed, final_state), ema_back = jax.vjp(
        ema_apply, normed, ema_rate, ema_damp, ema_in, ema_out, ema_skip, state_in
    )
    normed_low = normed.astype(jnp.bfloat16)
    mixed_low = ema_mixed.astype(jnp.bfloat16)
    pre_shared = jnp.dot(mixed_low, w_shared, preferred_element_type=jnp.float32)
    shared_act = jax.nn.silu(pre_shared)
    query_low = (shared_act * qk_gain[0] + qk_bias[0]).astype(jnp.bfloat16)
    key_low = (shared_act * qk_gain[1] + qk_bias[1]).astype(jnp.bfloat16)
    normed_all, mixed_all, query_all, key_all = (
        lax.all_gather(normed_low, "narrow", axis=0, tiled=True),
        lax.all_gather(mixed_low, "narrow", axis=0, tiled=True),
        lax.all_gather(query_low, "narrow", axis=0, tiled=True),
        lax.all_gather(key_low, "narrow", axis=0, tiled=True),
    )
    bias_table, offsets = block_bias(rel_bias, bucket_map)
    probs_low = attention_probs(query_all, key_all, segment_all, bias_table, offsets).astype(
        jnp.bfloat16
    )
    pre_value = jnp.dot(normed_all, w_value, preferred_element_type=jnp.float32)
    value_low = jax.nn.silu(pre_value).astype(jnp.bfloat16)
    value_blocks = value_low.reshape(blocks, BLOCK, -1)
    pre_reset = jnp.dot(mixed_all, w_reset, preferred_element_type=jnp.float32)
    reset_gate = jax.nn.silu(pre_reset)
    attended = jnp.einsum(
        "bij,bjv->biv", probs_low, value_blocks, preferred_element_type=jnp.float32
    ).reshape(group_rows, -1)
    gated_low = (reset_gate * attended).astype(jnp.bfloat16)
    piece = gated_low
    mix_part = lax.psum_scatter(
        jnp.dot(piece, w_mix, preferred_element_type=jnp.float32),
        "narrow",
        scatter_dimension=0,
        tiled=True,
    )
    pre_hidden = jnp.dot(mixed_low, w_hidden, preferred_element_type=jnp.float32) + mix_part
    hidden_act = jax.nn.silu(pre_hidden)
    pre_update = jnp.dot(mixed_low, w_update, preferred_element_type=jnp.float32) + b_update
    update_gate = jax.nn.sigmoid(pre_update)
    blended = update_gate * hidden_act + (1.0 - update_gate) * tokens_f
    normed2, norm2_back = jax.vjp(layer_norm, blended, norm2_gain, norm2_bias)
    normed2_low = normed2.astype(jnp.bfloat16)
    grad_out = cotangent.astype(jnp.float32) * live_rows[:, None]
    grad_out_low = grad_out.astype(jnp.bfloat16)
    normed2_all = lax.all_gather(normed2_low, "narrow", axis=0, tiled=True)
    pre_up = jnp.dot(normed2_all, w_up, preferred_element_type=jnp.float32) + b_up.astype(
        jnp.float32
    )
    up_low = jax.nn.silu(pre_up).astype(jnp.bfloat16)
    piece = up_low
    ffn_out = lax.psum_scatter(
        jnp.dot(piece, w_down, preferred_element_type=jnp.float32),
        "narrow",
        scatter_dimension=0,
        tiled=True,
    )
    grad_out_all = lax.all_gather(grad_out_low, "narrow", axis=0, tiled=True)
    grad_up = jnp.einsum("sd,fd->sf", grad_out_all, w_down, preferred_element_type=jnp.float32)
    grad_pre_up = (grad_up * silu_slope(pre_up)).astype(jnp.bfloat16)
    grad_w_down = jnp.einsum("sf,sd->fd", up_low, grad_out_all, preferred_element_type=jnp.float32)
    grad_w_up = jnp.einsum(
        "sd,sf->df", normed2_all, grad_pre_up, preferred_element_type=jnp.float32
    )
    grad_b_up = jnp.sum(grad_pre_up.astype(jnp.float32), axis=0)
    piece = grad_pre_up
    grad_normed2 = lax.psum_scatter(
        jnp.einsum("sf,df->sd", piece, w_up, preferred_element_type=jnp.float32),
        "narrow",
        scatter_dimension=0,
        tiled=True,
    )
    block_out = (blended + ffn_out).astype(jnp.bfloat16)
    grad_blended_norm, grad_norm2_gain, grad_norm2_bias = norm2_back(grad_normed2)
    grad_blended = grad_out + grad_blended_norm
    grad_hidden = grad_blended * update_gate
    grad_gate = grad_blended * (hidden_act - tokens_f)
    grad_tokens = grad_blended * (1.0 - update_gate)
    grad_pre_update = (grad_gate * update_gate * (1.0 - update_gate)).astype(jnp.bfloat16)
    grad_pre_hidden = (grad_hidden * silu_slope(pre_hidden)).astype(jnp.bfloat16)
    grad_b_update = jnp.sum(grad_pre_update.astype(jnp.float32), axis=0)
    grad_w_update = jnp.einsum(
        "sd,se->de", mixed_low, grad_pre_update, preferred_element_type=jnp.float32
    )
    grad_w_hidden = jnp.einsum(
        "sd,se->de", mixed_low, grad_pre_hidden, preferred_element_type=jnp.float32
    )
    hidden_all = lax.all_gather(grad_pre_hidden, "narrow", axis=0, tiled=True)
    grad_w_mix = jnp.einsum("sv,sd->vd", gated_low, hidden_all, preferred_element_type=jnp.float32)
    grad_gated = jnp.einsum("sd,vd->sv", hidden_all, w_mix, preferred_element_type=jnp.float32)
    grad_reset = grad_gated * attended
    grad_attended = (grad_gated * reset_gate).astype(jnp.bfloat16)
    grad_pre_reset = (grad_reset * silu_slope(pre_reset)).astype(jnp.bfloat16)
    grad_w_reset = jnp.einsum(
        "sd,sv->dv", mixed_all, grad_pre_reset, preferred_element_type=jnp.float32
    )
    attended_blocks = grad_attended.reshape(blocks, BLOCK, -1)
    probs_again = attention_probs(query_all, key_all, segment_all, bias_table, offsets)
    grad_probs = jnp.einsum(
        "biv,bjv->bij", attended_blocks, value_blocks, preferred_element_type=jnp.float32
    )
    grad_value = jnp.einsum(
        "bij,biv->bjv",
        probs_again.astype(jnp.bfloat16),
        attended_blocks,
        preferred_element_type=jnp.float32,
    ).reshape(group_rows, -1)
    grad_pre_value = (grad_value * silu_slope(pre_value)).astype(jnp.bfloat16)
    grad_w_value = jnp.einsum(
        "sd,sv->dv", normed_all, grad_pre_value, preferred_element_type=jnp.float32
    )
    mixed_cols = jnp.einsum(
        "sv,dv->sd", grad_pre_reset, w_reset, preferred_element_type=jnp.float32
    )
    normed_cols = jnp.einsum(
        "sv,dv->sd", grad_pre_value, w_value, preferred_element_type=jnp.float32
    )
    probs_rows, mixed_back, normed_back = (
        lax.psum_scatter(
            grad_probs.reshape(group_rows, BLOCK), "narrow", scatter_dimension=0, tiled=True
        ),
        lax.psum_scatter(mixed_cols, "narrow", scatter_dimension=0, tiled=True),
        lax.psum_scatter(normed_cols, "narrow", scatter_dimension=0, tiled=True),
    )
    probs_local = lax.dynamic_slice_in_dim(probs_again, narrow_rank * local_blocks, local_blocks, 0)
    grad_probs_local = probs_rows.reshape(local_blocks, BLOCK, BLOCK)
    grad_scores = probs_local * (
        grad_probs_local - jnp.sum(grad_probs_local * probs_local, axis=-1, keepdims=True)
    )
    grad_scores_low = grad_scores.astype(jnp.bfloat16)
    score_scale = query_low.shape[-1] ** (-0.5)
    query_blocks = query_low.reshape(local_blocks, BLOCK, -1)
    key_blocks = key_low.reshape(local_blocks, BLOCK, -1)
    grad_query = (
        jnp.einsum(
            "bij,bjk->bik", grad_scores_low, key_blocks, preferred_element_type=jnp.float32
        ).reshape(row_count, -1)
        * score_scale
    )
    grad_key = (
        jnp.einsum(
            "bij,bik->bjk", grad_scores_low, query_blocks, preferred_element_type=jnp.float32
        ).reshape(row_count, -1)
        * score_scale
    )
    score_total = jnp.sum(grad_scores_low.astype(jnp.float32), axis=0)
    offset_hits = (offsets[:, :, None] == jnp.arange(BLOCK, dtype=jnp.int32)[None, None, :]).astype(
        jnp.float32
    )
    grad_offset = jnp.sum(score_total[:, :, None] * offset_hits, axis=(0, 1))
    bucket_hits = (
        bucket_map[:, None] == jnp.arange(rel_bias.shape[0], dtype=jnp.int32)[None, :]
    ).astype(jnp.float32)
    grad_rel_bias = jnp.sum(grad_offset[:, None] * bucket_hits, axis=0)
    grad_shared_act = grad_query * qk_gain[0] + grad_key * qk_gain[1]
    grad_qk_gain = jnp.stack(
        [jnp.sum(grad_query * shared_act, axis=0), jnp.sum(grad_key * shared_act, axis=0)]
    )
    grad_qk_bias = jnp.stack([jnp.sum(grad_query, axis=0), jnp.sum(grad_key, axis=0)])
    grad_pre_shared = (grad_shared_act * silu_slope(pre_shared)).astype(jnp.bfloat16)
    grad_w_shared = jnp.einsum(
        "sd,sz->dz", mixed_low, grad_pre_shared, preferred_element_type=jnp.float32
    )
    grad_mixed = (
        mixed_back
        + jnp.einsum("sz,dz->sd", grad_pre_shared, w_shared, preferred_element_type=jnp.float32)
        + jnp.einsum("se,de->sd", grad_pre_hidden, w_hidden, preferred_element_type=jnp.float32)
        + jnp.einsum("se,de->sd", grad_pre_update, w_update, preferred_element_type=jnp.float32)
    )
    direct = ema_back((grad_mixed, zero_state))
    later_state = carried_in(
        (through, direct[6]), "narrow", combine_pair, (ones_state, zero_state), True
    )[1]
    chained = ema_back((jnp.zeros_like(ema_mixed), later_state))
    grad_normed = normed_back + direct[0] + chained[0]
    grad_tokens_norm, grad_norm1_gain, grad_norm1_bias = norm1_back(grad_normed)
    grad_tokens = grad_tokens + grad_tokens_norm
    grad_ema_rate = direct[1] + chained[1]
    grad_ema_damp = direct[2] + chained[2]
    grad_ema_in = direct[3] + chained[3]
    grad_ema_out = direct[4] + chained[4]
    grad_ema_skip = direct[5] + chained[5]
    grad_w_value, grad_w_reset, grad_w_mix, grad_w_up, grad_b_up, grad_w_down = lax.psum(
        (grad_w_value, grad_w_reset, grad_w_mix, grad_w_up, grad_b_up, grad_w_down), "wide"
    )
    (
        grad_norm1_gain,
        grad_norm1_bias,
        grad_ema_rate,
        grad_ema_damp,
        grad_ema_in,
        grad_ema_out,
        grad_ema_skip,
        grad_w_shared,
        grad_qk_gain,
        grad_qk_bias,
        grad_rel_bias,
        grad_w_hidden,
        grad_w_update,
        grad_b_update,
        grad_norm2_gain,
        grad_norm2_bias,
    ) = lax.psum(
        (
            grad_norm1_gain,
            grad_norm1_bias,
            grad_ema_rate,
            grad_ema_damp,
            grad_ema_in,
            grad_ema_out,
            grad_ema_skip,
            grad_w_shared,
            grad_qk_gain,
            grad_qk_bias,
            grad_rel_bias,
            grad_w_hidden,
            grad_w_update,
            grad_b_update,
            grad_norm2_gain,
            grad_norm2_bias,
        ),
        ("wide", "narrow"),
    )
    return (
        block_out,
        grad_tokens,
        grad_norm1_gain,
        grad_norm1_bias,
        grad_ema_rate,
        grad_ema_damp,
        grad_ema_in,
        grad_ema_out,
        grad_ema_skip,
        grad_w_shared,
        grad_qk_gain,
        grad_qk_bias,
        grad_rel_bias,
        grad_w_value,
        grad_w_reset,
        grad_w_mix,
        grad_w_hidden,
        grad_w_update,
        grad_b_update,
        grad_norm2_gain,
        grad_norm2_bias,
        grad_w_up,
        grad_b_up,
        grad_w_down,
    )


NZ = 4
ROOT = 1
NEAR = (0, 2, 3)
EVEN, ENDS = (0, 1, 2, 3), (0, 3, 0, 3)
MIXED = (0, 3, 1, 2)
UNITS = (
    (0, 1, 0, 512, ENDS), (0, 0, 512, 512, MIXED), (1, 0, 0, 512, ENDS), (1, 2, 512, 512, EVEN), (2, 1, 0, 1024, EVEN), (3, 1, 0, 1024, ENDS),
    (4, 1, 0, 1024, MIXED), (5, 0, 0, 512, MIXED), (5, 0, 512, 512, MIXED), (6, 1, 0, 256, EVEN), (6, 2, 256, 768, ENDS),
    (7, 1, 0, 512, ENDS), (7, 1, 512, 512, ENDS),
)
PHASES = (1.8, 1.2, 2.4, 1.8, 4.2, 1.4, 6.6, 1.8, 1.8, 1.8, 1.2, 1.2, 1.0, 1.8, 1.0, 2.4, 1.0, 1.2, 2.4, 1.6, 1.6, 1.6, 1.6, 4.8, 1.2)
RELEASE = {0: 0, 1: 0, 2: 3, 3: 3, 4: 12, 5: 14, 6: 16, 7: 17}
EARLY = tuple(u for u, t in enumerate(UNITS) if t[0] < 2)
UNIT, LAG = 3.0, 2.0
MARGIN, WINDOW = 0.0, 1000.0
RANKS = {"G": 1, "P": 1, "C": 1, "D": 1, "F": 2, "W": 2, "Y": 4, "X": 4, "S": 0}
BY_UNIT = False


def far_first(z, roots):
    return sorted(range(NZ), key=lambda k: (-abs(roots[k] - z), k))


def line_events(z):
    found = []
    for u, (i, first, _, rows, roots) in enumerate(UNITS):
        size = rows / (1024.0 if first else 512.0)
        late = RELEASE[i]
        for k in range(NZ):
            g = roots[k]
            left = ("l", z - 1, ("zr", u, k), size)
            right = ("r", z + 1, ("zl", u, k), size)
            cross = [("y", z, ("yf", u, k), size)]
            far = [("x", z, ("xf", u, k, 0), size)] if i == 5 else []
            far += [("c", z, ("cf", u, k, 0), size)]
            on = (cross if first == 1 else []) + far
            both = ([left] if z > 0 else []) + ([right] if z < NZ - 1 else []) + (cross if first else []) + far
            need = [("yr", u, k)] if first else []
            if first:
                found.append((("G", u, k), late, None, [], [("y", z, ("yr", u, k), size)], 0.1))
            if z > 0 and g >= z:
                need.append(("zl", u, k))
            if z < NZ - 1 and g <= z:
                need.append(("zr", u, k))
            if g != z:
                found.append((("P", u, k), late, None, need, [right if g > z else left], 0.4))
                further = [left] if g > z > 0 else [right] if g < z < NZ - 1 else []
                found.append((("F", u, k), late, ("P", u, k), [("zr" if g > z else "zl", u, k)], further + on, 0.2))
            else:
                swap = both if first else [("y", z, ("yr", u, k), size)]
                found.append((("C", u, k), late, None, need, swap, 0.4))
                if not first:
                    found.append((("D", u, k), late, ("C", u, k), [("yr", u, k)], both, 0.4))
            other = [("x", z, ("xf", u, k, 1), size)] if i == 5 else []
            other += [("c", z, ("cf", u, k, 1), size)]
            if first == 1:
                found.append((("Y", u, k), late, ("G", u, k), [("yf", u, k)], other, 0.2))
            if first == 2:
                left = ("l", z - 1, ("wr", u, k), size)
                right = ("r", z + 1, ("wl", u, k), size)
                if g == z:
                    both = ([left] if z > 0 else []) + ([right] if z < NZ - 1 else []) + other
                    found.append((("Y", u, k), late, ("G", u, k), [("yf", u, k)], both, 0.2))
                else:
                    further = [left] if g > z > 0 else [right] if g < z < NZ - 1 else []
                    found.append((("W", u, k), late, ("G", u, k), [("wr" if g > z else "wl", u, k)], further + other, 0.2))
            if i == 5:
                for h in range(2 if first else 1):
                    found.append((("X", u, k, h), late, None, [("xf", u, k, h)], [("c", z, ("cf", u, k, 2 + h), size)], 0.2))
    last = len(PHASES) - 1

    def small(n, after, need, out):
        found.append((("S", n, 0), last, after, need, out, 0.4))

    small(1, None, [], [("x", z, ("s1",), 0.7), ("c", z, ("s1c",), 0.7)])
    small(3, ("S", 1, 0), [("s1",)], [("y", z, ("s3",), 1.35)])
    inward = [] if z == ROOT else [("r" if z < ROOT else "l", ROOT, ("s4", z), 1.35)]
    small(4, ("S", 3, 0), [("s3",)], inward)
    tail = [("c", z, ("s6",), 1.35), ("x", z, ("s7",), 1.35)]
    if z == ROOT:
        out = [("l" if q < ROOT else "r", q, ("s5",), 1.35) for q in NEAR]
        small(6, ("S", 4, 0), [("s4", q) for q in NEAR], out + tail)
    else:
        small(7, ("S", 4, 0), [("s5",)], tail)
    return found


def make_plan():
    todo = [line_events(z) for z in range(NZ)]
    clock = [0.0] * NZ
    phase = [0] * NZ
    done = [set() for _ in range(NZ)]
    arrive = [{} for _ in range(NZ)]
    link = {}
    plan = [[[] for _ in range(len(PHASES) + 1)] for _ in range(NZ)]
    while any(todo) or min(phase) < len(PHASES):
        z = min(range(NZ), key=lambda q: (clock[q], q) if (todo[q] or phase[q] < len(PHASES)) else (1e9, q))
        now = clock[z]
        best = None
        for item in todo[z]:
            key, late, after, need, out, cost = item
            if phase[z] <= late or (after is not None and after not in done[z]):
                continue
            latest = 0.0
            for m in need:
                latest = max(latest, arrive[z].get(m, 1e9))
            if need and latest + (MARGIN if phase[z] < len(PHASES) else 0.0) > now:
                continue
            full = phase[z] >= len(PHASES) and key[0] != "S" and any(
                link.get((z, lane), 0.0) > now + WINDOW for lane, _, _, _ in out if lane in "ylr")
            if full:
                continue
            away = -abs(UNITS[key[1]][4][key[2]] - z) if key[0] != "S" else 0
            rank = RANKS[key[0]]
            if key[0] == "Y" and UNITS[key[1]][1] == 2:
                rank = RANKS["F"]
            order = (rank, key[1] if BY_UNIT else latest, away, key[1], key[2])
            if best is None or order < best[0]:
                best = (order, item)
        if best is not None:
            item = best[1]
            todo[z].remove(item)
            key, _, _, _, out, cost = item
            done[z].add(key)
            plan[z][phase[z]].append(key)
            clock[z] += 0.8 * cost
            for lane, dest, message, size in out:
                begin = max(link.get((z, lane), 0.0), clock[z])
                took = size * UNIT * (0.2 if lane == "c" else 1.0)
                link[(z, lane)] = begin + took
                arrive[dest][message] = begin + took + LAG
        elif phase[z] < len(PHASES):
            clock[z] += PHASES[phase[z]]
            phase[z] += 1
        else:
            clock[z] += 0.1
    ends = [max([clock[z]] + list(arrive[z].values())) for z in range(NZ)]
    return plan, ends

F32 = jnp.float32
BF = jnp.bfloat16
MESH = pl.DeviceIdType.MESH


def mm(a, b):
    return lax.dot_general(a, b, (((1,), (0,)), ((), ())), preferred_element_type=F32)


def mm_nt(a, b):
    return lax.dot_general(a, b, (((1,), (1,)), ((), ())), preferred_element_type=F32)


def mm_tn(a, b):
    return lax.dot_general(a, b, (((0,), (0,)), ((), ())), preferred_element_type=F32)


def sigm(v):
    return 1.0 / (1.0 + jnp.exp(-v))


def slope_of(pre, sig):
    return sig * (1.0 + pre * (1.0 - sig))


def cols(i, n):
    return pl.ds(pl.multiple_of(i * n, n), n)


def main_kernel(
    tok_h, cot_h, wsh_h, wv_h, wr_h, wm_h, wh_h, wu_h, wup_h, wdn_h,
    lens, relb, bmap, in_n1g, in_n1b, in_skip, in_bupd, in_n2g, in_n2b, rate, damp, ein, eout, qkg, qkb, in_bup,
    bo, gt, o_down, o_up, o_mix, o_hu, o_reset, o_value, o_shared, o_small,
    wsh, wv, wr, wm, wh, wu, wup, wdn,
    tok, gout, normed, nlow, mlow, pre_ema, xs, smo, pre_sh, qlow, klow, probs, plow,
    pre_v, att, pre_r, vlow, gated, part_s, mix_r, own_f, pre_hid, gate, blend, n2,
    gup, up, gpu, gn2_r, ffn_s, ffn_r, hid, upd, gpr, gpv, gp_acc, gp_r, gps,
    nb_s, mb_r, nb_r,
    p_normed, p_mixed, p_gout, p_up, p_n2, p_gpu, p_gated, p_hid, p_upd, p_gpr, p_gpv, p_gps,
    a_s, w_s, snap_s, snap_r, carry, carry_r, acc, keep, live, segc, vec, bup,
    g_v, ext, small, s_q, s_own, s_y, s_in,
    wsem, xsend, xrecv, csend, crecv, lsem, asend, arecv, ready,
):
    x = lax.axis_index("narrow")
    w = lax.axis_index("wide")
    other = 1 - x
    c = w % 2
    wpart = w + 1 - 2 * c
    y = (w // 2) % 2
    wy = w + 2 - 4 * y
    zi = w // 4
    wl = w - 4
    wr_ = w + 4
    H = tok.shape[0] // 2
    R = 2 * H
    own = pl.ds(pl.multiple_of(x * H, H), H)
    oth = pl.ds(pl.multiple_of(other * H, H), H)
    D = 1024
    VL = wv.shape[1]
    FL = wup.shape[1]
    EPS = EPSILON

    weights = [
        (tok_h, tok.at[own]), (cot_h, gout.at[own]), (wsh_h, wsh), (wv_h, wv), (wr_h, wr), (wm_h, wm), (wh_h, wh), (wu_h, wu), (wdn_h, wdn),
        (wup_h, wup),
    ]
    wcopies = [pltpu.make_async_copy(s, d, wsem.at[i]) for i, (s, d) in enumerate(weights)]
    wcopies[0].start()
    wcopies[1].start()

    barrier = pltpu.get_barrier_semaphore()
    w_root = w + 4 * (ROOT - zi)
    w_last = w + 4 * (NZ - 1 - zi)

    def greet(to):
        pl.semaphore_signal(barrier, inc=1, device_id=to, device_id_type=MESH)

    for to in ((w, other), (wpart, x), (wpart, other), (wy, x)):
        greet(to)
    for z in range(NZ):
        met = [wl] * (z > 0) + [wr_] * (z < NZ - 1) + [w_last] * (z == ROOT) + [w_root] * (z == NZ - 1)

        @pl.when(zi == z)
        def _(met=met):
            for to in met:
                greet((to, x))
            pl.semaphore_wait(barrier, 4 + len(met))

    def xcopy(i, src, dst):
        return pltpu.make_async_remote_copy(
            src_ref=src, dst_ref=dst, send_sem=xsend.at[i], recv_sem=xrecv.at[i],
            device_id=(w, other), device_id_type=MESH,
        )

    def ccopy(i, src, dst):
        return pltpu.make_async_remote_copy(
            src_ref=src, dst_ref=dst, send_sem=csend.at[i], recv_sem=crecv.at[i],
            device_id=(wpart, x), device_id_type=MESH,
        )

    HC = H // 4
    x_tok = [
        xcopy(0 if j == 0 else 16 + j, tok_h.at[j * HC : (j + 1) * HC], tok.at[pl.ds(pl.multiple_of(x * H + j * HC, HC), HC)])
        for j in range(4)
    ]
    x_cot = xcopy(1, cot_h, gout.at[own])
    for copy in x_tok:
        copy.start()
    for copy in wcopies[2:]:
        copy.start()

    gs = smo.at[0 : H * 8]
    gxs = smo.at[H * 8 : R * 8]
    nb_o = gup.at[0:H, 0:D]
    gres = gup.at[0:H, D : 2 * D]
    ffn_o = gup.at[H:R, 0:D]

    first_end = lens[0, 0]
    second_end = first_end + lens[0, 1]
    place = lax.broadcasted_iota(jnp.int32, (R, 128), 0)
    begins = (place == 0) | (place == first_end) | (place == second_end)
    keep[...] = jnp.where(begins, 0.0, 1.0)
    live[...] = jnp.where(place >= second_end, 0.0, 1.0)

    def segment_of(at):
        return jnp.where(at >= first_end, 1.0, 0.0) + jnp.where(at >= second_end, 1.0, 0.0)

    segc[...] = segment_of(place)

    for t in range(2):
        for j in range(8):
            rows_ = slice(t * 8, t * 8 + 8)
            lanes = slice(j * 128, j * 128 + 128)
            r_ = rate[rows_, lanes]
            a_s[pl.ds(t * 64 + j, 8, stride=8), :] = 1.0 - r_ * damp[rows_, lanes]
            w_s[pl.ds(t * 64 + j, 8, stride=8), :] = r_ * ein[rows_, lanes] * eout[rows_, lanes]

    for k, ref in enumerate((in_n1g, in_n1b, in_skip, in_bupd, in_n2g, in_n2b)):
        for j in range(8):
            vec[k : k + 1, j * 128 : (j + 1) * 128] = ref[j : j + 1, :]
    wide_bias = in_bup[...].astype(F32)
    for j in range(16):
        bup[0:1, j * 128 : (j + 1) * 128] = wide_bias[j : j + 1, :]

    def norm_rows(v):
        m = jnp.mean(v, axis=-1, keepdims=True)
        cen = v - m
        var = jnp.mean(cen * cen, axis=-1, keepdims=True)
        return cen, lax.rsqrt(var + EPS)

    def norm1(t):
        rr = cols(t, 16)
        cen, rstd = norm_rows(tok[rr, :].astype(F32))
        v = cen * rstd * vec[0:1, :] + vec[1:2, :]
        normed[rr, :] = v
        nlow[rr, :] = v.astype(BF)
        for j in range(8):
            xs[pl.ds(t * 128 + j, 16, stride=8), :] = v[:, j * 128 : (j + 1) * 128]

    HT = H // 16
    wcopies[0].wait()
    pl.loop(0, HT, unroll=2)(lambda t: norm1(x * HT + t))
    N = 16

    def coef(ref):
        return ref[...].reshape(N, 8, 128)

    zeros = jnp.zeros((N, 8, 128), F32)

    def forward(p, s):
        k = keep[pl.ds(p, 1), :]
        at = cols(p, 8)
        xr = xs[at, :] * live[pl.ds(p, 1), :]
        s = coef(a_s) * (s * k) + xr
        smo[at, :] = jnp.sum(coef(w_s) * s, axis=0)
        return s

    def mixed_rows(t):
        rr = cols(t, 16)
        for j in range(8):
            ll = slice(j * 128, (j + 1) * 128)
            pre = smo[pl.ds(t * 128 + j, 16, stride=8), :] + vec[2:3, ll] * normed[rr, ll]
            pre_ema[rr, ll] = pre
            mlow[rr, ll] = (pre * sigm(pre)).astype(BF)

    T = 256

    def value_tile(i, rows_):
        cc = cols(i, T)
        pv = mm(nlow[rows_, :], wv[:, cc])
        pre_v[rows_, cc] = pv
        vlow[rows_, cc] = (pv * sigm(pv)).astype(BF)

    wcopies[3].wait()
    pl.loop(0, VL // T, unroll=2)(lambda i: value_tile(i, own))
    state = zeros
    for j in range(8):

        @pl.when(x == (1 if j < 4 else 0))
        def _(j=j):
            x_tok[j % 4].wait_recv()
            pl.loop(j * (HC // 16), (j + 1) * (HC // 16), unroll=2)(norm1)

        state = lax.fori_loop(j * HC, (j + 1) * HC, forward, state, unroll=4)
        pl.loop(j * (HC // 16), (j + 1) * (HC // 16), unroll=2)(mixed_rows)

    for copy in x_tok:
        copy.wait_send()
    x_cot.start()
    c_normed = ccopy(0, nlow, p_normed)
    c_normed.start()
    c_mixed = ccopy(1, mlow, p_mixed)
    c_mixed.start()

    wcopies[2].wait()
    psh = mm(mlow[...], wsh[...])
    pre_sh[...] = psh
    sh = psh * sigm(psh)
    qlow[...] = (sh * qkg[0:1, :] + qkb[0:1, :]).astype(BF)
    klow[...] = (sh * qkg[1:2, :] + qkb[1:2, :]).astype(BF)

    BL = BLOCK
    ii = lax.broadcasted_iota(jnp.int32, (BL, BL), 0)
    jj = lax.broadcasted_iota(jnp.int32, (BL, BL), 1)

    def skew(tbl, left):
        for b in range(7):
            moved = pltpu.roll(tbl, (BL - (1 << b)) if left else (1 << b), 1)
            tbl = jnp.where(lax.rem(ii // (1 << b), 2) == 1, moved, tbl)
        return tbl

    buckets = bmap[0:1, :]
    by_offset = jnp.zeros((1, BL), F32)
    for b in range(relb.shape[1]):
        by_offset = by_offset + jnp.where(buckets == b, relb[0, b], 0.0)
    table = skew(jnp.broadcast_to(by_offset, (BL, BL)), False).T
    scale = float(qkg.shape[1]) ** (-0.5)
    for b in range(2):
        rb = slice(b * BL, (b + 1) * BL)
        sc = mm_nt(qlow[rb, :], klow[rb, :]) * scale
        ok = (segc[rb, :] == segment_of(lax.broadcasted_iota(jnp.int32, (1, BL), 1) + b * BL)) & (jj <= ii)
        sc = jnp.where(ok, sc + table, NEGATIVE)
        ex = jnp.exp(sc - jnp.max(sc, axis=-1, keepdims=True))
        pr = ex / jnp.sum(ex, axis=-1, keepdims=True)
        probs[rb, :] = pr
        plow[rb, :] = pr.astype(BF)

    wcopies[4].wait()

    def reset_tile(i):
        cc = cols(i, T)
        for b in range(2):
            rb = slice(b * BL, (b + 1) * BL)
            att[rb, cc] = mm(plow[rb, :], vlow[rb, cc])
        pr = mm(mlow[...], wr[:, cc])
        pre_r[:, cc] = pr
        gated[:, cc] = (pr * sigm(pr) * att[:, cc]).astype(BF)

    pl.loop(0, VL // T, unroll=2)(lambda i: value_tile(i, oth))
    pl.loop(0, VL // T, unroll=2)(reset_tile)

    wcopies[5].wait()

    HH = H // 2
    x_mix = []
    for h in range(2):
        src = pl.ds(pl.multiple_of(other * H + h * HH, HH), HH)
        hr = slice(h * HH, (h + 1) * HH)

        @pl.loop(0, D // T, unroll=2)
        def _(i, src=src, hr=hr):
            cc = cols(i, T)
            part_s[hr, cc] = mm(gated[src, :], wm[:, cc]).astype(BF)

        x_mix.append(xcopy((2, 13)[h], part_s.at[hr], mix_r.at[hr]))
        x_mix[h].start()

    c_gated = ccopy(2, gated, p_gated)
    c_gated.start()
    wcopies[6].wait()
    wcopies[7].wait()

    @pl.loop(0, D // T, unroll=2)
    def _(i):
        cc = cols(i, T)
        own_f[:, cc] = mm(gated[own, :], wm[:, cc])
        pre_hid[:, cc] = mm(mlow[own, :], wh[:, cc])
        gate[:, cc] = sigm(mm(mlow[own, :], wu[:, cc]) + vec[3:4, cc])

    wcopies[1].wait()
    x_cot.wait()

    @pl.loop(0, R // 16)
    def _(t):
        rr = cols(t, 16)
        gout[rr, :] = (gout[rr, :].astype(F32) * live[rr, 0:1]).astype(BF)

    c_gout = ccopy(3, gout, p_gout)
    c_gout.start()
    wcopies[8].wait()

    @pl.loop(0, FL // T, unroll=2)
    def _(i):
        cc = cols(i, T)
        gup[:, cc] = mm_nt(gout[...], wdn[cc, :])


    def blend_rows(t):
        rr = cols(t, 32)
        ro = pl.ds(pl.multiple_of(x * H + t * 32, 32), 32)
        ph = pre_hid[rr, :] + (own_f[rr, :] + mix_r[rr, :].astype(F32))
        pre_hid[rr, :] = ph
        u = gate[rr, :]
        bl = u * (ph * sigm(ph)) + (1.0 - u) * tok[ro, :].astype(F32)
        blend[rr, :] = bl
        cen, rstd = norm_rows(bl)
        n2[ro, :] = (cen * rstd * vec[4:5, :] + vec[5:6, :]).astype(BF)

    x_n2 = []
    for h in range(4):
        if h % 2 == 0:
            x_mix[h // 2].wait()
        pl.loop(h * (H // 128), (h + 1) * (H // 128))(blend_rows)
        part = pl.ds(pl.multiple_of(x * H + h * (H // 4), H // 4), H // 4)
        x_n2.append(xcopy(3 if h == 0 else 13 + h, n2.at[part], n2.at[part]))
        x_n2[h].start()

    wcopies[9].wait()
    FT = FL // T

    def up_tile(i, rows_, first):
        cc = cols(i, T)
        pu = mm(n2[rows_, :], wup[:, cc]) + bup[0:1, cc]
        sg = sigm(pu)
        up[rows_, cc] = (pu * sg).astype(BF)
        gp = (gup[rows_, cc] * slope_of(pu, sg)).astype(BF)
        gpu[rows_, cc] = gp
        sums = jnp.sum(gp.astype(F32), axis=0, keepdims=True)
        for h in range(2):
            at = pl.ds(304 + x * 16 + i * 2 + h, 1)
            part = sums[:, h * 128 : (h + 1) * 128]
            if first:
                small[at, :] = part
                small[pl.ds(304 + other * 16 + i * 2 + h, 1), :] = jnp.zeros((1, 128), F32)
            else:
                small[at, :] += part

    pl.loop(0, FT, unroll=2)(lambda i: up_tile(i, own, True))
    for copy in x_n2:
        copy.wait()
    c_n2 = ccopy(4, n2, p_n2)
    c_n2.start()
    halfF = FL // 2
    theirs_f = pl.ds(pl.multiple_of((1 - c) * halfF, halfF), halfF)
    pl.loop(0, FT // 2, unroll=2)(lambda i: up_tile((1 - c) * (FT // 2) + i, oth, False))
    c_up = ccopy(5, up.at[:, theirs_f], p_up)
    c_gpu = ccopy(6, gpu.at[:, theirs_f], p_gpu)
    c_up.start()
    c_gpu.start()
    pl.loop(0, FT // 2, unroll=2)(lambda i: up_tile(c * (FT // 2) + i, oth, False))
    P2 = g_v.shape[2]
    plan = make_plan()[0]
    numbers = {}
    locals_ = {}

    def number(*key):
        return numbers.setdefault(key, len(numbers))

    shelves = [[wup, 0, j, 0] for j in range(wup.shape[1] // P2)]
    shelves += [[wdn, 0, j, 0] for j in range(wdn.shape[1] // P2)] + [[ext, 0, 0, 0]]
    places = {}

    def place_of(key, n):
        if key not in places:
            for shelf in shelves:
                if (shelf[0] is ext) == (key[0] in EARLY) and shelf[1] + n <= shelf[0].shape[0]:
                    places[key] = (shelf[0], shelf[1], shelf[2] * P2)
                    shelf[1] += n
                    break
        ref, r0, c0 = places[key]
        return ref.at[r0 : r0 + n, c0 : c0 + P2]

    def chunk_rows(u):
        _, first, _, rows, _ = UNITS[u]
        return rows // 8 if first else rows // 4

    def earlier(u, k):
        roots = UNITS[u][4]
        return sum(roots[q] == roots[k] for q in range(k))

    def line_place(u, k):
        return place_of((u, "z", k), chunk_rows(u))

    def second_place(u, k):
        return place_of((u, "s", earlier(u, k)), chunk_rows(u))

    def cross_place(u, k):
        return place_of((u, "y", k if UNITS[u][1] else earlier(u, k)), chunk_rows(u))

    def from_right(u, k, z):
        return second_place(u, k) if UNITS[u][4][k] == z and z > 0 else line_place(u, k)

    def first_row(u, k, half):
        _, first, row0, rows, _ = UNITS[u]
        n = chunk_rows(u)
        if first:
            return row0 + half * (rows // 2) + k * n
        return row0 + k * n

    def rows_at(u, k, half):
        n = chunk_rows(u)
        if UNITS[u][1]:
            return pl.ds(pl.multiple_of(first_row(u, k, half), 16), n)
        return pl.ds(first_row(u, k, half), n)

    def chunk(u, k, half):
        return g_v.at[UNITS[u][0], rows_at(u, k, half)]

    def result(u, k, half, core, side):
        i = UNITS[u][0]
        n = chunk_rows(u)
        r0 = first_row(u, k, half)
        j = i % 2
        if i < 2:
            return o_down.at[pl.ds(pl.multiple_of(core * D + r0, 16), n), j * P2 : (j + 1) * P2]
        rr = pl.ds(pl.multiple_of(r0, 16), n)
        if i < 4:
            return o_up.at[rr, pl.ds(pl.multiple_of(core * D + j * P2, P2), P2)]
        if i == 5:
            return o_hu.at[2 * side + core, rr]
        ref = {4: o_mix, 6: o_reset, 7: o_value}[i]
        return ref.at[rr, pl.ds(pl.multiple_of(core * P2, P2), P2)]

    sent = [[] for _ in range(NZ)]

    def send(z, way, key, src, dst):
        dev = {
            "y": (wy, x), "l": (wl, x), "r": (wr_, x), "c": (wpart, x), "x": (w, other), "d": (wpart, other),
            "root": (w_root, x), "last": (w_last, x),
        }[way]
        n = number(*key)
        copy = pltpu.make_async_remote_copy(
            src_ref=src, dst_ref=dst, send_sem=asend.at[n], recv_sem=arecv.at[n],
            device_id=dev, device_id_type=MESH,
        )
        copy.start()
        sent[z].append((n, src.shape, src.dtype))

    def arrived(key, ref):
        n = number(*key)
        pltpu.make_async_remote_copy(
            src_ref=ref, dst_ref=ref, send_sem=asend.at[n], recv_sem=arecv.at[n],
            device_id=(w, other), device_id_type=MESH,
        ).wait_recv()

    def add_up(dst, terms):
        if terms:

            @pl.loop(0, dst.shape[0] // 32)
            def _(t):
                rr = cols(t, 32)
                v = dst[rr, :].astype(F32)
                for term in terms:
                    v = v + term[rr, :].astype(F32)
                dst[rr, :] = v.astype(BF)

    def own_copy(u, k, src, half):
        at = locals_.setdefault((u, k), len(locals_))
        return pltpu.make_async_copy(src, result(u, k, half, c, x), lsem.at[at])

    def share(z, u, k, src, half):
        dst = result(u, k, half, c, x)
        if z > 0:
            send(z, "l", ("zr", u, k), src, dst)
        if z < NZ - 1:
            send(z, "r", ("zl", u, k), src, dst)
        if UNITS[u][1]:
            send(z, "y", ("yf", u, k), src, dst)
        if UNITS[u][0] == 5:
            send(z, "x", ("xf", u, k, 0), src, dst)
        send(z, "c", ("cf", u, k, 0), src, dst)
        own_copy(u, k, src, half).start()

    def happen(z, key):
        kind, u, k = key[:3]
        if kind == "S":
            small_step(z, u)
            return
        i, first, _, _, roots = UNITS[u]
        own_half = y if first else 0
        g = roots[k]
        if kind == "G":
            send(z, "y", ("yr", u, k), chunk(u, k, 1 - y), cross_place(u, k))
            return
        if kind in "PC":
            terms = []
            if first:
                arrived(("yr", u, k), cross_place(u, k))
                terms.append(cross_place(u, k))
            if g >= z and z > 0:
                arrived(("zl", u, k), line_place(u, k))
                terms.append(line_place(u, k))
            if g <= z and z < NZ - 1:
                arrived(("zr", u, k), from_right(u, k, z))
                terms.append(from_right(u, k, z))
            mine = chunk(u, k, own_half)
            add_up(mine, terms)
            if kind == "P" and g > z:
                send(z, "r", ("zl", u, k), mine, line_place(u, k))
            elif kind == "P":
                send(z, "l", ("zr", u, k), mine, from_right(u, k, z - 1))
            elif first:
                share(z, u, k, mine, own_half)
            else:
                send(z, "y", ("yr", u, k), mine, cross_place(u, k))
        elif kind == "D":
            mine = cross_place(u, k)
            arrived(("yr", u, k), mine)
            add_up(mine, [chunk(u, k, 0)])
            share(z, u, k, mine, 0)
        elif kind == "F":
            ref = result(u, k, own_half, c, x)
            arrived(("zr" if g > z else "zl", u, k), ref)
            if g > z > 0:
                send(z, "l", ("zr", u, k), ref, ref)
            if g < z < NZ - 1:
                send(z, "r", ("zl", u, k), ref, ref)
            if first == 1:
                send(z, "y", ("yf", u, k), ref, ref)
            if i == 5:
                send(z, "x", ("xf", u, k, 0), ref, ref)
            send(z, "c", ("cf", u, k, 0), ref, ref)
        elif kind in "YW":
            ref = result(u, k, 1 - y, c, x)
            arrived(("yf" if kind == "Y" else "wr" if g > z else "wl", u, k), ref)
            if first == 2 and g >= z > 0:
                send(z, "l", ("wr", u, k), ref, ref)
            if first == 2 and g <= z < NZ - 1:
                send(z, "r", ("wl", u, k), ref, ref)
            if i == 5:
                send(z, "x", ("xf", u, k, 1), ref, ref)
            send(z, "c", ("cf", u, k, 1), ref, ref)
        elif kind == "X":
            h = key[3]
            half = (y if h == 0 else 1 - y) if first else 0
            ref = result(u, k, half, c, other)
            arrived(("xf", u, k, h), ref)
            send(z, "c", ("cf", u, k, 2 + h), ref, ref)

    def slot(n):
        for z in range(NZ):
            if plan[z][n]:

                @pl.when(zi == z)
                def _(z=z):
                    for key in plan[z][n]:
                        happen(z, key)

    def eight(start, n):
        return pl.ds(pl.multiple_of(start, 8), n)

    def quarter(side, core):
        return eight(side * 176 + core * 88, 88)

    def quarter_sh(side, core):
        return eight((2 * side + core) * 256, 256)

    around = (("x", other, c), ("c", x, 1 - c), ("d", other, 1 - c))

    def small_step(z, n):
        mine, mine_sh = quarter(x, c), quarter_sh(x, c)

        def give(total):
            o_small[mine, :] = total[0:88, :]
            o_shared[mine_sh, :] = total[88:344, :]
            for way, _, _ in around:
                send(z, way, ("s6", way), o_small.at[mine], o_small.at[mine])
                send(z, way, ("s7", way), o_shared.at[mine_sh], o_shared.at[mine_sh])

        if n == 1:
            for at, (way, side, core) in enumerate(around):
                send(z, way, ("s1", way), small.at[quarter(side, core)], s_q.at[at])
        elif n == 3:
            for at, (way, _, _) in enumerate(around):
                arrived(("s1", way), s_q.at[at])
            s_own[0:88, :] = (small[mine, :] + s_q[0]) + (s_q[1] + s_q[2])
            send(z, "y", ("s3",), s_own, s_y)
        elif n == 4:
            arrived(("s3",), s_y)
            s_y[...] = s_y[...] + s_own[...]
            if z != ROOT:
                send(z, "root", ("s4", z), s_y, s_in.at[NEAR.index(z)])
        elif n == 6:
            for at, q in enumerate(NEAR):
                arrived(("s4", q), s_in.at[at])
            s_y[...] = (s_y[...] + s_in[0]) + (s_in[1] + s_in[2])
            for q, way in zip(NEAR, ("l", "r", "last")):
                send(z, way, ("s5", q), s_y, s_in.at[0])
            give(s_y)
        elif n == 7:
            arrived(("s5", z), s_in.at[0])
            give(s_in.at[0])

    def finish():
        for z in range(NZ):

            @pl.when(zi == z)
            def _(z=z):
                for way, side, core in around:
                    arrived(("s6", way), o_small.at[quarter(side, core)])
                    arrived(("s7", way), o_shared.at[quarter_sh(side, core)])
                for u, (i, first, _, _, roots) in enumerate(UNITS):
                    for k in range(NZ):
                        half = y if first else 0
                        arrived(("cf", u, k, 0), result(u, k, half, 1 - c, x))
                        if first:
                            arrived(("cf", u, k, 1), result(u, k, 1 - y, 1 - c, x))
                        if i == 5:
                            for h in range(2 if first else 1):
                                at = (y if h == 0 else 1 - y) if first else 0
                                arrived(("cf", u, k, 2 + h), result(u, k, at, 1 - c, other))
                        if roots[k] == z:
                            own_copy(u, k, chunk(u, k, half), half).wait()
                for n, shape, dtype in sent[z]:
                    like = g_v.at[0, 0 : shape[0]] if dtype == BF else o_shared.at[0 : shape[0]]
                    pltpu.make_async_remote_copy(
                        src_ref=like, dst_ref=like, send_sem=asend.at[n], recv_sem=arecv.at[n],
                        device_id=(w, other), device_id_type=MESH,
                    ).wait_send()


    c_gout.wait()
    c_up.wait()
    P2 = g_v.shape[2]

    @pl.loop(0, 4)
    def _(i):
        mt = cols(i, 256)
        mf = pl.ds(pl.multiple_of(c * halfF + i * 256, 256), 256)
        la = up[:, mf]
        lb = p_up[:, mt]
        for j in range(2):
            nn = slice(j * P2, (j + 1) * P2)
            g_v[j, mt, :] = (mm_tn(la, gout[:, nn]) + mm_tn(lb, p_gout[:, nn])).astype(BF)

    slot(1)

    @pl.loop(0, D // T)
    def _(i):
        cc = cols(i, T)
        part_s[:, cc] = mm_nt(gpu[oth, :], wup[cc, :]).astype(BF)

    x_gn2 = xcopy(4, part_s, gn2_r)
    x_gn2.start()
    slot(2)

    @pl.loop(0, D // T)
    def _(i):
        cc = cols(i, T)
        own_f[:, cc] = mm_nt(gpu[own, :], wup[cc, :])
        ffn_s[:, cc] = mm(up[oth, :], wdn[:, cc]).astype(BF)
        ffn_o[:, cc] = mm(up[own, :], wdn[:, cc])


    pl.semaphore_signal(ready.at[0], inc=1, device_id=(wy, x), device_id_type=MESH)

    @pl.when(zi > 0)
    def _():
        pl.semaphore_signal(ready.at[2], inc=1, device_id=(wl, x), device_id_type=MESH)

    @pl.when(zi < NZ - 1)
    def _():
        pl.semaphore_signal(ready.at[1], inc=1, device_id=(wr_, x), device_id_type=MESH)

    pl.semaphore_wait(ready.at[0], 1)

    @pl.when(zi > 0)
    def _():
        pl.semaphore_wait(ready.at[1], 1)

    @pl.when(zi < NZ - 1)
    def _():
        pl.semaphore_wait(ready.at[2], 1)

    slot(3)
    c_n2.wait()
    c_gpu.wait()

    @pl.loop(0, 4)
    def _(i):
        mt = cols(i, 256)
        la = n2[:, mt]
        lb = p_n2[:, mt]
        for j in range(2):
            nf = pl.ds(pl.multiple_of(c * halfF + j * P2, P2), P2)
            nn = slice(j * P2, (j + 1) * P2)
            g_v[2 + j, mt, :] = (mm_tn(la, gpu[:, nf]) + mm_tn(lb, p_gpu[:, nn])).astype(BF)

    slot(4)
    x_gn2.wait()

    acc[...] = jnp.zeros_like(acc)

    def add_rows(k, v):
        acc[k * 8 : k * 8 + 8, :] += v[0:8, :] + v[8:16, :]

    def norm2_back(t):
        rr = cols(t, 16)
        ro = pl.ds(pl.multiple_of(x * H + t * 16, 16), 16)
        g = own_f[rr, :] + gn2_r[rr, :].astype(F32)
        cen, rstd = norm_rows(blend[rr, :])
        xh = cen * rstd
        add_rows(0, g * xh)
        add_rows(1, g)
        gy = g * vec[4:5, :]
        gb = rstd * (gy - jnp.mean(gy, axis=-1, keepdims=True) - xh * jnp.mean(gy * xh, axis=-1, keepdims=True))
        gb = gb + gout[ro, :].astype(F32)
        u = gate[rr, :]
        ph = pre_hid[rr, :]
        sg = sigm(ph)
        tk = tok[ro, :].astype(F32)
        gud = (gb * (ph * sg - tk) * u * (1.0 - u)).astype(BF)
        ghd = (gb * u * slope_of(ph, sg)).astype(BF)
        hid[ro, :] = ghd
        upd[ro, :] = gud
        add_rows(2, gud.astype(F32))
        gres[rr, :] = gb * (1.0 - u)

    halves = [pl.ds(pl.multiple_of(x * H + h * (H // 2), H // 2), H // 2) for h in range(2)]
    x_hid = [xcopy((5, 22)[h], hid.at[halves[h]], hid.at[halves[h]]) for h in range(2)]
    pl.loop(0, HT // 2)(norm2_back)
    x_hid[0].start()
    slot(5)
    pl.loop(HT // 2, HT)(norm2_back)
    x_hid[1].start()
    x_upd = xcopy(6, upd.at[own], upd.at[own])
    x_ffn = xcopy(7, ffn_s, ffn_r)

    def put_small(row, k):
        v = jnp.sum(acc[k * 8 : k * 8 + 8, :], axis=0, keepdims=True)
        for j in range(8):
            small[row + j : row + j + 1, :] = v[:, j * 128 : (j + 1) * 128]

    put_small(256 + 32, 0)
    put_small(256 + 40, 1)
    put_small(256 + 24, 2)
    slot(6)

    snap_s[...] = jnp.zeros_like(snap_s)
    snap_r[...] = jnp.zeros_like(snap_r)

    def sense(p, state):
        s, r = state
        k = keep[pl.ds(p, 1), :]
        a = coef(a_s)
        sk = s * k
        return a * sk + xs[cols(p, 8), :] * live[pl.ds(p, 1), :], a * (r * k) + sk

    @pl.when(x == 1)
    def _():
        s_mid, r_mid = lax.fori_loop(0, H, sense, (zeros, zeros), unroll=2)
        snap_s[...] = s_mid.reshape(N * 8, 128)
        snap_r[...] = r_mid.reshape(N * 8, 128)

    for copy in x_hid:
        copy.wait()
    x_upd.start()
    c_hid = ccopy(7, hid, p_hid)
    c_hid.start()
    gp_acc[...] = jnp.zeros_like(gp_acc)

    def gated_back(i):
        cc = cols(i, T)
        gg = mm_nt(hid[...], wm[cc, :])
        pr = pre_r[:, cc]
        sg = sigm(pr)
        ga = (gg * (pr * sg)).astype(BF)
        gpr[:, cc] = (gg * att[:, cc] * slope_of(pr, sg)).astype(BF)
        pv = pre_v[:, cc]
        sv = slope_of(pv, sigm(pv))
        for b in range(2):
            rb = slice(b * BL, (b + 1) * BL)
            gp_acc[rb, :] += mm_nt(ga[rb, :], vlow[rb, cc])
            gv = mm_tn(plow[rb, :], ga[rb, :])
            gpv[rb, cc] = (gv * sv[rb, :]).astype(BF)

    for i in range(VL // T):
        pl.loop(i, i + 1)(gated_back)
        slot(7 + i)
    x_gp = xcopy(8, gp_acc.at[oth], gp_r)
    x_gp.start()
    x_upd.wait()

    @pl.loop(0, D // T)
    def _(i):
        cc = cols(i, T)
        part_s[:, cc] = mm_nt(gpr[oth, :], wr[cc, :]).astype(BF)

    x_mb = xcopy(9, part_s, mb_r)
    x_mb.start()
    slot(11)

    @pl.loop(0, D // T)
    def _(i):
        cc = cols(i, T)
        nb_s[:, cc] = mm_nt(gpv[oth, :], wv[cc, :]).astype(BF)

    x_nb = xcopy(10, nb_s, nb_r)
    halfV = VL // 2
    c_gpr = ccopy(8, gpr.at[:, pl.ds(pl.multiple_of((1 - c) * halfV, halfV), halfV)], p_gpr)
    c_gpv = ccopy(9, gpv.at[:, pl.ds(pl.multiple_of((1 - c) * halfV, halfV), halfV)], p_gpv)
    c_upd = ccopy(10, upd, p_upd)
    c_gpr.start()
    c_gpv.start()
    c_upd.start()

    slot(12)
    c_hid.wait()
    c_gated.wait()
    hv = pl.ds(pl.multiple_of(c * P2, P2), P2)
    q4 = pl.ds(pl.multiple_of((2 * x + c) * 256, 256), 256)

    @pl.loop(0, 4)
    def _(i):
        mt = cols(i, 256)
        g_v[4, mt, :] = (mm_tn(gated[:, mt], hid[:, hv]) + mm_tn(p_gated[:, mt], p_hid[:, hv])).astype(BF)

    slot(13)

    x_gp.wait()
    gpb = gp_acc[own, :] + gp_r[...]
    po = probs[own, :]
    gsc = (po * (gpb - jnp.sum(gpb * po, axis=-1, keepdims=True))).astype(BF)
    gq = mm(gsc, klow[own, :]) * scale
    gk = mm_tn(gsc, qlow[own, :]) * scale
    psh = pre_sh[own, :]
    sgs = sigm(psh)
    sh = psh * sgs
    small[336:337, :] = jnp.sum(gq * sh, axis=0, keepdims=True)
    small[337:338, :] = jnp.sum(gk * sh, axis=0, keepdims=True)
    small[338:339, :] = jnp.sum(gq, axis=0, keepdims=True)
    small[339:340, :] = jnp.sum(gk, axis=0, keepdims=True)
    small[340:341, :] = jnp.sum(skew(gsc.astype(F32).T, True), axis=0, keepdims=True)
    small[341:352, :] = jnp.zeros((11, 128), F32)
    gps[own, :] = ((gq * qkg[0:1, :] + gk * qkg[1:2, :]) * slope_of(psh, sgs)).astype(BF)
    x_gps = xcopy(11, gps.at[own], gps.at[own])
    x_gps.start()
    x_nb.start()
    slot(14)
    c_mixed.wait()
    c_upd.wait()

    la = mlow[:, q4]
    lb = p_mixed[:, q4]
    for j in range(2):
        nn = slice(j * P2, (j + 1) * P2)
        g_v[5, j * 256 : j * 256 + 256, :] = (mm_tn(la, hid[:, nn]) + mm_tn(lb, p_hid[:, nn])).astype(BF)
        g_v[5, 512 + j * 256 : 768 + j * 256, :] = (mm_tn(la, upd[:, nn]) + mm_tn(lb, p_upd[:, nn])).astype(BF)

    slot(15)

    @pl.loop(0, D // T)
    def _(i):
        cc = cols(i, T)
        own_f[:, cc] = (
            mm_nt(gpr[own, :], wr[cc, :])
            + mm_nt(gps[own, :], wsh[cc, :])
            + mm_nt(hid[own, :], wh[cc, :])
            + mm_nt(upd[own, :], wu[cc, :])
        )
        nb_o[:, cc] = mm_nt(gpv[own, :], wv[cc, :])

    slot(16)
    x_gps.wait()
    c_gps = ccopy(11, gps, p_gps)
    c_gps.start()
    c_gpr.wait()

    @pl.loop(0, 4)
    def _(i):
        mt = cols(i, 256)
        g_v[6, mt, :] = (mm_tn(mlow[:, mt], gpr[:, hv]) + mm_tn(p_mixed[:, mt], p_gpr[...])).astype(BF)

    slot(17)
    c_normed.wait()
    c_gpv.wait()

    @pl.loop(0, 4)
    def _(i):
        mt = cols(i, 256)
        g_v[7, mt, :] = (mm_tn(nlow[:, mt], gpv[:, hv]) + mm_tn(p_normed[:, mt], p_gpv[...])).astype(BF)

    c_gps.wait()
    s_own[88:344, :] = mm_tn(mlow[:, q4], gps[...]) + mm_tn(p_mixed[:, q4], p_gps[...])
    slot(18)
    x_mb.wait()
    x_ffn.start()

    acc[...] = jnp.zeros_like(acc)

    @pl.loop(0, H // 16)
    def _(t):
        rr = cols(t, 16)
        ro = pl.ds(pl.multiple_of(x * H + t * 16, 16), 16)
        pre = pre_ema[ro, :]
        g = (own_f[rr, :] + mb_r[rr, :].astype(F32)) * slope_of(pre, sigm(pre))
        own_f[rr, :] = g
        add_rows(0, g * normed[ro, :])
        for j in range(8):
            gs[pl.ds(t * 128 + j, 16, stride=8), :] = g[:, j * 128 : (j + 1) * 128]

    put_small(256, 0)
    slot(19)

    def back(p_, cy):
        p = H - 1 - p_
        at = cols(p, 8)
        po_ = x * H + p
        mu = gs[at, :] + cy
        gxs[at, :] = jnp.sum(coef(w_s) * mu, axis=0) * live[pl.ds(po_, 1), :]
        return coef(a_s) * (mu * keep[pl.ds(po_, 1), :])

    x_carry = xcopy(12, carry, carry_r)

    @pl.when(x == 1)
    def _():
        cy = lax.fori_loop(0, H, back, zeros)
        carry[...] = cy.reshape(N * 8, 128)
        x_carry.start()

    slot(20)
    for q in range(2):
        nq = slice(q * 64, q * 64 + 64)

        def fwd(p, state, nq=nq):
            s, r, gw, gr = state
            at = cols(p, 8)
            po_ = x * H + p
            k = keep[pl.ds(po_, 1), :]
            xr = xs[cols(po_, 8), :] * live[pl.ds(po_, 1), :]
            a = a_s[nq, :].reshape(8, 8, 128)
            sk = s * k
            r = a * (r * k) + sk
            s = a * sk + xr
            g = gs[at, :]
            return s, r, gw + g * s, gr + g * r

        z8 = jnp.zeros((8, 8, 128), F32)
        s0 = snap_s[nq, :].reshape(8, 8, 128)
        r0 = snap_r[nq, :].reshape(8, 8, 128)
        _, _, gw, gr = lax.fori_loop(0, H, fwd, (s0, r0, z8, z8))
        small[nq, :] = gw.reshape(64, 128)
        small[128 + q * 64 : 192 + q * 64, :] = gr.reshape(64, 128) * w_s[nq, :]
        slot(21 + q)

    @pl.when(x == 0)
    def _():
        x_carry.wait_recv()
        lax.fori_loop(0, H, back, coef(carry_r))

    @pl.when(x == 1)
    def _():
        x_carry.wait_send()

    slot(23)
    x_nb.wait()

    @pl.loop(0, H // 16)
    def _(t):
        rr = cols(t, 16)
        ro = pl.ds(pl.multiple_of(x * H + t * 16, 16), 16)
        gx = jnp.concatenate([gxs[pl.ds(t * 128 + j, 16, stride=8), :] for j in range(8)], axis=1)
        g = nb_o[rr, :] + nb_r[rr, :].astype(F32) + vec[2:3, :] * own_f[rr, :] + gx
        cen, rstd = norm_rows(tok[ro, :].astype(F32))
        xh = cen * rstd
        add_rows(1, g * xh)
        add_rows(2, g)
        gy = g * vec[0:1, :]
        gb = rstd * (gy - jnp.mean(gy, axis=-1, keepdims=True) - xh * jnp.mean(gy * xh, axis=-1, keepdims=True))
        gt[rr, :] = gres[rr, :] + gb

    put_small(256 + 8, 1)
    put_small(256 + 16, 2)

    slot(24)

    x_ffn.wait()

    @pl.loop(0, H // 16)
    def _(t):
        rr = cols(t, 16)
        bo[rr, :] = (blend[rr, :] + (ffn_o[rr, :] + ffn_r[rr, :].astype(F32))).astype(BF)

    slot(25)
    finish()

def vm(shape, dtype=F32):
    return pltpu.VMEM(shape, dtype)


SEMS = 440


def run_main(tokens, cotangent, seq_lengths, bucket_map, norm1_gain, norm1_bias, ema_rate, ema_damp, ema_in, ema_out,
             ema_skip, w_shared, qk_gain, qk_bias, rel_bias, w_value, w_reset, w_mix, w_hidden, w_update, b_update,
             norm2_gain, norm2_bias, w_up, b_up, w_down):
    H = tokens.shape[0]
    R = 2 * H
    D = tokens.shape[1]
    VL = w_value.shape[1]
    FL = w_up.shape[1]
    Z = w_shared.shape[1]
    rows8 = [v.reshape(8, D // 8) for v in (norm1_gain, norm1_bias, ema_skip, b_update, norm2_gain, norm2_bias)]
    anyspec = pl.BlockSpec(memory_space=pl.ANY)
    vspec = pl.BlockSpec(memory_space=pltpu.VMEM)
    sspec = pl.BlockSpec(memory_space=pltpu.SMEM)
    P2 = D // 2
    outs = (
        jax.ShapeDtypeStruct((H, D), BF),
        jax.ShapeDtypeStruct((H, D), F32),
        jax.ShapeDtypeStruct((FL, D), BF),
        jax.ShapeDtypeStruct((D, FL), BF),
        jax.ShapeDtypeStruct((VL, D), BF),
        jax.ShapeDtypeStruct((4, D, P2), BF),
        jax.ShapeDtypeStruct((D, VL), BF),
        jax.ShapeDtypeStruct((D, VL), BF),
        jax.ShapeDtypeStruct((D, Z), F32),
        jax.ShapeDtypeStruct((352, 128), F32),
    )
    dma = pltpu.SemaphoreType.DMA
    scratch = [
        vm((D, Z), BF), vm((D, VL), BF), vm((D, VL), BF), vm((VL, D), BF), vm((D, D), BF), vm((D, D), BF), vm((D, FL), BF), vm((FL, D), BF),
        vm((R, D), BF), vm((R, D), BF), vm((R, D)), vm((R, D), BF), vm((R, D), BF), vm((R, D)), vm((R * 8, 128)), vm((R * 8, 128)),
        vm((R, Z)), vm((R, Z), BF), vm((R, Z), BF), vm((R, BLOCK)), vm((R, BLOCK), BF),
        vm((R, VL)), vm((R, VL)), vm((R, VL)), vm((R, VL), BF), vm((R, VL), BF), vm((H, D), BF), vm((H, D), BF), vm((H, D)), vm((H, D)), vm((H, D)), vm((H, D)), vm((R, D), BF),
        vm((R, FL)), vm((R, FL), BF), vm((R, FL), BF), vm((H, D), BF), vm((H, D), BF), vm((H, D), BF), vm((R, D), BF), vm((R, D), BF), vm((R, VL), BF), vm((R, VL), BF), vm((R, BLOCK)), vm((H, BLOCK)), vm((R, Z), BF),
        vm((H, D), BF), vm((H, D), BF), vm((H, D), BF),
        vm((R, D), BF), vm((R, D), BF), vm((R, D), BF), vm((R, FL // 2), BF), vm((R, D), BF), vm((R, FL // 2), BF), vm((R, VL), BF), vm((R, D), BF), vm((R, D), BF), vm((R, VL // 2), BF), vm((R, VL // 2), BF), vm((R, Z), BF),
        vm((128, 128)), vm((128, 128)), vm((128, 128)), vm((128, 128)), vm((128, 128)), vm((128, 128)), vm((24, D)), vm((R, 128)), vm((R, 128)), vm((R, 128)), vm((8, D)), vm((8, FL)),
        vm((8, D, P2), BF), vm((11 * 256, P2), BF), vm((352, 128)), vm((3, 88, 128)), vm((344, 128)), vm((344, 128)), vm((NZ - 1, 344, 128)),
        dma((10,)), dma((23,)), dma((23,)), dma((12,)), dma((12,)), dma((96,)), dma((SEMS,)), dma((SEMS,)), pltpu.SemaphoreType.REGULAR((3,)),
    ]
    return pl.pallas_call(
        main_kernel,
        out_shape=outs,
        in_specs=[anyspec] * 10 + [sspec, sspec] + [vspec] * 14,
        out_specs=(vspec, vspec) + (anyspec,) * 6 + (vspec, vspec),
        scratch_shapes=scratch,
        compiler_params=pltpu.CompilerParams(collective_id=0, has_side_effects=True, vmem_limit_bytes=63 * 1024 * 1024),
        cost_estimate=pl.CostEstimate(flops=15_000_000_000, bytes_accessed=40_000_000, transcendentals=0),
    )(
        tokens, cotangent, w_shared, w_value, w_reset, w_mix, w_hidden, w_update, w_up, w_down,
        seq_lengths, rel_bias.reshape(1, -1), bucket_map.reshape(1, -1), *rows8, ema_rate, ema_damp, ema_in, ema_out,
        qk_gain, qk_bias, b_up.reshape(-1, 128),
    )


def finish_kernel(down, up, mix, reset, value, hu, bo, gt, shared, small, rate, damp, ein, eout, bmap,
                  f_down, f_up, f_mix, f_reset, f_value, f_hid, f_upd, f_bo, f_gt, f_shared,
                  g_rate, g_damp, g_in, g_out, v0, v1, v2, v3, v4, v5, g_bup, g_gain, g_bias, g_rel,
                  b_down, b_up, b_mix, b_reset, b_value, b_hu, b_bo, b_gt, b_shared, stage, isem, osem, psem):
    rows_in = [pltpu.make_async_copy(a, b, psem.at[k]) for k, (a, b) in enumerate(((bo, b_bo), (gt, b_gt), (shared, b_shared)))]
    passed = [pltpu.make_async_copy(a, b, psem.at[3 + k]) for k, (a, b) in enumerate(((b_bo, f_bo), (b_gt, f_gt), (b_shared, f_shared)))]
    CR, CC = stage.shape[1], stage.shape[2]
    chunks = []
    for src, buf, dst in ((down, b_down, f_down), (up, b_up, f_up), (mix, b_mix, f_mix), (reset, b_reset, f_reset), (value, b_value, f_value)):
        for r in range(src.shape[0] // CR):
            for q in range(src.shape[1] // CC):
                at = (slice(r * CR, (r + 1) * CR), slice(q * CC, (q + 1) * CC))
                chunks.append(([(src.at[at], buf.at[at], slice(0, CC))], dst.at[at]))
    half = CC // 2
    for n, dst in ((0, f_hid), (2, f_upd)):
        for q in range(4):
            parts = []
            for j in range(2):
                at = (q, slice((n + j) * CR, (n + j + 1) * CR))
                parts.append((hu.at[at], b_hu.at[at], slice(j * half, (j + 1) * half)))
            chunks.append((parts, dst.at[q * CR : (q + 1) * CR]))
    ins, count = [], 0
    for parts, _ in chunks:
        ins.append([])
        for src, buf, _ in parts:
            copy = pltpu.make_async_copy(src, buf, isem.at[count])
            copy.start()
            ins[-1].append(copy)
            count += 1
    for copy in rows_in:
        copy.start()

    for t in range(2):
        for j in range(8):
            rows_ = slice(t * 8, t * 8 + 8)
            lanes = slice(j * 128, j * 128 + 128)
            gw = small[pl.ds(t * 64 + j, 8, stride=8), :]
            ga = small[pl.ds(128 + t * 64 + j, 8, stride=8), :]
            r_, d_ = rate[rows_, lanes], damp[rows_, lanes]
            i_, o_ = ein[rows_, lanes], eout[rows_, lanes]
            g_rate[rows_, lanes] = gw * (i_ * o_) - ga * d_
            g_damp[rows_, lanes] = -ga * r_
            g_in[rows_, lanes] = gw * (r_ * o_)
            g_out[rows_, lanes] = gw * (r_ * i_)
    for k, ref in enumerate((v0, v1, v2, v3, v4, v5)):
        ref[...] = small[256 + 8 * k : 264 + 8 * k, :]
    me = lax.axis_index("narrow")
    g_bup[...] = small[pl.ds(pl.multiple_of(304 + me * 16, 8), 16), :]
    g_gain[...] = small[336:338, :]
    g_bias[...] = small[338:340, :]
    n = bmap.shape[1]
    offs = jnp.broadcast_to(small[340:341, :], (n, n)).T
    which = jnp.broadcast_to(bmap[...].astype(F32), (n, n)).T
    lane = lax.broadcasted_iota(jnp.int32, (n, n), 1).astype(F32)
    hits = jnp.sum(jnp.where(which == lane, offs, 0.0), axis=0, keepdims=True)
    g_rel[...] = hits[:, 0 : g_rel.shape[1]]

    ring = stage.shape[0]
    outs = []
    for k, (parts, dst) in enumerate(chunks):
        if k >= ring:
            outs[k - ring].wait()
        for copy, (_, buf, at) in zip(ins[k], parts):
            copy.wait()

            @pl.loop(0, CR // 64)
            def _(t, buf=buf, at=at, k=k):
                rr = cols(t, 64)
                stage[k % ring, rr, at] = buf[rr, :].astype(F32)

        copy = pltpu.make_async_copy(stage.at[k % ring], dst, osem.at[k % ring])
        copy.start()
        outs.append(copy)
    for a, b in zip(rows_in, passed):
        a.wait()
        b.start()
    for copy in outs[len(chunks) - ring :] + passed:
        copy.wait()


def run_finish(grads, hu, whole, small, rate, damp, ein, eout, bucket_map, nbuck):
    bmap = bucket_map.reshape(1, -1)
    D = rate.shape[1]
    square = jax.ShapeDtypeStruct((D, D), F32)
    outs = [jax.ShapeDtypeStruct(a.shape, F32) for a in grads] + [square, square]
    outs += [jax.ShapeDtypeStruct(a.shape, a.dtype) for a in whole]
    kept = len(outs)
    outs += [jax.ShapeDtypeStruct(rate.shape, F32) for _ in range(4)]
    outs += [jax.ShapeDtypeStruct((8, 128), F32) for _ in range(6)]
    outs += [jax.ShapeDtypeStruct((16, 128), F32), jax.ShapeDtypeStruct((2, 128), F32), jax.ShapeDtypeStruct((2, 128), F32),
             jax.ShapeDtypeStruct((1, nbuck), F32)]
    anyspec = pl.BlockSpec(memory_space=pl.ANY)
    vspec = pl.BlockSpec(memory_space=pltpu.VMEM)
    dma = pltpu.SemaphoreType.DMA
    ring = 14
    res = pl.pallas_call(
        finish_kernel,
        out_shape=tuple(outs),
        in_specs=[anyspec] * (len(grads) + 4) + [vspec] * 6,
        out_specs=tuple([anyspec] * kept + [vspec] * (len(outs) - kept)),
        scratch_shapes=[vm(a.shape, BF) for a in grads] + [vm(hu.shape, BF)] + [vm(a.shape, a.dtype) for a in whole] + [vm((ring, D // 4, D)), dma((44,)), dma((ring,)), dma((6,))],
        compiler_params=pltpu.CompilerParams(vmem_limit_bytes=60 * 1024 * 1024),
    )(*grads, hu, *whole, small, rate, damp, ein, eout, bmap)
    return res


def shards_fast(*args):
    bo, gt, down, up, mix, hu, reset, value, shared, small = run_main(*args)
    (tokens, cotangent, seq_lengths, bucket_map, norm1_gain, norm1_bias, ema_rate, ema_damp, ema_in, ema_out,
     ema_skip, w_shared, qk_gain, qk_bias, rel_bias) = args[:15]
    (down, up, mix, reset, value, hidden, update, bo, gt, shared, g_rate, g_damp, g_in, g_out, skip, n1g, n1b, bupd, n2g, n2b,
     g_bup, g_gain, g_bias, g_rel) = run_finish(
        (down, up, mix, reset, value), hu, (bo, gt, shared), small, ema_rate, ema_damp, ema_in, ema_out, bucket_map,
        rel_bias.shape[0])
    skip, n1g, n1b, bupd, n2g, n2b = [v.reshape(-1) for v in (skip, n1g, n1b, bupd, n2g, n2b)]
    return (bo, gt, n1g, n1b, g_rate, g_damp, g_in, g_out, skip, shared, g_gain, g_bias, g_rel.reshape(-1),
            value, reset, mix, hidden, update, bupd, n2g, n2b, up, g_bup.reshape(-1), down)


def solution(mesh):
    in_specs = (
        P(("wide", "narrow"), None),
        P(("wide", "narrow"), None),
        P("wide", None),
        P(),
        P(),
        P(),
        P(),
        P(),
        P(),
        P(),
        P(),
        P(),
        P(),
        P(),
        P(),
        P(None, "narrow"),
        P(None, "narrow"),
        P("narrow", None),
        P(),
        P(),
        P(),
        P(),
        P(),
        P(None, "narrow"),
        P("narrow"),
        P("narrow", None),
    )
    out_specs = (
        P(("wide", "narrow"), None),
        P(("wide", "narrow"), None),
        P(),
        P(),
        P(),
        P(),
        P(),
        P(),
        P(),
        P(),
        P(),
        P(),
        P(),
        P(None, "narrow"),
        P(None, "narrow"),
        P("narrow", None),
        P(),
        P(),
        P(),
        P(),
        P(),
        P(None, "narrow"),
        P("narrow"),
        P("narrow", None),
    )
    body = shards_fast if (mesh.shape["wide"], mesh.shape["narrow"]) == (16, 2) else shards
    return jax.shard_map(body, mesh=mesh, in_specs=in_specs, out_specs=out_specs, check_vma=False)
```

```python
import jax
import jax.numpy as jnp
from jax import lax
from jax.experimental import pallas as pl
from jax.experimental.pallas import tpu as pltpu
from jax.sharding import PartitionSpec as P

BLOCK = 128


EPSILON = 1e-05
NEGATIVE = -1000000000.0


def carried_in(part, axis, combine, identity, reverse):
    count = lax.axis_size(axis)
    place = lax.axis_index(axis)
    ahead = count - 1 - place if reverse else place
    gathered = jax.tree.map(lambda a: lax.all_gather(a, axis), part)
    state = jax.tree.map(lambda a, e: jnp.zeros_like(a) + jnp.asarray(e, a.dtype), part, identity)

    def one(lap, state):
        source = count - 1 - lap if reverse else lap
        return combine(
            state, jax.tree.map(lambda a: lax.dynamic_index_in_dim(a, source, 0, False), gathered)
        )

    return lax.fori_loop(0, ahead, one, state)


def layer_norm(rows_in, gain, shift):
    row_mean = jnp.mean(rows_in, axis=-1, keepdims=True)
    centred = rows_in - row_mean
    row_var = jnp.mean(centred * centred, axis=-1, keepdims=True)
    return centred * lax.rsqrt(row_var + EPSILON) * gain + shift


def silu_slope(pre_act):
    sigmoid_val = jax.nn.sigmoid(pre_act)
    return sigmoid_val * (1.0 + pre_act * (1.0 - sigmoid_val))


def segment_info(lengths, positions):
    first_end = lengths[0]
    second_end = lengths[0] + lengths[1]
    segment = (positions >= first_end).astype(jnp.int32) + (positions >= second_end).astype(
        jnp.int32
    )
    starts = ((positions == 0) | (positions == first_end) | (positions == second_end)).astype(
        jnp.float32
    )
    live_rows = (segment < 2).astype(jnp.float32)
    return (segment, starts, live_rows)


def combine_pair(earlier, following):
    return (earlier[0] * following[0], earlier[1] * following[0] + following[1])


def ema_local(normed, live_rows, starts, ema_rate, ema_damp, ema_in, ema_out, ema_skip, state_in):
    inputs = normed * live_rows[:, None]
    keep_rate = 1.0 - ema_rate * ema_damp
    drive_rate = ema_rate * ema_in
    decay = keep_rate[None] * (1.0 - starts)[:, None, None]
    drive = drive_rate[None] * inputs[:, None, :]
    decay_cum, partial_state = lax.associative_scan(combine_pair, (decay, drive), axis=0)
    states = partial_state + decay_cum * state_in[None]
    smooth = jnp.sum(states * ema_out[None], axis=1)
    ema_mixed = jax.nn.silu(smooth + ema_skip * normed)
    return (ema_mixed, states[-1])


def block_bias(rel_bias, bucket_map):
    by_offset = jnp.take(rel_bias, bucket_map)
    row_index = jnp.arange(BLOCK, dtype=jnp.int32)
    offsets = row_index[:, None] - row_index[None, :]
    return (jnp.take(by_offset, jnp.clip(offsets, 0, BLOCK - 1)), offsets)


def attention_probs(query_all, key_all, segment_all, bias_table, offsets):
    blocks = query_all.shape[0] // BLOCK
    query_blocks = query_all.reshape(blocks, BLOCK, -1)
    key_blocks = key_all.reshape(blocks, BLOCK, -1)
    seg_blocks = segment_all.reshape(blocks, BLOCK)
    allowed = (seg_blocks[:, :, None] == seg_blocks[:, None, :]) & (offsets >= 0)[None]
    score_scale = query_all.shape[-1] ** (-0.5)
    scores = (
        jnp.einsum("bik,bjk->bij", query_blocks, key_blocks, preferred_element_type=jnp.float32)
        * score_scale
    )
    scores = jnp.where(allowed, scores + bias_table[None], NEGATIVE)
    row_max = jnp.max(scores, axis=-1, keepdims=True)
    weighted = jnp.exp(scores - row_max)
    return weighted / jnp.sum(weighted, axis=-1, keepdims=True)


def shards(
    tokens,
    cotangent,
    seq_lengths,
    bucket_map,
    norm1_gain,
    norm1_bias,
    ema_rate,
    ema_damp,
    ema_in,
    ema_out,
    ema_skip,
    w_shared,
    qk_gain,
    qk_bias,
    rel_bias,
    w_value,
    w_reset,
    w_mix,
    w_hidden,
    w_update,
    b_update,
    norm2_gain,
    norm2_bias,
    w_up,
    b_up,
    w_down,
):
    row_count = tokens.shape[0]
    narrow_count = lax.axis_size("narrow")
    narrow_rank = lax.axis_index("narrow")
    group_rows = row_count * narrow_count
    blocks = group_rows // BLOCK
    local_blocks = row_count // BLOCK
    lengths = seq_lengths[0]
    local_positions = narrow_rank * row_count + jnp.arange(row_count, dtype=jnp.int32)
    segment_local, starts, live_rows = segment_info(lengths, local_positions)
    segment_all = segment_info(lengths, jnp.arange(group_rows, dtype=jnp.int32))[0]
    tokens_f = tokens.astype(jnp.float32)
    normed, norm1_back = jax.vjp(layer_norm, tokens_f, norm1_gain, norm1_bias)

    def ema_apply(normed_in, rate_in, damp_in, in_weight, out_weight, skip_in, state_in):
        return ema_local(
            normed_in, live_rows, starts, rate_in, damp_in, in_weight, out_weight, skip_in, state_in
        )

    zero_state = jnp.zeros_like(ema_rate)
    ones_state = jnp.ones_like(ema_rate)
    local_final = ema_apply(normed, ema_rate, ema_damp, ema_in, ema_out, ema_skip, zero_state)[1]
    through = jnp.power(1.0 - ema_rate * ema_damp, row_count) * (1.0 - jnp.max(starts))
    state_in = carried_in(
        (through, local_final), "narrow", combine_pair, (ones_state, zero_state), False
    )[1]
    (ema_mixed, final_state), ema_back = jax.vjp(
        ema_apply, normed, ema_rate, ema_damp, ema_in, ema_out, ema_skip, state_in
    )
    normed_low = normed.astype(jnp.bfloat16)
    mixed_low = ema_mixed.astype(jnp.bfloat16)
    pre_shared = jnp.dot(mixed_low, w_shared, preferred_element_type=jnp.float32)
    shared_act = jax.nn.silu(pre_shared)
    query_low = (shared_act * qk_gain[0] + qk_bias[0]).astype(jnp.bfloat16)
    key_low = (shared_act * qk_gain[1] + qk_bias[1]).astype(jnp.bfloat16)
    normed_all, mixed_all, query_all, key_all = (
        lax.all_gather(normed_low, "narrow", axis=0, tiled=True),
        lax.all_gather(mixed_low, "narrow", axis=0, tiled=True),
        lax.all_gather(query_low, "narrow", axis=0, tiled=True),
        lax.all_gather(key_low, "narrow", axis=0, tiled=True),
    )
    bias_table, offsets = block_bias(rel_bias, bucket_map)
    probs_low = attention_probs(query_all, key_all, segment_all, bias_table, offsets).astype(
        jnp.bfloat16
    )
    pre_value = jnp.dot(normed_all, w_value, preferred_element_type=jnp.float32)
    value_low = jax.nn.silu(pre_value).astype(jnp.bfloat16)
    value_blocks = value_low.reshape(blocks, BLOCK, -1)
    pre_reset = jnp.dot(mixed_all, w_reset, preferred_element_type=jnp.float32)
    reset_gate = jax.nn.silu(pre_reset)
    attended = jnp.einsum(
        "bij,bjv->biv", probs_low, value_blocks, preferred_element_type=jnp.float32
    ).reshape(group_rows, -1)
    gated_low = (reset_gate * attended).astype(jnp.bfloat16)
    piece = gated_low
    mix_part = lax.psum_scatter(
        jnp.dot(piece, w_mix, preferred_element_type=jnp.float32),
        "narrow",
        scatter_dimension=0,
        tiled=True,
    )
    pre_hidden = jnp.dot(mixed_low, w_hidden, preferred_element_type=jnp.float32) + mix_part
    hidden_act = jax.nn.silu(pre_hidden)
    pre_update = jnp.dot(mixed_low, w_update, preferred_element_type=jnp.float32) + b_update
    update_gate = jax.nn.sigmoid(pre_update)
    blended = update_gate * hidden_act + (1.0 - update_gate) * tokens_f
    normed2, norm2_back = jax.vjp(layer_norm, blended, norm2_gain, norm2_bias)
    normed2_low = normed2.astype(jnp.bfloat16)
    grad_out = cotangent.astype(jnp.float32) * live_rows[:, None]
    grad_out_low = grad_out.astype(jnp.bfloat16)
    normed2_all = lax.all_gather(normed2_low, "narrow", axis=0, tiled=True)
    pre_up = jnp.dot(normed2_all, w_up, preferred_element_type=jnp.float32) + b_up.astype(
        jnp.float32
    )
    up_low = jax.nn.silu(pre_up).astype(jnp.bfloat16)
    piece = up_low
    ffn_out = lax.psum_scatter(
        jnp.dot(piece, w_down, preferred_element_type=jnp.float32),
        "narrow",
        scatter_dimension=0,
        tiled=True,
    )
    grad_out_all = lax.all_gather(grad_out_low, "narrow", axis=0, tiled=True)
    grad_up = jnp.einsum("sd,fd->sf", grad_out_all, w_down, preferred_element_type=jnp.float32)
    grad_pre_up = (grad_up * silu_slope(pre_up)).astype(jnp.bfloat16)
    grad_w_down = jnp.einsum("sf,sd->fd", up_low, grad_out_all, preferred_element_type=jnp.float32)
    grad_w_up = jnp.einsum(
        "sd,sf->df", normed2_all, grad_pre_up, preferred_element_type=jnp.float32
    )
    grad_b_up = jnp.sum(grad_pre_up.astype(jnp.float32), axis=0)
    piece = grad_pre_up
    grad_normed2 = lax.psum_scatter(
        jnp.einsum("sf,df->sd", piece, w_up, preferred_element_type=jnp.float32),
        "narrow",
        scatter_dimension=0,
        tiled=True,
    )
    block_out = (blended + ffn_out).astype(jnp.bfloat16)
    grad_blended_norm, grad_norm2_gain, grad_norm2_bias = norm2_back(grad_normed2)
    grad_blended = grad_out + grad_blended_norm
    grad_hidden = grad_blended * update_gate
    grad_gate = grad_blended * (hidden_act - tokens_f)
    grad_tokens = grad_blended * (1.0 - update_gate)
    grad_pre_update = (grad_gate * update_gate * (1.0 - update_gate)).astype(jnp.bfloat16)
    grad_pre_hidden = (grad_hidden * silu_slope(pre_hidden)).astype(jnp.bfloat16)
    grad_b_update = jnp.sum(grad_pre_update.astype(jnp.float32), axis=0)
    grad_w_update = jnp.einsum(
        "sd,se->de", mixed_low, grad_pre_update, preferred_element_type=jnp.float32
    )
    grad_w_hidden = jnp.einsum(
        "sd,se->de", mixed_low, grad_pre_hidden, preferred_element_type=jnp.float32
    )
    hidden_all = lax.all_gather(grad_pre_hidden, "narrow", axis=0, tiled=True)
    grad_w_mix = jnp.einsum("sv,sd->vd", gated_low, hidden_all, preferred_element_type=jnp.float32)
    grad_gated = jnp.einsum("sd,vd->sv", hidden_all, w_mix, preferred_element_type=jnp.float32)
    grad_reset = grad_gated * attended
    grad_attended = (grad_gated * reset_gate).astype(jnp.bfloat16)
    grad_pre_reset = (grad_reset * silu_slope(pre_reset)).astype(jnp.bfloat16)
    grad_w_reset = jnp.einsum(
        "sd,sv->dv", mixed_all, grad_pre_reset, preferred_element_type=jnp.float32
    )
    attended_blocks = grad_attended.reshape(blocks, BLOCK, -1)
    probs_again = attention_probs(query_all, key_all, segment_all, bias_table, offsets)
    grad_probs = jnp.einsum(
        "biv,bjv->bij", attended_blocks, value_blocks, preferred_element_type=jnp.float32
    )
    grad_value = jnp.einsum(
        "bij,biv->bjv",
        probs_again.astype(jnp.bfloat16),
        attended_blocks,
        preferred_element_type=jnp.float32,
    ).reshape(group_rows, -1)
    grad_pre_value = (grad_value * silu_slope(pre_value)).astype(jnp.bfloat16)
    grad_w_value = jnp.einsum(
        "sd,sv->dv", normed_all, grad_pre_value, preferred_element_type=jnp.float32
    )
    mixed_cols = jnp.einsum(
        "sv,dv->sd", grad_pre_reset, w_reset, preferred_element_type=jnp.float32
    )
    normed_cols = jnp.einsum(
        "sv,dv->sd", grad_pre_value, w_value, preferred_element_type=jnp.float32
    )
    probs_rows, mixed_back, normed_back = (
        lax.psum_scatter(
            grad_probs.reshape(group_rows, BLOCK), "narrow", scatter_dimension=0, tiled=True
        ),
        lax.psum_scatter(mixed_cols, "narrow", scatter_dimension=0, tiled=True),
        lax.psum_scatter(normed_cols, "narrow", scatter_dimension=0, tiled=True),
    )
    probs_local = lax.dynamic_slice_in_dim(probs_again, narrow_rank * local_blocks, local_blocks, 0)
    grad_probs_local = probs_rows.reshape(local_blocks, BLOCK, BLOCK)
    grad_scores = probs_local * (
        grad_probs_local - jnp.sum(grad_probs_local * probs_local, axis=-1, keepdims=True)
    )
    grad_scores_low = grad_scores.astype(jnp.bfloat16)
    score_scale = query_low.shape[-1] ** (-0.5)
    query_blocks = query_low.reshape(local_blocks, BLOCK, -1)
    key_blocks = key_low.reshape(local_blocks, BLOCK, -1)
    grad_query = (
        jnp.einsum(
            "bij,bjk->bik", grad_scores_low, key_blocks, preferred_element_type=jnp.float32
        ).reshape(row_count, -1)
        * score_scale
    )
    grad_key = (
        jnp.einsum(
            "bij,bik->bjk", grad_scores_low, query_blocks, preferred_element_type=jnp.float32
        ).reshape(row_count, -1)
        * score_scale
    )
    score_total = jnp.sum(grad_scores_low.astype(jnp.float32), axis=0)
    offset_hits = (offsets[:, :, None] == jnp.arange(BLOCK, dtype=jnp.int32)[None, None, :]).astype(
        jnp.float32
    )
    grad_offset = jnp.sum(score_total[:, :, None] * offset_hits, axis=(0, 1))
    bucket_hits = (
        bucket_map[:, None] == jnp.arange(rel_bias.shape[0], dtype=jnp.int32)[None, :]
    ).astype(jnp.float32)
    grad_rel_bias = jnp.sum(grad_offset[:, None] * bucket_hits, axis=0)
    grad_shared_act = grad_query * qk_gain[0] + grad_key * qk_gain[1]
    grad_qk_gain = jnp.stack(
        [jnp.sum(grad_query * shared_act, axis=0), jnp.sum(grad_key * shared_act, axis=0)]
    )
    grad_qk_bias = jnp.stack([jnp.sum(grad_query, axis=0), jnp.sum(grad_key, axis=0)])
    grad_pre_shared = (grad_shared_act * silu_slope(pre_shared)).astype(jnp.bfloat16)
    grad_w_shared = jnp.einsum(
        "sd,sz->dz", mixed_low, grad_pre_shared, preferred_element_type=jnp.float32
    )
    grad_mixed = (
        mixed_back
        + jnp.einsum("sz,dz->sd", grad_pre_shared, w_shared, preferred_element_type=jnp.float32)
        + jnp.einsum("se,de->sd", grad_pre_hidden, w_hidden, preferred_element_type=jnp.float32)
        + jnp.einsum("se,de->sd", grad_pre_update, w_update, preferred_element_type=jnp.float32)
    )
    direct = ema_back((grad_mixed, zero_state))
    later_state = carried_in(
        (through, direct[6]), "narrow", combine_pair, (ones_state, zero_state), True
    )[1]
    chained = ema_back((jnp.zeros_like(ema_mixed), later_state))
    grad_normed = normed_back + direct[0] + chained[0]
    grad_tokens_norm, grad_norm1_gain, grad_norm1_bias = norm1_back(grad_normed)
    grad_tokens = grad_tokens + grad_tokens_norm
    grad_ema_rate = direct[1] + chained[1]
    grad_ema_damp = direct[2] + chained[2]
    grad_ema_in = direct[3] + chained[3]
    grad_ema_out = direct[4] + chained[4]
    grad_ema_skip = direct[5] + chained[5]
    grad_w_value, grad_w_reset, grad_w_mix, grad_w_up, grad_b_up, grad_w_down = lax.psum(
        (grad_w_value, grad_w_reset, grad_w_mix, grad_w_up, grad_b_up, grad_w_down), "wide"
    )
    (
        grad_norm1_gain,
        grad_norm1_bias,
        grad_ema_rate,
        grad_ema_damp,
        grad_ema_in,
        grad_ema_out,
        grad_ema_skip,
        grad_w_shared,
        grad_qk_gain,
        grad_qk_bias,
        grad_rel_bias,
        grad_w_hidden,
        grad_w_update,
        grad_b_update,
        grad_norm2_gain,
        grad_norm2_bias,
    ) = lax.psum(
        (
            grad_norm1_gain,
            grad_norm1_bias,
            grad_ema_rate,
            grad_ema_damp,
            grad_ema_in,
            grad_ema_out,
            grad_ema_skip,
            grad_w_shared,
            grad_qk_gain,
            grad_qk_bias,
            grad_rel_bias,
            grad_w_hidden,
            grad_w_update,
            grad_b_update,
            grad_norm2_gain,
            grad_norm2_bias,
        ),
        ("wide", "narrow"),
    )
    return (
        block_out,
        grad_tokens,
        grad_norm1_gain,
        grad_norm1_bias,
        grad_ema_rate,
        grad_ema_damp,
        grad_ema_in,
        grad_ema_out,
        grad_ema_skip,
        grad_w_shared,
        grad_qk_gain,
        grad_qk_bias,
        grad_rel_bias,
        grad_w_value,
        grad_w_reset,
        grad_w_mix,
        grad_w_hidden,
        grad_w_update,
        grad_b_update,
        grad_norm2_gain,
        grad_norm2_bias,
        grad_w_up,
        grad_b_up,
        grad_w_down,
    )


NZ = 4
ROOT = 1
NEAR = (0, 2, 3)
EVEN, ENDS = (0, 1, 2, 3), (0, 3, 0, 3)
MIXED = (0, 3, 1, 2)
UNITS = (
    (0, 1, 0, 512, ENDS), (0, 0, 512, 512, MIXED), (1, 0, 0, 512, ENDS), (1, 2, 512, 512, EVEN), (2, 1, 0, 1024, EVEN), (3, 1, 0, 1024, ENDS),
    (4, 1, 0, 1024, MIXED), (5, 0, 0, 512, MIXED), (5, 0, 512, 512, MIXED), (6, 1, 0, 256, EVEN), (6, 2, 256, 768, ENDS),
    (7, 1, 0, 512, ENDS), (7, 1, 512, 512, ENDS),
)
PHASES = (1.8, 1.2, 2.4, 1.8, 4.2, 1.4, 6.6, 1.8, 1.8, 1.8, 1.2, 1.2, 1.0, 1.8, 1.0, 2.4, 1.0, 1.2, 2.4, 1.6, 1.6, 1.6, 1.6, 4.8, 1.2)
RELEASE = {0: 0, 1: 0, 2: 3, 3: 3, 4: 12, 5: 14, 6: 16, 7: 17}
EARLY = tuple(u for u, t in enumerate(UNITS) if t[0] < 2)
UNIT, LAG = 3.0, 2.0
MARGIN, WINDOW = 0.0, 1000.0
RANKS = {"G": 1, "P": 1, "C": 1, "D": 1, "F": 2, "W": 2, "Y": 4, "X": 4, "S": 0}
BY_UNIT = False


def far_first(z, roots):
    return sorted(range(NZ), key=lambda k: (-abs(roots[k] - z), k))


def line_events(z):
    found = []
    for u, (i, first, _, rows, roots) in enumerate(UNITS):
        size = rows / (1024.0 if first else 512.0)
        late = RELEASE[i]
        for k in range(NZ):
            g = roots[k]
            left = ("l", z - 1, ("zr", u, k), size)
            right = ("r", z + 1, ("zl", u, k), size)
            cross = [("y", z, ("yf", u, k), size)]
            far = [("x", z, ("xf", u, k, 0), size)] if i == 5 else []
            far += [("c", z, ("cf", u, k, 0), size)]
            on = (cross if first == 1 else []) + far
            both = ([left] if z > 0 else []) + ([right] if z < NZ - 1 else []) + (cross if first else []) + far
            need = [("yr", u, k)] if first else []
            if first:
                found.append((("G", u, k), late, None, [], [("y", z, ("yr", u, k), size)], 0.1))
            if z > 0 and g >= z:
                need.append(("zl", u, k))
            if z < NZ - 1 and g <= z:
                need.append(("zr", u, k))
            if g != z:
                found.append((("P", u, k), late, None, need, [right if g > z else left], 0.4))
                further = [left] if g > z > 0 else [right] if g < z < NZ - 1 else []
                found.append((("F", u, k), late, ("P", u, k), [("zr" if g > z else "zl", u, k)], further + on, 0.2))
            else:
                swap = both if first else [("y", z, ("yr", u, k), size)]
                found.append((("C", u, k), late, None, need, swap, 0.4))
                if not first:
                    found.append((("D", u, k), late, ("C", u, k), [("yr", u, k)], both, 0.4))
            other = [("x", z, ("xf", u, k, 1), size)] if i == 5 else []
            other += [("c", z, ("cf", u, k, 1), size)]
            if first == 1:
                found.append((("Y", u, k), late, ("G", u, k), [("yf", u, k)], other, 0.2))
            if first == 2:
                left = ("l", z - 1, ("wr", u, k), size)
                right = ("r", z + 1, ("wl", u, k), size)
                if g == z:
                    both = ([left] if z > 0 else []) + ([right] if z < NZ - 1 else []) + other
                    found.append((("Y", u, k), late, ("G", u, k), [("yf", u, k)], both, 0.2))
                else:
                    further = [left] if g > z > 0 else [right] if g < z < NZ - 1 else []
                    found.append((("W", u, k), late, ("G", u, k), [("wr" if g > z else "wl", u, k)], further + other, 0.2))
            if i == 5:
                for h in range(2 if first else 1):
                    found.append((("X", u, k, h), late, None, [("xf", u, k, h)], [("c", z, ("cf", u, k, 2 + h), size)], 0.2))
    last = len(PHASES) - 1

    def small(n, after, need, out):
        found.append((("S", n, 0), last, after, need, out, 0.4))

    small(1, None, [], [("x", z, ("s1",), 0.7), ("c", z, ("s1c",), 0.7)])
    small(3, ("S", 1, 0), [("s1",)], [("y", z, ("s3",), 1.35)])
    inward = [] if z == ROOT else [("r" if z < ROOT else "l", ROOT, ("s4", z), 1.35)]
    small(4, ("S", 3, 0), [("s3",)], inward)
    tail = [("c", z, ("s6",), 1.35), ("x", z, ("s7",), 1.35)]
    if z == ROOT:
        out = [("l" if q < ROOT else "r", q, ("s5",), 1.35) for q in NEAR]
        small(6, ("S", 4, 0), [("s4", q) for q in NEAR], out + tail)
    else:
        small(7, ("S", 4, 0), [("s5",)], tail)
    return found


def make_plan():
    todo = [line_events(z) for z in range(NZ)]
    clock = [0.0] * NZ
    phase = [0] * NZ
    done = [set() for _ in range(NZ)]
    arrive = [{} for _ in range(NZ)]
    link = {}
    plan = [[[] for _ in range(len(PHASES) + 1)] for _ in range(NZ)]
    while any(todo) or min(phase) < len(PHASES):
        z = min(range(NZ), key=lambda q: (clock[q], q) if (todo[q] or phase[q] < len(PHASES)) else (1e9, q))
        now = clock[z]
        best = None
        for item in todo[z]:
            key, late, after, need, out, cost = item
            if phase[z] <= late or (after is not None and after not in done[z]):
                continue
            latest = 0.0
            for m in need:
                latest = max(latest, arrive[z].get(m, 1e9))
            if need and latest + (MARGIN if phase[z] < len(PHASES) else 0.0) > now:
                continue
            full = phase[z] >= len(PHASES) and key[0] != "S" and any(
                link.get((z, lane), 0.0) > now + WINDOW for lane, _, _, _ in out if lane in "ylr")
            if full:
                continue
            away = -abs(UNITS[key[1]][4][key[2]] - z) if key[0] != "S" else 0
            rank = RANKS[key[0]]
            if key[0] == "Y" and UNITS[key[1]][1] == 2:
                rank = RANKS["F"]
            order = (rank, key[1] if BY_UNIT else latest, away, key[1], key[2])
            if best is None or order < best[0]:
                best = (order, item)
        if best is not None:
            item = best[1]
            todo[z].remove(item)
            key, _, _, _, out, cost = item
            done[z].add(key)
            plan[z][phase[z]].append(key)
            clock[z] += 0.8 * cost
            for lane, dest, message, size in out:
                begin = max(link.get((z, lane), 0.0), clock[z])
                took = size * UNIT * (0.2 if lane == "c" else 1.0)
                link[(z, lane)] = begin + took
                arrive[dest][message] = begin + took + LAG
        elif phase[z] < len(PHASES):
            clock[z] += PHASES[phase[z]]
            phase[z] += 1
        else:
            clock[z] += 0.1
    ends = [max([clock[z]] + list(arrive[z].values())) for z in range(NZ)]
    return plan, ends

F32 = jnp.float32
BF = jnp.bfloat16
MESH = pl.DeviceIdType.MESH


def mm(a, b):
    return lax.dot_general(a, b, (((1,), (0,)), ((), ())), preferred_element_type=F32)


def mm_nt(a, b):
    return lax.dot_general(a, b, (((1,), (1,)), ((), ())), preferred_element_type=F32)


def mm_tn(a, b):
    return lax.dot_general(a, b, (((0,), (0,)), ((), ())), preferred_element_type=F32)


def sigm(v):
    return 1.0 / (1.0 + jnp.exp(-v))


def slope_of(pre, sig):
    return sig * (1.0 + pre * (1.0 - sig))


def cols(i, n):
    return pl.ds(pl.multiple_of(i * n, n), n)


def main_kernel(
    tok_h, cot_h, wsh_h, wv_h, wr_h, wm_h, wh_h, wu_h, wup_h, wdn_h,
    lens, relb, bmap, in_n1g, in_n1b, in_skip, in_bupd, in_n2g, in_n2b, rate, damp, ein, eout, qkg, qkb, in_bup,
    bo, gt, o_all, o_hu, o_shared, o_small,
    wsh, wv, wr, wm, wh, wu, wup, wdn,
    tok, gout, normed, nlow, mlow, pre_ema, xs, smo, pre_sh, qlow, klow, probs, plow,
    pre_v, att, pre_r, vlow, gated, part_s, mix_r, own_f, pre_hid, gate, blend, n2,
    gup, up, gpu, gn2_r, ffn_s, ffn_r, hid, upd, gpr, gpv, gp_acc, gp_r, gps,
    nb_s, mb_r, nb_r,
    p_normed, p_mixed, p_gout, p_up, p_n2, p_gpu, p_gated, p_hid, p_upd, p_gpr, p_gpv, p_gps,
    a_s, w_s, snap_s, snap_r, carry, carry_r, acc, keep, live, segc, vec, bup,
    g_v, ext, small, s_q, s_own, s_y, s_in,
    wsem, xsend, xrecv, csend, crecv, lsem, asend, arecv, ready,
):
    x = lax.axis_index("narrow")
    w = lax.axis_index("wide")
    other = 1 - x
    c = w % 2
    wpart = w + 1 - 2 * c
    y = (w // 2) % 2
    wy = w + 2 - 4 * y
    zi = w // 4
    wl = w - 4
    wr_ = w + 4
    H = tok.shape[0] // 2
    R = 2 * H
    own = pl.ds(pl.multiple_of(x * H, H), H)
    oth = pl.ds(pl.multiple_of(other * H, H), H)
    D = 1024
    VL = wv.shape[1]
    FL = wup.shape[0] * wup.shape[2]
    EPS = EPSILON

    weights = [
        (tok_h, tok.at[own]), (cot_h, gout.at[own]), (wsh_h, wsh), (wv_h, wv), (wr_h, wr), (wm_h, wm), (wh_h, wh), (wu_h, wu),
    ]
    wcopies = [pltpu.make_async_copy(s, d, wsem.at[i]) for i, (s, d) in enumerate(weights)]
    FB = D // 2
    down_copies = [pltpu.make_async_copy(wdn_h.at[:, b * FB : (b + 1) * FB], wdn.at[b], wsem.at[8 + b]) for b in range(D // FB)]
    up_copies = [pltpu.make_async_copy(wup_h.at[:, b * FB : (b + 1) * FB], wup.at[b], wsem.at[10 + b]) for b in range(FL // FB)]
    wcopies[0].start()
    wcopies[1].start()

    barrier = pltpu.get_barrier_semaphore()
    w_root = w + 4 * (ROOT - zi)
    w_last = w + 4 * (NZ - 1 - zi)

    def greet(to):
        pl.semaphore_signal(barrier, inc=1, device_id=to, device_id_type=MESH)

    for to in ((w, other), (wpart, x), (wpart, other), (wy, x)):
        greet(to)
    for z in range(NZ):
        met = [wl] * (z > 0) + [wr_] * (z < NZ - 1) + [w_last] * (z == ROOT) + [w_root] * (z == NZ - 1)

        @pl.when(zi == z)
        def _(met=met):
            for to in met:
                greet((to, x))
            pl.semaphore_wait(barrier, 4 + len(met))

    def xcopy(i, src, dst):
        return pltpu.make_async_remote_copy(
            src_ref=src, dst_ref=dst, send_sem=xsend.at[i], recv_sem=xrecv.at[i],
            device_id=(w, other), device_id_type=MESH,
        )

    def ccopy(i, src, dst):
        return pltpu.make_async_remote_copy(
            src_ref=src, dst_ref=dst, send_sem=csend.at[i], recv_sem=crecv.at[i],
            device_id=(wpart, x), device_id_type=MESH,
        )

    HC = H // 4
    x_tok = [
        xcopy(0 if j == 0 else 16 + j, tok_h.at[j * HC : (j + 1) * HC], tok.at[pl.ds(pl.multiple_of(x * H + j * HC, HC), HC)])
        for j in range(4)
    ]
    x_cot = xcopy(1, cot_h, gout.at[own])
    for copy in x_tok:
        copy.start()
    for copy in wcopies[2:] + down_copies + up_copies:
        copy.start()

    gs = smo.at[0 : H * 8]
    gxs = smo.at[H * 8 : R * 8]
    nb_o = gup.at[0:H, 0:D]
    gres = gup.at[0:H, D : 2 * D]
    ffn_o = gup.at[H:R, 0:D]

    first_end = lens[0, 0]
    second_end = first_end + lens[0, 1]
    place = lax.broadcasted_iota(jnp.int32, (R, 128), 0)
    begins = (place == 0) | (place == first_end) | (place == second_end)
    keep[...] = jnp.where(begins, 0.0, 1.0)
    live[...] = jnp.where(place >= second_end, 0.0, 1.0)

    def segment_of(at):
        return jnp.where(at >= first_end, 1.0, 0.0) + jnp.where(at >= second_end, 1.0, 0.0)

    segc[...] = segment_of(place)

    for t in range(2):
        for j in range(8):
            rows_ = slice(t * 8, t * 8 + 8)
            lanes = slice(j * 128, j * 128 + 128)
            r_ = rate[rows_, lanes]
            a_s[pl.ds(t * 64 + j, 8, stride=8), :] = 1.0 - r_ * damp[rows_, lanes]
            w_s[pl.ds(t * 64 + j, 8, stride=8), :] = r_ * ein[rows_, lanes] * eout[rows_, lanes]

    for k, ref in enumerate((in_n1g, in_n1b, in_skip, in_bupd, in_n2g, in_n2b)):
        for j in range(8):
            vec[k : k + 1, j * 128 : (j + 1) * 128] = ref[j : j + 1, :]
    wide_bias = in_bup[...].astype(F32)
    for j in range(16):
        bup[0:1, j * 128 : (j + 1) * 128] = wide_bias[j : j + 1, :]

    def norm_rows(v):
        m = jnp.mean(v, axis=-1, keepdims=True)
        cen = v - m
        var = jnp.mean(cen * cen, axis=-1, keepdims=True)
        return cen, lax.rsqrt(var + EPS)

    def norm1(t):
        rr = cols(t, 16)
        cen, rstd = norm_rows(tok[rr, :].astype(F32))
        v = cen * rstd * vec[0:1, :] + vec[1:2, :]
        normed[rr, :] = v
        nlow[rr, :] = v.astype(BF)
        for j in range(8):
            xs[pl.ds(t * 128 + j, 16, stride=8), :] = v[:, j * 128 : (j + 1) * 128]

    HT = H // 16
    wcopies[0].wait()
    pl.loop(0, HT, unroll=2)(lambda t: norm1(x * HT + t))
    N = 16

    def coef(ref):
        return ref[...].reshape(N, 8, 128)

    zeros = jnp.zeros((N, 8, 128), F32)

    def forward(p, s):
        k = keep[pl.ds(p, 1), :]
        at = cols(p, 8)
        xr = xs[at, :] * live[pl.ds(p, 1), :]
        s = coef(a_s) * (s * k) + xr
        smo[at, :] = jnp.sum(coef(w_s) * s, axis=0)
        return s

    def mixed_rows(t):
        rr = cols(t, 16)
        for j in range(8):
            ll = slice(j * 128, (j + 1) * 128)
            pre = smo[pl.ds(t * 128 + j, 16, stride=8), :] + vec[2:3, ll] * normed[rr, ll]
            pre_ema[rr, ll] = pre
            mlow[rr, ll] = (pre * sigm(pre)).astype(BF)

    T = 256

    def value_tile(i, rows_):
        cc = cols(i, T)
        pv = mm(nlow[rows_, :], wv[:, cc])
        pre_v[rows_, cc] = pv
        vlow[rows_, cc] = (pv * sigm(pv)).astype(BF)

    wcopies[3].wait()
    pl.loop(0, VL // T, unroll=2)(lambda i: value_tile(i, own))
    state = zeros
    for j in range(8):

        @pl.when(x == (1 if j < 4 else 0))
        def _(j=j):
            x_tok[j % 4].wait_recv()
            pl.loop(j * (HC // 16), (j + 1) * (HC // 16), unroll=2)(norm1)

        state = lax.fori_loop(j * HC, (j + 1) * HC, forward, state, unroll=4)
        pl.loop(j * (HC // 16), (j + 1) * (HC // 16), unroll=2)(mixed_rows)

    for copy in x_tok:
        copy.wait_send()
    x_cot.start()
    c_normed = ccopy(0, nlow, p_normed)
    c_normed.start()
    c_mixed = ccopy(1, mlow, p_mixed)
    c_mixed.start()

    wcopies[2].wait()
    psh = mm(mlow[...], wsh[...])
    pre_sh[...] = psh
    sh = psh * sigm(psh)
    qlow[...] = (sh * qkg[0:1, :] + qkb[0:1, :]).astype(BF)
    klow[...] = (sh * qkg[1:2, :] + qkb[1:2, :]).astype(BF)

    BL = BLOCK
    ii = lax.broadcasted_iota(jnp.int32, (BL, BL), 0)
    jj = lax.broadcasted_iota(jnp.int32, (BL, BL), 1)

    def skew(tbl, left):
        for b in range(7):
            moved = pltpu.roll(tbl, (BL - (1 << b)) if left else (1 << b), 1)
            tbl = jnp.where(lax.rem(ii // (1 << b), 2) == 1, moved, tbl)
        return tbl

    buckets = bmap[0:1, :]
    by_offset = jnp.zeros((1, BL), F32)
    for b in range(relb.shape[1]):
        by_offset = by_offset + jnp.where(buckets == b, relb[0, b], 0.0)
    table = skew(jnp.broadcast_to(by_offset, (BL, BL)), False).T
    scale = float(qkg.shape[1]) ** (-0.5)
    for b in range(2):
        rb = slice(b * BL, (b + 1) * BL)
        sc = mm_nt(qlow[rb, :], klow[rb, :]) * scale
        ok = (segc[rb, :] == segment_of(lax.broadcasted_iota(jnp.int32, (1, BL), 1) + b * BL)) & (jj <= ii)
        sc = jnp.where(ok, sc + table, NEGATIVE)
        ex = jnp.exp(sc - jnp.max(sc, axis=-1, keepdims=True))
        pr = ex / jnp.sum(ex, axis=-1, keepdims=True)
        probs[rb, :] = pr
        plow[rb, :] = pr.astype(BF)

    wcopies[4].wait()

    def reset_tile(i):
        cc = cols(i, T)
        for b in range(2):
            rb = slice(b * BL, (b + 1) * BL)
            att[rb, cc] = mm(plow[rb, :], vlow[rb, cc])
        pr = mm(mlow[...], wr[:, cc])
        pre_r[:, cc] = pr
        gated[:, cc] = (pr * sigm(pr) * att[:, cc]).astype(BF)

    pl.loop(0, VL // T, unroll=2)(lambda i: value_tile(i, oth))
    pl.loop(0, VL // T, unroll=2)(reset_tile)

    wcopies[5].wait()

    HH = H // 2
    x_mix = []
    for h in range(2):
        src = pl.ds(pl.multiple_of(other * H + h * HH, HH), HH)
        hr = slice(h * HH, (h + 1) * HH)

        @pl.loop(0, D // T, unroll=2)
        def _(i, src=src, hr=hr):
            cc = cols(i, T)
            part_s[hr, cc] = mm(gated[src, :], wm[:, cc]).astype(BF)

        x_mix.append(xcopy((2, 13)[h], part_s.at[hr], mix_r.at[hr]))
        x_mix[h].start()

    c_gated = ccopy(2, gated, p_gated)
    c_gated.start()
    wcopies[6].wait()
    wcopies[7].wait()

    @pl.loop(0, D // T, unroll=2)
    def _(i):
        cc = cols(i, T)
        own_f[:, cc] = mm(gated[own, :], wm[:, cc])
        pre_hid[:, cc] = mm(mlow[own, :], wh[:, cc])
        gate[:, cc] = sigm(mm(mlow[own, :], wu[:, cc]) + vec[3:4, cc])

    wcopies[1].wait()
    x_cot.wait()

    @pl.loop(0, R // 16)
    def _(t):
        rr = cols(t, 16)
        gout[rr, :] = (gout[rr, :].astype(F32) * live[rr, 0:1]).astype(BF)

    c_gout = ccopy(3, gout, p_gout)
    c_gout.start()
    for copy in down_copies:
        copy.wait()

    @pl.loop(0, FL // T, unroll=2)
    def _(i):
        cc = cols(i, T)
        gup[:, cc] = mm_nt(gout[:, 0:FB], wdn[0, cc, :]) + mm_nt(gout[:, FB:D], wdn[1, cc, :])


    def blend_rows(t):
        rr = cols(t, 32)
        ro = pl.ds(pl.multiple_of(x * H + t * 32, 32), 32)
        ph = pre_hid[rr, :] + (own_f[rr, :] + mix_r[rr, :].astype(F32))
        pre_hid[rr, :] = ph
        u = gate[rr, :]
        bl = u * (ph * sigm(ph)) + (1.0 - u) * tok[ro, :].astype(F32)
        blend[rr, :] = bl
        cen, rstd = norm_rows(bl)
        n2[ro, :] = (cen * rstd * vec[4:5, :] + vec[5:6, :]).astype(BF)

    x_n2 = []
    for h in range(4):
        if h % 2 == 0:
            x_mix[h // 2].wait()
        pl.loop(h * (H // 128), (h + 1) * (H // 128))(blend_rows)
        part = pl.ds(pl.multiple_of(x * H + h * (H // 4), H // 4), H // 4)
        x_n2.append(xcopy(3 if h == 0 else 13 + h, n2.at[part], n2.at[part]))
        x_n2[h].start()

    for copy in up_copies:
        copy.wait()
    FT = FL // T

    def up_tile(i, rows_, first):
        cc = cols(i, T)
        pu = mm(n2[rows_, :], wup[i // 2, :, cols(i % 2, T)]) + bup[0:1, cc]
        sg = sigm(pu)
        up[rows_, cc] = (pu * sg).astype(BF)
        gp = (gup[rows_, cc] * slope_of(pu, sg)).astype(BF)
        gpu[rows_, cc] = gp
        sums = jnp.sum(gp.astype(F32), axis=0, keepdims=True)
        for h in range(2):
            at = pl.ds(304 + x * 16 + i * 2 + h, 1)
            part = sums[:, h * 128 : (h + 1) * 128]
            if first:
                small[at, :] = part
                small[pl.ds(304 + other * 16 + i * 2 + h, 1), :] = jnp.zeros((1, 128), F32)
            else:
                small[at, :] += part

    pl.loop(0, FT, unroll=2)(lambda i: up_tile(i, own, True))
    for copy in x_n2:
        copy.wait()
    c_n2 = ccopy(4, n2, p_n2)
    c_n2.start()
    halfF = FL // 2
    theirs_f = pl.ds(pl.multiple_of((1 - c) * halfF, halfF), halfF)
    pl.loop(0, FT // 2, unroll=2)(lambda i: up_tile((1 - c) * (FT // 2) + i, oth, False))
    c_up = ccopy(5, up.at[:, theirs_f], p_up)
    c_gpu = ccopy(6, gpu.at[:, theirs_f], p_gpu)
    c_up.start()
    c_gpu.start()
    pl.loop(0, FT // 2, unroll=2)(lambda i: up_tile(c * (FT // 2) + i, oth, False))
    P2 = g_v.shape[2]
    plan = make_plan()[0]
    numbers = {}
    locals_ = {}

    def number(*key):
        return numbers.setdefault(key, len(numbers))

    shelves = [[wup, 0, b] for b in range(wup.shape[0])] + [[wdn, 0, b] for b in range(wdn.shape[0])] + [[ext, 0, 0]]
    places = {}

    def place_of(key, n):
        if key not in places:
            for shelf in shelves:
                if (shelf[0] is ext) == (key[0] in EARLY) and shelf[1] + n <= shelf[0].shape[1]:
                    places[key] = (shelf[0], shelf[1], shelf[2])
                    shelf[1] += n
                    break
        ref, r0, b = places[key]
        return ref.at[b, r0 : r0 + n]

    def chunk_rows(u):
        _, first, _, rows, _ = UNITS[u]
        return rows // 8 if first else rows // 4

    def earlier(u, k):
        roots = UNITS[u][4]
        return sum(roots[q] == roots[k] for q in range(k))

    def line_place(u, k):
        return place_of((u, "z", k), chunk_rows(u))

    def second_place(u, k):
        return place_of((u, "s", earlier(u, k)), chunk_rows(u))

    def cross_place(u, k):
        return place_of((u, "y", k if UNITS[u][1] else earlier(u, k)), chunk_rows(u))

    def from_right(u, k, z):
        return second_place(u, k) if UNITS[u][4][k] == z and z > 0 else line_place(u, k)

    def first_row(u, k, half):
        _, first, row0, rows, _ = UNITS[u]
        n = chunk_rows(u)
        if first:
            return row0 + half * (rows // 2) + k * n
        return row0 + k * n

    def rows_at(u, k, half):
        n = chunk_rows(u)
        if UNITS[u][1]:
            return pl.ds(pl.multiple_of(first_row(u, k, half), 16), n)
        return pl.ds(first_row(u, k, half), n)

    def chunk(u, k, half):
        return g_v.at[UNITS[u][0], rows_at(u, k, half)]

    def result(u, k, half, core, side):
        i = UNITS[u][0]
        rr = rows_at(u, k, half)
        if i == 5:
            return o_hu.at[2 * side + core, rr]
        return o_all.at[core, i - (i > 5), rr]

    sent = [[] for _ in range(NZ)]

    def send(z, way, key, src, dst):
        dev = {
            "y": (wy, x), "l": (wl, x), "r": (wr_, x), "c": (wpart, x), "x": (w, other), "d": (wpart, other),
            "root": (w_root, x), "last": (w_last, x),
        }[way]
        n = number(*key)
        copy = pltpu.make_async_remote_copy(
            src_ref=src, dst_ref=dst, send_sem=asend.at[n], recv_sem=arecv.at[n],
            device_id=dev, device_id_type=MESH,
        )
        copy.start()
        sent[z].append((n, src.shape, src.dtype))

    def arrived(key, ref):
        n = number(*key)
        pltpu.make_async_remote_copy(
            src_ref=ref, dst_ref=ref, send_sem=asend.at[n], recv_sem=arecv.at[n],
            device_id=(w, other), device_id_type=MESH,
        ).wait_recv()

    def add_up(dst, terms):
        if terms:

            @pl.loop(0, dst.shape[0] // 32)
            def _(t):
                rr = cols(t, 32)
                v = dst[rr, :].astype(F32)
                for term in terms:
                    v = v + term[rr, :].astype(F32)
                dst[rr, :] = v.astype(BF)

    def own_copy(u, k, src, half):
        at = locals_.setdefault((u, k), len(locals_))
        return pltpu.make_async_copy(src, result(u, k, half, c, x), lsem.at[at])

    def share(z, u, k, src, half):
        dst = result(u, k, half, c, x)
        if z > 0:
            send(z, "l", ("zr", u, k), src, dst)
        if z < NZ - 1:
            send(z, "r", ("zl", u, k), src, dst)
        if UNITS[u][1]:
            send(z, "y", ("yf", u, k), src, dst)
        if UNITS[u][0] == 5:
            send(z, "x", ("xf", u, k, 0), src, dst)
        send(z, "c", ("cf", u, k, 0), src, dst)
        own_copy(u, k, src, half).start()

    def happen(z, key):
        kind, u, k = key[:3]
        if kind == "S":
            small_step(z, u)
            return
        i, first, _, _, roots = UNITS[u]
        own_half = y if first else 0
        g = roots[k]
        if kind == "G":
            send(z, "y", ("yr", u, k), chunk(u, k, 1 - y), cross_place(u, k))
            return
        if kind in "PC":
            terms = []
            if first:
                arrived(("yr", u, k), cross_place(u, k))
                terms.append(cross_place(u, k))
            if g >= z and z > 0:
                arrived(("zl", u, k), line_place(u, k))
                terms.append(line_place(u, k))
            if g <= z and z < NZ - 1:
                arrived(("zr", u, k), from_right(u, k, z))
                terms.append(from_right(u, k, z))
            mine = chunk(u, k, own_half)
            add_up(mine, terms)
            if kind == "P" and g > z:
                send(z, "r", ("zl", u, k), mine, line_place(u, k))
            elif kind == "P":
                send(z, "l", ("zr", u, k), mine, from_right(u, k, z - 1))
            elif first:
                share(z, u, k, mine, own_half)
            else:
                send(z, "y", ("yr", u, k), mine, cross_place(u, k))
        elif kind == "D":
            mine = cross_place(u, k)
            arrived(("yr", u, k), mine)
            add_up(mine, [chunk(u, k, 0)])
            share(z, u, k, mine, 0)
        elif kind == "F":
            ref = result(u, k, own_half, c, x)
            arrived(("zr" if g > z else "zl", u, k), ref)
            if g > z > 0:
                send(z, "l", ("zr", u, k), ref, ref)
            if g < z < NZ - 1:
                send(z, "r", ("zl", u, k), ref, ref)
            if first == 1:
                send(z, "y", ("yf", u, k), ref, ref)
            if i == 5:
                send(z, "x", ("xf", u, k, 0), ref, ref)
            send(z, "c", ("cf", u, k, 0), ref, ref)
        elif kind in "YW":
            ref = result(u, k, 1 - y, c, x)
            arrived(("yf" if kind == "Y" else "wr" if g > z else "wl", u, k), ref)
            if first == 2 and g >= z > 0:
                send(z, "l", ("wr", u, k), ref, ref)
            if first == 2 and g <= z < NZ - 1:
                send(z, "r", ("wl", u, k), ref, ref)
            if i == 5:
                send(z, "x", ("xf", u, k, 1), ref, ref)
            send(z, "c", ("cf", u, k, 1), ref, ref)
        elif kind == "X":
            h = key[3]
            half = (y if h == 0 else 1 - y) if first else 0
            ref = result(u, k, half, c, other)
            arrived(("xf", u, k, h), ref)
            send(z, "c", ("cf", u, k, 2 + h), ref, ref)

    def slot(n):
        for z in range(NZ):
            if plan[z][n]:

                @pl.when(zi == z)
                def _(z=z):
                    for key in plan[z][n]:
                        happen(z, key)

    def eight(start, n):
        return pl.ds(pl.multiple_of(start, 8), n)

    def quarter(side, core):
        return eight(side * 176 + core * 88, 88)

    def quarter_sh(side, core):
        return eight((2 * side + core) * 256, 256)

    around = (("x", other, c), ("c", x, 1 - c), ("d", other, 1 - c))

    def small_step(z, n):
        mine, mine_sh = quarter(x, c), quarter_sh(x, c)

        def give(total):
            o_small[mine, :] = total[0:88, :]
            o_shared[mine_sh, :] = total[88:344, :]
            for way, _, _ in around:
                send(z, way, ("s6", way), o_small.at[mine], o_small.at[mine])
                send(z, way, ("s7", way), o_shared.at[mine_sh], o_shared.at[mine_sh])

        if n == 1:
            for at, (way, side, core) in enumerate(around):
                send(z, way, ("s1", way), small.at[quarter(side, core)], s_q.at[at])
        elif n == 3:
            for at, (way, _, _) in enumerate(around):
                arrived(("s1", way), s_q.at[at])
            s_own[0:88, :] = (small[mine, :] + s_q[0]) + (s_q[1] + s_q[2])
            send(z, "y", ("s3",), s_own, s_y)
        elif n == 4:
            arrived(("s3",), s_y)
            s_y[...] = s_y[...] + s_own[...]
            if z != ROOT:
                send(z, "root", ("s4", z), s_y, s_in.at[NEAR.index(z)])
        elif n == 6:
            for at, q in enumerate(NEAR):
                arrived(("s4", q), s_in.at[at])
            s_y[...] = (s_y[...] + s_in[0]) + (s_in[1] + s_in[2])
            for q, way in zip(NEAR, ("l", "r", "last")):
                send(z, way, ("s5", q), s_y, s_in.at[0])
            give(s_y)
        elif n == 7:
            arrived(("s5", z), s_in.at[0])
            give(s_in.at[0])

    def finish():
        for z in range(NZ):

            @pl.when(zi == z)
            def _(z=z):
                for way, side, core in around:
                    arrived(("s6", way), o_small.at[quarter(side, core)])
                    arrived(("s7", way), o_shared.at[quarter_sh(side, core)])
                for u, (i, first, _, _, roots) in enumerate(UNITS):
                    for k in range(NZ):
                        half = y if first else 0
                        arrived(("cf", u, k, 0), result(u, k, half, 1 - c, x))
                        if first:
                            arrived(("cf", u, k, 1), result(u, k, 1 - y, 1 - c, x))
                        if i == 5:
                            for h in range(2 if first else 1):
                                at = (y if h == 0 else 1 - y) if first else 0
                                arrived(("cf", u, k, 2 + h), result(u, k, at, 1 - c, other))
                        if roots[k] == z:
                            own_copy(u, k, chunk(u, k, half), half).wait()
                for n, shape, dtype in sent[z]:
                    like = g_v.at[0, 0 : shape[0]] if dtype == BF else o_shared.at[0 : shape[0]]
                    pltpu.make_async_remote_copy(
                        src_ref=like, dst_ref=like, send_sem=asend.at[n], recv_sem=arecv.at[n],
                        device_id=(w, other), device_id_type=MESH,
                    ).wait_send()


    c_gout.wait()
    c_up.wait()
    P2 = g_v.shape[2]

    @pl.loop(0, 4)
    def _(i):
        mt = cols(i, 256)
        mf = pl.ds(pl.multiple_of(c * halfF + i * 256, 256), 256)
        la = up[:, mf]
        lb = p_up[:, mt]
        for j in range(2):
            nn = slice(j * P2, (j + 1) * P2)
            g_v[j, mt, :] = (mm_tn(la, gout[:, nn]) + mm_tn(lb, p_gout[:, nn])).astype(BF)

    slot(1)

    def up_back(rows_, cc):
        parts = [mm_nt(gpu[rows_, b * FB : (b + 1) * FB], wup[b, cc, :]) for b in range(FL // FB)]
        return (parts[0] + parts[1]) + (parts[2] + parts[3])

    @pl.loop(0, D // T)
    def _(i):
        cc = cols(i, T)
        part_s[:, cc] = up_back(oth, cc).astype(BF)

    x_gn2 = xcopy(4, part_s, gn2_r)
    x_gn2.start()
    slot(2)

    @pl.loop(0, D // T)
    def _(i):
        cc = cols(i, T)
        own_f[:, cc] = up_back(own, cc)
        ffn_s[:, cc] = mm(up[oth, :], wdn[i // 2, :, cols(i % 2, T)]).astype(BF)
        ffn_o[:, cc] = mm(up[own, :], wdn[i // 2, :, cols(i % 2, T)])


    pl.semaphore_signal(ready.at[0], inc=1, device_id=(wy, x), device_id_type=MESH)

    @pl.when(zi > 0)
    def _():
        pl.semaphore_signal(ready.at[2], inc=1, device_id=(wl, x), device_id_type=MESH)

    @pl.when(zi < NZ - 1)
    def _():
        pl.semaphore_signal(ready.at[1], inc=1, device_id=(wr_, x), device_id_type=MESH)

    pl.semaphore_wait(ready.at[0], 1)

    @pl.when(zi > 0)
    def _():
        pl.semaphore_wait(ready.at[1], 1)

    @pl.when(zi < NZ - 1)
    def _():
        pl.semaphore_wait(ready.at[2], 1)

    slot(3)
    c_n2.wait()
    c_gpu.wait()

    @pl.loop(0, 4)
    def _(i):
        mt = cols(i, 256)
        la = n2[:, mt]
        lb = p_n2[:, mt]
        for j in range(2):
            nf = pl.ds(pl.multiple_of(c * halfF + j * P2, P2), P2)
            nn = slice(j * P2, (j + 1) * P2)
            g_v[2 + j, mt, :] = (mm_tn(la, gpu[:, nf]) + mm_tn(lb, p_gpu[:, nn])).astype(BF)

    slot(4)
    x_gn2.wait()

    acc[...] = jnp.zeros_like(acc)

    def add_rows(k, v):
        acc[k * 8 : k * 8 + 8, :] += v[0:8, :] + v[8:16, :]

    def norm2_back(t):
        rr = cols(t, 16)
        ro = pl.ds(pl.multiple_of(x * H + t * 16, 16), 16)
        g = own_f[rr, :] + gn2_r[rr, :].astype(F32)
        cen, rstd = norm_rows(blend[rr, :])
        xh = cen * rstd
        add_rows(0, g * xh)
        add_rows(1, g)
        gy = g * vec[4:5, :]
        gb = rstd * (gy - jnp.mean(gy, axis=-1, keepdims=True) - xh * jnp.mean(gy * xh, axis=-1, keepdims=True))
        gb = gb + gout[ro, :].astype(F32)
        u = gate[rr, :]
        ph = pre_hid[rr, :]
        sg = sigm(ph)
        tk = tok[ro, :].astype(F32)
        gud = (gb * (ph * sg - tk) * u * (1.0 - u)).astype(BF)
        ghd = (gb * u * slope_of(ph, sg)).astype(BF)
        hid[ro, :] = ghd
        upd[ro, :] = gud
        add_rows(2, gud.astype(F32))
        gres[rr, :] = gb * (1.0 - u)

    halves = [pl.ds(pl.multiple_of(x * H + h * (H // 2), H // 2), H // 2) for h in range(2)]
    x_hid = [xcopy((5, 22)[h], hid.at[halves[h]], hid.at[halves[h]]) for h in range(2)]
    pl.loop(0, HT // 2)(norm2_back)
    x_hid[0].start()
    slot(5)
    pl.loop(HT // 2, HT)(norm2_back)
    x_hid[1].start()
    x_upd = xcopy(6, upd.at[own], upd.at[own])
    x_ffn = xcopy(7, ffn_s, ffn_r)

    def put_small(row, k):
        v = jnp.sum(acc[k * 8 : k * 8 + 8, :], axis=0, keepdims=True)
        for j in range(8):
            small[row + j : row + j + 1, :] = v[:, j * 128 : (j + 1) * 128]

    put_small(256 + 32, 0)
    put_small(256 + 40, 1)
    put_small(256 + 24, 2)
    slot(6)

    snap_s[...] = jnp.zeros_like(snap_s)
    snap_r[...] = jnp.zeros_like(snap_r)

    def sense(p, state):
        s, r = state
        k = keep[pl.ds(p, 1), :]
        a = coef(a_s)
        sk = s * k
        return a * sk + xs[cols(p, 8), :] * live[pl.ds(p, 1), :], a * (r * k) + sk

    @pl.when(x == 1)
    def _():
        s_mid, r_mid = lax.fori_loop(0, H, sense, (zeros, zeros), unroll=2)
        snap_s[...] = s_mid.reshape(N * 8, 128)
        snap_r[...] = r_mid.reshape(N * 8, 128)

    for copy in x_hid:
        copy.wait()
    x_upd.start()
    c_hid = ccopy(7, hid, p_hid)
    c_hid.start()
    gp_acc[...] = jnp.zeros_like(gp_acc)

    def gated_back(i):
        cc = cols(i, T)
        gg = mm_nt(hid[...], wm[cc, :])
        pr = pre_r[:, cc]
        sg = sigm(pr)
        ga = (gg * (pr * sg)).astype(BF)
        gpr[:, cc] = (gg * att[:, cc] * slope_of(pr, sg)).astype(BF)
        pv = pre_v[:, cc]
        sv = slope_of(pv, sigm(pv))
        for b in range(2):
            rb = slice(b * BL, (b + 1) * BL)
            gp_acc[rb, :] += mm_nt(ga[rb, :], vlow[rb, cc])
            gv = mm_tn(plow[rb, :], ga[rb, :])
            gpv[rb, cc] = (gv * sv[rb, :]).astype(BF)

    for i in range(VL // T):
        pl.loop(i, i + 1)(gated_back)
        slot(7 + i)
    x_gp = xcopy(8, gp_acc.at[oth], gp_r)
    x_gp.start()
    x_upd.wait()

    @pl.loop(0, D // T)
    def _(i):
        cc = cols(i, T)
        part_s[:, cc] = mm_nt(gpr[oth, :], wr[cc, :]).astype(BF)

    x_mb = xcopy(9, part_s, mb_r)
    x_mb.start()
    slot(11)

    @pl.loop(0, D // T)
    def _(i):
        cc = cols(i, T)
        nb_s[:, cc] = mm_nt(gpv[oth, :], wv[cc, :]).astype(BF)

    x_nb = xcopy(10, nb_s, nb_r)
    halfV = VL // 2
    c_gpr = ccopy(8, gpr.at[:, pl.ds(pl.multiple_of((1 - c) * halfV, halfV), halfV)], p_gpr)
    c_gpv = ccopy(9, gpv.at[:, pl.ds(pl.multiple_of((1 - c) * halfV, halfV), halfV)], p_gpv)
    c_upd = ccopy(10, upd, p_upd)
    c_gpr.start()
    c_gpv.start()
    c_upd.start()

    slot(12)
    c_hid.wait()
    c_gated.wait()
    hv = pl.ds(pl.multiple_of(c * P2, P2), P2)
    q4 = pl.ds(pl.multiple_of((2 * x + c) * 256, 256), 256)

    @pl.loop(0, 4)
    def _(i):
        mt = cols(i, 256)
        g_v[4, mt, :] = (mm_tn(gated[:, mt], hid[:, hv]) + mm_tn(p_gated[:, mt], p_hid[:, hv])).astype(BF)

    slot(13)

    x_gp.wait()
    gpb = gp_acc[own, :] + gp_r[...]
    po = probs[own, :]
    gsc = (po * (gpb - jnp.sum(gpb * po, axis=-1, keepdims=True))).astype(BF)
    gq = mm(gsc, klow[own, :]) * scale
    gk = mm_tn(gsc, qlow[own, :]) * scale
    psh = pre_sh[own, :]
    sgs = sigm(psh)
    sh = psh * sgs
    small[336:337, :] = jnp.sum(gq * sh, axis=0, keepdims=True)
    small[337:338, :] = jnp.sum(gk * sh, axis=0, keepdims=True)
    small[338:339, :] = jnp.sum(gq, axis=0, keepdims=True)
    small[339:340, :] = jnp.sum(gk, axis=0, keepdims=True)
    small[340:341, :] = jnp.sum(skew(gsc.astype(F32).T, True), axis=0, keepdims=True)
    small[341:352, :] = jnp.zeros((11, 128), F32)
    gps[own, :] = ((gq * qkg[0:1, :] + gk * qkg[1:2, :]) * slope_of(psh, sgs)).astype(BF)
    x_gps = xcopy(11, gps.at[own], gps.at[own])
    x_gps.start()
    x_nb.start()
    slot(14)
    c_mixed.wait()
    c_upd.wait()

    la = mlow[:, q4]
    lb = p_mixed[:, q4]
    for j in range(2):
        nn = slice(j * P2, (j + 1) * P2)
        g_v[5, j * 256 : j * 256 + 256, :] = (mm_tn(la, hid[:, nn]) + mm_tn(lb, p_hid[:, nn])).astype(BF)
        g_v[5, 512 + j * 256 : 768 + j * 256, :] = (mm_tn(la, upd[:, nn]) + mm_tn(lb, p_upd[:, nn])).astype(BF)

    slot(15)

    @pl.loop(0, D // T)
    def _(i):
        cc = cols(i, T)
        own_f[:, cc] = (
            mm_nt(gpr[own, :], wr[cc, :])
            + mm_nt(gps[own, :], wsh[cc, :])
            + mm_nt(hid[own, :], wh[cc, :])
            + mm_nt(upd[own, :], wu[cc, :])
        )
        nb_o[:, cc] = mm_nt(gpv[own, :], wv[cc, :])

    slot(16)
    x_gps.wait()
    c_gps = ccopy(11, gps, p_gps)
    c_gps.start()
    c_gpr.wait()

    @pl.loop(0, 4)
    def _(i):
        mt = cols(i, 256)
        g_v[6, mt, :] = (mm_tn(mlow[:, mt], gpr[:, hv]) + mm_tn(p_mixed[:, mt], p_gpr[...])).astype(BF)

    slot(17)
    c_normed.wait()
    c_gpv.wait()

    @pl.loop(0, 4)
    def _(i):
        mt = cols(i, 256)
        g_v[7, mt, :] = (mm_tn(nlow[:, mt], gpv[:, hv]) + mm_tn(p_normed[:, mt], p_gpv[...])).astype(BF)

    c_gps.wait()
    s_own[88:344, :] = mm_tn(mlow[:, q4], gps[...]) + mm_tn(p_mixed[:, q4], p_gps[...])
    slot(18)
    x_mb.wait()
    x_ffn.start()

    acc[...] = jnp.zeros_like(acc)

    @pl.loop(0, H // 16)
    def _(t):
        rr = cols(t, 16)
        ro = pl.ds(pl.multiple_of(x * H + t * 16, 16), 16)
        pre = pre_ema[ro, :]
        g = (own_f[rr, :] + mb_r[rr, :].astype(F32)) * slope_of(pre, sigm(pre))
        own_f[rr, :] = g
        add_rows(0, g * normed[ro, :])
        for j in range(8):
            gs[pl.ds(t * 128 + j, 16, stride=8), :] = g[:, j * 128 : (j + 1) * 128]

    put_small(256, 0)
    slot(19)

    def back(p_, cy):
        p = H - 1 - p_
        at = cols(p, 8)
        po_ = x * H + p
        mu = gs[at, :] + cy
        gxs[at, :] = jnp.sum(coef(w_s) * mu, axis=0) * live[pl.ds(po_, 1), :]
        return coef(a_s) * (mu * keep[pl.ds(po_, 1), :])

    x_carry = xcopy(12, carry, carry_r)

    @pl.when(x == 1)
    def _():
        cy = lax.fori_loop(0, H, back, zeros)
        carry[...] = cy.reshape(N * 8, 128)
        x_carry.start()

    slot(20)
    for q in range(2):
        nq = slice(q * 64, q * 64 + 64)

        def fwd(p, state, nq=nq):
            s, r, gw, gr = state
            at = cols(p, 8)
            po_ = x * H + p
            k = keep[pl.ds(po_, 1), :]
            xr = xs[cols(po_, 8), :] * live[pl.ds(po_, 1), :]
            a = a_s[nq, :].reshape(8, 8, 128)
            sk = s * k
            r = a * (r * k) + sk
            s = a * sk + xr
            g = gs[at, :]
            return s, r, gw + g * s, gr + g * r

        z8 = jnp.zeros((8, 8, 128), F32)
        s0 = snap_s[nq, :].reshape(8, 8, 128)
        r0 = snap_r[nq, :].reshape(8, 8, 128)
        _, _, gw, gr = lax.fori_loop(0, H, fwd, (s0, r0, z8, z8))
        small[nq, :] = gw.reshape(64, 128)
        small[128 + q * 64 : 192 + q * 64, :] = gr.reshape(64, 128) * w_s[nq, :]
        slot(21 + q)

    @pl.when(x == 0)
    def _():
        x_carry.wait_recv()
        lax.fori_loop(0, H, back, coef(carry_r))

    @pl.when(x == 1)
    def _():
        x_carry.wait_send()

    slot(23)
    x_nb.wait()

    @pl.loop(0, H // 16)
    def _(t):
        rr = cols(t, 16)
        ro = pl.ds(pl.multiple_of(x * H + t * 16, 16), 16)
        gx = jnp.concatenate([gxs[pl.ds(t * 128 + j, 16, stride=8), :] for j in range(8)], axis=1)
        g = nb_o[rr, :] + nb_r[rr, :].astype(F32) + vec[2:3, :] * own_f[rr, :] + gx
        cen, rstd = norm_rows(tok[ro, :].astype(F32))
        xh = cen * rstd
        add_rows(1, g * xh)
        add_rows(2, g)
        gy = g * vec[0:1, :]
        gb = rstd * (gy - jnp.mean(gy, axis=-1, keepdims=True) - xh * jnp.mean(gy * xh, axis=-1, keepdims=True))
        gt[rr, :] = gres[rr, :] + gb

    put_small(256 + 8, 1)
    put_small(256 + 16, 2)

    slot(24)

    x_ffn.wait()

    @pl.loop(0, H // 16)
    def _(t):
        rr = cols(t, 16)
        bo[rr, :] = (blend[rr, :] + (ffn_o[rr, :] + ffn_r[rr, :].astype(F32))).astype(BF)

    slot(25)
    finish()

def vm(shape, dtype=F32):
    return pltpu.VMEM(shape, dtype)


SEMS = 440


def run_main(tokens, cotangent, seq_lengths, bucket_map, norm1_gain, norm1_bias, ema_rate, ema_damp, ema_in, ema_out,
             ema_skip, w_shared, qk_gain, qk_bias, rel_bias, w_value, w_reset, w_mix, w_hidden, w_update, b_update,
             norm2_gain, norm2_bias, w_up, b_up, w_down):
    H = tokens.shape[0]
    R = 2 * H
    D = tokens.shape[1]
    VL = w_value.shape[1]
    FL = w_up.shape[1]
    Z = w_shared.shape[1]
    rows8 = [v.reshape(8, D // 8) for v in (norm1_gain, norm1_bias, ema_skip, b_update, norm2_gain, norm2_bias)]
    anyspec = pl.BlockSpec(memory_space=pl.ANY)
    vspec = pl.BlockSpec(memory_space=pltpu.VMEM)
    sspec = pl.BlockSpec(memory_space=pltpu.SMEM)
    P2 = D // 2
    outs = (
        jax.ShapeDtypeStruct((H, D), BF),
        jax.ShapeDtypeStruct((H, D), F32),
        jax.ShapeDtypeStruct((2, 7, D, P2), BF),
        jax.ShapeDtypeStruct((4, D, P2), BF),
        jax.ShapeDtypeStruct((D, Z), F32),
        jax.ShapeDtypeStruct((352, 128), F32),
    )
    dma = pltpu.SemaphoreType.DMA
    scratch = [
        vm((D, Z), BF), vm((D, VL), BF), vm((D, VL), BF), vm((VL, D), BF), vm((D, D), BF), vm((D, D), BF), vm((FL // P2, D, P2), BF), vm((2, FL, P2), BF),
        vm((R, D), BF), vm((R, D), BF), vm((R, D)), vm((R, D), BF), vm((R, D), BF), vm((R, D)), vm((R * 8, 128)), vm((R * 8, 128)),
        vm((R, Z)), vm((R, Z), BF), vm((R, Z), BF), vm((R, BLOCK)), vm((R, BLOCK), BF),
        vm((R, VL)), vm((R, VL)), vm((R, VL)), vm((R, VL), BF), vm((R, VL), BF), vm((H, D), BF), vm((H, D), BF), vm((H, D)), vm((H, D)), vm((H, D)), vm((H, D)), vm((R, D), BF),
        vm((R, FL)), vm((R, FL), BF), vm((R, FL), BF), vm((H, D), BF), vm((H, D), BF), vm((H, D), BF), vm((R, D), BF), vm((R, D), BF), vm((R, VL), BF), vm((R, VL), BF), vm((R, BLOCK)), vm((H, BLOCK)), vm((R, Z), BF),
        vm((H, D), BF), vm((H, D), BF), vm((H, D), BF),
        vm((R, D), BF), vm((R, D), BF), vm((R, D), BF), vm((R, FL // 2), BF), vm((R, D), BF), vm((R, FL // 2), BF), vm((R, VL), BF), vm((R, D), BF), vm((R, D), BF), vm((R, VL // 2), BF), vm((R, VL // 2), BF), vm((R, Z), BF),
        vm((128, 128)), vm((128, 128)), vm((128, 128)), vm((128, 128)), vm((128, 128)), vm((128, 128)), vm((24, D)), vm((R, 128)), vm((R, 128)), vm((R, 128)), vm((8, D)), vm((8, FL)),
        vm((8, D, P2), BF), vm((1, 11 * 256, P2), BF), vm((352, 128)), vm((3, 88, 128)), vm((344, 128)), vm((344, 128)), vm((NZ - 1, 344, 128)),
        dma((14,)), dma((23,)), dma((23,)), dma((12,)), dma((12,)), dma((96,)), dma((SEMS,)), dma((SEMS,)), pltpu.SemaphoreType.REGULAR((3,)),
    ]
    return pl.pallas_call(
        main_kernel,
        out_shape=outs,
        in_specs=[anyspec] * 10 + [sspec, sspec] + [vspec] * 14,
        out_specs=(vspec, vspec) + (anyspec,) * 2 + (vspec, vspec),
        scratch_shapes=scratch,
        compiler_params=pltpu.CompilerParams(collective_id=0, has_side_effects=True, vmem_limit_bytes=63 * 1024 * 1024),
        cost_estimate=pl.CostEstimate(flops=15_000_000_000, bytes_accessed=40_000_000, transcendentals=0),
    )(
        tokens, cotangent, w_shared, w_value, w_reset, w_mix, w_hidden, w_update, w_up, w_down,
        seq_lengths, rel_bias.reshape(1, -1), bucket_map.reshape(1, -1), *rows8, ema_rate, ema_damp, ema_in, ema_out,
        qk_gain, qk_bias, b_up.reshape(-1, 128),
    )


def finish_kernel(every, hu, bo, gt, shared, small, rate, damp, ein, eout, bmap,
                  f_down, f_up, f_mix, f_reset, f_value, f_hid, f_upd, f_bo, f_gt, f_shared,
                  g_rate, g_damp, g_in, g_out, v0, v1, v2, v3, v4, v5, g_bup, g_gain, g_bias, g_rel,
                  b_every, b_hu, b_bo, b_gt, b_shared, stage, isem, osem, psem):
    rows_in = [pltpu.make_async_copy(a, b, psem.at[k]) for k, (a, b) in enumerate(((bo, b_bo), (gt, b_gt), (shared, b_shared)))]
    passed = [pltpu.make_async_copy(a, b, psem.at[3 + k]) for k, (a, b) in enumerate(((b_bo, f_bo), (b_gt, f_gt), (b_shared, f_shared)))]
    CR, CC = stage.shape[1], stage.shape[2]
    half = CC // 2
    chunks = []

    def gather(sources, dst):
        chunks.append(([(a, b, slice(j * half, (j + 1) * half)) for j, (a, b) in enumerate(sources)], dst))

    def piece(core, i, r):
        at = (core, i, slice(r * CR, (r + 1) * CR))
        return every.at[at], b_every.at[at]

    def quarter(q, n):
        at = (q, slice(n * CR, (n + 1) * CR))
        return hu.at[at], b_hu.at[at]

    for core in range(2):
        for r in range(4):
            gather([piece(core, 0, r), piece(core, 1, r)], f_down.at[core * 4 * CR + r * CR : core * 4 * CR + (r + 1) * CR])
            gather([piece(core, 2, r), piece(core, 3, r)], f_up.at[r * CR : (r + 1) * CR, core * CC : (core + 1) * CC])
    for i, dst in ((4, f_mix), (5, f_reset), (6, f_value)):
        for r in range(4):
            gather([piece(0, i, r), piece(1, i, r)], dst.at[r * CR : (r + 1) * CR])
    for n, dst in ((0, f_hid), (2, f_upd)):
        for q in range(4):
            gather([quarter(q, n), quarter(q, n + 1)], dst.at[q * CR : (q + 1) * CR])
    ins, count = [], 0
    for parts, _ in chunks:
        ins.append([])
        for src, buf, _ in parts:
            copy = pltpu.make_async_copy(src, buf, isem.at[count])
            copy.start()
            ins[-1].append(copy)
            count += 1
    for copy in rows_in:
        copy.start()

    for t in range(2):
        for j in range(8):
            rows_ = slice(t * 8, t * 8 + 8)
            lanes = slice(j * 128, j * 128 + 128)
            gw = small[pl.ds(t * 64 + j, 8, stride=8), :]
            ga = small[pl.ds(128 + t * 64 + j, 8, stride=8), :]
            r_, d_ = rate[rows_, lanes], damp[rows_, lanes]
            i_, o_ = ein[rows_, lanes], eout[rows_, lanes]
            g_rate[rows_, lanes] = gw * (i_ * o_) - ga * d_
            g_damp[rows_, lanes] = -ga * r_
            g_in[rows_, lanes] = gw * (r_ * o_)
            g_out[rows_, lanes] = gw * (r_ * i_)
    for k, ref in enumerate((v0, v1, v2, v3, v4, v5)):
        ref[...] = small[256 + 8 * k : 264 + 8 * k, :]
    me = lax.axis_index("narrow")
    g_bup[...] = small[pl.ds(pl.multiple_of(304 + me * 16, 8), 16), :]
    g_gain[...] = small[336:338, :]
    g_bias[...] = small[338:340, :]
    n = bmap.shape[1]
    offs = jnp.broadcast_to(small[340:341, :], (n, n)).T
    which = jnp.broadcast_to(bmap[...].astype(F32), (n, n)).T
    lane = lax.broadcasted_iota(jnp.int32, (n, n), 1).astype(F32)
    hits = jnp.sum(jnp.where(which == lane, offs, 0.0), axis=0, keepdims=True)
    g_rel[...] = hits[:, 0 : g_rel.shape[1]]

    ring = stage.shape[0]
    outs = []
    for k, (parts, dst) in enumerate(chunks):
        if k >= ring:
            outs[k - ring].wait()
        for copy, (_, buf, at) in zip(ins[k], parts):
            copy.wait()

            @pl.loop(0, CR // 64)
            def _(t, buf=buf, at=at, k=k):
                rr = cols(t, 64)
                stage[k % ring, rr, at] = buf[rr, :].astype(F32)

        copy = pltpu.make_async_copy(stage.at[k % ring], dst, osem.at[k % ring])
        copy.start()
        outs.append(copy)
    for a, b in zip(rows_in, passed):
        a.wait()
        b.start()
    for copy in outs[len(chunks) - ring :] + passed:
        copy.wait()


def run_finish(every, hu, whole, shapes, small, rate, damp, ein, eout, bucket_map, nbuck):
    bmap = bucket_map.reshape(1, -1)
    D = rate.shape[1]
    square = jax.ShapeDtypeStruct((D, D), F32)
    outs = [jax.ShapeDtypeStruct(a.shape, F32) for a in shapes] + [square, square]
    outs += [jax.ShapeDtypeStruct(a.shape, a.dtype) for a in whole]
    kept = len(outs)
    outs += [jax.ShapeDtypeStruct(rate.shape, F32) for _ in range(4)]
    outs += [jax.ShapeDtypeStruct((8, 128), F32) for _ in range(6)]
    outs += [jax.ShapeDtypeStruct((16, 128), F32), jax.ShapeDtypeStruct((2, 128), F32), jax.ShapeDtypeStruct((2, 128), F32),
             jax.ShapeDtypeStruct((1, nbuck), F32)]
    anyspec = pl.BlockSpec(memory_space=pl.ANY)
    vspec = pl.BlockSpec(memory_space=pltpu.VMEM)
    dma = pltpu.SemaphoreType.DMA
    ring = 14
    res = pl.pallas_call(
        finish_kernel,
        out_shape=tuple(outs),
        in_specs=[anyspec] * 5 + [vspec] * 6,
        out_specs=tuple([anyspec] * kept + [vspec] * (len(outs) - kept)),
        scratch_shapes=[vm(every.shape, BF), vm(hu.shape, BF)] + [vm(a.shape, a.dtype) for a in whole] + [vm((ring, D // 4, D)), dma((72,)), dma((ring,)), dma((6,))],
        compiler_params=pltpu.CompilerParams(vmem_limit_bytes=60 * 1024 * 1024),
    )(every, hu, *whole, small, rate, damp, ein, eout, bmap)
    return res


def shards_fast(*args):
    bo, gt, every, hu, shared, small = run_main(*args)
    w_value, w_reset, w_mix = args[15:18]
    w_up, w_down = args[23], args[25]
    (tokens, cotangent, seq_lengths, bucket_map, norm1_gain, norm1_bias, ema_rate, ema_damp, ema_in, ema_out,
     ema_skip, w_shared, qk_gain, qk_bias, rel_bias) = args[:15]
    (down, up, mix, reset, value, hidden, update, bo, gt, shared, g_rate, g_damp, g_in, g_out, skip, n1g, n1b, bupd, n2g, n2b,
     g_bup, g_gain, g_bias, g_rel) = run_finish(
        every, hu, (bo, gt, shared), (w_down, w_up, w_mix, w_reset, w_value), small, ema_rate, ema_damp, ema_in, ema_out, bucket_map,
        rel_bias.shape[0])
    skip, n1g, n1b, bupd, n2g, n2b = [v.reshape(-1) for v in (skip, n1g, n1b, bupd, n2g, n2b)]
    return (bo, gt, n1g, n1b, g_rate, g_damp, g_in, g_out, skip, shared, g_gain, g_bias, g_rel.reshape(-1),
            value, reset, mix, hidden, update, bupd, n2g, n2b, up, g_bup.reshape(-1), down)


def solution(mesh):
    in_specs = (
        P(("wide", "narrow"), None),
        P(("wide", "narrow"), None),
        P("wide", None),
        P(),
        P(),
        P(),
        P(),
        P(),
        P(),
        P(),
        P(),
        P(),
        P(),
        P(),
        P(),
        P(None, "narrow"),
        P(None, "narrow"),
        P("narrow", None),
        P(),
        P(),
        P(),
        P(),
        P(),
        P(None, "narrow"),
        P("narrow"),
        P("narrow", None),
    )
    out_specs = (
        P(("wide", "narrow"), None),
        P(("wide", "narrow"), None),
        P(),
        P(),
        P(),
        P(),
        P(),
        P(),
        P(),
        P(),
        P(),
        P(),
        P(),
        P(None, "narrow"),
        P(None, "narrow"),
        P("narrow", None),
        P(),
        P(),
        P(),
        P(),
        P(),
        P(None, "narrow"),
        P("narrow"),
        P("narrow", None),
    )
    body = shards_fast if (mesh.shape["wide"], mesh.shape["narrow"]) == (16, 2) else shards
    return jax.shard_map(body, mesh=mesh, in_specs=in_specs, out_specs=out_specs, check_vma=False)
```

```python
import jax
import jax.numpy as jnp
from jax import lax
from jax.experimental import pallas as pl
from jax.experimental.pallas import tpu as pltpu
from jax.sharding import PartitionSpec as P

BLOCK = 128


EPSILON = 1e-05
NEGATIVE = -1000000000.0


def carried_in(part, axis, combine, identity, reverse):
    count = lax.axis_size(axis)
    place = lax.axis_index(axis)
    ahead = count - 1 - place if reverse else place
    gathered = jax.tree.map(lambda a: lax.all_gather(a, axis), part)
    state = jax.tree.map(lambda a, e: jnp.zeros_like(a) + jnp.asarray(e, a.dtype), part, identity)

    def one(lap, state):
        source = count - 1 - lap if reverse else lap
        return combine(
            state, jax.tree.map(lambda a: lax.dynamic_index_in_dim(a, source, 0, False), gathered)
        )

    return lax.fori_loop(0, ahead, one, state)


def layer_norm(rows_in, gain, shift):
    row_mean = jnp.mean(rows_in, axis=-1, keepdims=True)
    centred = rows_in - row_mean
    row_var = jnp.mean(centred * centred, axis=-1, keepdims=True)
    return centred * lax.rsqrt(row_var + EPSILON) * gain + shift


def silu_slope(pre_act):
    sigmoid_val = jax.nn.sigmoid(pre_act)
    return sigmoid_val * (1.0 + pre_act * (1.0 - sigmoid_val))


def segment_info(lengths, positions):
    first_end = lengths[0]
    second_end = lengths[0] + lengths[1]
    segment = (positions >= first_end).astype(jnp.int32) + (positions >= second_end).astype(
        jnp.int32
    )
    starts = ((positions == 0) | (positions == first_end) | (positions == second_end)).astype(
        jnp.float32
    )
    live_rows = (segment < 2).astype(jnp.float32)
    return (segment, starts, live_rows)


def combine_pair(earlier, following):
    return (earlier[0] * following[0], earlier[1] * following[0] + following[1])


def ema_local(normed, live_rows, starts, ema_rate, ema_damp, ema_in, ema_out, ema_skip, state_in):
    inputs = normed * live_rows[:, None]
    keep_rate = 1.0 - ema_rate * ema_damp
    drive_rate = ema_rate * ema_in
    decay = keep_rate[None] * (1.0 - starts)[:, None, None]
    drive = drive_rate[None] * inputs[:, None, :]
    decay_cum, partial_state = lax.associative_scan(combine_pair, (decay, drive), axis=0)
    states = partial_state + decay_cum * state_in[None]
    smooth = jnp.sum(states * ema_out[None], axis=1)
    ema_mixed = jax.nn.silu(smooth + ema_skip * normed)
    return (ema_mixed, states[-1])


def block_bias(rel_bias, bucket_map):
    by_offset = jnp.take(rel_bias, bucket_map)
    row_index = jnp.arange(BLOCK, dtype=jnp.int32)
    offsets = row_index[:, None] - row_index[None, :]
    return (jnp.take(by_offset, jnp.clip(offsets, 0, BLOCK - 1)), offsets)


def attention_probs(query_all, key_all, segment_all, bias_table, offsets):
    blocks = query_all.shape[0] // BLOCK
    query_blocks = query_all.reshape(blocks, BLOCK, -1)
    key_blocks = key_all.reshape(blocks, BLOCK, -1)
    seg_blocks = segment_all.reshape(blocks, BLOCK)
    allowed = (seg_blocks[:, :, None] == seg_blocks[:, None, :]) & (offsets >= 0)[None]
    score_scale = query_all.shape[-1] ** (-0.5)
    scores = (
        jnp.einsum("bik,bjk->bij", query_blocks, key_blocks, preferred_element_type=jnp.float32)
        * score_scale
    )
    scores = jnp.where(allowed, scores + bias_table[None], NEGATIVE)
    row_max = jnp.max(scores, axis=-1, keepdims=True)
    weighted = jnp.exp(scores - row_max)
    return weighted / jnp.sum(weighted, axis=-1, keepdims=True)


def shards(
    tokens,
    cotangent,
    seq_lengths,
    bucket_map,
    norm1_gain,
    norm1_bias,
    ema_rate,
    ema_damp,
    ema_in,
    ema_out,
    ema_skip,
    w_shared,
    qk_gain,
    qk_bias,
    rel_bias,
    w_value,
    w_reset,
    w_mix,
    w_hidden,
    w_update,
    b_update,
    norm2_gain,
    norm2_bias,
    w_up,
    b_up,
    w_down,
):
    row_count = tokens.shape[0]
    narrow_count = lax.axis_size("narrow")
    narrow_rank = lax.axis_index("narrow")
    group_rows = row_count * narrow_count
    blocks = group_rows // BLOCK
    local_blocks = row_count // BLOCK
    lengths = seq_lengths[0]
    local_positions = narrow_rank * row_count + jnp.arange(row_count, dtype=jnp.int32)
    segment_local, starts, live_rows = segment_info(lengths, local_positions)
    segment_all = segment_info(lengths, jnp.arange(group_rows, dtype=jnp.int32))[0]
    tokens_f = tokens.astype(jnp.float32)
    normed, norm1_back = jax.vjp(layer_norm, tokens_f, norm1_gain, norm1_bias)

    def ema_apply(normed_in, rate_in, damp_in, in_weight, out_weight, skip_in, state_in):
        return ema_local(
            normed_in, live_rows, starts, rate_in, damp_in, in_weight, out_weight, skip_in, state_in
        )

    zero_state = jnp.zeros_like(ema_rate)
    ones_state = jnp.ones_like(ema_rate)
    local_final = ema_apply(normed, ema_rate, ema_damp, ema_in, ema_out, ema_skip, zero_state)[1]
    through = jnp.power(1.0 - ema_rate * ema_damp, row_count) * (1.0 - jnp.max(starts))
    state_in = carried_in(
        (through, local_final), "narrow", combine_pair, (ones_state, zero_state), False
    )[1]
    (ema_mixed, final_state), ema_back = jax.vjp(
        ema_apply, normed, ema_rate, ema_damp, ema_in, ema_out, ema_skip, state_in
    )
    normed_low = normed.astype(jnp.bfloat16)
    mixed_low = ema_mixed.astype(jnp.bfloat16)
    pre_shared = jnp.dot(mixed_low, w_shared, preferred_element_type=jnp.float32)
    shared_act = jax.nn.silu(pre_shared)
    query_low = (shared_act * qk_gain[0] + qk_bias[0]).astype(jnp.bfloat16)
    key_low = (shared_act * qk_gain[1] + qk_bias[1]).astype(jnp.bfloat16)
    normed_all, mixed_all, query_all, key_all = (
        lax.all_gather(normed_low, "narrow", axis=0, tiled=True),
        lax.all_gather(mixed_low, "narrow", axis=0, tiled=True),
        lax.all_gather(query_low, "narrow", axis=0, tiled=True),
        lax.all_gather(key_low, "narrow", axis=0, tiled=True),
    )
    bias_table, offsets = block_bias(rel_bias, bucket_map)
    probs_low = attention_probs(query_all, key_all, segment_all, bias_table, offsets).astype(
        jnp.bfloat16
    )
    pre_value = jnp.dot(normed_all, w_value, preferred_element_type=jnp.float32)
    value_low = jax.nn.silu(pre_value).astype(jnp.bfloat16)
    value_blocks = value_low.reshape(blocks, BLOCK, -1)
    pre_reset = jnp.dot(mixed_all, w_reset, preferred_element_type=jnp.float32)
    reset_gate = jax.nn.silu(pre_reset)
    attended = jnp.einsum(
        "bij,bjv->biv", probs_low, value_blocks, preferred_element_type=jnp.float32
    ).reshape(group_rows, -1)
    gated_low = (reset_gate * attended).astype(jnp.bfloat16)
    piece = gated_low
    mix_part = lax.psum_scatter(
        jnp.dot(piece, w_mix, preferred_element_type=jnp.float32),
        "narrow",
        scatter_dimension=0,
        tiled=True,
    )
    pre_hidden = jnp.dot(mixed_low, w_hidden, preferred_element_type=jnp.float32) + mix_part
    hidden_act = jax.nn.silu(pre_hidden)
    pre_update = jnp.dot(mixed_low, w_update, preferred_element_type=jnp.float32) + b_update
    update_gate = jax.nn.sigmoid(pre_update)
    blended = update_gate * hidden_act + (1.0 - update_gate) * tokens_f
    normed2, norm2_back = jax.vjp(layer_norm, blended, norm2_gain, norm2_bias)
    normed2_low = normed2.astype(jnp.bfloat16)
    grad_out = cotangent.astype(jnp.float32) * live_rows[:, None]
    grad_out_low = grad_out.astype(jnp.bfloat16)
    normed2_all = lax.all_gather(normed2_low, "narrow", axis=0, tiled=True)
    pre_up = jnp.dot(normed2_all, w_up, preferred_element_type=jnp.float32) + b_up.astype(
        jnp.float32
    )
    up_low = jax.nn.silu(pre_up).astype(jnp.bfloat16)
    piece = up_low
    ffn_out = lax.psum_scatter(
        jnp.dot(piece, w_down, preferred_element_type=jnp.float32),
        "narrow",
        scatter_dimension=0,
        tiled=True,
    )
    grad_out_all = lax.all_gather(grad_out_low, "narrow", axis=0, tiled=True)
    grad_up = jnp.einsum("sd,fd->sf", grad_out_all, w_down, preferred_element_type=jnp.float32)
    grad_pre_up = (grad_up * silu_slope(pre_up)).astype(jnp.bfloat16)
    grad_w_down = jnp.einsum("sf,sd->fd", up_low, grad_out_all, preferred_element_type=jnp.float32)
    grad_w_up = jnp.einsum(
        "sd,sf->df", normed2_all, grad_pre_up, preferred_element_type=jnp.float32
    )
    grad_b_up = jnp.sum(grad_pre_up.astype(jnp.float32), axis=0)
    piece = grad_pre_up
    grad_normed2 = lax.psum_scatter(
        jnp.einsum("sf,df->sd", piece, w_up, preferred_element_type=jnp.float32),
        "narrow",
        scatter_dimension=0,
        tiled=True,
    )
    block_out = (blended + ffn_out).astype(jnp.bfloat16)
    grad_blended_norm, grad_norm2_gain, grad_norm2_bias = norm2_back(grad_normed2)
    grad_blended = grad_out + grad_blended_norm
    grad_hidden = grad_blended * update_gate
    grad_gate = grad_blended * (hidden_act - tokens_f)
    grad_tokens = grad_blended * (1.0 - update_gate)
    grad_pre_update = (grad_gate * update_gate * (1.0 - update_gate)).astype(jnp.bfloat16)
    grad_pre_hidden = (grad_hidden * silu_slope(pre_hidden)).astype(jnp.bfloat16)
    grad_b_update = jnp.sum(grad_pre_update.astype(jnp.float32), axis=0)
    grad_w_update = jnp.einsum(
        "sd,se->de", mixed_low, grad_pre_update, preferred_element_type=jnp.float32
    )
    grad_w_hidden = jnp.einsum(
        "sd,se->de", mixed_low, grad_pre_hidden, preferred_element_type=jnp.float32
    )
    hidden_all = lax.all_gather(grad_pre_hidden, "narrow", axis=0, tiled=True)
    grad_w_mix = jnp.einsum("sv,sd->vd", gated_low, hidden_all, preferred_element_type=jnp.float32)
    grad_gated = jnp.einsum("sd,vd->sv", hidden_all, w_mix, preferred_element_type=jnp.float32)
    grad_reset = grad_gated * attended
    grad_attended = (grad_gated * reset_gate).astype(jnp.bfloat16)
    grad_pre_reset = (grad_reset * silu_slope(pre_reset)).astype(jnp.bfloat16)
    grad_w_reset = jnp.einsum(
        "sd,sv->dv", mixed_all, grad_pre_reset, preferred_element_type=jnp.float32
    )
    attended_blocks = grad_attended.reshape(blocks, BLOCK, -1)
    probs_again = attention_probs(query_all, key_all, segment_all, bias_table, offsets)
    grad_probs = jnp.einsum(
        "biv,bjv->bij", attended_blocks, value_blocks, preferred_element_type=jnp.float32
    )
    grad_value = jnp.einsum(
        "bij,biv->bjv",
        probs_again.astype(jnp.bfloat16),
        attended_blocks,
        preferred_element_type=jnp.float32,
    ).reshape(group_rows, -1)
    grad_pre_value = (grad_value * silu_slope(pre_value)).astype(jnp.bfloat16)
    grad_w_value = jnp.einsum(
        "sd,sv->dv", normed_all, grad_pre_value, preferred_element_type=jnp.float32
    )
    mixed_cols = jnp.einsum(
        "sv,dv->sd", grad_pre_reset, w_reset, preferred_element_type=jnp.float32
    )
    normed_cols = jnp.einsum(
        "sv,dv->sd", grad_pre_value, w_value, preferred_element_type=jnp.float32
    )
    probs_rows, mixed_back, normed_back = (
        lax.psum_scatter(
            grad_probs.reshape(group_rows, BLOCK), "narrow", scatter_dimension=0, tiled=True
        ),
        lax.psum_scatter(mixed_cols, "narrow", scatter_dimension=0, tiled=True),
        lax.psum_scatter(normed_cols, "narrow", scatter_dimension=0, tiled=True),
    )
    probs_local = lax.dynamic_slice_in_dim(probs_again, narrow_rank * local_blocks, local_blocks, 0)
    grad_probs_local = probs_rows.reshape(local_blocks, BLOCK, BLOCK)
    grad_scores = probs_local * (
        grad_probs_local - jnp.sum(grad_probs_local * probs_local, axis=-1, keepdims=True)
    )
    grad_scores_low = grad_scores.astype(jnp.bfloat16)
    score_scale = query_low.shape[-1] ** (-0.5)
    query_blocks = query_low.reshape(local_blocks, BLOCK, -1)
    key_blocks = key_low.reshape(local_blocks, BLOCK, -1)
    grad_query = (
        jnp.einsum(
            "bij,bjk->bik", grad_scores_low, key_blocks, preferred_element_type=jnp.float32
        ).reshape(row_count, -1)
        * score_scale
    )
    grad_key = (
        jnp.einsum(
            "bij,bik->bjk", grad_scores_low, query_blocks, preferred_element_type=jnp.float32
        ).reshape(row_count, -1)
        * score_scale
    )
    score_total = jnp.sum(grad_scores_low.astype(jnp.float32), axis=0)
    offset_hits = (offsets[:, :, None] == jnp.arange(BLOCK, dtype=jnp.int32)[None, None, :]).astype(
        jnp.float32
    )
    grad_offset = jnp.sum(score_total[:, :, None] * offset_hits, axis=(0, 1))
    bucket_hits = (
        bucket_map[:, None] == jnp.arange(rel_bias.shape[0], dtype=jnp.int32)[None, :]
    ).astype(jnp.float32)
    grad_rel_bias = jnp.sum(grad_offset[:, None] * bucket_hits, axis=0)
    grad_shared_act = grad_query * qk_gain[0] + grad_key * qk_gain[1]
    grad_qk_gain = jnp.stack(
        [jnp.sum(grad_query * shared_act, axis=0), jnp.sum(grad_key * shared_act, axis=0)]
    )
    grad_qk_bias = jnp.stack([jnp.sum(grad_query, axis=0), jnp.sum(grad_key, axis=0)])
    grad_pre_shared = (grad_shared_act * silu_slope(pre_shared)).astype(jnp.bfloat16)
    grad_w_shared = jnp.einsum(
        "sd,sz->dz", mixed_low, grad_pre_shared, preferred_element_type=jnp.float32
    )
    grad_mixed = (
        mixed_back
        + jnp.einsum("sz,dz->sd", grad_pre_shared, w_shared, preferred_element_type=jnp.float32)
        + jnp.einsum("se,de->sd", grad_pre_hidden, w_hidden, preferred_element_type=jnp.float32)
        + jnp.einsum("se,de->sd", grad_pre_update, w_update, preferred_element_type=jnp.float32)
    )
    direct = ema_back((grad_mixed, zero_state))
    later_state = carried_in(
        (through, direct[6]), "narrow", combine_pair, (ones_state, zero_state), True
    )[1]
    chained = ema_back((jnp.zeros_like(ema_mixed), later_state))
    grad_normed = normed_back + direct[0] + chained[0]
    grad_tokens_norm, grad_norm1_gain, grad_norm1_bias = norm1_back(grad_normed)
    grad_tokens = grad_tokens + grad_tokens_norm
    grad_ema_rate = direct[1] + chained[1]
    grad_ema_damp = direct[2] + chained[2]
    grad_ema_in = direct[3] + chained[3]
    grad_ema_out = direct[4] + chained[4]
    grad_ema_skip = direct[5] + chained[5]
    grad_w_value, grad_w_reset, grad_w_mix, grad_w_up, grad_b_up, grad_w_down = lax.psum(
        (grad_w_value, grad_w_reset, grad_w_mix, grad_w_up, grad_b_up, grad_w_down), "wide"
    )
    (
        grad_norm1_gain,
        grad_norm1_bias,
        grad_ema_rate,
        grad_ema_damp,
        grad_ema_in,
        grad_ema_out,
        grad_ema_skip,
        grad_w_shared,
        grad_qk_gain,
        grad_qk_bias,
        grad_rel_bias,
        grad_w_hidden,
        grad_w_update,
        grad_b_update,
        grad_norm2_gain,
        grad_norm2_bias,
    ) = lax.psum(
        (
            grad_norm1_gain,
            grad_norm1_bias,
            grad_ema_rate,
            grad_ema_damp,
            grad_ema_in,
            grad_ema_out,
            grad_ema_skip,
            grad_w_shared,
            grad_qk_gain,
            grad_qk_bias,
            grad_rel_bias,
            grad_w_hidden,
            grad_w_update,
            grad_b_update,
            grad_norm2_gain,
            grad_norm2_bias,
        ),
        ("wide", "narrow"),
    )
    return (
        block_out,
        grad_tokens,
        grad_norm1_gain,
        grad_norm1_bias,
        grad_ema_rate,
        grad_ema_damp,
        grad_ema_in,
        grad_ema_out,
        grad_ema_skip,
        grad_w_shared,
        grad_qk_gain,
        grad_qk_bias,
        grad_rel_bias,
        grad_w_value,
        grad_w_reset,
        grad_w_mix,
        grad_w_hidden,
        grad_w_update,
        grad_b_update,
        grad_norm2_gain,
        grad_norm2_bias,
        grad_w_up,
        grad_b_up,
        grad_w_down,
    )


NZ = 4
ROOT = 1
NEAR = (0, 2, 3)
EVEN, ENDS = (0, 1, 2, 3), (0, 3, 0, 3)
MIXED = (0, 3, 1, 2)
UNITS = (
    (0, 1, 0, 512, ENDS), (0, 0, 512, 512, MIXED), (1, 0, 0, 512, ENDS), (1, 2, 512, 512, EVEN), (2, 1, 0, 1024, EVEN), (3, 1, 0, 1024, ENDS),
    (4, 1, 0, 1024, MIXED), (5, 0, 0, 512, MIXED), (5, 0, 512, 512, MIXED), (6, 1, 0, 256, EVEN), (6, 2, 256, 768, ENDS),
    (7, 1, 0, 512, ENDS), (7, 1, 512, 512, ENDS),
)
PHASES = (1.8, 1.2, 2.4, 1.8, 4.2, 1.4, 6.6, 1.8, 1.8, 1.8, 1.2, 1.2, 1.0, 1.8, 1.0, 2.4, 1.0, 1.2, 2.4, 1.6, 1.6, 1.6, 1.6, 4.8, 1.2)
RELEASE = {0: 0, 1: 0, 2: 3, 3: 3, 4: 12, 5: 14, 6: 16, 7: 17}
EARLY = tuple(u for u, t in enumerate(UNITS) if t[0] < 2)
UNIT, LAG = 3.0, 2.0
MARGIN, WINDOW = 0.0, 1000.0
RANKS = {"G": 1, "P": 1, "C": 1, "D": 1, "F": 2, "W": 2, "Y": 4, "X": 4, "S": 0}
BY_UNIT = False


def far_first(z, roots):
    return sorted(range(NZ), key=lambda k: (-abs(roots[k] - z), k))


def line_events(z):
    found = []
    for u, (i, first, _, rows, roots) in enumerate(UNITS):
        size = rows / (1024.0 if first else 512.0)
        late = RELEASE[i]
        for k in range(NZ):
            g = roots[k]
            left = ("l", z - 1, ("zr", u, k), size)
            right = ("r", z + 1, ("zl", u, k), size)
            cross = [("y", z, ("yf", u, k), size)]
            far = [("x", z, ("xf", u, k, 0), size)] if i == 5 else []
            far += [("c", z, ("cf", u, k, 0), size)]
            on = (cross if first == 1 else []) + far
            both = ([left] if z > 0 else []) + ([right] if z < NZ - 1 else []) + (cross if first else []) + far
            need = [("yr", u, k)] if first else []
            if first:
                found.append((("G", u, k), late, None, [], [("y", z, ("yr", u, k), size)], 0.1))
            if z > 0 and g >= z:
                need.append(("zl", u, k))
            if z < NZ - 1 and g <= z:
                need.append(("zr", u, k))
            if g != z:
                found.append((("P", u, k), late, None, need, [right if g > z else left], 0.4))
                further = [left] if g > z > 0 else [right] if g < z < NZ - 1 else []
                found.append((("F", u, k), late, ("P", u, k), [("zr" if g > z else "zl", u, k)], further + on, 0.2))
            else:
                swap = both if first else [("y", z, ("yr", u, k), size)]
                found.append((("C", u, k), late, None, need, swap, 0.4))
                if not first:
                    found.append((("D", u, k), late, ("C", u, k), [("yr", u, k)], both, 0.4))
            other = [("x", z, ("xf", u, k, 1), size)] if i == 5 else []
            other += [("c", z, ("cf", u, k, 1), size)]
            if first == 1:
                found.append((("Y", u, k), late, ("G", u, k), [("yf", u, k)], other, 0.2))
            if first == 2:
                left = ("l", z - 1, ("wr", u, k), size)
                right = ("r", z + 1, ("wl", u, k), size)
                if g == z:
                    both = ([left] if z > 0 else []) + ([right] if z < NZ - 1 else []) + other
                    found.append((("Y", u, k), late, ("G", u, k), [("yf", u, k)], both, 0.2))
                else:
                    further = [left] if g > z > 0 else [right] if g < z < NZ - 1 else []
                    found.append((("W", u, k), late, ("G", u, k), [("wr" if g > z else "wl", u, k)], further + other, 0.2))
            if i == 5:
                for h in range(2 if first else 1):
                    found.append((("X", u, k, h), late, None, [("xf", u, k, h)], [("c", z, ("cf", u, k, 2 + h), size)], 0.2))
    last = len(PHASES) - 1

    def small(n, after, need, out):
        found.append((("S", n, 0), last, after, need, out, 0.4))

    small(1, None, [], [("x", z, ("s1",), 0.7), ("c", z, ("s1c",), 0.7)])
    small(3, ("S", 1, 0), [("s1",)], [("y", z, ("s3",), 1.35)])
    inward = [] if z == ROOT else [("r" if z < ROOT else "l", ROOT, ("s4", z), 1.35)]
    small(4, ("S", 3, 0), [("s3",)], inward)
    tail = [("c", z, ("s6",), 1.35), ("x", z, ("s7",), 1.35)]
    if z == ROOT:
        out = [("l" if q < ROOT else "r", q, ("s5",), 1.35) for q in NEAR]
        small(6, ("S", 4, 0), [("s4", q) for q in NEAR], out + tail)
    else:
        small(7, ("S", 4, 0), [("s5",)], tail)
    return found


def make_plan():
    todo = [line_events(z) for z in range(NZ)]
    clock = [0.0] * NZ
    phase = [0] * NZ
    done = [set() for _ in range(NZ)]
    arrive = [{} for _ in range(NZ)]
    link = {}
    plan = [[[] for _ in range(len(PHASES) + 1)] for _ in range(NZ)]
    while any(todo) or min(phase) < len(PHASES):
        z = min(range(NZ), key=lambda q: (clock[q], q) if (todo[q] or phase[q] < len(PHASES)) else (1e9, q))
        now = clock[z]
        best = None
        for item in todo[z]:
            key, late, after, need, out, cost = item
            if phase[z] <= late or (after is not None and after not in done[z]):
                continue
            latest = 0.0
            for m in need:
                latest = max(latest, arrive[z].get(m, 1e9))
            if need and latest + (MARGIN if phase[z] < len(PHASES) else 0.0) > now:
                continue
            full = phase[z] >= len(PHASES) and key[0] != "S" and any(
                link.get((z, lane), 0.0) > now + WINDOW for lane, _, _, _ in out if lane in "ylr")
            if full:
                continue
            away = -abs(UNITS[key[1]][4][key[2]] - z) if key[0] != "S" else 0
            rank = RANKS[key[0]]
            if key[0] == "Y" and UNITS[key[1]][1] == 2:
                rank = RANKS["F"]
            order = (rank, key[1] if BY_UNIT else latest, away, key[1], key[2])
            if best is None or order < best[0]:
                best = (order, item)
        if best is not None:
            item = best[1]
            todo[z].remove(item)
            key, _, _, _, out, cost = item
            done[z].add(key)
            plan[z][phase[z]].append(key)
            clock[z] += 0.8 * cost
            for lane, dest, message, size in out:
                begin = max(link.get((z, lane), 0.0), clock[z])
                took = size * UNIT * (0.2 if lane == "c" else 1.0)
                link[(z, lane)] = begin + took
                arrive[dest][message] = begin + took + LAG
        elif phase[z] < len(PHASES):
            clock[z] += PHASES[phase[z]]
            phase[z] += 1
        else:
            clock[z] += 0.1
    ends = [max([clock[z]] + list(arrive[z].values())) for z in range(NZ)]
    return plan, ends

F32 = jnp.float32
BF = jnp.bfloat16
MESH = pl.DeviceIdType.MESH


def mm(a, b):
    return lax.dot_general(a, b, (((1,), (0,)), ((), ())), preferred_element_type=F32)


def mm_nt(a, b):
    return lax.dot_general(a, b, (((1,), (1,)), ((), ())), preferred_element_type=F32)


def mm_tn(a, b):
    return lax.dot_general(a, b, (((0,), (0,)), ((), ())), preferred_element_type=F32)


def sigm(v):
    return 1.0 / (1.0 + jnp.exp(-v))


def slope_of(pre, sig):
    return sig * (1.0 + pre * (1.0 - sig))


def cols(i, n):
    return pl.ds(pl.multiple_of(i * n, n), n)


def main_kernel(
    tok_h, cot_h, wsh_h, wv_h, wr_h, wm_h, wh_h, wu_h, wup_h, wdn_h,
    lens, relb, bmap, in_n1g, in_n1b, in_skip, in_bupd, in_n2g, in_n2b, rate, damp, ein, eout, qkg, qkb, in_bup,
    bo, gt, o_all, o_hu, o_shared, o_small,
    wsh, wv, wr, wm, wh, wu, wup, wdn,
    tok, gout, normed, nlow, mlow, pre_ema, xs, smo, pre_sh, qlow, klow, probs, plow,
    pre_v, att, pre_r, vlow, gated, part_s, mix_r, own_f, pre_hid, gate, blend, n2,
    gup, up, gpu, gn2_r, ffn_s, ffn_r, hid, upd, gpr, gpv, gp_acc, gp_r, gps,
    nb_s, mb_r, nb_r,
    p_normed, p_mixed, p_gout, p_up, p_n2, p_gpu, p_gated, p_hid, p_upd, p_gpr, p_gpv, p_gps,
    a_s, w_s, snap_s, snap_r, carry, carry_r, acc, keep, live, segc, vec, bup,
    g_v, ext, small, s_q, s_own, s_y, s_in,
    wsem, xsend, xrecv, csend, crecv, lsem, asend, arecv, ready,
):
    x = lax.axis_index("narrow")
    w = lax.axis_index("wide")
    other = 1 - x
    c = w % 2
    wpart = w + 1 - 2 * c
    y = (w // 2) % 2
    wy = w + 2 - 4 * y
    zi = w // 4
    wl = w - 4
    wr_ = w + 4
    H = tok.shape[0] // 2
    R = 2 * H
    own = pl.ds(pl.multiple_of(x * H, H), H)
    oth = pl.ds(pl.multiple_of(other * H, H), H)
    D = 1024
    VL = wv.shape[1]
    FL = wup.shape[0] * wup.shape[2]
    EPS = EPSILON

    weights = [
        (tok_h, tok.at[own]), (cot_h, gout.at[own]), (wsh_h, wsh), (wv_h, wv), (wr_h, wr), (wm_h, wm), (wh_h, wh), (wu_h, wu),
    ]
    wcopies = [pltpu.make_async_copy(s, d, wsem.at[i]) for i, (s, d) in enumerate(weights)]
    FB = D // 2
    down_copies = [pltpu.make_async_copy(wdn_h.at[:, b * FB : (b + 1) * FB], wdn.at[b], wsem.at[8 + b]) for b in range(D // FB)]
    up_copies = [pltpu.make_async_copy(wup_h.at[:, b * FB : (b + 1) * FB], wup.at[b], wsem.at[10 + b]) for b in range(FL // FB)]
    wcopies[0].start()
    wcopies[1].start()

    barrier = pltpu.get_barrier_semaphore()
    w_root = w + 4 * (ROOT - zi)
    w_last = w + 4 * (NZ - 1 - zi)

    def greet(to):
        pl.semaphore_signal(barrier, inc=1, device_id=to, device_id_type=MESH)

    for to in ((w, other), (wpart, x), (wpart, other), (wy, x)):
        greet(to)
    for z in range(NZ):
        met = [wl] * (z > 0) + [wr_] * (z < NZ - 1) + [w_last] * (z == ROOT) + [w_root] * (z == NZ - 1)

        @pl.when(zi == z)
        def _(met=met):
            for to in met:
                greet((to, x))
            pl.semaphore_wait(barrier, 4 + len(met))

    def xcopy(i, src, dst):
        return pltpu.make_async_remote_copy(
            src_ref=src, dst_ref=dst, send_sem=xsend.at[i], recv_sem=xrecv.at[i],
            device_id=(w, other), device_id_type=MESH,
        )

    def ccopy(i, src, dst):
        return pltpu.make_async_remote_copy(
            src_ref=src, dst_ref=dst, send_sem=csend.at[i], recv_sem=crecv.at[i],
            device_id=(wpart, x), device_id_type=MESH,
        )

    HC = H // 4
    x_tok = [
        xcopy(0 if j == 0 else 16 + j, tok_h.at[j * HC : (j + 1) * HC], tok.at[pl.ds(pl.multiple_of(x * H + j * HC, HC), HC)])
        for j in range(4)
    ]
    x_cot = xcopy(1, cot_h, gout.at[own])
    for copy in x_tok:
        copy.start()
    for copy in wcopies[2:] + down_copies + up_copies:
        copy.start()

    gs = smo.at[0 : H * 8]
    gxs = smo.at[H * 8 : R * 8]
    nb_o = gup.at[0:H, 0:D]
    gres = gup.at[0:H, D : 2 * D]
    ffn_o = gup.at[H:R, 0:D]

    first_end = lens[0, 0]
    second_end = first_end + lens[0, 1]
    place = lax.broadcasted_iota(jnp.int32, (R, 128), 0)
    begins = (place == 0) | (place == first_end) | (place == second_end)
    keep[...] = jnp.where(begins, 0.0, 1.0)
    live[...] = jnp.where(place >= second_end, 0.0, 1.0)

    def segment_of(at):
        return jnp.where(at >= first_end, 1.0, 0.0) + jnp.where(at >= second_end, 1.0, 0.0)

    segc[...] = segment_of(place)

    for t in range(2):
        for j in range(8):
            rows_ = slice(t * 8, t * 8 + 8)
            lanes = slice(j * 128, j * 128 + 128)
            r_ = rate[rows_, lanes]
            a_s[pl.ds(t * 64 + j, 8, stride=8), :] = 1.0 - r_ * damp[rows_, lanes]
            w_s[pl.ds(t * 64 + j, 8, stride=8), :] = r_ * ein[rows_, lanes] * eout[rows_, lanes]

    for k, ref in enumerate((in_n1g, in_n1b, in_skip, in_bupd, in_n2g, in_n2b)):
        for j in range(8):
            vec[k : k + 1, j * 128 : (j + 1) * 128] = ref[j : j + 1, :]
    wide_bias = in_bup[...].astype(F32)
    for j in range(16):
        bup[0:1, j * 128 : (j + 1) * 128] = wide_bias[j : j + 1, :]

    def norm_rows(v):
        m = jnp.mean(v, axis=-1, keepdims=True)
        cen = v - m
        var = jnp.mean(cen * cen, axis=-1, keepdims=True)
        return cen, lax.rsqrt(var + EPS)

    def norm1(t):
        rr = cols(t, 16)
        cen, rstd = norm_rows(tok[rr, :].astype(F32))
        v = cen * rstd * vec[0:1, :] + vec[1:2, :]
        normed[rr, :] = v
        nlow[rr, :] = v.astype(BF)
        for j in range(8):
            xs[pl.ds(t * 128 + j, 16, stride=8), :] = v[:, j * 128 : (j + 1) * 128]

    HT = H // 16
    wcopies[0].wait()
    pl.loop(0, HT, unroll=2)(lambda t: norm1(x * HT + t))
    N = 16

    def coef(ref):
        return ref[...].reshape(N, 8, 128)

    zeros = jnp.zeros((N, 8, 128), F32)

    def forward(p, s):
        k = keep[pl.ds(p, 1), :]
        at = cols(p, 8)
        xr = xs[at, :] * live[pl.ds(p, 1), :]
        s = coef(a_s) * (s * k) + xr
        smo[at, :] = jnp.sum(coef(w_s) * s, axis=0)
        return s

    def mixed_rows(t):
        rr = cols(t, 16)
        for j in range(8):
            ll = slice(j * 128, (j + 1) * 128)
            pre = smo[pl.ds(t * 128 + j, 16, stride=8), :] + vec[2:3, ll] * normed[rr, ll]
            pre_ema[rr, ll] = pre
            mlow[rr, ll] = (pre * sigm(pre)).astype(BF)

    T = 256

    def value_tile(i, rows_):
        cc = cols(i, T)
        pv = mm(nlow[rows_, :], wv[:, cc])
        pre_v[rows_, cc] = pv
        vlow[rows_, cc] = (pv * sigm(pv)).astype(BF)

    wcopies[3].wait()
    pl.loop(0, VL // T, unroll=2)(lambda i: value_tile(i, own))
    state = zeros
    for j in range(8):

        @pl.when(x == (1 if j < 4 else 0))
        def _(j=j):
            x_tok[j % 4].wait_recv()
            pl.loop(j * (HC // 16), (j + 1) * (HC // 16), unroll=2)(norm1)

        state = lax.fori_loop(j * HC, (j + 1) * HC, forward, state, unroll=4)
        pl.loop(j * (HC // 16), (j + 1) * (HC // 16), unroll=2)(mixed_rows)

    for copy in x_tok:
        copy.wait_send()
    x_cot.start()
    c_normed = ccopy(0, nlow, p_normed)
    c_mixed = ccopy(1, mlow, p_mixed)

    wcopies[2].wait()
    psh = mm(mlow[...], wsh[...])
    pre_sh[...] = psh
    sh = psh * sigm(psh)
    qlow[...] = (sh * qkg[0:1, :] + qkb[0:1, :]).astype(BF)
    klow[...] = (sh * qkg[1:2, :] + qkb[1:2, :]).astype(BF)

    BL = BLOCK
    ii = lax.broadcasted_iota(jnp.int32, (BL, BL), 0)
    jj = lax.broadcasted_iota(jnp.int32, (BL, BL), 1)

    def skew(tbl, left):
        for b in range(7):
            moved = pltpu.roll(tbl, (BL - (1 << b)) if left else (1 << b), 1)
            tbl = jnp.where(lax.rem(ii // (1 << b), 2) == 1, moved, tbl)
        return tbl

    buckets = bmap[0:1, :]
    by_offset = jnp.zeros((1, BL), F32)
    for b in range(relb.shape[1]):
        by_offset = by_offset + jnp.where(buckets == b, relb[0, b], 0.0)
    table = skew(jnp.broadcast_to(by_offset, (BL, BL)), False).T
    scale = float(qkg.shape[1]) ** (-0.5)
    for b in range(2):
        rb = slice(b * BL, (b + 1) * BL)
        sc = mm_nt(qlow[rb, :], klow[rb, :]) * scale
        ok = (segc[rb, :] == segment_of(lax.broadcasted_iota(jnp.int32, (1, BL), 1) + b * BL)) & (jj <= ii)
        sc = jnp.where(ok, sc + table, NEGATIVE)
        ex = jnp.exp(sc - jnp.max(sc, axis=-1, keepdims=True))
        pr = ex / jnp.sum(ex, axis=-1, keepdims=True)
        probs[rb, :] = pr
        plow[rb, :] = pr.astype(BF)

    wcopies[4].wait()

    def reset_tile(i):
        cc = cols(i, T)
        for b in range(2):
            rb = slice(b * BL, (b + 1) * BL)
            att[rb, cc] = mm(plow[rb, :], vlow[rb, cc])
        pr = mm(mlow[...], wr[:, cc])
        pre_r[:, cc] = pr
        gated[:, cc] = (pr * sigm(pr) * att[:, cc]).astype(BF)

    pl.loop(0, VL // T, unroll=2)(lambda i: value_tile(i, oth))
    pl.loop(0, VL // T, unroll=2)(reset_tile)

    wcopies[5].wait()

    HH = H // 2
    x_mix = []
    for h in range(2):
        src = pl.ds(pl.multiple_of(other * H + h * HH, HH), HH)
        hr = slice(h * HH, (h + 1) * HH)

        @pl.loop(0, D // T, unroll=2)
        def _(i, src=src, hr=hr):
            cc = cols(i, T)
            part_s[hr, cc] = mm(gated[src, :], wm[:, cc]).astype(BF)

        x_mix.append(xcopy((2, 13)[h], part_s.at[hr], mix_r.at[hr]))
        x_mix[h].start()

    c_gated = ccopy(2, gated, p_gated)
    wcopies[6].wait()
    wcopies[7].wait()

    @pl.loop(0, D // T, unroll=2)
    def _(i):
        cc = cols(i, T)
        own_f[:, cc] = mm(gated[own, :], wm[:, cc])
        pre_hid[:, cc] = mm(mlow[own, :], wh[:, cc])
        gate[:, cc] = sigm(mm(mlow[own, :], wu[:, cc]) + vec[3:4, cc])

    wcopies[1].wait()
    x_cot.wait()

    @pl.loop(0, R // 16)
    def _(t):
        rr = cols(t, 16)
        gout[rr, :] = (gout[rr, :].astype(F32) * live[rr, 0:1]).astype(BF)

    c_gout = ccopy(3, gout, p_gout)
    c_gout.start()
    for copy in down_copies:
        copy.wait()

    @pl.loop(0, FL // T, unroll=2)
    def _(i):
        cc = cols(i, T)
        gup[:, cc] = mm_nt(gout[:, 0:FB], wdn[0, cc, :]) + mm_nt(gout[:, FB:D], wdn[1, cc, :])


    def blend_rows(t):
        rr = cols(t, 32)
        ro = pl.ds(pl.multiple_of(x * H + t * 32, 32), 32)
        ph = pre_hid[rr, :] + (own_f[rr, :] + mix_r[rr, :].astype(F32))
        pre_hid[rr, :] = ph
        u = gate[rr, :]
        bl = u * (ph * sigm(ph)) + (1.0 - u) * tok[ro, :].astype(F32)
        blend[rr, :] = bl
        cen, rstd = norm_rows(bl)
        n2[ro, :] = (cen * rstd * vec[4:5, :] + vec[5:6, :]).astype(BF)

    x_n2 = []
    for h in range(4):
        if h % 2 == 0:
            x_mix[h // 2].wait()
        pl.loop(h * (H // 128), (h + 1) * (H // 128))(blend_rows)
        part = pl.ds(pl.multiple_of(x * H + h * (H // 4), H // 4), H // 4)
        x_n2.append(xcopy(3 if h == 0 else 13 + h, n2.at[part], n2.at[part]))
        x_n2[h].start()

    for copy in up_copies:
        copy.wait()
    FT = FL // T

    def up_tile(i, rows_, first):
        cc = cols(i, T)
        pu = mm(n2[rows_, :], wup[i // 2, :, cols(i % 2, T)]) + bup[0:1, cc]
        sg = sigm(pu)
        up[rows_, cc] = (pu * sg).astype(BF)
        gp = (gup[rows_, cc] * slope_of(pu, sg)).astype(BF)
        gpu[rows_, cc] = gp
        sums = jnp.sum(gp.astype(F32), axis=0, keepdims=True)
        for h in range(2):
            at = pl.ds(304 + x * 16 + i * 2 + h, 1)
            part = sums[:, h * 128 : (h + 1) * 128]
            if first:
                small[at, :] = part
                small[pl.ds(304 + other * 16 + i * 2 + h, 1), :] = jnp.zeros((1, 128), F32)
            else:
                small[at, :] += part

    pl.loop(0, FT, unroll=2)(lambda i: up_tile(i, own, True))
    for copy in x_n2:
        copy.wait()
    c_n2 = ccopy(4, n2, p_n2)
    halfF = FL // 2
    theirs_f = pl.ds(pl.multiple_of((1 - c) * halfF, halfF), halfF)
    pl.loop(0, FT // 2, unroll=2)(lambda i: up_tile((1 - c) * (FT // 2) + i, oth, False))
    c_up = ccopy(5, up.at[:, theirs_f], p_up)
    c_gpu = ccopy(6, gpu.at[:, theirs_f], p_gpu)
    c_up.start()
    pl.loop(0, FT // 2, unroll=2)(lambda i: up_tile(c * (FT // 2) + i, oth, False))
    c_gpu.start()
    c_n2.start()
    P2 = g_v.shape[2]
    plan = make_plan()[0]
    numbers = {}
    locals_ = {}

    def number(*key):
        return numbers.setdefault(key, len(numbers))

    shelves = [[wup, 0, b] for b in range(wup.shape[0])] + [[wdn, 0, b] for b in range(wdn.shape[0])] + [[ext, 0, 0]]
    places = {}

    def place_of(key, n):
        if key not in places:
            for shelf in shelves:
                if (shelf[0] is ext) == (key[0] in EARLY) and shelf[1] + n <= shelf[0].shape[1]:
                    places[key] = (shelf[0], shelf[1], shelf[2])
                    shelf[1] += n
                    break
        ref, r0, b = places[key]
        return ref.at[b, r0 : r0 + n]

    def chunk_rows(u):
        _, first, _, rows, _ = UNITS[u]
        return rows // 8 if first else rows // 4

    def earlier(u, k):
        roots = UNITS[u][4]
        return sum(roots[q] == roots[k] for q in range(k))

    def line_place(u, k):
        return place_of((u, "z", k), chunk_rows(u))

    def second_place(u, k):
        return place_of((u, "s", earlier(u, k)), chunk_rows(u))

    def cross_place(u, k):
        return place_of((u, "y", k if UNITS[u][1] else earlier(u, k)), chunk_rows(u))

    def from_right(u, k, z):
        return second_place(u, k) if UNITS[u][4][k] == z and z > 0 else line_place(u, k)

    def first_row(u, k, half):
        _, first, row0, rows, _ = UNITS[u]
        n = chunk_rows(u)
        if first:
            return row0 + half * (rows // 2) + k * n
        return row0 + k * n

    def rows_at(u, k, half):
        n = chunk_rows(u)
        if UNITS[u][1]:
            return pl.ds(pl.multiple_of(first_row(u, k, half), 16), n)
        return pl.ds(first_row(u, k, half), n)

    def chunk(u, k, half):
        return g_v.at[UNITS[u][0], rows_at(u, k, half)]

    def result(u, k, half, core, side):
        i = UNITS[u][0]
        rr = rows_at(u, k, half)
        if i == 5:
            return o_hu.at[2 * side + core, rr]
        return o_all.at[core, i - (i > 5), rr]

    sent = [[] for _ in range(NZ)]

    def send(z, way, key, src, dst):
        dev = {
            "y": (wy, x), "l": (wl, x), "r": (wr_, x), "c": (wpart, x), "x": (w, other), "d": (wpart, other),
            "root": (w_root, x), "last": (w_last, x),
        }[way]
        n = number(*key)
        copy = pltpu.make_async_remote_copy(
            src_ref=src, dst_ref=dst, send_sem=asend.at[n], recv_sem=arecv.at[n],
            device_id=dev, device_id_type=MESH,
        )
        copy.start()
        sent[z].append((n, src.shape, src.dtype))

    def arrived(key, ref):
        n = number(*key)
        pltpu.make_async_remote_copy(
            src_ref=ref, dst_ref=ref, send_sem=asend.at[n], recv_sem=arecv.at[n],
            device_id=(w, other), device_id_type=MESH,
        ).wait_recv()

    def add_up(dst, terms):
        if terms:

            @pl.loop(0, dst.shape[0] // 32)
            def _(t):
                rr = cols(t, 32)
                v = dst[rr, :].astype(F32)
                for term in terms:
                    v = v + term[rr, :].astype(F32)
                dst[rr, :] = v.astype(BF)

    def own_copy(u, k, src, half):
        at = locals_.setdefault((u, k), len(locals_))
        return pltpu.make_async_copy(src, result(u, k, half, c, x), lsem.at[at])

    def share(z, u, k, src, half):
        dst = result(u, k, half, c, x)
        if z > 0:
            send(z, "l", ("zr", u, k), src, dst)
        if z < NZ - 1:
            send(z, "r", ("zl", u, k), src, dst)
        if UNITS[u][1]:
            send(z, "y", ("yf", u, k), src, dst)
        if UNITS[u][0] == 5:
            send(z, "x", ("xf", u, k, 0), src, dst)
        send(z, "c", ("cf", u, k, 0), src, dst)
        own_copy(u, k, src, half).start()

    def happen(z, key):
        kind, u, k = key[:3]
        if kind == "S":
            small_step(z, u)
            return
        i, first, _, _, roots = UNITS[u]
        own_half = y if first else 0
        g = roots[k]
        if kind == "G":
            send(z, "y", ("yr", u, k), chunk(u, k, 1 - y), cross_place(u, k))
            return
        if kind in "PC":
            terms = []
            if first:
                arrived(("yr", u, k), cross_place(u, k))
                terms.append(cross_place(u, k))
            if g >= z and z > 0:
                arrived(("zl", u, k), line_place(u, k))
                terms.append(line_place(u, k))
            if g <= z and z < NZ - 1:
                arrived(("zr", u, k), from_right(u, k, z))
                terms.append(from_right(u, k, z))
            mine = chunk(u, k, own_half)
            add_up(mine, terms)
            if kind == "P" and g > z:
                send(z, "r", ("zl", u, k), mine, line_place(u, k))
            elif kind == "P":
                send(z, "l", ("zr", u, k), mine, from_right(u, k, z - 1))
            elif first:
                share(z, u, k, mine, own_half)
            else:
                send(z, "y", ("yr", u, k), mine, cross_place(u, k))
        elif kind == "D":
            mine = cross_place(u, k)
            arrived(("yr", u, k), mine)
            add_up(mine, [chunk(u, k, 0)])
            share(z, u, k, mine, 0)
        elif kind == "F":
            ref = result(u, k, own_half, c, x)
            arrived(("zr" if g > z else "zl", u, k), ref)
            if g > z > 0:
                send(z, "l", ("zr", u, k), ref, ref)
            if g < z < NZ - 1:
                send(z, "r", ("zl", u, k), ref, ref)
            if first == 1:
                send(z, "y", ("yf", u, k), ref, ref)
            if i == 5:
                send(z, "x", ("xf", u, k, 0), ref, ref)
            send(z, "c", ("cf", u, k, 0), ref, ref)
        elif kind in "YW":
            ref = result(u, k, 1 - y, c, x)
            arrived(("yf" if kind == "Y" else "wr" if g > z else "wl", u, k), ref)
            if first == 2 and g >= z > 0:
                send(z, "l", ("wr", u, k), ref, ref)
            if first == 2 and g <= z < NZ - 1:
                send(z, "r", ("wl", u, k), ref, ref)
            if i == 5:
                send(z, "x", ("xf", u, k, 1), ref, ref)
            send(z, "c", ("cf", u, k, 1), ref, ref)
        elif kind == "X":
            h = key[3]
            half = (y if h == 0 else 1 - y) if first else 0
            ref = result(u, k, half, c, other)
            arrived(("xf", u, k, h), ref)
            send(z, "c", ("cf", u, k, 2 + h), ref, ref)

    def slot(n):
        for z in range(NZ):
            if plan[z][n]:

                @pl.when(zi == z)
                def _(z=z):
                    for key in plan[z][n]:
                        happen(z, key)

    def eight(start, n):
        return pl.ds(pl.multiple_of(start, 8), n)

    def quarter(side, core):
        return eight(side * 176 + core * 88, 88)

    def quarter_sh(side, core):
        return eight((2 * side + core) * 256, 256)

    around = (("x", other, c), ("c", x, 1 - c), ("d", other, 1 - c))

    def small_step(z, n):
        mine, mine_sh = quarter(x, c), quarter_sh(x, c)

        def give(total):
            o_small[mine, :] = total[0:88, :]
            o_shared[mine_sh, :] = total[88:344, :]
            for way, _, _ in around:
                send(z, way, ("s6", way), o_small.at[mine], o_small.at[mine])
                send(z, way, ("s7", way), o_shared.at[mine_sh], o_shared.at[mine_sh])

        if n == 1:
            for at, (way, side, core) in enumerate(around):
                send(z, way, ("s1", way), small.at[quarter(side, core)], s_q.at[at])
        elif n == 3:
            for at, (way, _, _) in enumerate(around):
                arrived(("s1", way), s_q.at[at])
            s_own[0:88, :] = (small[mine, :] + s_q[0]) + (s_q[1] + s_q[2])
            send(z, "y", ("s3",), s_own, s_y)
        elif n == 4:
            arrived(("s3",), s_y)
            s_y[...] = s_y[...] + s_own[...]
            if z != ROOT:
                send(z, "root", ("s4", z), s_y, s_in.at[NEAR.index(z)])
        elif n == 6:
            for at, q in enumerate(NEAR):
                arrived(("s4", q), s_in.at[at])
            s_y[...] = (s_y[...] + s_in[0]) + (s_in[1] + s_in[2])
            for q, way in zip(NEAR, ("l", "r", "last")):
                send(z, way, ("s5", q), s_y, s_in.at[0])
            give(s_y)
        elif n == 7:
            arrived(("s5", z), s_in.at[0])
            give(s_in.at[0])

    def finish():
        for z in range(NZ):

            @pl.when(zi == z)
            def _(z=z):
                for way, side, core in around:
                    arrived(("s6", way), o_small.at[quarter(side, core)])
                    arrived(("s7", way), o_shared.at[quarter_sh(side, core)])
                for u, (i, first, _, _, roots) in enumerate(UNITS):
                    for k in range(NZ):
                        half = y if first else 0
                        arrived(("cf", u, k, 0), result(u, k, half, 1 - c, x))
                        if first:
                            arrived(("cf", u, k, 1), result(u, k, 1 - y, 1 - c, x))
                        if i == 5:
                            for h in range(2 if first else 1):
                                at = (y if h == 0 else 1 - y) if first else 0
                                arrived(("cf", u, k, 2 + h), result(u, k, at, 1 - c, other))
                        if roots[k] == z:
                            own_copy(u, k, chunk(u, k, half), half).wait()
                for n, shape, dtype in sent[z]:
                    like = g_v.at[0, 0 : shape[0]] if dtype == BF else o_shared.at[0 : shape[0]]
                    pltpu.make_async_remote_copy(
                        src_ref=like, dst_ref=like, send_sem=asend.at[n], recv_sem=arecv.at[n],
                        device_id=(w, other), device_id_type=MESH,
                    ).wait_send()


    c_gout.wait()
    c_up.wait()
    P2 = g_v.shape[2]

    @pl.loop(0, 4)
    def _(i):
        mt = cols(i, 256)
        mf = pl.ds(pl.multiple_of(c * halfF + i * 256, 256), 256)
        la = up[:, mf]
        lb = p_up[:, mt]
        for j in range(2):
            nn = slice(j * P2, (j + 1) * P2)
            g_v[j, mt, :] = (mm_tn(la, gout[:, nn]) + mm_tn(lb, p_gout[:, nn])).astype(BF)

    slot(1)

    def up_back(rows_, cc):
        parts = [mm_nt(gpu[rows_, b * FB : (b + 1) * FB], wup[b, cc, :]) for b in range(FL // FB)]
        return (parts[0] + parts[1]) + (parts[2] + parts[3])

    @pl.loop(0, D // T)
    def _(i):
        cc = cols(i, T)
        part_s[:, cc] = up_back(oth, cc).astype(BF)

    x_gn2 = xcopy(4, part_s, gn2_r)
    x_gn2.start()
    slot(2)

    @pl.loop(0, D // T)
    def _(i):
        cc = cols(i, T)
        own_f[:, cc] = up_back(own, cc)
        ffn_s[:, cc] = mm(up[oth, :], wdn[i // 2, :, cols(i % 2, T)]).astype(BF)
        ffn_o[:, cc] = mm(up[own, :], wdn[i // 2, :, cols(i % 2, T)])


    pl.semaphore_signal(ready.at[0], inc=1, device_id=(wy, x), device_id_type=MESH)

    @pl.when(zi > 0)
    def _():
        pl.semaphore_signal(ready.at[2], inc=1, device_id=(wl, x), device_id_type=MESH)

    @pl.when(zi < NZ - 1)
    def _():
        pl.semaphore_signal(ready.at[1], inc=1, device_id=(wr_, x), device_id_type=MESH)

    pl.semaphore_wait(ready.at[0], 1)

    @pl.when(zi > 0)
    def _():
        pl.semaphore_wait(ready.at[1], 1)

    @pl.when(zi < NZ - 1)
    def _():
        pl.semaphore_wait(ready.at[2], 1)

    slot(3)
    c_n2.wait()
    c_gpu.wait()

    @pl.loop(0, 4)
    def _(i):
        mt = cols(i, 256)
        la = n2[:, mt]
        lb = p_n2[:, mt]
        for j in range(2):
            nf = pl.ds(pl.multiple_of(c * halfF + j * P2, P2), P2)
            nn = slice(j * P2, (j + 1) * P2)
            g_v[2 + j, mt, :] = (mm_tn(la, gpu[:, nf]) + mm_tn(lb, p_gpu[:, nn])).astype(BF)

    c_gated.start()
    c_mixed.start()
    c_normed.start()
    slot(4)
    x_gn2.wait()

    acc[...] = jnp.zeros_like(acc)

    def add_rows(k, v):
        acc[k * 8 : k * 8 + 8, :] += v[0:8, :] + v[8:16, :]

    def norm2_back(t):
        rr = cols(t, 16)
        ro = pl.ds(pl.multiple_of(x * H + t * 16, 16), 16)
        g = own_f[rr, :] + gn2_r[rr, :].astype(F32)
        cen, rstd = norm_rows(blend[rr, :])
        xh = cen * rstd
        add_rows(0, g * xh)
        add_rows(1, g)
        gy = g * vec[4:5, :]
        gb = rstd * (gy - jnp.mean(gy, axis=-1, keepdims=True) - xh * jnp.mean(gy * xh, axis=-1, keepdims=True))
        gb = gb + gout[ro, :].astype(F32)
        u = gate[rr, :]
        ph = pre_hid[rr, :]
        sg = sigm(ph)
        tk = tok[ro, :].astype(F32)
        gud = (gb * (ph * sg - tk) * u * (1.0 - u)).astype(BF)
        ghd = (gb * u * slope_of(ph, sg)).astype(BF)
        hid[ro, :] = ghd
        upd[ro, :] = gud
        add_rows(2, gud.astype(F32))
        gres[rr, :] = gb * (1.0 - u)

    halves = [pl.ds(pl.multiple_of(x * H + h * (H // 2), H // 2), H // 2) for h in range(2)]
    x_hid = [xcopy((5, 22)[h], hid.at[halves[h]], hid.at[halves[h]]) for h in range(2)]
    pl.loop(0, HT // 2)(norm2_back)
    x_hid[0].start()
    slot(5)
    pl.loop(HT // 2, HT)(norm2_back)
    x_hid[1].start()
    x_upd = xcopy(6, upd.at[own], upd.at[own])
    x_ffn = xcopy(7, ffn_s, ffn_r)

    def put_small(row, k):
        v = jnp.sum(acc[k * 8 : k * 8 + 8, :], axis=0, keepdims=True)
        for j in range(8):
            small[row + j : row + j + 1, :] = v[:, j * 128 : (j + 1) * 128]

    put_small(256 + 32, 0)
    put_small(256 + 40, 1)
    put_small(256 + 24, 2)
    slot(6)

    snap_s[...] = jnp.zeros_like(snap_s)
    snap_r[...] = jnp.zeros_like(snap_r)

    def sense(p, state):
        s, r = state
        k = keep[pl.ds(p, 1), :]
        a = coef(a_s)
        sk = s * k
        return a * sk + xs[cols(p, 8), :] * live[pl.ds(p, 1), :], a * (r * k) + sk

    @pl.when(x == 1)
    def _():
        s_mid, r_mid = lax.fori_loop(0, H, sense, (zeros, zeros), unroll=2)
        snap_s[...] = s_mid.reshape(N * 8, 128)
        snap_r[...] = r_mid.reshape(N * 8, 128)

    for copy in x_hid:
        copy.wait()
    x_upd.start()
    c_hid = ccopy(7, hid, p_hid)
    c_hid.start()
    gp_acc[...] = jnp.zeros_like(gp_acc)

    def gated_back(i):
        cc = cols(i, T)
        gg = mm_nt(hid[...], wm[cc, :])
        pr = pre_r[:, cc]
        sg = sigm(pr)
        ga = (gg * (pr * sg)).astype(BF)
        gpr[:, cc] = (gg * att[:, cc] * slope_of(pr, sg)).astype(BF)
        pv = pre_v[:, cc]
        sv = slope_of(pv, sigm(pv))
        for b in range(2):
            rb = slice(b * BL, (b + 1) * BL)
            gp_acc[rb, :] += mm_nt(ga[rb, :], vlow[rb, cc])
            gv = mm_tn(plow[rb, :], ga[rb, :])
            gpv[rb, cc] = (gv * sv[rb, :]).astype(BF)

    for i in range(VL // T):
        pl.loop(i, i + 1)(gated_back)
        slot(7 + i)
    x_gp = xcopy(8, gp_acc.at[oth], gp_r)
    x_gp.start()
    x_upd.wait()

    @pl.loop(0, D // T)
    def _(i):
        cc = cols(i, T)
        part_s[:, cc] = mm_nt(gpr[oth, :], wr[cc, :]).astype(BF)

    x_mb = xcopy(9, part_s, mb_r)
    x_mb.start()
    slot(11)

    @pl.loop(0, D // T)
    def _(i):
        cc = cols(i, T)
        nb_s[:, cc] = mm_nt(gpv[oth, :], wv[cc, :]).astype(BF)

    x_nb = xcopy(10, nb_s, nb_r)
    halfV = VL // 2
    c_gpr = ccopy(8, gpr.at[:, pl.ds(pl.multiple_of((1 - c) * halfV, halfV), halfV)], p_gpr)
    c_gpv = ccopy(9, gpv.at[:, pl.ds(pl.multiple_of((1 - c) * halfV, halfV), halfV)], p_gpv)
    c_upd = ccopy(10, upd, p_upd)
    c_gpr.start()
    c_gpv.start()
    c_upd.start()

    slot(12)
    c_hid.wait()
    c_gated.wait()
    hv = pl.ds(pl.multiple_of(c * P2, P2), P2)
    q4 = pl.ds(pl.multiple_of((2 * x + c) * 256, 256), 256)

    @pl.loop(0, 4)
    def _(i):
        mt = cols(i, 256)
        g_v[4, mt, :] = (mm_tn(gated[:, mt], hid[:, hv]) + mm_tn(p_gated[:, mt], p_hid[:, hv])).astype(BF)

    slot(13)

    x_gp.wait()
    gpb = gp_acc[own, :] + gp_r[...]
    po = probs[own, :]
    gsc = (po * (gpb - jnp.sum(gpb * po, axis=-1, keepdims=True))).astype(BF)
    gq = mm(gsc, klow[own, :]) * scale
    gk = mm_tn(gsc, qlow[own, :]) * scale
    psh = pre_sh[own, :]
    sgs = sigm(psh)
    sh = psh * sgs
    small[336:337, :] = jnp.sum(gq * sh, axis=0, keepdims=True)
    small[337:338, :] = jnp.sum(gk * sh, axis=0, keepdims=True)
    small[338:339, :] = jnp.sum(gq, axis=0, keepdims=True)
    small[339:340, :] = jnp.sum(gk, axis=0, keepdims=True)
    small[340:341, :] = jnp.sum(skew(gsc.astype(F32).T, True), axis=0, keepdims=True)
    small[341:352, :] = jnp.zeros((11, 128), F32)
    gps[own, :] = ((gq * qkg[0:1, :] + gk * qkg[1:2, :]) * slope_of(psh, sgs)).astype(BF)
    x_gps = xcopy(11, gps.at[own], gps.at[own])
    x_gps.start()
    x_nb.start()
    slot(14)
    c_mixed.wait()
    c_upd.wait()

    la = mlow[:, q4]
    lb = p_mixed[:, q4]
    for j in range(2):
        nn = slice(j * P2, (j + 1) * P2)
        g_v[5, j * 256 : j * 256 + 256, :] = (mm_tn(la, hid[:, nn]) + mm_tn(lb, p_hid[:, nn])).astype(BF)
        g_v[5, 512 + j * 256 : 768 + j * 256, :] = (mm_tn(la, upd[:, nn]) + mm_tn(lb, p_upd[:, nn])).astype(BF)

    slot(15)

    @pl.loop(0, D // T)
    def _(i):
        cc = cols(i, T)
        own_f[:, cc] = (
            mm_nt(gpr[own, :], wr[cc, :])
            + mm_nt(gps[own, :], wsh[cc, :])
            + mm_nt(hid[own, :], wh[cc, :])
            + mm_nt(upd[own, :], wu[cc, :])
        )
        nb_o[:, cc] = mm_nt(gpv[own, :], wv[cc, :])

    slot(16)
    x_gps.wait()
    c_gps = ccopy(11, gps, p_gps)
    c_gps.start()
    c_gpr.wait()

    @pl.loop(0, 4)
    def _(i):
        mt = cols(i, 256)
        g_v[6, mt, :] = (mm_tn(mlow[:, mt], gpr[:, hv]) + mm_tn(p_mixed[:, mt], p_gpr[...])).astype(BF)

    slot(17)
    c_normed.wait()
    c_gpv.wait()

    @pl.loop(0, 4)
    def _(i):
        mt = cols(i, 256)
        g_v[7, mt, :] = (mm_tn(nlow[:, mt], gpv[:, hv]) + mm_tn(p_normed[:, mt], p_gpv[...])).astype(BF)

    c_gps.wait()
    s_own[88:344, :] = mm_tn(mlow[:, q4], gps[...]) + mm_tn(p_mixed[:, q4], p_gps[...])
    slot(18)
    x_mb.wait()
    x_ffn.start()

    acc[...] = jnp.zeros_like(acc)

    @pl.loop(0, H // 16)
    def _(t):
        rr = cols(t, 16)
        ro = pl.ds(pl.multiple_of(x * H + t * 16, 16), 16)
        pre = pre_ema[ro, :]
        g = (own_f[rr, :] + mb_r[rr, :].astype(F32)) * slope_of(pre, sigm(pre))
        own_f[rr, :] = g
        add_rows(0, g * normed[ro, :])
        for j in range(8):
            gs[pl.ds(t * 128 + j, 16, stride=8), :] = g[:, j * 128 : (j + 1) * 128]

    put_small(256, 0)
    slot(19)

    def back(p_, cy):
        p = H - 1 - p_
        at = cols(p, 8)
        po_ = x * H + p
        mu = gs[at, :] + cy
        gxs[at, :] = jnp.sum(coef(w_s) * mu, axis=0) * live[pl.ds(po_, 1), :]
        return coef(a_s) * (mu * keep[pl.ds(po_, 1), :])

    x_carry = xcopy(12, carry, carry_r)

    @pl.when(x == 1)
    def _():
        cy = lax.fori_loop(0, H, back, zeros)
        carry[...] = cy.reshape(N * 8, 128)
        x_carry.start()

    slot(20)
    for q in range(2):
        nq = slice(q * 64, q * 64 + 64)

        def fwd(p, state, nq=nq):
            s, r, gw, gr = state
            at = cols(p, 8)
            po_ = x * H + p
            k = keep[pl.ds(po_, 1), :]
            xr = xs[cols(po_, 8), :] * live[pl.ds(po_, 1), :]
            a = a_s[nq, :].reshape(8, 8, 128)
            sk = s * k
            r = a * (r * k) + sk
            s = a * sk + xr
            g = gs[at, :]
            return s, r, gw + g * s, gr + g * r

        z8 = jnp.zeros((8, 8, 128), F32)
        s0 = snap_s[nq, :].reshape(8, 8, 128)
        r0 = snap_r[nq, :].reshape(8, 8, 128)
        _, _, gw, gr = lax.fori_loop(0, H, fwd, (s0, r0, z8, z8))
        small[nq, :] = gw.reshape(64, 128)
        small[128 + q * 64 : 192 + q * 64, :] = gr.reshape(64, 128) * w_s[nq, :]
        slot(21 + q)

    @pl.when(x == 0)
    def _():
        x_carry.wait_recv()
        lax.fori_loop(0, H, back, coef(carry_r))

    @pl.when(x == 1)
    def _():
        x_carry.wait_send()

    slot(23)
    x_nb.wait()

    @pl.loop(0, H // 16)
    def _(t):
        rr = cols(t, 16)
        ro = pl.ds(pl.multiple_of(x * H + t * 16, 16), 16)
        gx = jnp.concatenate([gxs[pl.ds(t * 128 + j, 16, stride=8), :] for j in range(8)], axis=1)
        g = nb_o[rr, :] + nb_r[rr, :].astype(F32) + vec[2:3, :] * own_f[rr, :] + gx
        cen, rstd = norm_rows(tok[ro, :].astype(F32))
        xh = cen * rstd
        add_rows(1, g * xh)
        add_rows(2, g)
        gy = g * vec[0:1, :]
        gb = rstd * (gy - jnp.mean(gy, axis=-1, keepdims=True) - xh * jnp.mean(gy * xh, axis=-1, keepdims=True))
        gt[rr, :] = gres[rr, :] + gb

    put_small(256 + 8, 1)
    put_small(256 + 16, 2)

    slot(24)

    x_ffn.wait()

    @pl.loop(0, H // 16)
    def _(t):
        rr = cols(t, 16)
        bo[rr, :] = (blend[rr, :] + (ffn_o[rr, :] + ffn_r[rr, :].astype(F32))).astype(BF)

    slot(25)
    finish()

def vm(shape, dtype=F32):
    return pltpu.VMEM(shape, dtype)


SEMS = 440


def run_main(tokens, cotangent, seq_lengths, bucket_map, norm1_gain, norm1_bias, ema_rate, ema_damp, ema_in, ema_out,
             ema_skip, w_shared, qk_gain, qk_bias, rel_bias, w_value, w_reset, w_mix, w_hidden, w_update, b_update,
             norm2_gain, norm2_bias, w_up, b_up, w_down):
    H = tokens.shape[0]
    R = 2 * H
    D = tokens.shape[1]
    VL = w_value.shape[1]
    FL = w_up.shape[1]
    Z = w_shared.shape[1]
    rows8 = [v.reshape(8, D // 8) for v in (norm1_gain, norm1_bias, ema_skip, b_update, norm2_gain, norm2_bias)]
    anyspec = pl.BlockSpec(memory_space=pl.ANY)
    vspec = pl.BlockSpec(memory_space=pltpu.VMEM)
    sspec = pl.BlockSpec(memory_space=pltpu.SMEM)
    P2 = D // 2
    outs = (
        jax.ShapeDtypeStruct((H, D), BF),
        jax.ShapeDtypeStruct((H, D), F32),
        jax.ShapeDtypeStruct((2, 7, D, P2), BF),
        jax.ShapeDtypeStruct((4, D, P2), BF),
        jax.ShapeDtypeStruct((D, Z), F32),
        jax.ShapeDtypeStruct((352, 128), F32),
    )
    dma = pltpu.SemaphoreType.DMA
    scratch = [
        vm((D, Z), BF), vm((D, VL), BF), vm((D, VL), BF), vm((VL, D), BF), vm((D, D), BF), vm((D, D), BF), vm((FL // P2, D, P2), BF), vm((2, FL, P2), BF),
        vm((R, D), BF), vm((R, D), BF), vm((R, D)), vm((R, D), BF), vm((R, D), BF), vm((R, D)), vm((R * 8, 128)), vm((R * 8, 128)),
        vm((R, Z)), vm((R, Z), BF), vm((R, Z), BF), vm((R, BLOCK)), vm((R, BLOCK), BF),
        vm((R, VL)), vm((R, VL)), vm((R, VL)), vm((R, VL), BF), vm((R, VL), BF), vm((H, D), BF), vm((H, D), BF), vm((H, D)), vm((H, D)), vm((H, D)), vm((H, D)), vm((R, D), BF),
        vm((R, FL)), vm((R, FL), BF), vm((R, FL), BF), vm((H, D), BF), vm((H, D), BF), vm((H, D), BF), vm((R, D), BF), vm((R, D), BF), vm((R, VL), BF), vm((R, VL), BF), vm((R, BLOCK)), vm((H, BLOCK)), vm((R, Z), BF),
        vm((H, D), BF), vm((H, D), BF), vm((H, D), BF),
        vm((R, D), BF), vm((R, D), BF), vm((R, D), BF), vm((R, FL // 2), BF), vm((R, D), BF), vm((R, FL // 2), BF), vm((R, VL), BF), vm((R, D), BF), vm((R, D), BF), vm((R, VL // 2), BF), vm((R, VL // 2), BF), vm((R, Z), BF),
        vm((128, 128)), vm((128, 128)), vm((128, 128)), vm((128, 128)), vm((128, 128)), vm((128, 128)), vm((24, D)), vm((R, 128)), vm((R, 128)), vm((R, 128)), vm((8, D)), vm((8, FL)),
        vm((8, D, P2), BF), vm((1, 11 * 256, P2), BF), vm((352, 128)), vm((3, 88, 128)), vm((344, 128)), vm((344, 128)), vm((NZ - 1, 344, 128)),
        dma((14,)), dma((23,)), dma((23,)), dma((12,)), dma((12,)), dma((96,)), dma((SEMS,)), dma((SEMS,)), pltpu.SemaphoreType.REGULAR((3,)),
    ]
    return pl.pallas_call(
        main_kernel,
        out_shape=outs,
        in_specs=[anyspec] * 10 + [sspec, sspec] + [vspec] * 14,
        out_specs=(vspec, vspec) + (anyspec,) * 2 + (vspec, vspec),
        scratch_shapes=scratch,
        compiler_params=pltpu.CompilerParams(collective_id=0, has_side_effects=True, vmem_limit_bytes=63 * 1024 * 1024),
        cost_estimate=pl.CostEstimate(flops=15_000_000_000, bytes_accessed=40_000_000, transcendentals=0),
    )(
        tokens, cotangent, w_shared, w_value, w_reset, w_mix, w_hidden, w_update, w_up, w_down,
        seq_lengths, rel_bias.reshape(1, -1), bucket_map.reshape(1, -1), *rows8, ema_rate, ema_damp, ema_in, ema_out,
        qk_gain, qk_bias, b_up.reshape(-1, 128),
    )


def finish_kernel(every, hu, bo, gt, shared, small, rate, damp, ein, eout, bmap,
                  f_down, f_up, f_mix, f_reset, f_value, f_hid, f_upd, f_bo, f_gt, f_shared,
                  g_rate, g_damp, g_in, g_out, v0, v1, v2, v3, v4, v5, g_bup, g_gain, g_bias, g_rel,
                  b_every, b_hu, b_bo, b_gt, b_shared, stage, isem, osem, psem):
    rows_in = [pltpu.make_async_copy(a, b, psem.at[k]) for k, (a, b) in enumerate(((bo, b_bo), (gt, b_gt), (shared, b_shared)))]
    passed = [pltpu.make_async_copy(a, b, psem.at[3 + k]) for k, (a, b) in enumerate(((b_bo, f_bo), (b_gt, f_gt), (b_shared, f_shared)))]
    CR, CC = stage.shape[1], stage.shape[2]
    half = CC // 2
    chunks = []

    def gather(sources, dst):
        chunks.append(([(a, b, slice(j * half, (j + 1) * half)) for j, (a, b) in enumerate(sources)], dst))

    def piece(core, i, r):
        at = (core, i, slice(r * CR, (r + 1) * CR))
        return every.at[at], b_every.at[at]

    def quarter(q, n):
        at = (q, slice(n * CR, (n + 1) * CR))
        return hu.at[at], b_hu.at[at]

    for core in range(2):
        for r in range(4):
            gather([piece(core, 0, r), piece(core, 1, r)], f_down.at[core * 4 * CR + r * CR : core * 4 * CR + (r + 1) * CR])
            gather([piece(core, 2, r), piece(core, 3, r)], f_up.at[r * CR : (r + 1) * CR, core * CC : (core + 1) * CC])
    for i, dst in ((4, f_mix), (5, f_reset), (6, f_value)):
        for r in range(4):
            gather([piece(0, i, r), piece(1, i, r)], dst.at[r * CR : (r + 1) * CR])
    for n, dst in ((0, f_hid), (2, f_upd)):
        for q in range(4):
            gather([quarter(q, n), quarter(q, n + 1)], dst.at[q * CR : (q + 1) * CR])
    ins, count = [], 0
    for parts, _ in chunks:
        ins.append([])
        for src, buf, _ in parts:
            copy = pltpu.make_async_copy(src, buf, isem.at[count])
            copy.start()
            ins[-1].append(copy)
            count += 1
    for copy in rows_in:
        copy.start()

    for t in range(2):
        for j in range(8):
            rows_ = slice(t * 8, t * 8 + 8)
            lanes = slice(j * 128, j * 128 + 128)
            gw = small[pl.ds(t * 64 + j, 8, stride=8), :]
            ga = small[pl.ds(128 + t * 64 + j, 8, stride=8), :]
            r_, d_ = rate[rows_, lanes], damp[rows_, lanes]
            i_, o_ = ein[rows_, lanes], eout[rows_, lanes]
            g_rate[rows_, lanes] = gw * (i_ * o_) - ga * d_
            g_damp[rows_, lanes] = -ga * r_
            g_in[rows_, lanes] = gw * (r_ * o_)
            g_out[rows_, lanes] = gw * (r_ * i_)
    for k, ref in enumerate((v0, v1, v2, v3, v4, v5)):
        ref[...] = small[256 + 8 * k : 264 + 8 * k, :]
    me = lax.axis_index("narrow")
    g_bup[...] = small[pl.ds(pl.multiple_of(304 + me * 16, 8), 16), :]
    g_gain[...] = small[336:338, :]
    g_bias[...] = small[338:340, :]
    n = bmap.shape[1]
    offs = jnp.broadcast_to(small[340:341, :], (n, n)).T
    which = jnp.broadcast_to(bmap[...].astype(F32), (n, n)).T
    lane = lax.broadcasted_iota(jnp.int32, (n, n), 1).astype(F32)
    hits = jnp.sum(jnp.where(which == lane, offs, 0.0), axis=0, keepdims=True)
    g_rel[...] = hits[:, 0 : g_rel.shape[1]]

    ring = stage.shape[0]
    outs = []
    for k, (parts, dst) in enumerate(chunks):
        if k >= ring:
            outs[k - ring].wait()
        for copy, (_, buf, at) in zip(ins[k], parts):
            copy.wait()

            @pl.loop(0, CR // 64)
            def _(t, buf=buf, at=at, k=k):
                rr = cols(t, 64)
                stage[k % ring, rr, at] = buf[rr, :].astype(F32)

        copy = pltpu.make_async_copy(stage.at[k % ring], dst, osem.at[k % ring])
        copy.start()
        outs.append(copy)
    for a, b in zip(rows_in, passed):
        a.wait()
        b.start()
    for copy in outs[len(chunks) - ring :] + passed:
        copy.wait()


def run_finish(every, hu, whole, shapes, small, rate, damp, ein, eout, bucket_map, nbuck):
    bmap = bucket_map.reshape(1, -1)
    D = rate.shape[1]
    square = jax.ShapeDtypeStruct((D, D), F32)
    outs = [jax.ShapeDtypeStruct(a.shape, F32) for a in shapes] + [square, square]
    outs += [jax.ShapeDtypeStruct(a.shape, a.dtype) for a in whole]
    kept = len(outs)
    outs += [jax.ShapeDtypeStruct(rate.shape, F32) for _ in range(4)]
    outs += [jax.ShapeDtypeStruct((8, 128), F32) for _ in range(6)]
    outs += [jax.ShapeDtypeStruct((16, 128), F32), jax.ShapeDtypeStruct((2, 128), F32), jax.ShapeDtypeStruct((2, 128), F32),
             jax.ShapeDtypeStruct((1, nbuck), F32)]
    anyspec = pl.BlockSpec(memory_space=pl.ANY)
    vspec = pl.BlockSpec(memory_space=pltpu.VMEM)
    dma = pltpu.SemaphoreType.DMA
    ring = 14
    res = pl.pallas_call(
        finish_kernel,
        out_shape=tuple(outs),
        in_specs=[anyspec] * 5 + [vspec] * 6,
        out_specs=tuple([anyspec] * kept + [vspec] * (len(outs) - kept)),
        scratch_shapes=[vm(every.shape, BF), vm(hu.shape, BF)] + [vm(a.shape, a.dtype) for a in whole] + [vm((ring, D // 4, D)), dma((72,)), dma((ring,)), dma((6,))],
        compiler_params=pltpu.CompilerParams(vmem_limit_bytes=60 * 1024 * 1024),
    )(every, hu, *whole, small, rate, damp, ein, eout, bmap)
    return res


def shards_fast(*args):
    bo, gt, every, hu, shared, small = run_main(*args)
    w_value, w_reset, w_mix = args[15:18]
    w_up, w_down = args[23], args[25]
    (tokens, cotangent, seq_lengths, bucket_map, norm1_gain, norm1_bias, ema_rate, ema_damp, ema_in, ema_out,
     ema_skip, w_shared, qk_gain, qk_bias, rel_bias) = args[:15]
    (down, up, mix, reset, value, hidden, update, bo, gt, shared, g_rate, g_damp, g_in, g_out, skip, n1g, n1b, bupd, n2g, n2b,
     g_bup, g_gain, g_bias, g_rel) = run_finish(
        every, hu, (bo, gt, shared), (w_down, w_up, w_mix, w_reset, w_value), small, ema_rate, ema_damp, ema_in, ema_out, bucket_map,
        rel_bias.shape[0])
    skip, n1g, n1b, bupd, n2g, n2b = [v.reshape(-1) for v in (skip, n1g, n1b, bupd, n2g, n2b)]
    return (bo, gt, n1g, n1b, g_rate, g_damp, g_in, g_out, skip, shared, g_gain, g_bias, g_rel.reshape(-1),
            value, reset, mix, hidden, update, bupd, n2g, n2b, up, g_bup.reshape(-1), down)


def solution(mesh):
    in_specs = (
        P(("wide", "narrow"), None),
        P(("wide", "narrow"), None),
        P("wide", None),
        P(),
        P(),
        P(),
        P(),
        P(),
        P(),
        P(),
        P(),
        P(),
        P(),
        P(),
        P(),
        P(None, "narrow"),
        P(None, "narrow"),
        P("narrow", None),
        P(),
        P(),
        P(),
        P(),
        P(),
        P(None, "narrow"),
        P("narrow"),
        P("narrow", None),
    )
    out_specs = (
        P(("wide", "narrow"), None),
        P(("wide", "narrow"), None),
        P(),
        P(),
        P(),
        P(),
        P(),
        P(),
        P(),
        P(),
        P(),
        P(),
        P(),
        P(None, "narrow"),
        P(None, "narrow"),
        P("narrow", None),
        P(),
        P(),
        P(),
        P(),
        P(),
        P(None, "narrow"),
        P("narrow"),
        P("narrow", None),
    )
    body = shards_fast if (mesh.shape["wide"], mesh.shape["narrow"]) == (16, 2) else shards
    return jax.shard_map(body, mesh=mesh, in_specs=in_specs, out_specs=out_specs, check_vma=False)
```

```python
import jax
import jax.numpy as jnp
from jax import lax
from jax.experimental import pallas as pl
from jax.experimental.pallas import tpu as pltpu
from jax.sharding import PartitionSpec as P

BLOCK = 128


EPSILON = 1e-05
NEGATIVE = -1000000000.0


def carried_in(part, axis, combine, identity, reverse):
    count = lax.axis_size(axis)
    place = lax.axis_index(axis)
    ahead = count - 1 - place if reverse else place
    gathered = jax.tree.map(lambda a: lax.all_gather(a, axis), part)
    state = jax.tree.map(lambda a, e: jnp.zeros_like(a) + jnp.asarray(e, a.dtype), part, identity)

    def one(lap, state):
        source = count - 1 - lap if reverse else lap
        return combine(
            state, jax.tree.map(lambda a: lax.dynamic_index_in_dim(a, source, 0, False), gathered)
        )

    return lax.fori_loop(0, ahead, one, state)


def layer_norm(rows_in, gain, shift):
    row_mean = jnp.mean(rows_in, axis=-1, keepdims=True)
    centred = rows_in - row_mean
    row_var = jnp.mean(centred * centred, axis=-1, keepdims=True)
    return centred * lax.rsqrt(row_var + EPSILON) * gain + shift


def silu_slope(pre_act):
    sigmoid_val = jax.nn.sigmoid(pre_act)
    return sigmoid_val * (1.0 + pre_act * (1.0 - sigmoid_val))


def segment_info(lengths, positions):
    first_end = lengths[0]
    second_end = lengths[0] + lengths[1]
    segment = (positions >= first_end).astype(jnp.int32) + (positions >= second_end).astype(
        jnp.int32
    )
    starts = ((positions == 0) | (positions == first_end) | (positions == second_end)).astype(
        jnp.float32
    )
    live_rows = (segment < 2).astype(jnp.float32)
    return (segment, starts, live_rows)


def combine_pair(earlier, following):
    return (earlier[0] * following[0], earlier[1] * following[0] + following[1])


def ema_local(normed, live_rows, starts, ema_rate, ema_damp, ema_in, ema_out, ema_skip, state_in):
    inputs = normed * live_rows[:, None]
    keep_rate = 1.0 - ema_rate * ema_damp
    drive_rate = ema_rate * ema_in
    decay = keep_rate[None] * (1.0 - starts)[:, None, None]
    drive = drive_rate[None] * inputs[:, None, :]
    decay_cum, partial_state = lax.associative_scan(combine_pair, (decay, drive), axis=0)
    states = partial_state + decay_cum * state_in[None]
    smooth = jnp.sum(states * ema_out[None], axis=1)
    ema_mixed = jax.nn.silu(smooth + ema_skip * normed)
    return (ema_mixed, states[-1])


def block_bias(rel_bias, bucket_map):
    by_offset = jnp.take(rel_bias, bucket_map)
    row_index = jnp.arange(BLOCK, dtype=jnp.int32)
    offsets = row_index[:, None] - row_index[None, :]
    return (jnp.take(by_offset, jnp.clip(offsets, 0, BLOCK - 1)), offsets)


def attention_probs(query_all, key_all, segment_all, bias_table, offsets):
    blocks = query_all.shape[0] // BLOCK
    query_blocks = query_all.reshape(blocks, BLOCK, -1)
    key_blocks = key_all.reshape(blocks, BLOCK, -1)
    seg_blocks = segment_all.reshape(blocks, BLOCK)
    allowed = (seg_blocks[:, :, None] == seg_blocks[:, None, :]) & (offsets >= 0)[None]
    score_scale = query_all.shape[-1] ** (-0.5)
    scores = (
        jnp.einsum("bik,bjk->bij", query_blocks, key_blocks, preferred_element_type=jnp.float32)
        * score_scale
    )
    scores = jnp.where(allowed, scores + bias_table[None], NEGATIVE)
    row_max = jnp.max(scores, axis=-1, keepdims=True)
    weighted = jnp.exp(scores - row_max)
    return weighted / jnp.sum(weighted, axis=-1, keepdims=True)


def shards(
    tokens,
    cotangent,
    seq_lengths,
    bucket_map,
    norm1_gain,
    norm1_bias,
    ema_rate,
    ema_damp,
    ema_in,
    ema_out,
    ema_skip,
    w_shared,
    qk_gain,
    qk_bias,
    rel_bias,
    w_value,
    w_reset,
    w_mix,
    w_hidden,
    w_update,
    b_update,
    norm2_gain,
    norm2_bias,
    w_up,
    b_up,
    w_down,
):
    row_count = tokens.shape[0]
    narrow_count = lax.axis_size("narrow")
    narrow_rank = lax.axis_index("narrow")
    group_rows = row_count * narrow_count
    blocks = group_rows // BLOCK
    local_blocks = row_count // BLOCK
    lengths = seq_lengths[0]
    local_positions = narrow_rank * row_count + jnp.arange(row_count, dtype=jnp.int32)
    segment_local, starts, live_rows = segment_info(lengths, local_positions)
    segment_all = segment_info(lengths, jnp.arange(group_rows, dtype=jnp.int32))[0]
    tokens_f = tokens.astype(jnp.float32)
    normed, norm1_back = jax.vjp(layer_norm, tokens_f, norm1_gain, norm1_bias)

    def ema_apply(normed_in, rate_in, damp_in, in_weight, out_weight, skip_in, state_in):
        return ema_local(
            normed_in, live_rows, starts, rate_in, damp_in, in_weight, out_weight, skip_in, state_in
        )

    zero_state = jnp.zeros_like(ema_rate)
    ones_state = jnp.ones_like(ema_rate)
    local_final = ema_apply(normed, ema_rate, ema_damp, ema_in, ema_out, ema_skip, zero_state)[1]
    through = jnp.power(1.0 - ema_rate * ema_damp, row_count) * (1.0 - jnp.max(starts))
    state_in = carried_in(
        (through, local_final), "narrow", combine_pair, (ones_state, zero_state), False
    )[1]
    (ema_mixed, final_state), ema_back = jax.vjp(
        ema_apply, normed, ema_rate, ema_damp, ema_in, ema_out, ema_skip, state_in
    )
    normed_low = normed.astype(jnp.bfloat16)
    mixed_low = ema_mixed.astype(jnp.bfloat16)
    pre_shared = jnp.dot(mixed_low, w_shared, preferred_element_type=jnp.float32)
    shared_act = jax.nn.silu(pre_shared)
    query_low = (shared_act * qk_gain[0] + qk_bias[0]).astype(jnp.bfloat16)
    key_low = (shared_act * qk_gain[1] + qk_bias[1]).astype(jnp.bfloat16)
    normed_all, mixed_all, query_all, key_all = (
        lax.all_gather(normed_low, "narrow", axis=0, tiled=True),
        lax.all_gather(mixed_low, "narrow", axis=0, tiled=True),
        lax.all_gather(query_low, "narrow", axis=0, tiled=True),
        lax.all_gather(key_low, "narrow", axis=0, tiled=True),
    )
    bias_table, offsets = block_bias(rel_bias, bucket_map)
    probs_low = attention_probs(query_all, key_all, segment_all, bias_table, offsets).astype(
        jnp.bfloat16
    )
    pre_value = jnp.dot(normed_all, w_value, preferred_element_type=jnp.float32)
    value_low = jax.nn.silu(pre_value).astype(jnp.bfloat16)
    value_blocks = value_low.reshape(blocks, BLOCK, -1)
    pre_reset = jnp.dot(mixed_all, w_reset, preferred_element_type=jnp.float32)
    reset_gate = jax.nn.silu(pre_reset)
    attended = jnp.einsum(
        "bij,bjv->biv", probs_low, value_blocks, preferred_element_type=jnp.float32
    ).reshape(group_rows, -1)
    gated_low = (reset_gate * attended).astype(jnp.bfloat16)
    piece = gated_low
    mix_part = lax.psum_scatter(
        jnp.dot(piece, w_mix, preferred_element_type=jnp.float32),
        "narrow",
        scatter_dimension=0,
        tiled=True,
    )
    pre_hidden = jnp.dot(mixed_low, w_hidden, preferred_element_type=jnp.float32) + mix_part
    hidden_act = jax.nn.silu(pre_hidden)
    pre_update = jnp.dot(mixed_low, w_update, preferred_element_type=jnp.float32) + b_update
    update_gate = jax.nn.sigmoid(pre_update)
    blended = update_gate * hidden_act + (1.0 - update_gate) * tokens_f
    normed2, norm2_back = jax.vjp(layer_norm, blended, norm2_gain, norm2_bias)
    normed2_low = normed2.astype(jnp.bfloat16)
    grad_out = cotangent.astype(jnp.float32) * live_rows[:, None]
    grad_out_low = grad_out.astype(jnp.bfloat16)
    normed2_all = lax.all_gather(normed2_low, "narrow", axis=0, tiled=True)
    pre_up = jnp.dot(normed2_all, w_up, preferred_element_type=jnp.float32) + b_up.astype(
        jnp.float32
    )
    up_low = jax.nn.silu(pre_up).astype(jnp.bfloat16)
    piece = up_low
    ffn_out = lax.psum_scatter(
        jnp.dot(piece, w_down, preferred_element_type=jnp.float32),
        "narrow",
        scatter_dimension=0,
        tiled=True,
    )
    grad_out_all = lax.all_gather(grad_out_low, "narrow", axis=0, tiled=True)
    grad_up = jnp.einsum("sd,fd->sf", grad_out_all, w_down, preferred_element_type=jnp.float32)
    grad_pre_up = (grad_up * silu_slope(pre_up)).astype(jnp.bfloat16)
    grad_w_down = jnp.einsum("sf,sd->fd", up_low, grad_out_all, preferred_element_type=jnp.float32)
    grad_w_up = jnp.einsum(
        "sd,sf->df", normed2_all, grad_pre_up, preferred_element_type=jnp.float32
    )
    grad_b_up = jnp.sum(grad_pre_up.astype(jnp.float32), axis=0)
    piece = grad_pre_up
    grad_normed2 = lax.psum_scatter(
        jnp.einsum("sf,df->sd", piece, w_up, preferred_element_type=jnp.float32),
        "narrow",
        scatter_dimension=0,
        tiled=True,
    )
    block_out = (blended + ffn_out).astype(jnp.bfloat16)
    grad_blended_norm, grad_norm2_gain, grad_norm2_bias = norm2_back(grad_normed2)
    grad_blended = grad_out + grad_blended_norm
    grad_hidden = grad_blended * update_gate
    grad_gate = grad_blended * (hidden_act - tokens_f)
    grad_tokens = grad_blended * (1.0 - update_gate)
    grad_pre_update = (grad_gate * update_gate * (1.0 - update_gate)).astype(jnp.bfloat16)
    grad_pre_hidden = (grad_hidden * silu_slope(pre_hidden)).astype(jnp.bfloat16)
    grad_b_update = jnp.sum(grad_pre_update.astype(jnp.float32), axis=0)
    grad_w_update = jnp.einsum(
        "sd,se->de", mixed_low, grad_pre_update, preferred_element_type=jnp.float32
    )
    grad_w_hidden = jnp.einsum(
        "sd,se->de", mixed_low, grad_pre_hidden, preferred_element_type=jnp.float32
    )
    hidden_all = lax.all_gather(grad_pre_hidden, "narrow", axis=0, tiled=True)
    grad_w_mix = jnp.einsum("sv,sd->vd", gated_low, hidden_all, preferred_element_type=jnp.float32)
    grad_gated = jnp.einsum("sd,vd->sv", hidden_all, w_mix, preferred_element_type=jnp.float32)
    grad_reset = grad_gated * attended
    grad_attended = (grad_gated * reset_gate).astype(jnp.bfloat16)
    grad_pre_reset = (grad_reset * silu_slope(pre_reset)).astype(jnp.bfloat16)
    grad_w_reset = jnp.einsum(
        "sd,sv->dv", mixed_all, grad_pre_reset, preferred_element_type=jnp.float32
    )
    attended_blocks = grad_attended.reshape(blocks, BLOCK, -1)
    probs_again = attention_probs(query_all, key_all, segment_all, bias_table, offsets)
    grad_probs = jnp.einsum(
        "biv,bjv->bij", attended_blocks, value_blocks, preferred_element_type=jnp.float32
    )
    grad_value = jnp.einsum(
        "bij,biv->bjv",
        probs_again.astype(jnp.bfloat16),
        attended_blocks,
        preferred_element_type=jnp.float32,
    ).reshape(group_rows, -1)
    grad_pre_value = (grad_value * silu_slope(pre_value)).astype(jnp.bfloat16)
    grad_w_value = jnp.einsum(
        "sd,sv->dv", normed_all, grad_pre_value, preferred_element_type=jnp.float32
    )
    mixed_cols = jnp.einsum(
        "sv,dv->sd", grad_pre_reset, w_reset, preferred_element_type=jnp.float32
    )
    normed_cols = jnp.einsum(
        "sv,dv->sd", grad_pre_value, w_value, preferred_element_type=jnp.float32
    )
    probs_rows, mixed_back, normed_back = (
        lax.psum_scatter(
            grad_probs.reshape(group_rows, BLOCK), "narrow", scatter_dimension=0, tiled=True
        ),
        lax.psum_scatter(mixed_cols, "narrow", scatter_dimension=0, tiled=True),
        lax.psum_scatter(normed_cols, "narrow", scatter_dimension=0, tiled=True),
    )
    probs_local = lax.dynamic_slice_in_dim(probs_again, narrow_rank * local_blocks, local_blocks, 0)
    grad_probs_local = probs_rows.reshape(local_blocks, BLOCK, BLOCK)
    grad_scores = probs_local * (
        grad_probs_local - jnp.sum(grad_probs_local * probs_local, axis=-1, keepdims=True)
    )
    grad_scores_low = grad_scores.astype(jnp.bfloat16)
    score_scale = query_low.shape[-1] ** (-0.5)
    query_blocks = query_low.reshape(local_blocks, BLOCK, -1)
    key_blocks = key_low.reshape(local_blocks, BLOCK, -1)
    grad_query = (
        jnp.einsum(
            "bij,bjk->bik", grad_scores_low, key_blocks, preferred_element_type=jnp.float32
        ).reshape(row_count, -1)
        * score_scale
    )
    grad_key = (
        jnp.einsum(
            "bij,bik->bjk", grad_scores_low, query_blocks, preferred_element_type=jnp.float32
        ).reshape(row_count, -1)
        * score_scale
    )
    score_total = jnp.sum(grad_scores_low.astype(jnp.float32), axis=0)
    offset_hits = (offsets[:, :, None] == jnp.arange(BLOCK, dtype=jnp.int32)[None, None, :]).astype(
        jnp.float32
    )
    grad_offset = jnp.sum(score_total[:, :, None] * offset_hits, axis=(0, 1))
    bucket_hits = (
        bucket_map[:, None] == jnp.arange(rel_bias.shape[0], dtype=jnp.int32)[None, :]
    ).astype(jnp.float32)
    grad_rel_bias = jnp.sum(grad_offset[:, None] * bucket_hits, axis=0)
    grad_shared_act = grad_query * qk_gain[0] + grad_key * qk_gain[1]
    grad_qk_gain = jnp.stack(
        [jnp.sum(grad_query * shared_act, axis=0), jnp.sum(grad_key * shared_act, axis=0)]
    )
    grad_qk_bias = jnp.stack([jnp.sum(grad_query, axis=0), jnp.sum(grad_key, axis=0)])
    grad_pre_shared = (grad_shared_act * silu_slope(pre_shared)).astype(jnp.bfloat16)
    grad_w_shared = jnp.einsum(
        "sd,sz->dz", mixed_low, grad_pre_shared, preferred_element_type=jnp.float32
    )
    grad_mixed = (
        mixed_back
        + jnp.einsum("sz,dz->sd", grad_pre_shared, w_shared, preferred_element_type=jnp.float32)
        + jnp.einsum("se,de->sd", grad_pre_hidden, w_hidden, preferred_element_type=jnp.float32)
        + jnp.einsum("se,de->sd", grad_pre_update, w_update, preferred_element_type=jnp.float32)
    )
    direct = ema_back((grad_mixed, zero_state))
    later_state = carried_in(
        (through, direct[6]), "narrow", combine_pair, (ones_state, zero_state), True
    )[1]
    chained = ema_back((jnp.zeros_like(ema_mixed), later_state))
    grad_normed = normed_back + direct[0] + chained[0]
    grad_tokens_norm, grad_norm1_gain, grad_norm1_bias = norm1_back(grad_normed)
    grad_tokens = grad_tokens + grad_tokens_norm
    grad_ema_rate = direct[1] + chained[1]
    grad_ema_damp = direct[2] + chained[2]
    grad_ema_in = direct[3] + chained[3]
    grad_ema_out = direct[4] + chained[4]
    grad_ema_skip = direct[5] + chained[5]
    grad_w_value, grad_w_reset, grad_w_mix, grad_w_up, grad_b_up, grad_w_down = lax.psum(
        (grad_w_value, grad_w_reset, grad_w_mix, grad_w_up, grad_b_up, grad_w_down), "wide"
    )
    (
        grad_norm1_gain,
        grad_norm1_bias,
        grad_ema_rate,
        grad_ema_damp,
        grad_ema_in,
        grad_ema_out,
        grad_ema_skip,
        grad_w_shared,
        grad_qk_gain,
        grad_qk_bias,
        grad_rel_bias,
        grad_w_hidden,
        grad_w_update,
        grad_b_update,
        grad_norm2_gain,
        grad_norm2_bias,
    ) = lax.psum(
        (
            grad_norm1_gain,
            grad_norm1_bias,
            grad_ema_rate,
            grad_ema_damp,
            grad_ema_in,
            grad_ema_out,
            grad_ema_skip,
            grad_w_shared,
            grad_qk_gain,
            grad_qk_bias,
            grad_rel_bias,
            grad_w_hidden,
            grad_w_update,
            grad_b_update,
            grad_norm2_gain,
            grad_norm2_bias,
        ),
        ("wide", "narrow"),
    )
    return (
        block_out,
        grad_tokens,
        grad_norm1_gain,
        grad_norm1_bias,
        grad_ema_rate,
        grad_ema_damp,
        grad_ema_in,
        grad_ema_out,
        grad_ema_skip,
        grad_w_shared,
        grad_qk_gain,
        grad_qk_bias,
        grad_rel_bias,
        grad_w_value,
        grad_w_reset,
        grad_w_mix,
        grad_w_hidden,
        grad_w_update,
        grad_b_update,
        grad_norm2_gain,
        grad_norm2_bias,
        grad_w_up,
        grad_b_up,
        grad_w_down,
    )


NZ = 4
ROOT = 1
NEAR = (0, 2, 3)
EVEN, ENDS = (0, 1, 2, 3), (0, 3, 0, 3)
MIXED = (0, 3, 1, 2)
UNITS = (
    (0, 1, 0, 512, ENDS), (0, 0, 512, 512, MIXED), (1, 0, 0, 512, ENDS), (1, 2, 512, 512, EVEN), (2, 1, 0, 1024, EVEN), (3, 1, 0, 1024, ENDS),
    (4, 1, 0, 1024, MIXED), (5, 0, 0, 512, MIXED), (5, 0, 512, 512, MIXED), (6, 1, 0, 256, EVEN), (6, 2, 256, 768, ENDS),
    (7, 1, 0, 512, ENDS), (7, 1, 512, 512, ENDS),
)
PHASES = (2.2, 1.5, 3.0, 2.2, 5.2, 1.8, 8.2, 2.2, 2.2, 2.2, 1.5, 1.5, 1.2, 2.2, 1.2, 3.0, 1.2, 1.5, 3.0, 2.0, 2.0, 2.0, 2.0, 6.0, 1.5)
RELEASE = {0: 0, 1: 0, 2: 3, 3: 3, 4: 12, 5: 14, 6: 16, 7: 17}
EARLY = tuple(u for u, t in enumerate(UNITS) if t[0] < 2)
UNIT, LAG = 3.0, 2.0
MARGIN, WINDOW = 0.0, 1000.0
RANKS = {"G": 1, "P": 1, "C": 1, "D": 1, "F": 2, "W": 2, "Y": 4, "X": 4, "S": 0}
BY_UNIT = False


def far_first(z, roots):
    return sorted(range(NZ), key=lambda k: (-abs(roots[k] - z), k))


def line_events(z):
    found = []
    for u, (i, first, _, rows, roots) in enumerate(UNITS):
        size = rows / (1024.0 if first else 512.0)
        late = RELEASE[i]
        for k in range(NZ):
            g = roots[k]
            left = ("l", z - 1, ("zr", u, k), size)
            right = ("r", z + 1, ("zl", u, k), size)
            cross = [("y", z, ("yf", u, k), size)]
            far = [("x", z, ("xf", u, k, 0), size)] if i == 5 else []
            far += [("c", z, ("cf", u, k, 0), size)]
            on = (cross if first == 1 else []) + far
            both = ([left] if z > 0 else []) + ([right] if z < NZ - 1 else []) + (cross if first else []) + far
            need = [("yr", u, k)] if first else []
            if first:
                found.append((("G", u, k), late, None, [], [("y", z, ("yr", u, k), size)], 0.1))
            if z > 0 and g >= z:
                need.append(("zl", u, k))
            if z < NZ - 1 and g <= z:
                need.append(("zr", u, k))
            if g != z:
                found.append((("P", u, k), late, None, need, [right if g > z else left], 0.4))
                further = [left] if g > z > 0 else [right] if g < z < NZ - 1 else []
                found.append((("F", u, k), late, ("P", u, k), [("zr" if g > z else "zl", u, k)], further + on, 0.2))
            else:
                swap = both if first else [("y", z, ("yr", u, k), size)]
                found.append((("C", u, k), late, None, need, swap, 0.4))
                if not first:
                    found.append((("D", u, k), late, ("C", u, k), [("yr", u, k)], both, 0.4))
            other = [("x", z, ("xf", u, k, 1), size)] if i == 5 else []
            other += [("c", z, ("cf", u, k, 1), size)]
            if first == 1:
                found.append((("Y", u, k), late, ("G", u, k), [("yf", u, k)], other, 0.2))
            if first == 2:
                left = ("l", z - 1, ("wr", u, k), size)
                right = ("r", z + 1, ("wl", u, k), size)
                if g == z:
                    both = ([left] if z > 0 else []) + ([right] if z < NZ - 1 else []) + other
                    found.append((("Y", u, k), late, ("G", u, k), [("yf", u, k)], both, 0.2))
                else:
                    further = [left] if g > z > 0 else [right] if g < z < NZ - 1 else []
                    found.append((("W", u, k), late, ("G", u, k), [("wr" if g > z else "wl", u, k)], further + other, 0.2))
            if i == 5:
                for h in range(2 if first else 1):
                    found.append((("X", u, k, h), late, None, [("xf", u, k, h)], [("c", z, ("cf", u, k, 2 + h), size)], 0.2))
    last = len(PHASES) - 1

    def small(n, after, need, out):
        found.append((("S", n, 0), last, after, need, out, 0.4))

    small(1, None, [], [("x", z, ("s1",), 0.7), ("c", z, ("s1c",), 0.7)])
    small(3, ("S", 1, 0), [("s1",)], [("y", z, ("s3",), 1.35)])
    inward = [] if z == ROOT else [("r" if z < ROOT else "l", ROOT, ("s4", z), 1.35)]
    small(4, ("S", 3, 0), [("s3",)], inward)
    tail = [("c", z, ("s6",), 1.35), ("x", z, ("s7",), 1.35)]
    if z == ROOT:
        out = [("l" if q < ROOT else "r", q, ("s5",), 1.35) for q in NEAR]
        small(6, ("S", 4, 0), [("s4", q) for q in NEAR], out + tail)
    else:
        small(7, ("S", 4, 0), [("s5",)], tail)
    return found


def make_plan():
    todo = [line_events(z) for z in range(NZ)]
    clock = [0.0] * NZ
    phase = [0] * NZ
    done = [set() for _ in range(NZ)]
    arrive = [{} for _ in range(NZ)]
    link = {}
    plan = [[[] for _ in range(len(PHASES) + 1)] for _ in range(NZ)]
    while any(todo) or min(phase) < len(PHASES):
        z = min(range(NZ), key=lambda q: (clock[q], q) if (todo[q] or phase[q] < len(PHASES)) else (1e9, q))
        now = clock[z]
        best = None
        for item in todo[z]:
            key, late, after, need, out, cost = item
            if phase[z] <= late or (after is not None and after not in done[z]):
                continue
            latest = 0.0
            for m in need:
                latest = max(latest, arrive[z].get(m, 1e9))
            if need and latest + (MARGIN if phase[z] < len(PHASES) else 0.0) > now:
                continue
            full = phase[z] >= len(PHASES) and key[0] != "S" and any(
                link.get((z, lane), 0.0) > now + WINDOW for lane, _, _, _ in out if lane in "ylr")
            if full:
                continue
            away = -abs(UNITS[key[1]][4][key[2]] - z) if key[0] != "S" else 0
            rank = RANKS[key[0]]
            if key[0] == "Y" and UNITS[key[1]][1] == 2:
                rank = RANKS["F"]
            order = (rank, key[1] if BY_UNIT else latest, away, key[1], key[2])
            if best is None or order < best[0]:
                best = (order, item)
        if best is not None:
            item = best[1]
            todo[z].remove(item)
            key, _, _, _, out, cost = item
            done[z].add(key)
            plan[z][phase[z]].append(key)
            clock[z] += 0.8 * cost
            for lane, dest, message, size in out:
                begin = max(link.get((z, lane), 0.0), clock[z])
                took = size * UNIT * (0.2 if lane == "c" else 1.0)
                link[(z, lane)] = begin + took
                arrive[dest][message] = begin + took + LAG
        elif phase[z] < len(PHASES):
            clock[z] += PHASES[phase[z]]
            phase[z] += 1
        else:
            clock[z] += 0.1
    ends = [max([clock[z]] + list(arrive[z].values())) for z in range(NZ)]
    return plan, ends

F32 = jnp.float32
BF = jnp.bfloat16
MESH = pl.DeviceIdType.MESH


def mm(a, b):
    return lax.dot_general(a, b, (((1,), (0,)), ((), ())), preferred_element_type=F32)


def mm_nt(a, b):
    return lax.dot_general(a, b, (((1,), (1,)), ((), ())), preferred_element_type=F32)


def mm_tn(a, b):
    return lax.dot_general(a, b, (((0,), (0,)), ((), ())), preferred_element_type=F32)


def sigm(v):
    return 1.0 / (1.0 + jnp.exp(-v))


def slope_of(pre, sig):
    return sig * (1.0 + pre * (1.0 - sig))


def cols(i, n):
    return pl.ds(pl.multiple_of(i * n, n), n)


def main_kernel(
    tok_h, cot_h, wsh_h, wv_h, wr_h, wm_h, wh_h, wu_h, wup_h, wdn_h,
    lens, relb, bmap, in_n1g, in_n1b, in_skip, in_bupd, in_n2g, in_n2b, rate, damp, ein, eout, qkg, qkb, in_bup,
    bo, gt, o_all, o_hu, o_shared, o_small,
    wsh, wv, wr, wm, wh, wu, wup, wdn,
    tok, gout, normed, nlow, mlow, pre_ema, xs, smo, pre_sh, qlow, klow, probs, plow,
    pre_v, att, pre_r, vlow, gated, part_s, mix_r, own_f, pre_hid, gate, blend, n2,
    gup, up, gpu, gn2_r, ffn_s, ffn_r, hid, upd, gpr, gpv, gp_acc, gp_r, gps,
    nb_s, mb_r, nb_r,
    p_normed, p_mixed, p_gout, p_up, p_n2, p_gpu, p_gated, p_hid, p_upd, p_gpr, p_gpv, p_gps,
    a_s, w_s, snap_s, snap_r, carry, carry_r, acc, keep, live, segc, vec, bup,
    g_v, ext, small, s_q, s_own, s_y, s_in,
    wsem, xsend, xrecv, csend, crecv, lsem, asend, arecv, ready,
):
    x = lax.axis_index("narrow")
    w = lax.axis_index("wide")
    other = 1 - x
    c = w % 2
    wpart = w + 1 - 2 * c
    y = (w // 2) % 2
    wy = w + 2 - 4 * y
    zi = w // 4
    wl = w - 4
    wr_ = w + 4
    H = tok.shape[0] // 2
    R = 2 * H
    own = pl.ds(pl.multiple_of(x * H, H), H)
    oth = pl.ds(pl.multiple_of(other * H, H), H)
    D = 1024
    VL = wv.shape[1]
    FL = wup.shape[0] * wup.shape[2]
    EPS = EPSILON

    weights = [
        (tok_h, tok.at[own]), (cot_h, gout.at[own]), (wsh_h, wsh), (wv_h, wv), (wr_h, wr), (wm_h, wm), (wh_h, wh), (wu_h, wu),
    ]
    wcopies = [pltpu.make_async_copy(s, d, wsem.at[i]) for i, (s, d) in enumerate(weights)]
    FB = D // 2
    down_copies = [pltpu.make_async_copy(wdn_h.at[:, b * FB : (b + 1) * FB], wdn.at[b], wsem.at[8 + b]) for b in range(D // FB)]
    up_copies = [pltpu.make_async_copy(wup_h.at[:, b * FB : (b + 1) * FB], wup.at[b], wsem.at[10 + b]) for b in range(FL // FB)]
    wcopies[0].start()
    wcopies[1].start()

    barrier = pltpu.get_barrier_semaphore()
    w_root = w + 4 * (ROOT - zi)
    w_last = w + 4 * (NZ - 1 - zi)

    def greet(to):
        pl.semaphore_signal(barrier, inc=1, device_id=to, device_id_type=MESH)

    for to in ((w, other), (wpart, x), (wpart, other), (wy, x)):
        greet(to)
    for z in range(NZ):
        met = [wl] * (z > 0) + [wr_] * (z < NZ - 1) + [w_last] * (z == ROOT) + [w_root] * (z == NZ - 1)

        @pl.when(zi == z)
        def _(met=met):
            for to in met:
                greet((to, x))
            pl.semaphore_wait(barrier, 4 + len(met))

    def xcopy(i, src, dst):
        return pltpu.make_async_remote_copy(
            src_ref=src, dst_ref=dst, send_sem=xsend.at[i], recv_sem=xrecv.at[i],
            device_id=(w, other), device_id_type=MESH,
        )

    def ccopy(i, src, dst):
        return pltpu.make_async_remote_copy(
            src_ref=src, dst_ref=dst, send_sem=csend.at[i], recv_sem=crecv.at[i],
            device_id=(wpart, x), device_id_type=MESH,
        )

    HC = H // 4
    x_tok = [
        xcopy(0 if j == 0 else 16 + j, tok_h.at[j * HC : (j + 1) * HC], tok.at[pl.ds(pl.multiple_of(x * H + j * HC, HC), HC)])
        for j in range(4)
    ]
    x_cot = xcopy(1, cot_h, gout.at[own])
    for copy in x_tok:
        copy.start()
    for copy in wcopies[2:] + down_copies + up_copies:
        copy.start()

    gs = smo.at[0 : H * 8]
    gxs = smo.at[H * 8 : R * 8]
    nb_o = gup.at[0:H, 0:D]
    gres = gup.at[0:H, D : 2 * D]
    ffn_o = gup.at[H:R, 0:D]

    first_end = lens[0, 0]
    second_end = first_end + lens[0, 1]
    place = lax.broadcasted_iota(jnp.int32, (R, 128), 0)
    begins = (place == 0) | (place == first_end) | (place == second_end)
    keep[...] = jnp.where(begins, 0.0, 1.0)
    live[...] = jnp.where(place >= second_end, 0.0, 1.0)

    def segment_of(at):
        return jnp.where(at >= first_end, 1.0, 0.0) + jnp.where(at >= second_end, 1.0, 0.0)

    segc[...] = segment_of(place)

    for t in range(2):
        for j in range(8):
            rows_ = slice(t * 8, t * 8 + 8)
            lanes = slice(j * 128, j * 128 + 128)
            r_ = rate[rows_, lanes]
            a_s[pl.ds(t * 64 + j, 8, stride=8), :] = 1.0 - r_ * damp[rows_, lanes]
            w_s[pl.ds(t * 64 + j, 8, stride=8), :] = r_ * ein[rows_, lanes] * eout[rows_, lanes]

    for k, ref in enumerate((in_n1g, in_n1b, in_skip, in_bupd, in_n2g, in_n2b)):
        for j in range(8):
            vec[k : k + 1, j * 128 : (j + 1) * 128] = ref[j : j + 1, :]
    wide_bias = in_bup[...].astype(F32)
    for j in range(16):
        bup[0:1, j * 128 : (j + 1) * 128] = wide_bias[j : j + 1, :]

    def norm_rows(v):
        m = jnp.mean(v, axis=-1, keepdims=True)
        cen = v - m
        var = jnp.mean(cen * cen, axis=-1, keepdims=True)
        return cen, lax.rsqrt(var + EPS)

    def norm1(t):
        rr = cols(t, 16)
        cen, rstd = norm_rows(tok[rr, :].astype(F32))
        v = cen * rstd * vec[0:1, :] + vec[1:2, :]
        normed[rr, :] = v
        nlow[rr, :] = v.astype(BF)
        for j in range(8):
            xs[pl.ds(t * 128 + j, 16, stride=8), :] = v[:, j * 128 : (j + 1) * 128]

    HT = H // 16
    wcopies[0].wait()
    pl.loop(0, HT, unroll=2)(lambda t: norm1(x * HT + t))
    N = 16

    def coef(ref):
        return ref[...].reshape(N, 8, 128)

    zeros = jnp.zeros((N, 8, 128), F32)

    def forward(p, s):
        k = keep[pl.ds(p, 1), :]
        at = cols(p, 8)
        xr = xs[at, :] * live[pl.ds(p, 1), :]
        s = coef(a_s) * (s * k) + xr
        smo[at, :] = jnp.sum(coef(w_s) * s, axis=0)
        return s

    def mixed_rows(t):
        rr = cols(t, 16)
        for j in range(8):
            ll = slice(j * 128, (j + 1) * 128)
            pre = smo[pl.ds(t * 128 + j, 16, stride=8), :] + vec[2:3, ll] * normed[rr, ll]
            pre_ema[rr, ll] = pre
            mlow[rr, ll] = (pre * sigm(pre)).astype(BF)

    T = 256

    def value_tile(i, rows_):
        cc = cols(i, T)
        pv = mm(nlow[rows_, :], wv[:, cc])
        pre_v[rows_, cc] = pv
        vlow[rows_, cc] = (pv * sigm(pv)).astype(BF)

    wcopies[3].wait()
    pl.loop(0, VL // T, unroll=2)(lambda i: value_tile(i, own))
    state = zeros
    for j in range(8):

        @pl.when(x == (1 if j < 4 else 0))
        def _(j=j):
            x_tok[j % 4].wait_recv()
            pl.loop(j * (HC // 16), (j + 1) * (HC // 16), unroll=2)(norm1)

        state = lax.fori_loop(j * HC, (j + 1) * HC, forward, state, unroll=4)
        pl.loop(j * (HC // 16), (j + 1) * (HC // 16), unroll=2)(mixed_rows)

    for copy in x_tok:
        copy.wait_send()
    x_cot.start()
    c_normed = ccopy(0, nlow, p_normed)
    c_mixed = ccopy(1, mlow, p_mixed)

    wcopies[2].wait()
    psh = mm(mlow[...], wsh[...])
    pre_sh[...] = psh
    sh = psh * sigm(psh)
    qlow[...] = (sh * qkg[0:1, :] + qkb[0:1, :]).astype(BF)
    klow[...] = (sh * qkg[1:2, :] + qkb[1:2, :]).astype(BF)

    BL = BLOCK
    ii = lax.broadcasted_iota(jnp.int32, (BL, BL), 0)
    jj = lax.broadcasted_iota(jnp.int32, (BL, BL), 1)

    def skew(tbl, left):
        for b in range(7):
            moved = pltpu.roll(tbl, (BL - (1 << b)) if left else (1 << b), 1)
            tbl = jnp.where(lax.rem(ii // (1 << b), 2) == 1, moved, tbl)
        return tbl

    buckets = bmap[0:1, :]
    by_offset = jnp.zeros((1, BL), F32)
    for b in range(relb.shape[1]):
        by_offset = by_offset + jnp.where(buckets == b, relb[0, b], 0.0)
    table = skew(jnp.broadcast_to(by_offset, (BL, BL)), False).T
    scale = float(qkg.shape[1]) ** (-0.5)
    for b in range(2):
        rb = slice(b * BL, (b + 1) * BL)
        sc = mm_nt(qlow[rb, :], klow[rb, :]) * scale
        ok = (segc[rb, :] == segment_of(lax.broadcasted_iota(jnp.int32, (1, BL), 1) + b * BL)) & (jj <= ii)
        sc = jnp.where(ok, sc + table, NEGATIVE)
        ex = jnp.exp(sc - jnp.max(sc, axis=-1, keepdims=True))
        pr = ex / jnp.sum(ex, axis=-1, keepdims=True)
        probs[rb, :] = pr
        plow[rb, :] = pr.astype(BF)

    wcopies[4].wait()

    def reset_tile(i):
        cc = cols(i, T)
        for b in range(2):
            rb = slice(b * BL, (b + 1) * BL)
            att[rb, cc] = mm(plow[rb, :], vlow[rb, cc])
        pr = mm(mlow[...], wr[:, cc])
        pre_r[:, cc] = pr
        gated[:, cc] = (pr * sigm(pr) * att[:, cc]).astype(BF)

    pl.loop(0, VL // T, unroll=2)(lambda i: value_tile(i, oth))
    pl.loop(0, VL // T, unroll=2)(reset_tile)

    wcopies[5].wait()

    HH = H // 2
    x_mix = []
    for h in range(2):
        src = pl.ds(pl.multiple_of(other * H + h * HH, HH), HH)
        hr = slice(h * HH, (h + 1) * HH)

        @pl.loop(0, D // T, unroll=2)
        def _(i, src=src, hr=hr):
            cc = cols(i, T)
            part_s[hr, cc] = mm(gated[src, :], wm[:, cc]).astype(BF)

        x_mix.append(xcopy((2, 13)[h], part_s.at[hr], mix_r.at[hr]))
        x_mix[h].start()

    c_gated = ccopy(2, gated, p_gated)
    wcopies[6].wait()
    wcopies[7].wait()

    @pl.loop(0, D // T, unroll=2)
    def _(i):
        cc = cols(i, T)
        own_f[:, cc] = mm(gated[own, :], wm[:, cc])
        pre_hid[:, cc] = mm(mlow[own, :], wh[:, cc])
        gate[:, cc] = sigm(mm(mlow[own, :], wu[:, cc]) + vec[3:4, cc])

    wcopies[1].wait()
    x_cot.wait()

    @pl.loop(0, R // 16)
    def _(t):
        rr = cols(t, 16)
        gout[rr, :] = (gout[rr, :].astype(F32) * live[rr, 0:1]).astype(BF)

    c_gout = ccopy(3, gout, p_gout)
    c_gout.start()
    for copy in down_copies:
        copy.wait()

    @pl.loop(0, FL // T, unroll=2)
    def _(i):
        cc = cols(i, T)
        gup[:, cc] = mm_nt(gout[:, 0:FB], wdn[0, cc, :]) + mm_nt(gout[:, FB:D], wdn[1, cc, :])


    def blend_rows(t):
        rr = cols(t, 32)
        ro = pl.ds(pl.multiple_of(x * H + t * 32, 32), 32)
        ph = pre_hid[rr, :] + (own_f[rr, :] + mix_r[rr, :].astype(F32))
        pre_hid[rr, :] = ph
        u = gate[rr, :]
        bl = u * (ph * sigm(ph)) + (1.0 - u) * tok[ro, :].astype(F32)
        blend[rr, :] = bl
        cen, rstd = norm_rows(bl)
        n2[ro, :] = (cen * rstd * vec[4:5, :] + vec[5:6, :]).astype(BF)

    x_n2 = []
    for h in range(4):
        if h % 2 == 0:
            x_mix[h // 2].wait()
        pl.loop(h * (H // 128), (h + 1) * (H // 128))(blend_rows)
        part = pl.ds(pl.multiple_of(x * H + h * (H // 4), H // 4), H // 4)
        x_n2.append(xcopy(3 if h == 0 else 13 + h, n2.at[part], n2.at[part]))
        x_n2[h].start()

    for copy in up_copies:
        copy.wait()
    FT = FL // T

    def up_tile(i, rows_, first):
        cc = cols(i, T)
        pu = mm(n2[rows_, :], wup[i // 2, :, cols(i % 2, T)]) + bup[0:1, cc]
        sg = sigm(pu)
        up[rows_, cc] = (pu * sg).astype(BF)
        gp = (gup[rows_, cc] * slope_of(pu, sg)).astype(BF)
        gpu[rows_, cc] = gp
        sums = jnp.sum(gp.astype(F32), axis=0, keepdims=True)
        for h in range(2):
            at = pl.ds(304 + x * 16 + i * 2 + h, 1)
            part = sums[:, h * 128 : (h + 1) * 128]
            if first:
                small[at, :] = part
                small[pl.ds(304 + other * 16 + i * 2 + h, 1), :] = jnp.zeros((1, 128), F32)
            else:
                small[at, :] += part

    pl.loop(0, FT, unroll=2)(lambda i: up_tile(i, own, True))
    for copy in x_n2:
        copy.wait()
    c_n2 = ccopy(4, n2, p_n2)
    halfF = FL // 2
    theirs_f = pl.ds(pl.multiple_of((1 - c) * halfF, halfF), halfF)
    pl.loop(0, FT // 2, unroll=2)(lambda i: up_tile((1 - c) * (FT // 2) + i, oth, False))
    c_up = ccopy(5, up.at[:, theirs_f], p_up)
    c_gpu = ccopy(6, gpu.at[:, theirs_f], p_gpu)
    c_up.start()
    pl.loop(0, FT // 2, unroll=2)(lambda i: up_tile(c * (FT // 2) + i, oth, False))
    c_gpu.start()
    c_n2.start()
    P2 = g_v.shape[2]
    plan = make_plan()[0]
    numbers = {}
    locals_ = {}

    def number(*key):
        return numbers.setdefault(key, len(numbers))

    shelves = [[wup, 0, b] for b in range(wup.shape[0])] + [[wdn, 0, b] for b in range(wdn.shape[0])] + [[ext, 0, 0]]
    places = {}

    def place_of(key, n):
        if key not in places:
            for shelf in shelves:
                if (shelf[0] is ext) == (key[0] in EARLY) and shelf[1] + n <= shelf[0].shape[1]:
                    places[key] = (shelf[0], shelf[1], shelf[2])
                    shelf[1] += n
                    break
        ref, r0, b = places[key]
        return ref.at[b, r0 : r0 + n]

    def chunk_rows(u):
        _, first, _, rows, _ = UNITS[u]
        return rows // 8 if first else rows // 4

    def earlier(u, k):
        roots = UNITS[u][4]
        return sum(roots[q] == roots[k] for q in range(k))

    def line_place(u, k):
        return place_of((u, "z", k), chunk_rows(u))

    def second_place(u, k):
        return place_of((u, "s", earlier(u, k)), chunk_rows(u))

    def cross_place(u, k):
        return place_of((u, "y", k if UNITS[u][1] else earlier(u, k)), chunk_rows(u))

    def from_right(u, k, z):
        return second_place(u, k) if UNITS[u][4][k] == z and z > 0 else line_place(u, k)

    def first_row(u, k, half):
        _, first, row0, rows, _ = UNITS[u]
        n = chunk_rows(u)
        if first:
            return row0 + half * (rows // 2) + k * n
        return row0 + k * n

    def rows_at(u, k, half):
        n = chunk_rows(u)
        if UNITS[u][1]:
            return pl.ds(pl.multiple_of(first_row(u, k, half), 16), n)
        return pl.ds(first_row(u, k, half), n)

    def chunk(u, k, half):
        return g_v.at[UNITS[u][0], rows_at(u, k, half)]

    def result(u, k, half, core, side):
        i = UNITS[u][0]
        rr = rows_at(u, k, half)
        if i == 5:
            return o_hu.at[2 * side + core, rr]
        return o_all.at[core, i - (i > 5), rr]

    sent = [[] for _ in range(NZ)]

    def send(z, way, key, src, dst):
        dev = {
            "y": (wy, x), "l": (wl, x), "r": (wr_, x), "c": (wpart, x), "x": (w, other), "d": (wpart, other),
            "root": (w_root, x), "last": (w_last, x),
        }[way]
        n = number(*key)
        copy = pltpu.make_async_remote_copy(
            src_ref=src, dst_ref=dst, send_sem=asend.at[n], recv_sem=arecv.at[n],
            device_id=dev, device_id_type=MESH,
        )
        copy.start()
        sent[z].append((n, src.shape, src.dtype))

    def arrived(key, ref):
        n = number(*key)
        pltpu.make_async_remote_copy(
            src_ref=ref, dst_ref=ref, send_sem=asend.at[n], recv_sem=arecv.at[n],
            device_id=(w, other), device_id_type=MESH,
        ).wait_recv()

    def add_up(dst, terms):
        if terms:

            @pl.loop(0, dst.shape[0] // 32)
            def _(t):
                rr = cols(t, 32)
                v = dst[rr, :].astype(F32)
                for term in terms:
                    v = v + term[rr, :].astype(F32)
                dst[rr, :] = v.astype(BF)

    def own_copy(u, k, src, half):
        at = locals_.setdefault((u, k), len(locals_))
        return pltpu.make_async_copy(src, result(u, k, half, c, x), lsem.at[at])

    def share(z, u, k, src, half):
        dst = result(u, k, half, c, x)
        if z > 0:
            send(z, "l", ("zr", u, k), src, dst)
        if z < NZ - 1:
            send(z, "r", ("zl", u, k), src, dst)
        if UNITS[u][1]:
            send(z, "y", ("yf", u, k), src, dst)
        if UNITS[u][0] == 5:
            send(z, "x", ("xf", u, k, 0), src, dst)
        send(z, "c", ("cf", u, k, 0), src, dst)
        own_copy(u, k, src, half).start()

    def happen(z, key):
        kind, u, k = key[:3]
        if kind == "S":
            small_step(z, u)
            return
        i, first, _, _, roots = UNITS[u]
        own_half = y if first else 0
        g = roots[k]
        if kind == "G":
            send(z, "y", ("yr", u, k), chunk(u, k, 1 - y), cross_place(u, k))
            return
        if kind in "PC":
            terms = []
            if first:
                arrived(("yr", u, k), cross_place(u, k))
                terms.append(cross_place(u, k))
            if g >= z and z > 0:
                arrived(("zl", u, k), line_place(u, k))
                terms.append(line_place(u, k))
            if g <= z and z < NZ - 1:
                arrived(("zr", u, k), from_right(u, k, z))
                terms.append(from_right(u, k, z))
            mine = chunk(u, k, own_half)
            add_up(mine, terms)
            if kind == "P" and g > z:
                send(z, "r", ("zl", u, k), mine, line_place(u, k))
            elif kind == "P":
                send(z, "l", ("zr", u, k), mine, from_right(u, k, z - 1))
            elif first:
                share(z, u, k, mine, own_half)
            else:
                send(z, "y", ("yr", u, k), mine, cross_place(u, k))
        elif kind == "D":
            mine = cross_place(u, k)
            arrived(("yr", u, k), mine)
            add_up(mine, [chunk(u, k, 0)])
            share(z, u, k, mine, 0)
        elif kind == "F":
            ref = result(u, k, own_half, c, x)
            arrived(("zr" if g > z else "zl", u, k), ref)
            if g > z > 0:
                send(z, "l", ("zr", u, k), ref, ref)
            if g < z < NZ - 1:
                send(z, "r", ("zl", u, k), ref, ref)
            if first == 1:
                send(z, "y", ("yf", u, k), ref, ref)
            if i == 5:
                send(z, "x", ("xf", u, k, 0), ref, ref)
            send(z, "c", ("cf", u, k, 0), ref, ref)
        elif kind in "YW":
            ref = result(u, k, 1 - y, c, x)
            arrived(("yf" if kind == "Y" else "wr" if g > z else "wl", u, k), ref)
            if first == 2 and g >= z > 0:
                send(z, "l", ("wr", u, k), ref, ref)
            if first == 2 and g <= z < NZ - 1:
                send(z, "r", ("wl", u, k), ref, ref)
            if i == 5:
                send(z, "x", ("xf", u, k, 1), ref, ref)
            send(z, "c", ("cf", u, k, 1), ref, ref)
        elif kind == "X":
            h = key[3]
            half = (y if h == 0 else 1 - y) if first else 0
            ref = result(u, k, half, c, other)
            arrived(("xf", u, k, h), ref)
            send(z, "c", ("cf", u, k, 2 + h), ref, ref)

    def slot(n):
        for z in range(NZ):
            if plan[z][n]:

                @pl.when(zi == z)
                def _(z=z):
                    for key in plan[z][n]:
                        happen(z, key)

    def eight(start, n):
        return pl.ds(pl.multiple_of(start, 8), n)

    def quarter(side, core):
        return eight(side * 176 + core * 88, 88)

    def quarter_sh(side, core):
        return eight((2 * side + core) * 256, 256)

    around = (("x", other, c), ("c", x, 1 - c), ("d", other, 1 - c))

    def small_step(z, n):
        mine, mine_sh = quarter(x, c), quarter_sh(x, c)

        def give(total):
            o_small[mine, :] = total[0:88, :]
            o_shared[mine_sh, :] = total[88:344, :]
            for way, _, _ in around:
                send(z, way, ("s6", way), o_small.at[mine], o_small.at[mine])
                send(z, way, ("s7", way), o_shared.at[mine_sh], o_shared.at[mine_sh])

        if n == 1:
            for at, (way, side, core) in enumerate(around):
                send(z, way, ("s1", way), small.at[quarter(side, core)], s_q.at[at])
        elif n == 3:
            for at, (way, _, _) in enumerate(around):
                arrived(("s1", way), s_q.at[at])
            s_own[0:88, :] = (small[mine, :] + s_q[0]) + (s_q[1] + s_q[2])
            send(z, "y", ("s3",), s_own, s_y)
        elif n == 4:
            arrived(("s3",), s_y)
            s_y[...] = s_y[...] + s_own[...]
            if z != ROOT:
                send(z, "root", ("s4", z), s_y, s_in.at[NEAR.index(z)])
        elif n == 6:
            for at, q in enumerate(NEAR):
                arrived(("s4", q), s_in.at[at])
            s_y[...] = (s_y[...] + s_in[0]) + (s_in[1] + s_in[2])
            for q, way in zip(NEAR, ("l", "r", "last")):
                send(z, way, ("s5", q), s_y, s_in.at[0])
            give(s_y)
        elif n == 7:
            arrived(("s5", z), s_in.at[0])
            give(s_in.at[0])

    def finish():
        for z in range(NZ):

            @pl.when(zi == z)
            def _(z=z):
                for way, side, core in around:
                    arrived(("s6", way), o_small.at[quarter(side, core)])
                    arrived(("s7", way), o_shared.at[quarter_sh(side, core)])
                for u, (i, first, _, _, roots) in enumerate(UNITS):
                    for k in range(NZ):
                        half = y if first else 0
                        arrived(("cf", u, k, 0), result(u, k, half, 1 - c, x))
                        if first:
                            arrived(("cf", u, k, 1), result(u, k, 1 - y, 1 - c, x))
                        if i == 5:
                            for h in range(2 if first else 1):
                                at = (y if h == 0 else 1 - y) if first else 0
                                arrived(("cf", u, k, 2 + h), result(u, k, at, 1 - c, other))
                        if roots[k] == z:
                            own_copy(u, k, chunk(u, k, half), half).wait()
                for n, shape, dtype in sent[z]:
                    like = g_v.at[0, 0 : shape[0]] if dtype == BF else o_shared.at[0 : shape[0]]
                    pltpu.make_async_remote_copy(
                        src_ref=like, dst_ref=like, send_sem=asend.at[n], recv_sem=arecv.at[n],
                        device_id=(w, other), device_id_type=MESH,
                    ).wait_send()


    c_gout.wait()
    c_up.wait()
    P2 = g_v.shape[2]

    @pl.loop(0, 4)
    def _(i):
        mt = cols(i, 256)
        mf = pl.ds(pl.multiple_of(c * halfF + i * 256, 256), 256)
        la = up[:, mf]
        lb = p_up[:, mt]
        for j in range(2):
            nn = slice(j * P2, (j + 1) * P2)
            g_v[j, mt, :] = (mm_tn(la, gout[:, nn]) + mm_tn(lb, p_gout[:, nn])).astype(BF)

    slot(1)

    def up_back(rows_, cc):
        parts = [mm_nt(gpu[rows_, b * FB : (b + 1) * FB], wup[b, cc, :]) for b in range(FL // FB)]
        return (parts[0] + parts[1]) + (parts[2] + parts[3])

    @pl.loop(0, D // T)
    def _(i):
        cc = cols(i, T)
        part_s[:, cc] = up_back(oth, cc).astype(BF)

    x_gn2 = xcopy(4, part_s, gn2_r)
    x_gn2.start()
    slot(2)

    @pl.loop(0, D // T)
    def _(i):
        cc = cols(i, T)
        own_f[:, cc] = up_back(own, cc)
        ffn_s[:, cc] = mm(up[oth, :], wdn[i // 2, :, cols(i % 2, T)]).astype(BF)
        ffn_o[:, cc] = mm(up[own, :], wdn[i // 2, :, cols(i % 2, T)])


    pl.semaphore_signal(ready.at[0], inc=1, device_id=(wy, x), device_id_type=MESH)

    @pl.when(zi > 0)
    def _():
        pl.semaphore_signal(ready.at[2], inc=1, device_id=(wl, x), device_id_type=MESH)

    @pl.when(zi < NZ - 1)
    def _():
        pl.semaphore_signal(ready.at[1], inc=1, device_id=(wr_, x), device_id_type=MESH)

    pl.semaphore_wait(ready.at[0], 1)

    @pl.when(zi > 0)
    def _():
        pl.semaphore_wait(ready.at[1], 1)

    @pl.when(zi < NZ - 1)
    def _():
        pl.semaphore_wait(ready.at[2], 1)

    slot(3)
    c_n2.wait()
    c_gpu.wait()

    @pl.loop(0, 4)
    def _(i):
        mt = cols(i, 256)
        la = n2[:, mt]
        lb = p_n2[:, mt]
        for j in range(2):
            nf = pl.ds(pl.multiple_of(c * halfF + j * P2, P2), P2)
            nn = slice(j * P2, (j + 1) * P2)
            g_v[2 + j, mt, :] = (mm_tn(la, gpu[:, nf]) + mm_tn(lb, p_gpu[:, nn])).astype(BF)

    c_gated.start()
    c_mixed.start()
    c_normed.start()
    slot(4)
    x_gn2.wait()

    acc[...] = jnp.zeros_like(acc)

    def add_rows(k, v):
        acc[k * 8 : k * 8 + 8, :] += v[0:8, :] + v[8:16, :]

    def norm2_back(t):
        rr = cols(t, 16)
        ro = pl.ds(pl.multiple_of(x * H + t * 16, 16), 16)
        g = own_f[rr, :] + gn2_r[rr, :].astype(F32)
        cen, rstd = norm_rows(blend[rr, :])
        xh = cen * rstd
        add_rows(0, g * xh)
        add_rows(1, g)
        gy = g * vec[4:5, :]
        gb = rstd * (gy - jnp.mean(gy, axis=-1, keepdims=True) - xh * jnp.mean(gy * xh, axis=-1, keepdims=True))
        gb = gb + gout[ro, :].astype(F32)
        u = gate[rr, :]
        ph = pre_hid[rr, :]
        sg = sigm(ph)
        tk = tok[ro, :].astype(F32)
        gud = (gb * (ph * sg - tk) * u * (1.0 - u)).astype(BF)
        ghd = (gb * u * slope_of(ph, sg)).astype(BF)
        hid[ro, :] = ghd
        upd[ro, :] = gud
        add_rows(2, gud.astype(F32))
        gres[rr, :] = gb * (1.0 - u)

    halves = [pl.ds(pl.multiple_of(x * H + h * (H // 2), H // 2), H // 2) for h in range(2)]
    x_hid = [xcopy((5, 22)[h], hid.at[halves[h]], hid.at[halves[h]]) for h in range(2)]
    pl.loop(0, HT // 2)(norm2_back)
    x_hid[0].start()
    slot(5)
    pl.loop(HT // 2, HT)(norm2_back)
    x_hid[1].start()
    x_upd = xcopy(6, upd.at[own], upd.at[own])
    x_ffn = xcopy(7, ffn_s, ffn_r)

    def put_small(row, k):
        v = jnp.sum(acc[k * 8 : k * 8 + 8, :], axis=0, keepdims=True)
        for j in range(8):
            small[row + j : row + j + 1, :] = v[:, j * 128 : (j + 1) * 128]

    put_small(256 + 32, 0)
    put_small(256 + 40, 1)
    put_small(256 + 24, 2)
    slot(6)

    snap_s[...] = jnp.zeros_like(snap_s)
    snap_r[...] = jnp.zeros_like(snap_r)

    def sense(p, state):
        s, r = state
        k = keep[pl.ds(p, 1), :]
        a = coef(a_s)
        sk = s * k
        return a * sk + xs[cols(p, 8), :] * live[pl.ds(p, 1), :], a * (r * k) + sk

    @pl.when(x == 1)
    def _():
        s_mid, r_mid = lax.fori_loop(0, H, sense, (zeros, zeros), unroll=2)
        snap_s[...] = s_mid.reshape(N * 8, 128)
        snap_r[...] = r_mid.reshape(N * 8, 128)

    for copy in x_hid:
        copy.wait()
    x_upd.start()
    c_hid = ccopy(7, hid, p_hid)
    c_hid.start()
    gp_acc[...] = jnp.zeros_like(gp_acc)

    def gated_back(i):
        cc = cols(i, T)
        gg = mm_nt(hid[...], wm[cc, :])
        pr = pre_r[:, cc]
        sg = sigm(pr)
        ga = (gg * (pr * sg)).astype(BF)
        gpr[:, cc] = (gg * att[:, cc] * slope_of(pr, sg)).astype(BF)
        pv = pre_v[:, cc]
        sv = slope_of(pv, sigm(pv))
        for b in range(2):
            rb = slice(b * BL, (b + 1) * BL)
            gp_acc[rb, :] += mm_nt(ga[rb, :], vlow[rb, cc])
            gv = mm_tn(plow[rb, :], ga[rb, :])
            gpv[rb, cc] = (gv * sv[rb, :]).astype(BF)

    for i in range(VL // T):
        pl.loop(i, i + 1)(gated_back)
        slot(7 + i)
    x_gp = xcopy(8, gp_acc.at[oth], gp_r)
    x_gp.start()
    x_upd.wait()

    @pl.loop(0, D // T)
    def _(i):
        cc = cols(i, T)
        part_s[:, cc] = mm_nt(gpr[oth, :], wr[cc, :]).astype(BF)

    x_mb = xcopy(9, part_s, mb_r)
    x_mb.start()
    slot(11)

    @pl.loop(0, D // T)
    def _(i):
        cc = cols(i, T)
        nb_s[:, cc] = mm_nt(gpv[oth, :], wv[cc, :]).astype(BF)

    x_nb = xcopy(10, nb_s, nb_r)
    halfV = VL // 2
    c_gpr = ccopy(8, gpr.at[:, pl.ds(pl.multiple_of((1 - c) * halfV, halfV), halfV)], p_gpr)
    c_gpv = ccopy(9, gpv.at[:, pl.ds(pl.multiple_of((1 - c) * halfV, halfV), halfV)], p_gpv)
    c_upd = ccopy(10, upd, p_upd)
    c_gpr.start()
    c_gpv.start()
    c_upd.start()

    slot(12)
    c_hid.wait()
    c_gated.wait()
    hv = pl.ds(pl.multiple_of(c * P2, P2), P2)
    q4 = pl.ds(pl.multiple_of((2 * x + c) * 256, 256), 256)

    @pl.loop(0, 4)
    def _(i):
        mt = cols(i, 256)
        g_v[4, mt, :] = (mm_tn(gated[:, mt], hid[:, hv]) + mm_tn(p_gated[:, mt], p_hid[:, hv])).astype(BF)

    slot(13)

    x_gp.wait()
    gpb = gp_acc[own, :] + gp_r[...]
    po = probs[own, :]
    gsc = (po * (gpb - jnp.sum(gpb * po, axis=-1, keepdims=True))).astype(BF)
    gq = mm(gsc, klow[own, :]) * scale
    gk = mm_tn(gsc, qlow[own, :]) * scale
    psh = pre_sh[own, :]
    sgs = sigm(psh)
    sh = psh * sgs
    small[336:337, :] = jnp.sum(gq * sh, axis=0, keepdims=True)
    small[337:338, :] = jnp.sum(gk * sh, axis=0, keepdims=True)
    small[338:339, :] = jnp.sum(gq, axis=0, keepdims=True)
    small[339:340, :] = jnp.sum(gk, axis=0, keepdims=True)
    small[340:341, :] = jnp.sum(skew(gsc.astype(F32).T, True), axis=0, keepdims=True)
    small[341:352, :] = jnp.zeros((11, 128), F32)
    gps[own, :] = ((gq * qkg[0:1, :] + gk * qkg[1:2, :]) * slope_of(psh, sgs)).astype(BF)
    x_gps = xcopy(11, gps.at[own], gps.at[own])
    x_gps.start()
    x_nb.start()
    slot(14)
    c_mixed.wait()
    c_upd.wait()

    la = mlow[:, q4]
    lb = p_mixed[:, q4]
    for j in range(2):
        nn = slice(j * P2, (j + 1) * P2)
        g_v[5, j * 256 : j * 256 + 256, :] = (mm_tn(la, hid[:, nn]) + mm_tn(lb, p_hid[:, nn])).astype(BF)
        g_v[5, 512 + j * 256 : 768 + j * 256, :] = (mm_tn(la, upd[:, nn]) + mm_tn(lb, p_upd[:, nn])).astype(BF)

    slot(15)

    @pl.loop(0, D // T)
    def _(i):
        cc = cols(i, T)
        own_f[:, cc] = (
            mm_nt(gpr[own, :], wr[cc, :])
            + mm_nt(gps[own, :], wsh[cc, :])
            + mm_nt(hid[own, :], wh[cc, :])
            + mm_nt(upd[own, :], wu[cc, :])
        )
        nb_o[:, cc] = mm_nt(gpv[own, :], wv[cc, :])

    slot(16)
    x_gps.wait()
    c_gps = ccopy(11, gps, p_gps)
    c_gps.start()
    c_gpr.wait()

    @pl.loop(0, 4)
    def _(i):
        mt = cols(i, 256)
        g_v[6, mt, :] = (mm_tn(mlow[:, mt], gpr[:, hv]) + mm_tn(p_mixed[:, mt], p_gpr[...])).astype(BF)

    slot(17)
    c_normed.wait()
    c_gpv.wait()

    @pl.loop(0, 4)
    def _(i):
        mt = cols(i, 256)
        g_v[7, mt, :] = (mm_tn(nlow[:, mt], gpv[:, hv]) + mm_tn(p_normed[:, mt], p_gpv[...])).astype(BF)

    c_gps.wait()
    s_own[88:344, :] = mm_tn(mlow[:, q4], gps[...]) + mm_tn(p_mixed[:, q4], p_gps[...])
    slot(18)
    x_mb.wait()
    x_ffn.start()

    acc[...] = jnp.zeros_like(acc)

    @pl.loop(0, H // 16)
    def _(t):
        rr = cols(t, 16)
        ro = pl.ds(pl.multiple_of(x * H + t * 16, 16), 16)
        pre = pre_ema[ro, :]
        g = (own_f[rr, :] + mb_r[rr, :].astype(F32)) * slope_of(pre, sigm(pre))
        own_f[rr, :] = g
        add_rows(0, g * normed[ro, :])
        for j in range(8):
            gs[pl.ds(t * 128 + j, 16, stride=8), :] = g[:, j * 128 : (j + 1) * 128]

    put_small(256, 0)
    slot(19)

    def back(p_, cy):
        p = H - 1 - p_
        at = cols(p, 8)
        po_ = x * H + p
        mu = gs[at, :] + cy
        gxs[at, :] = jnp.sum(coef(w_s) * mu, axis=0) * live[pl.ds(po_, 1), :]
        return coef(a_s) * (mu * keep[pl.ds(po_, 1), :])

    x_carry = xcopy(12, carry, carry_r)

    @pl.when(x == 1)
    def _():
        cy = lax.fori_loop(0, H, back, zeros)
        carry[...] = cy.reshape(N * 8, 128)
        x_carry.start()

    slot(20)
    for q in range(2):
        nq = slice(q * 64, q * 64 + 64)

        def fwd(p, state, nq=nq):
            s, r, gw, gr = state
            at = cols(p, 8)
            po_ = x * H + p
            k = keep[pl.ds(po_, 1), :]
            xr = xs[cols(po_, 8), :] * live[pl.ds(po_, 1), :]
            a = a_s[nq, :].reshape(8, 8, 128)
            sk = s * k
            r = a * (r * k) + sk
            s = a * sk + xr
            g = gs[at, :]
            return s, r, gw + g * s, gr + g * r

        z8 = jnp.zeros((8, 8, 128), F32)
        s0 = snap_s[nq, :].reshape(8, 8, 128)
        r0 = snap_r[nq, :].reshape(8, 8, 128)
        _, _, gw, gr = lax.fori_loop(0, H, fwd, (s0, r0, z8, z8))
        small[nq, :] = gw.reshape(64, 128)
        small[128 + q * 64 : 192 + q * 64, :] = gr.reshape(64, 128) * w_s[nq, :]
        slot(21 + q)

    @pl.when(x == 0)
    def _():
        x_carry.wait_recv()
        lax.fori_loop(0, H, back, coef(carry_r))

    @pl.when(x == 1)
    def _():
        x_carry.wait_send()

    slot(23)
    x_nb.wait()

    @pl.loop(0, H // 16)
    def _(t):
        rr = cols(t, 16)
        ro = pl.ds(pl.multiple_of(x * H + t * 16, 16), 16)
        gx = jnp.concatenate([gxs[pl.ds(t * 128 + j, 16, stride=8), :] for j in range(8)], axis=1)
        g = nb_o[rr, :] + nb_r[rr, :].astype(F32) + vec[2:3, :] * own_f[rr, :] + gx
        cen, rstd = norm_rows(tok[ro, :].astype(F32))
        xh = cen * rstd
        add_rows(1, g * xh)
        add_rows(2, g)
        gy = g * vec[0:1, :]
        gb = rstd * (gy - jnp.mean(gy, axis=-1, keepdims=True) - xh * jnp.mean(gy * xh, axis=-1, keepdims=True))
        gt[rr, :] = gres[rr, :] + gb

    put_small(256 + 8, 1)
    put_small(256 + 16, 2)

    slot(24)

    x_ffn.wait()

    @pl.loop(0, H // 16)
    def _(t):
        rr = cols(t, 16)
        bo[rr, :] = (blend[rr, :] + (ffn_o[rr, :] + ffn_r[rr, :].astype(F32))).astype(BF)

    slot(25)
    finish()

def vm(shape, dtype=F32):
    return pltpu.VMEM(shape, dtype)


SEMS = 440


def run_main(tokens, cotangent, seq_lengths, bucket_map, norm1_gain, norm1_bias, ema_rate, ema_damp, ema_in, ema_out,
             ema_skip, w_shared, qk_gain, qk_bias, rel_bias, w_value, w_reset, w_mix, w_hidden, w_update, b_update,
             norm2_gain, norm2_bias, w_up, b_up, w_down):
    H = tokens.shape[0]
    R = 2 * H
    D = tokens.shape[1]
    VL = w_value.shape[1]
    FL = w_up.shape[1]
    Z = w_shared.shape[1]
    rows8 = [v.reshape(8, D // 8) for v in (norm1_gain, norm1_bias, ema_skip, b_update, norm2_gain, norm2_bias)]
    anyspec = pl.BlockSpec(memory_space=pl.ANY)
    vspec = pl.BlockSpec(memory_space=pltpu.VMEM)
    sspec = pl.BlockSpec(memory_space=pltpu.SMEM)
    P2 = D // 2
    outs = (
        jax.ShapeDtypeStruct((H, D), BF),
        jax.ShapeDtypeStruct((H, D), F32),
        jax.ShapeDtypeStruct((2, 7, D, P2), BF),
        jax.ShapeDtypeStruct((4, D, P2), BF),
        jax.ShapeDtypeStruct((D, Z), F32),
        jax.ShapeDtypeStruct((352, 128), F32),
    )
    dma = pltpu.SemaphoreType.DMA
    scratch = [
        vm((D, Z), BF), vm((D, VL), BF), vm((D, VL), BF), vm((VL, D), BF), vm((D, D), BF), vm((D, D), BF), vm((FL // P2, D, P2), BF), vm((2, FL, P2), BF),
        vm((R, D), BF), vm((R, D), BF), vm((R, D)), vm((R, D), BF), vm((R, D), BF), vm((R, D)), vm((R * 8, 128)), vm((R * 8, 128)),
        vm((R, Z)), vm((R, Z), BF), vm((R, Z), BF), vm((R, BLOCK)), vm((R, BLOCK), BF),
        vm((R, VL)), vm((R, VL)), vm((R, VL)), vm((R, VL), BF), vm((R, VL), BF), vm((H, D), BF), vm((H, D), BF), vm((H, D)), vm((H, D)), vm((H, D)), vm((H, D)), vm((R, D), BF),
        vm((R, FL)), vm((R, FL), BF), vm((R, FL), BF), vm((H, D), BF), vm((H, D), BF), vm((H, D), BF), vm((R, D), BF), vm((R, D), BF), vm((R, VL), BF), vm((R, VL), BF), vm((R, BLOCK)), vm((H, BLOCK)), vm((R, Z), BF),
        vm((H, D), BF), vm((H, D), BF), vm((H, D), BF),
        vm((R, D), BF), vm((R, D), BF), vm((R, D), BF), vm((R, FL // 2), BF), vm((R, D), BF), vm((R, FL // 2), BF), vm((R, VL), BF), vm((R, D), BF), vm((R, D), BF), vm((R, VL // 2), BF), vm((R, VL // 2), BF), vm((R, Z), BF),
        vm((128, 128)), vm((128, 128)), vm((128, 128)), vm((128, 128)), vm((128, 128)), vm((128, 128)), vm((24, D)), vm((R, 128)), vm((R, 128)), vm((R, 128)), vm((8, D)), vm((8, FL)),
        vm((8, D, P2), BF), vm((1, 11 * 256, P2), BF), vm((352, 128)), vm((3, 88, 128)), vm((344, 128)), vm((344, 128)), vm((NZ - 1, 344, 128)),
        dma((14,)), dma((23,)), dma((23,)), dma((12,)), dma((12,)), dma((96,)), dma((SEMS,)), dma((SEMS,)), pltpu.SemaphoreType.REGULAR((3,)),
    ]
    return pl.pallas_call(
        main_kernel,
        out_shape=outs,
        in_specs=[anyspec] * 10 + [sspec, sspec] + [vspec] * 14,
        out_specs=(vspec, vspec) + (anyspec,) * 2 + (vspec, vspec),
        scratch_shapes=scratch,
        compiler_params=pltpu.CompilerParams(collective_id=0, has_side_effects=True, vmem_limit_bytes=63 * 1024 * 1024),
        cost_estimate=pl.CostEstimate(flops=15_000_000_000, bytes_accessed=40_000_000, transcendentals=0),
    )(
        tokens, cotangent, w_shared, w_value, w_reset, w_mix, w_hidden, w_update, w_up, w_down,
        seq_lengths, rel_bias.reshape(1, -1), bucket_map.reshape(1, -1), *rows8, ema_rate, ema_damp, ema_in, ema_out,
        qk_gain, qk_bias, b_up.reshape(-1, 128),
    )


def finish_kernel(every, hu, bo, gt, shared, small, rate, damp, ein, eout, bmap,
                  f_down, f_up, f_mix, f_reset, f_value, f_hid, f_upd, f_bo, f_gt, f_shared,
                  g_rate, g_damp, g_in, g_out, v0, v1, v2, v3, v4, v5, g_bup, g_gain, g_bias, g_rel,
                  b_every, b_hu, b_bo, b_gt, b_shared, stage, isem, osem, psem):
    rows_in = [pltpu.make_async_copy(a, b, psem.at[k]) for k, (a, b) in enumerate(((bo, b_bo), (gt, b_gt), (shared, b_shared)))]
    passed = [pltpu.make_async_copy(a, b, psem.at[3 + k]) for k, (a, b) in enumerate(((b_bo, f_bo), (b_gt, f_gt), (b_shared, f_shared)))]
    CR, CC = stage.shape[1], stage.shape[2]
    half = CC // 2
    chunks = []

    def gather(sources, dst):
        chunks.append(([(a, b, slice(j * half, (j + 1) * half)) for j, (a, b) in enumerate(sources)], dst))

    def piece(core, i, r):
        at = (core, i, slice(r * CR, (r + 1) * CR))
        return every.at[at], b_every.at[at]

    def quarter(q, n):
        at = (q, slice(n * CR, (n + 1) * CR))
        return hu.at[at], b_hu.at[at]

    for core in range(2):
        for r in range(4):
            gather([piece(core, 0, r), piece(core, 1, r)], f_down.at[core * 4 * CR + r * CR : core * 4 * CR + (r + 1) * CR])
            gather([piece(core, 2, r), piece(core, 3, r)], f_up.at[r * CR : (r + 1) * CR, core * CC : (core + 1) * CC])
    for i, dst in ((4, f_mix), (5, f_reset), (6, f_value)):
        for r in range(4):
            gather([piece(0, i, r), piece(1, i, r)], dst.at[r * CR : (r + 1) * CR])
    for n, dst in ((0, f_hid), (2, f_upd)):
        for q in range(4):
            gather([quarter(q, n), quarter(q, n + 1)], dst.at[q * CR : (q + 1) * CR])
    ins, count = [], 0
    for parts, _ in chunks:
        ins.append([])
        for src, buf, _ in parts:
            copy = pltpu.make_async_copy(src, buf, isem.at[count])
            copy.start()
            ins[-1].append(copy)
            count += 1
    for copy in rows_in:
        copy.start()

    for t in range(2):
        for j in range(8):
            rows_ = slice(t * 8, t * 8 + 8)
            lanes = slice(j * 128, j * 128 + 128)
            gw = small[pl.ds(t * 64 + j, 8, stride=8), :]
            ga = small[pl.ds(128 + t * 64 + j, 8, stride=8), :]
            r_, d_ = rate[rows_, lanes], damp[rows_, lanes]
            i_, o_ = ein[rows_, lanes], eout[rows_, lanes]
            g_rate[rows_, lanes] = gw * (i_ * o_) - ga * d_
            g_damp[rows_, lanes] = -ga * r_
            g_in[rows_, lanes] = gw * (r_ * o_)
            g_out[rows_, lanes] = gw * (r_ * i_)
    for k, ref in enumerate((v0, v1, v2, v3, v4, v5)):
        ref[...] = small[256 + 8 * k : 264 + 8 * k, :]
    me = lax.axis_index("narrow")
    g_bup[...] = small[pl.ds(pl.multiple_of(304 + me * 16, 8), 16), :]
    g_gain[...] = small[336:338, :]
    g_bias[...] = small[338:340, :]
    n = bmap.shape[1]
    offs = jnp.broadcast_to(small[340:341, :], (n, n)).T
    which = jnp.broadcast_to(bmap[...].astype(F32), (n, n)).T
    lane = lax.broadcasted_iota(jnp.int32, (n, n), 1).astype(F32)
    hits = jnp.sum(jnp.where(which == lane, offs, 0.0), axis=0, keepdims=True)
    g_rel[...] = hits[:, 0 : g_rel.shape[1]]

    ring = stage.shape[0]
    outs = []
    for k, (parts, dst) in enumerate(chunks):
        if k >= ring:
            outs[k - ring].wait()
        for copy, (_, buf, at) in zip(ins[k], parts):
            copy.wait()

            @pl.loop(0, CR // 64)
            def _(t, buf=buf, at=at, k=k):
                rr = cols(t, 64)
                stage[k % ring, rr, at] = buf[rr, :].astype(F32)

        copy = pltpu.make_async_copy(stage.at[k % ring], dst, osem.at[k % ring])
        copy.start()
        outs.append(copy)
    for a, b in zip(rows_in, passed):
        a.wait()
        b.start()
    for copy in outs[len(chunks) - ring :] + passed:
        copy.wait()


def run_finish(every, hu, whole, shapes, small, rate, damp, ein, eout, bucket_map, nbuck):
    bmap = bucket_map.reshape(1, -1)
    D = rate.shape[1]
    square = jax.ShapeDtypeStruct((D, D), F32)
    outs = [jax.ShapeDtypeStruct(a.shape, F32) for a in shapes] + [square, square]
    outs += [jax.ShapeDtypeStruct(a.shape, a.dtype) for a in whole]
    kept = len(outs)
    outs += [jax.ShapeDtypeStruct(rate.shape, F32) for _ in range(4)]
    outs += [jax.ShapeDtypeStruct((8, 128), F32) for _ in range(6)]
    outs += [jax.ShapeDtypeStruct((16, 128), F32), jax.ShapeDtypeStruct((2, 128), F32), jax.ShapeDtypeStruct((2, 128), F32),
             jax.ShapeDtypeStruct((1, nbuck), F32)]
    anyspec = pl.BlockSpec(memory_space=pl.ANY)
    vspec = pl.BlockSpec(memory_space=pltpu.VMEM)
    dma = pltpu.SemaphoreType.DMA
    ring = 14
    res = pl.pallas_call(
        finish_kernel,
        out_shape=tuple(outs),
        in_specs=[anyspec] * 5 + [vspec] * 6,
        out_specs=tuple([anyspec] * kept + [vspec] * (len(outs) - kept)),
        scratch_shapes=[vm(every.shape, BF), vm(hu.shape, BF)] + [vm(a.shape, a.dtype) for a in whole] + [vm((ring, D // 4, D)), dma((72,)), dma((ring,)), dma((6,))],
        compiler_params=pltpu.CompilerParams(vmem_limit_bytes=60 * 1024 * 1024),
    )(every, hu, *whole, small, rate, damp, ein, eout, bmap)
    return res


def shards_fast(*args):
    bo, gt, every, hu, shared, small = run_main(*args)
    w_value, w_reset, w_mix = args[15:18]
    w_up, w_down = args[23], args[25]
    (tokens, cotangent, seq_lengths, bucket_map, norm1_gain, norm1_bias, ema_rate, ema_damp, ema_in, ema_out,
     ema_skip, w_shared, qk_gain, qk_bias, rel_bias) = args[:15]
    (down, up, mix, reset, value, hidden, update, bo, gt, shared, g_rate, g_damp, g_in, g_out, skip, n1g, n1b, bupd, n2g, n2b,
     g_bup, g_gain, g_bias, g_rel) = run_finish(
        every, hu, (bo, gt, shared), (w_down, w_up, w_mix, w_reset, w_value), small, ema_rate, ema_damp, ema_in, ema_out, bucket_map,
        rel_bias.shape[0])
    skip, n1g, n1b, bupd, n2g, n2b = [v.reshape(-1) for v in (skip, n1g, n1b, bupd, n2g, n2b)]
    return (bo, gt, n1g, n1b, g_rate, g_damp, g_in, g_out, skip, shared, g_gain, g_bias, g_rel.reshape(-1),
            value, reset, mix, hidden, update, bupd, n2g, n2b, up, g_bup.reshape(-1), down)


def solution(mesh):
    in_specs = (
        P(("wide", "narrow"), None),
        P(("wide", "narrow"), None),
        P("wide", None),
        P(),
        P(),
        P(),
        P(),
        P(),
        P(),
        P(),
        P(),
        P(),
        P(),
        P(),
        P(),
        P(None, "narrow"),
        P(None, "narrow"),
        P("narrow", None),
        P(),
        P(),
        P(),
        P(),
        P(),
        P(None, "narrow"),
        P("narrow"),
        P("narrow", None),
    )
    out_specs = (
        P(("wide", "narrow"), None),
        P(("wide", "narrow"), None),
        P(),
        P(),
        P(),
        P(),
        P(),
        P(),
        P(),
        P(),
        P(),
        P(),
        P(),
        P(None, "narrow"),
        P(None, "narrow"),
        P("narrow", None),
        P(),
        P(),
        P(),
        P(),
        P(),
        P(None, "narrow"),
        P("narrow"),
        P("narrow", None),
    )
    body = shards_fast if (mesh.shape["wide"], mesh.shape["narrow"]) == (16, 2) else shards
    return jax.shard_map(body, mesh=mesh, in_specs=in_specs, out_specs=out_specs, check_vma=False)
```
